32 devices in a mesh: nar: 4 (over x, core), wide: 8 (over z, y).
Axes of the slice: x: 2, y: 2, z: 4, core: 2. Of those that a mesh axis runs over, the one named last changes fastest.
Arguments:
- tokens: bfloat16 [32768, 768], P(('nar', 'wide')), may hold values from -6 to 6
- cotangent: bfloat16 [32768, 768], P(('nar', 'wide')), may hold values from -6 to 6
- image_ids: int32 [32, 1024], P(('nar', 'wide')), may hold values from -1 to 3, as said below
- w_in: bfloat16 [5376, 768], P('wide'), may hold values from -0.21875 to 0.21875
- w_out: bfloat16 [3840, 768], P('wide'), may hold values from -0.8164966 to 0.8164966
- gains: float32 [896], replicated, may hold values from 0.25 to 1.75
- mom_in: float32 [5376, 768], P('wide'), may hold values from -832 to 832
- mom_out: float32 [3840, 768], P('wide'), may hold values from -832 to 832
- gain_m: float32 [896], replicated, may hold values from -112 to 112
- gain_v: float32 [896], replicated, may hold values from 1092 to 6553
Outputs:
- result: bfloat16 [32768, 768], P(('nar', 'wide'))
- grad_tokens: bfloat16 [32768, 768], P(('nar', 'wide'))
- grad_w_in: float32 [5376, 768], P('wide')
- grad_w_out: float32 [3840, 768], P('wide')
- grad_gains: float32 [896], replicated
- mom_in_new: float32 [5376, 768], P('wide')
- mom_out_new: float32 [3840, 768], P('wide')
- gain_m_new: float32 [896], replicated
- gain_v_new: float32 [896], replicated
- w_in_new: float32 [5376, 768], P('wide')
- w_out_new: float32 [3840, 768], P('wide')
- gains_new: float32 [896], replicated
The draws below stay inside these ranges and needn't reach their ends.
Inputs may be any that keep to these rules, and one draw needn't show every extreme that they name: `image_ids`: each row is one packed sequence: images numbered 0 to 3 in increasing order, each a contiguous run of tokens (earlier ones may be empty, the last is not), followed by padding marked -1.
All inputs are finite; a program needn't handle non-finite values.
Results may differ from the reference program's by a relative error of at most 0.015.
Values may be sent and summed in bfloat16 or wider, within the bound.
No kernel may reach another device: no remote copies, remote signals or barrier semaphores. Data moves between devices by JAX's collectives and lax.ppermute only.
A program may use at most 320 MiB of HBM per device.

```python
import math
import jax
import jax.numpy as jnp
from jax import lax

D = 768
HEADS = 12
HEAD = 64
MLP = 3072
LEN = 1024
IMAGES = 4
SWEEPS = 5
STEP = 10
FIN = 5376
FOUT = 3840
GV = 896
SEQS = 32
TOKENS = 32768


def draw_image_ids(key, part):
    key = jax.random.fold_in(key, 11)
    key_pad, key_size = jax.random.split(key)
    seq_index = jnp.arange(SEQS, dtype=jnp.int32)
    pad_fixed = 2 * LEN * (SEQS - 1 - seq_index) // (3 * max(SEQS - 1, 1))
    pad_random = jax.random.randint(key_pad, (SEQS,), 0, LEN // 8 + 1, dtype=jnp.int32)
    live_count = LEN - pad_fixed - pad_random
    image_weights = jax.random.randint(key_size, (SEQS, IMAGES), 1, 9, dtype=jnp.int32)
    cumulative = jnp.cumsum(image_weights, axis=1)
    bounds = live_count[:, None] * cumulative[:, :-1] // cumulative[:, -1:]
    position = jnp.arange(LEN, dtype=jnp.int32)
    image_number = jnp.sum((position[None, :, None] >= bounds[:, None, :]).astype(jnp.int32), axis=2)
    return jnp.where(position[None, :] < live_count[:, None], image_number, -1).astype(jnp.int32)


def draw_w_out(key, part):
    key = jax.random.fold_in(key, 5)
    values = jnp.clip(jax.random.normal(key, (FOUT, D), jnp.float32), -4.0, 4.0)
    row_index = jnp.arange(FOUT)[:, None]
    scaling = jnp.where(row_index < D, (D // 32) ** (-0.5), MLP ** (-0.5))
    return (values * scaling).astype(jnp.bfloat16)


def rising_rows(key, row_total, base_scale, rise):
    key_values, key_rows = jax.random.split(key)
    values = jnp.clip(jax.random.normal(key_values, (row_total, D), jnp.float32), -4.0, 4.0)
    row_factor = jax.random.uniform(key_rows, (row_total, 1), jnp.float32, 0.7, 1.4)
    ramp = rise ** (jnp.arange(row_total, dtype=jnp.float32)[:, None] / (row_total - 1))
    return values * row_factor * ramp * (base_scale / rise ** 0.5)


def draw_mom_in(key, part):
    key = jax.random.fold_in(key, 7)
    return rising_rows(key, FIN, (TOKENS // 8) ** 0.5, 3.0)


def draw_mom_out(key, part):
    key = jax.random.fold_in(key, 9)
    return rising_rows(key, FOUT, (TOKENS // 8) ** 0.5, 3.0)


def levels(stream_key, dims, cuts, least, high):
    loudness, own = 1.0, jax.random.fold_in(stream_key, 6)
    for axis_at, blocks in cuts:
        steps = jnp.exp(jax.random.uniform(jax.random.fold_in(own, axis_at), (blocks,), jnp.float32, least / len(cuts), high / len(cuts)))
        loudness = loudness * jnp.repeat(steps, dims[axis_at] // blocks).reshape([-1 if axis == axis_at else 1 for axis in range(len(dims))])
    return loudness


def gaussian(key, extent, scale, bound, cuts=(), held_as=jnp.bfloat16):
    drawn = scale * jax.random.normal(key, extent, jnp.float32)
    if cuts:
        drawn = drawn * levels(key, extent, cuts, -0.22, 0.18)
    return jnp.clip(drawn, -bound, bound).astype(held_as)


def setup_inputs(seed: int = 0) -> dict:
    key_list = jax.random.split(jax.random.key(seed), 11)
    tokens = gaussian(key_list[0], (TOKENS, D), 1.0, 6.0, ((0, 32),))
    cotangent = gaussian(key_list[1], (TOKENS, D), 1.0, 6.0, ((0, 32),))
    image_ids = draw_image_ids(jax.random.fold_in(key_list[10], 71), 0)
    w_in = gaussian(key_list[3], (FIN, D), D ** -0.5, 0.21875, ((0, 8),))
    w_out = draw_w_out(jax.random.fold_in(key_list[10], 71), 0)
    gains = jnp.clip(1.0 + 0.15 * jax.random.normal(key_list[5], (GV,), jnp.float32), 0.25, 1.75)
    mom_in = draw_mom_in(jax.random.fold_in(key_list[10], 71), 0)
    mom_out = draw_mom_out(jax.random.fold_in(key_list[10], 71), 0)
    gain_m = gaussian(key_list[8], (GV,), ((TOKENS // 100) ** 0.5), 112.0, (), jnp.float32)
    gain_v = jnp.clip(jnp.exp(jax.random.uniform(key_list[9], (GV,), jnp.float32, math.log(1092.0), math.log(6553.0))), 1092.0, 6553.0)
    return {"tokens": tokens, "cotangent": cotangent, "image_ids": image_ids, "w_in": w_in, "w_out": w_out, "gains": gains, "mom_in": mom_in, "mom_out": mom_out, "gain_m": gain_m, "gain_v": gain_v}


highest = lax.Precision.HIGHEST
ns_linear = 3.4445
ns_cubic = -4.775
ns_quintic = 2.0315
muon_beta = 0.5
muon_rate = 0.8
muon_decay = 0.1
adam_rate = 0.8
adam_first = 0.9
adam_second = 0.95
adam_eps = 1e-08
norm_eps = 1e-06
masked_score = -1e+30

@jax.custom_vjp
def low(v):
    return lax.optimization_barrier(v.astype(jnp.bfloat16)).astype(jnp.float32)

@jax.custom_vjp
def low_back(v):
    return v

def low_keep(v):
    return (low(v), None)

def low_pass(kept, grad):
    return (grad,)

def back_keep(v):
    return (v, None)

def back_low(kept, grad):
    return (low(grad),)
low.defvjp(low_keep, low_pass)
low_back.defvjp(back_keep, back_low)

def normalize(values):
    center = values - lax.optimization_barrier(jnp.mean(values, axis=-1, keepdims=True))
    variance = lax.optimization_barrier(jnp.mean(center * center, axis=-1, keepdims=True))
    return center * lax.rsqrt(variance + norm_eps)

def attend_block(query_block, ids_block, key_seq, value_seq, ids_seq):
    scores = HEAD ** (-0.5) * jnp.einsum('qhd,khd->hqk', query_block, key_seq, precision=highest)
    scores = low_back(scores)
    allowed = ids_block[:, None] == ids_seq[None, :]
    scores = jnp.where(allowed[None], scores, masked_score)
    softmax_w = low(jax.nn.softmax(scores, axis=-1))
    return jnp.einsum('hqk,khd->qhd', softmax_w, value_seq, precision=highest)

def attend_sequence(inputs):
    query_seq, key_seq, value_seq, ids_seq = inputs
    block_rows = min(512, LEN)
    query_blocks = query_seq.reshape(LEN // block_rows, block_rows, HEADS, HEAD)
    ids_blocks = ids_seq.reshape(LEN // block_rows, block_rows)

    def one_block(pair):
        return attend_block(pair[0], pair[1], key_seq, value_seq, ids_seq)
    outputs = lax.map(jax.checkpoint(one_block), (query_blocks, ids_blocks))
    return outputs.reshape(LEN, HEADS, HEAD)

def layer(x_rows, gains, w_in, w_out, ids_group):
    ln_gain = gains[:D]
    q_gain = gains[D:D + HEAD]
    k_gain = gains[D + HEAD:]
    row_count = x_rows.shape[0]
    seq_count = row_count // LEN
    x_low = low(normalize(x_rows) * ln_gain)
    joined_rows = low_back(low(jnp.dot(x_low, w_in.T, precision=highest)))
    queries = joined_rows[:, :D].reshape(row_count, HEADS, HEAD)
    keys_part = joined_rows[:, D:2 * D].reshape(row_count, HEADS, HEAD)
    values_part = joined_rows[:, 2 * D:3 * D].reshape(row_count, HEADS, HEAD)
    upward = joined_rows[:, 3 * D:]
    query_low = low(normalize(queries) * q_gain)
    key_low = low(normalize(keys_part) * k_gain)
    shape_seq = (seq_count, LEN, HEADS, HEAD)
    attended = lax.map(attend_sequence, (query_low.reshape(shape_seq), key_low.reshape(shape_seq), values_part.reshape(shape_seq), ids_group))
    attended_low = low_back(low(attended.reshape(row_count, D)))
    active = low(jax.nn.gelu(upward, approximate=False))
    hidden = jnp.concatenate([attended_low, active], axis=1)
    return x_rows + jnp.dot(hidden, w_out, precision=highest)

def orthogonal(momentum):
    matrix = momentum / (jnp.sqrt(jnp.sum(momentum * momentum)) + 1e-07)
    for ns_sweep in range(SWEEPS):
        gram = jnp.dot(matrix.T, matrix, precision=highest)
        mixing = ns_cubic * gram + ns_quintic * jnp.dot(gram, gram, precision=highest)
        matrix = ns_linear * matrix + jnp.dot(matrix, mixing, precision=highest)
    return matrix

def reference(tokens, cotangent, image_ids, w_in, w_out, gains, mom_in, mom_out, gain_m, gain_v):
    group_seqs = 4
    groups = SEQS // group_seqs
    w_in_float = w_in.astype(jnp.float32)
    w_out_float = w_out.astype(jnp.float32)

    def one_group(sums, inputs):
        x_rows, cot_rows, ids_group = inputs
        live = (ids_group.reshape(-1) >= 0)[:, None]
        cot_float = cot_rows.astype(jnp.float32)
        grad_y = jnp.where(live, cot_float, jnp.zeros_like(cot_float))

        def local(x_arg, gains_arg, w_in_arg, w_out_arg):
            return layer(x_arg, gains_arg, w_in_arg, w_out_arg, ids_group)
        output, pullback = jax.vjp(local, x_rows.astype(jnp.float32), gains, w_in_float, w_out_float)
        grad_x, grad_g, grad_i, grad_o = pullback(grad_y)
        sums = (sums[0] + grad_g, sums[1] + grad_i, sums[2] + grad_o)
        return (sums, (output.astype(jnp.bfloat16), grad_x.astype(jnp.bfloat16)))
    start_sums = (jnp.zeros((GV,), jnp.float32), jnp.zeros((FIN, D), jnp.float32), jnp.zeros((FOUT, D), jnp.float32))
    inputs = (tokens.reshape(groups, group_seqs * LEN, D), cotangent.reshape(groups, group_seqs * LEN, D), image_ids.reshape(groups, group_seqs, LEN))
    sums, outputs = lax.scan(one_group, start_sums, inputs)
    grad_gains, grad_w_in, grad_w_out = sums
    result = outputs[0].reshape(TOKENS, D)
    grad_tokens = outputs[1].reshape(TOKENS, D)
    mom_in_new = muon_beta * mom_in + grad_w_in
    mom_out_new = muon_beta * mom_out + grad_w_out
    w_in_new = w_in_float * (1 - muon_rate * muon_decay) - muon_rate * (FIN / D) ** 0.5 * orthogonal(mom_in_new)
    w_out_new = w_out_float * (1 - muon_rate * muon_decay) - muon_rate * (FOUT / D) ** 0.5 * orthogonal(mom_out_new)
    gain_m_new = adam_first * gain_m + (1 - adam_first) * grad_gains
    gain_v_new = adam_second * gain_v + (1 - adam_second) * grad_gains * grad_gains
    gains_new = gains - adam_rate * (gain_m_new / (1 - adam_first ** STEP)) / (jnp.sqrt(gain_v_new / (1 - adam_second ** STEP)) + adam_eps)
    return (result, grad_tokens, grad_w_in, grad_w_out, grad_gains, mom_in_new, mom_out_new, gain_m_new, gain_v_new, w_in_new, w_out_new, gains_new)
```

```python
from functools import partial

import jax
import jax.numpy as jnp
from jax import lax
from jax.experimental import pallas as pl
from jax.experimental.pallas import tpu as pltpu
from jax.sharding import PartitionSpec as P

D = 768
HEADS = 12
HEAD = 64
LEN = 1024
STEP = 10
FIN = 5376
FOUT = 3840
QKV = 3 * D

f32 = jnp.float32
bf16 = jnp.bfloat16
ns_linear = 3.4445
ns_cubic = -4.775
ns_quintic = 2.0315
muon_beta = 0.5
muon_rate = 0.8
muon_decay = 0.1
adam_rate = 0.8
adam_first = 0.9
adam_second = 0.95
adam_eps = 1e-08
norm_eps = 1e-06
penalty = 16384.0
vmem_bytes = 60 * 1024 * 1024
tile_rows = 256
pair = 2 * HEAD


def normalize(values):
    center = values - jnp.mean(values, axis=-1, keepdims=True)
    variance = jnp.mean(center * center, axis=-1, keepdims=True)
    inverse = lax.rsqrt(variance + norm_eps)
    return (center * inverse, inverse)


def norm_backward(grad_scaled, normed, inverse, axis=-1):
    mean_grad = jnp.mean(grad_scaled, axis=axis, keepdims=True)
    mean_cross = jnp.mean(grad_scaled * normed, axis=axis, keepdims=True)
    return inverse * (grad_scaled - mean_grad - normed * mean_cross)


def nn(a, b):
    return jnp.dot(a, b, preferred_element_type=f32)


def contract(a, b, dim_a, dim_b):
    return lax.dot_general(a, b, (((dim_a,), (dim_b,)), ((), ())), preferred_element_type=f32)


def normalize_columns(columns):
    center = columns - jnp.mean(columns, axis=0, keepdims=True)
    variance = jnp.mean(center * center, axis=0, keepdims=True)
    inverse = lax.rsqrt(variance + norm_eps)
    return (center * inverse, inverse)


def attention_kernel(
    q_ref, k_ref, v_ref, do_ref, onek_ref, penq_ref, gq_ref, gk_ref,
    att_ref, dq_ref, dk_ref, dv_ref, ggq_ref, ggk_ref,
    kaug, qaug_t, vaug_t, vaug, qnat, klow_t, exps, out_t, doaug_t, donat,
):
    length = q_ref.shape[0]
    step = pl.program_id(0)
    q_t = q_ref[...].T
    k_t = k_ref[...].T
    v_t = v_ref[...].T
    do_t = do_ref[...].T
    q_gain = gq_ref[...]
    k_gain = gk_ref[...]
    att_parts, dq_parts, dk_parts, dv_parts = [], [], [], []
    q_gain_grad = jnp.zeros((HEAD, 1), f32)
    k_gain_grad = jnp.zeros((HEAD, 1), f32)
    for h in range(2):
        rows = slice(HEAD * h, HEAD * (h + 1))
        q_hat, q_inverse = normalize_columns(q_t[rows].astype(f32))
        k_hat, k_inverse = normalize_columns(k_t[rows].astype(f32))
        q_low = (q_hat * q_gain).astype(bf16)
        k_low = (k_hat * k_gain).astype(bf16)
        klow_t[...] = k_low
        kaug[:, :HEAD] = k_low.T
        kaug[:, HEAD:] = onek_ref[...]
        qaug_t[:HEAD, :] = (q_low.astype(f32) * HEAD ** (-0.5)).astype(bf16)
        qaug_t[HEAD:, :] = penq_ref[...]
        qnat[...] = q_low.T
        v_head = v_t[rows]
        vaug_t[:HEAD, :] = v_head
        vaug_t[HEAD:, :] = jnp.ones((16, length), bf16)
        vaug[:, :HEAD] = v_head.T
        vaug[:, HEAD:] = jnp.ones((length, 16), bf16)
        terms = jnp.exp(nn(kaug[...], qaug_t[...])).astype(bf16)
        exps[...] = terms
        out_t[...] = nn(vaug_t[...], terms)
        summed = out_t[...]
        inverse_sum = 1.0 / summed[HEAD : HEAD + 1]
        attended = summed[:HEAD] * inverse_sum
        att_parts.append(attended)
        do_head = do_t[rows].astype(f32)
        inner = -jnp.sum(do_head * attended, axis=0, keepdims=True) * inverse_sum
        do_low = (do_head * inverse_sum).astype(bf16)
        inner_high = inner.astype(bf16).astype(f32)
        extra = lax.broadcasted_iota(jnp.int32, (16, length), 0)
        extra = jnp.where(extra == 0, inner_high, jnp.where(extra == 1, inner - inner_high, 0.0))
        doaug_t[:HEAD, :] = do_low
        doaug_t[HEAD:, :] = extra.astype(bf16)
        donat[...] = do_low.T
        terms = exps[...]
        dscores = (terms.astype(f32) * nn(vaug[...], doaug_t[...])).astype(bf16)
        dvalue = nn(terms, donat[...])
        dkey = nn(dscores, qnat[...]).T * HEAD ** (-0.5)
        dquery = nn(klow_t[...], dscores) * HEAD ** (-0.5)
        q_gain_grad += jnp.sum(dquery * q_hat, axis=1, keepdims=True)
        k_gain_grad += jnp.sum(dkey * k_hat, axis=1, keepdims=True)
        dq_parts.append(norm_backward(dquery * q_gain, q_hat, q_inverse, 0))
        dk_parts.append(norm_backward(dkey * k_gain, k_hat, k_inverse, 0))
        dv_parts.append(dvalue.T)
    att_ref[...] = jnp.concatenate(att_parts, 0).T.astype(bf16)
    dq_ref[...] = jnp.concatenate(dq_parts, 0).T.astype(bf16)
    dk_ref[...] = jnp.concatenate(dk_parts, 0).T.astype(bf16)
    dv_ref[...] = jnp.concatenate(dv_parts, 0).T.astype(bf16)

    @pl.when(step == 0)
    def _():
        ggq_ref[...] = jnp.zeros_like(ggq_ref)
        ggk_ref[...] = jnp.zeros_like(ggk_ref)

    ggq_ref[...] += jnp.broadcast_to(q_gain_grad, ggq_ref.shape)
    ggk_ref[...] += jnp.broadcast_to(k_gain_grad, ggk_ref.shape)


def attention(joined, dattended, ids, q_gain, k_gain):
    length = joined.shape[0]
    pairs = D // pair
    image = jnp.where(ids < 0, 4, ids)
    number = jnp.arange(16)
    onek = (image[:, None] == number[None, :]).astype(bf16)
    penq = jnp.where(image[None, :] == number[:, None], 0.0, -penalty).astype(bf16)

    def block(part):
        return pl.BlockSpec((length, pair), lambda p: (0, part * pairs + p))

    def whole(shape):
        return pl.BlockSpec(shape, lambda p: (0, 0))

    out = jax.ShapeDtypeStruct((length, D), bf16)
    gain = jax.ShapeDtypeStruct((HEAD, 128), f32)
    outs = pl.pallas_call(
        attention_kernel,
        grid=(pairs,),
        in_specs=[
            block(0), block(1), block(2), block(0),
            whole((length, 16)), whole((16, length)), whole((HEAD, 1)), whole((HEAD, 1)),
        ],
        out_specs=[block(0)] * 4 + [whole((HEAD, 128))] * 2,
        out_shape=[out] * 4 + [gain] * 2,
        scratch_shapes=[
            pltpu.VMEM((length, HEAD + 16), bf16),
            pltpu.VMEM((HEAD + 16, length), bf16),
            pltpu.VMEM((HEAD + 16, length), bf16),
            pltpu.VMEM((length, HEAD + 16), bf16),
            pltpu.VMEM((length, HEAD), bf16),
            pltpu.VMEM((HEAD, length), bf16),
            pltpu.VMEM((length, length), bf16),
            pltpu.VMEM((HEAD + 16, length), f32),
            pltpu.VMEM((HEAD + 16, length), bf16),
            pltpu.VMEM((length, HEAD), bf16),
        ],
        compiler_params=pltpu.CompilerParams(vmem_limit_bytes=vmem_bytes),
        cost_estimate=pl.CostEstimate(
            flops=HEADS * 12 * length * length * 256,
            bytes_accessed=16 * length * D,
            transcendentals=HEADS * length * length,
        ),
        name="attention",
    )(joined, joined, joined, dattended, onek, penq, q_gain.reshape(HEAD, 1), k_gain.reshape(HEAD, 1))
    return (*outs[:4], outs[4][:, 0], outs[5][:, 0])


def gelu_pair(u):
    z = jnp.abs(u) * 0.7071067811865476
    t = 1.0 / (1.0 + 0.3275911 * z)
    e = jnp.exp(-z * z)
    poly = t * (0.127414796 + t * (-0.142248368 + t * (0.7107068705 + t * (-0.7265760135 + t * 0.5307027145))))
    half = poly * e
    phi = jnp.where(u >= 0, 1.0 - half, half)
    return (u * phi, phi + u * (0.3989422804014327 * e))


def mlp_kernel(x_ref, gy_ref, wu_ref, wd_ref, res_ref, gn_ref, gwu_ref, gwd_ref):
    @pl.when(pl.program_id(0) == 0)
    def _():
        res_ref[...] = jnp.zeros_like(res_ref)
        gn_ref[...] = jnp.zeros_like(gn_ref)

    x, grad_y, wu, wd = x_ref[...], gy_ref[...], wu_ref[...], wd_ref[...]
    upward = contract(x, wu, 1, 1).astype(bf16).astype(f32)
    grad_hidden = contract(grad_y, wd, 1, 1)
    active, slope = gelu_pair(upward)
    active = active.astype(bf16)
    dupward = (grad_hidden * slope).astype(bf16)
    res_ref[...] += contract(active, wd, 1, 0)
    gn_ref[...] += contract(dupward, wu, 1, 0)
    gwu_ref[...] = contract(dupward, x, 0, 0).astype(bf16)
    gwd_ref[...] = contract(active, grad_y, 0, 0).astype(bf16)


def mlp(x_low, grad_y, w_up, w_down):
    length = x_low.shape[0]
    hidden = w_up.shape[0]
    tile = 512 if hidden % 512 == 0 else hidden
    whole = pl.BlockSpec((length, D), lambda t: (0, 0))
    part = pl.BlockSpec((tile, D), lambda t: (t, 0))
    total = jax.ShapeDtypeStruct((length, D), f32)
    grad = jax.ShapeDtypeStruct((hidden, D), bf16)
    return pl.pallas_call(
        mlp_kernel,
        grid=(hidden // tile,),
        in_specs=[whole, whole, part, part],
        out_specs=[whole, whole, part, part],
        out_shape=[total, total, grad, grad],
        compiler_params=pltpu.CompilerParams(vmem_limit_bytes=vmem_bytes),
        cost_estimate=pl.CostEstimate(
            flops=18 * length * D * hidden,
            bytes_accessed=12 * length * D + 8 * hidden * D,
            transcendentals=length * hidden,
        ),
        name="mlp",
    )(x_low, grad_y, w_up, w_down)


def split(values):
    high = values.astype(bf16)
    return (high, (values - high.astype(f32)).astype(bf16))


def newton_kernel(g_ref, m_ref, w_ref, o_ref, gh, gl, sh, sl, ph, pw, g32, x32, *, rate, decay):
    count = D // tile_rows

    def span(i):
        return slice(i * tile_rows, (i + 1) * tile_rows)

    def store(high_ref, low_ref, i, j, value):
        high_ref[span(i), span(j)], low_ref[span(i), span(j)] = split(value)
        if i != j:
            high_ref[span(j), span(i)], low_ref[span(j), span(i)] = split(value.T)

    def symmetric(ah, al, bh, bl, post):
        for i in range(count):
            for j in range(i, count):
                rows, columns = span(i), span(j)
                post(
                    i,
                    j,
                    nn(ah[rows, :], bh[:, columns])
                    + (nn(ah[rows, :], bl[:, columns]) + nn(al[rows, :], bh[:, columns])),
                )

    def diagonal(size):
        shape = (size, size)
        return lax.broadcasted_iota(jnp.int32, shape, 0) == lax.broadcasted_iota(jnp.int32, shape, 1)

    gram = g_ref[...]
    trace = jnp.sum(jnp.where(diagonal(D), gram, 0.0), axis=0, keepdims=True)
    trace = jnp.sum(trace, axis=1, keepdims=True)
    inverse = 1.0 / (jnp.sqrt(trace) + 1e-07)
    gram = gram * (inverse * inverse)
    g32[...] = gram
    gh[...], gl[...] = split(gram)
    x32[...] = m_ref[...] * inverse

    def sweep(last):
        def keep_factor(i, j, value):
            value = ns_cubic * g32[span(i), span(j)] + ns_quintic * value
            if i == j:
                value = value + jnp.where(diagonal(tile_rows), ns_linear, 0.0)
            store(ph, pw, i, j, value)

        def keep_gram(i, j, value):
            g32[span(i), span(j)] = value
            store(gh, gl, i, j, value)

        symmetric(gh, gl, gh, gl, keep_factor)
        xh, xl = split(x32[...])
        x32[...] = nn(xh, ph[...]) + (nn(xh, pw[...]) + nn(xl, ph[...]))
        if not last:
            symmetric(gh, gl, ph, pw, partial(store, sh, sl))
            symmetric(sh, sl, ph, pw, keep_gram)

    @pl.loop(0, 4)
    def _(k):
        sweep(False)

    sweep(True)
    o_ref[...] = w_ref[...].astype(f32) * decay - rate * x32[...]


def newton(gram, momentum, weights, rate):
    rows = momentum.shape[0]
    whole = pl.BlockSpec(memory_space=pltpu.VMEM)
    return pl.pallas_call(
        partial(newton_kernel, rate=rate, decay=1 - muon_rate * muon_decay),
        in_specs=[whole] * 3,
        out_specs=whole,
        out_shape=jax.ShapeDtypeStruct((rows, D), f32),
        scratch_shapes=[pltpu.VMEM((D, D), bf16)] * 6 + [pltpu.VMEM((D, D), f32), pltpu.VMEM((rows, D), f32)],
        compiler_params=pltpu.CompilerParams(vmem_limit_bytes=vmem_bytes),
        cost_estimate=pl.CostEstimate(
            flops=6 * D * D * (9 * D + 5 * rows), bytes_accessed=4 * D * D + 10 * rows * D, transcendentals=0
        ),
        name="newton",
    )(gram, momentum, weights)


def gram_matrix(rows):
    return lax.dot_general(
        rows, rows, (((0,), (0,)), ((), ())), precision=lax.Precision.HIGH, preferred_element_type=f32
    )


def swap(values, axis, bit):
    size = lax.axis_size(axis)
    return lax.ppermute(values, axis, [(i, i ^ bit) for i in range(size)])


def bits(size):
    return [1 << b for b in range(size.bit_length() - 1)]


def sum_over(values, halving, full):
    sides = []
    for axis, bit in halving:
        upper = (lax.axis_index(axis) & bit) != 0
        size = values.shape[0] // 2
        low, high = values[:size], values[size:]
        kept, sent = jnp.where(upper, high, low), jnp.where(upper, low, high)
        values = kept + swap(sent, axis, bit)
        sides.append(upper)
    for axis, bit in full:
        values = values + swap(values, axis, bit)
    for (axis, bit), upper in zip(reversed(halving), reversed(sides), strict=True):
        other = swap(values, axis, bit)
        values = jnp.where(
            upper, jnp.concatenate([other, values], 0), jnp.concatenate([values, other], 0)
        )
    return values


def fold(gram):
    half = D // 2
    i = lax.broadcasted_iota(jnp.int32, (half, half), 0)
    j = lax.broadcasted_iota(jnp.int32, (half, half), 1)
    corner = jnp.where(i <= j, gram[:half, :half], gram[half:, half:])
    diagonal = jnp.sum(jnp.where(i == j, gram[half:, half:], 0.0), axis=0)
    return (jnp.concatenate([corner, gram[:half, half:]], axis=1), diagonal)


def unfold(folded, diagonal):
    half = D // 2
    i = lax.broadcasted_iota(jnp.int32, (half, half), 0)
    j = lax.broadcasted_iota(jnp.int32, (half, half), 1)
    corner, side = folded[:, :half], folded[:, half:]
    first = jnp.where(i <= j, corner, corner.T)
    last = jnp.where(i > j, corner, jnp.where(i == j, diagonal[None, :], corner.T))
    return jnp.concatenate(
        [jnp.concatenate([first, side], axis=1), jnp.concatenate([side.T, last], axis=1)], axis=0
    )


def on_device(tokens, cotangent, image_ids, w_in, w_out, gains, mom_in, mom_out, gain_m, gain_v):
    row_count = tokens.shape[0]
    rows_in = w_in.shape[0]
    rows_out = w_out.shape[0]
    nar_count = lax.axis_size("nar")
    wide_count = lax.axis_size("wide")
    nar_place = lax.axis_index("nar")
    share_in = rows_in // nar_count
    share_out = rows_out // nar_count
    everyone = ("wide", "nar")

    def share(rows, size):
        return lax.dynamic_slice_in_dim(rows, nar_place * size, size, 0)

    w_in_all = lax.all_gather(share(w_in, share_in), everyone, axis=0, tiled=True)
    w_out_all = lax.all_gather(share(w_out, share_out), everyone, axis=0, tiled=True)

    x_float = tokens.astype(f32)
    ln_gain = gains[:D]
    x_hat, x_inverse = normalize(x_float)
    x_low = (x_hat * ln_gain).astype(bf16)
    live = (image_ids.reshape(row_count) >= 0)[:, None]
    grad_y = jnp.where(live, cotangent, jnp.zeros_like(cotangent))

    w_qkv, w_up = w_in_all[:QKV], w_in_all[QKV:]
    w_att, w_down = w_out_all[:D], w_out_all[D:]
    joined = contract(x_low, w_qkv, 1, 1).astype(bf16)
    dattended = contract(grad_y, w_att, 1, 1).astype(bf16)
    attended, dqueries, dkeys, dvalues, q_gain_grad, k_gain_grad = attention(
        joined, dattended, image_ids.reshape(row_count), gains[D : D + HEAD], gains[D + HEAD :]
    )
    mlp_result, mlp_normed, grad_up, grad_down = mlp(x_low, grad_y, w_up, w_down)

    result = (x_float + (mlp_result + nn(attended, w_att))).astype(bf16)
    grad_qkv = jnp.concatenate([dqueries, dkeys, dvalues], axis=1)
    grad_normed = mlp_normed + nn(grad_qkv, w_qkv)
    ln_grad = jnp.sum(grad_normed * x_hat, axis=0)
    grad_tokens = (
        grad_y.astype(f32) + norm_backward(grad_normed * ln_gain, x_hat, x_inverse)
    ).astype(bf16)

    grad_out_local = jnp.concatenate([contract(attended, grad_y, 0, 0).astype(bf16), grad_down], axis=0)
    grad_in_local = jnp.concatenate([contract(grad_qkv, x_low, 0, 0).astype(bf16), grad_up], axis=0)
    part_out = lax.psum_scatter(grad_out_local, everyone, scatter_dimension=0, tiled=True)
    part_in = lax.psum_scatter(grad_in_local, everyone, scatter_dimension=0, tiled=True)
    grad_w_out = lax.all_gather(part_out, "nar", axis=0, tiled=True).astype(f32)
    grad_w_in = lax.all_gather(part_in, "nar", axis=0, tiled=True).astype(f32)
    mom_in_new = muon_beta * mom_in + grad_w_in
    mom_out_new = muon_beta * mom_out + grad_w_out

    folded_in, diagonal_in = fold(
        gram_matrix(muon_beta * share(mom_in, share_in) + part_in.astype(f32))
    )
    folded_out, diagonal_out = fold(
        gram_matrix(muon_beta * share(mom_out, share_out) + part_out.astype(f32))
    )
    wide_bits = bits(wide_count)
    halving = [("nar", 1), ("wide", wide_bits[0]), ("nar", 2)]
    full = [("wide", bit) for bit in wide_bits[1:]]
    gain_terms = jnp.concatenate([ln_grad, q_gain_grad, k_gain_grad])
    extra = jnp.concatenate([gain_terms, diagonal_in, diagonal_out])
    extra = jnp.pad(extra, (0, 64 * D - extra.shape[0])).reshape(64, D)
    summed = sum_over(jnp.concatenate([folded_in, folded_out, extra], axis=0), halving, full)
    half = D // 2
    extra = summed[2 * half :].reshape(64 * D)
    count = gain_terms.shape[0]
    grad_gains = extra[:count]
    gram_in = unfold(summed[:half], extra[count : count + half])
    gram_out = unfold(summed[half : 2 * half], extra[count + half : count + 2 * half])

    w_in_new = newton(gram_in, mom_in_new, w_in, muon_rate * (FIN / D) ** 0.5)
    w_out_new = newton(gram_out, mom_out_new, w_out, muon_rate * (FOUT / D) ** 0.5)
    gain_m_new = adam_first * gain_m + (1 - adam_first) * grad_gains
    gain_v_new = adam_second * gain_v + (1 - adam_second) * grad_gains * grad_gains
    gains_new = gains - adam_rate * (gain_m_new / (1 - adam_first**STEP)) / (
        jnp.sqrt(gain_v_new / (1 - adam_second**STEP)) + adam_eps
    )
    return (
        result,
        grad_tokens,
        grad_w_in,
        grad_w_out,
        grad_gains,
        mom_in_new,
        mom_out_new,
        gain_m_new,
        gain_v_new,
        w_in_new,
        w_out_new,
        gains_new,
    )


def solution(mesh):
    rows = P(("nar", "wide"), None)
    wide = P("wide", None)
    return jax.shard_map(
        on_device,
        mesh=mesh,
        in_specs=(rows, rows, rows, wide, wide, P(), wide, wide, P(), P()),
        out_specs=(rows, rows, wide, wide, P(), wide, wide, P(), P(), wide, wide, P()),
        check_vma=False,
    )
```

```python
from functools import partial

import jax
import jax.numpy as jnp
from jax import lax
from jax.experimental import pallas as pl
from jax.experimental.pallas import tpu as pltpu
from jax.sharding import PartitionSpec as P

D = 768
HEADS = 12
HEAD = 64
LEN = 1024
STEP = 10
FIN = 5376
FOUT = 3840
QKV = 3 * D

f32 = jnp.float32
bf16 = jnp.bfloat16
ns_linear = 3.4445
ns_cubic = -4.775
ns_quintic = 2.0315
muon_beta = 0.5
muon_rate = 0.8
muon_decay = 0.1
adam_rate = 0.8
adam_first = 0.9
adam_second = 0.95
adam_eps = 1e-08
norm_eps = 1e-06
penalty = 16384.0
vmem_bytes = 60 * 1024 * 1024
tile_rows = 256
extra_rows = 64
pair = 2 * HEAD


def normalize(values):
    center = values - jnp.mean(values, axis=-1, keepdims=True)
    variance = jnp.mean(center * center, axis=-1, keepdims=True)
    inverse = lax.rsqrt(variance + norm_eps)
    return (center * inverse, inverse)


def norm_backward(grad_scaled, normed, inverse, axis=-1):
    mean_grad = jnp.mean(grad_scaled, axis=axis, keepdims=True)
    mean_cross = jnp.mean(grad_scaled * normed, axis=axis, keepdims=True)
    return inverse * (grad_scaled - mean_grad - normed * mean_cross)


def nn(a, b):
    return jnp.dot(a, b, preferred_element_type=f32)


def contract(a, b, dim_a, dim_b):
    return lax.dot_general(a, b, (((dim_a,), (dim_b,)), ((), ())), preferred_element_type=f32)


def normalize_columns(columns):
    center = columns - jnp.mean(columns, axis=0, keepdims=True)
    variance = jnp.mean(center * center, axis=0, keepdims=True)
    inverse = lax.rsqrt(variance + norm_eps)
    return (center * inverse, inverse)


core_spec = pl.BlockSpec(memory_space=pltpu.SMEM)


def halves(values, core_ref, keep_ref, send_ref):
    half = D // 2
    left, right = values[:, :half], values[:, half:]
    first = core_ref[0] == 0
    keep_ref[...] = jnp.where(first, left, right).reshape(keep_ref.shape)
    send_ref[...] = jnp.where(first, right, left).reshape(send_ref.shape)


def forward_kernel(
    q_ref, k_ref, v_ref, onek_ref, penq_ref, gq_ref, gk_ref, gy_ref, core_ref,
    att_ref, terms_ref, exact_ref, sum_ref, keep_ref, send_ref, kaug, qaug_t, vaug_t,
):
    length = q_ref.shape[0]
    q_t = q_ref[...].T
    k_t = k_ref[...].T
    v_t = v_ref[...].T
    parts = []
    for h in range(2):
        rows = slice(HEAD * h, HEAD * (h + 1))
        q_hat, _ = normalize_columns(q_t[rows].astype(f32))
        k_hat, _ = normalize_columns(k_t[rows].astype(f32))
        q_low = (q_hat * gq_ref[...]).astype(bf16)
        k_low = (k_hat * gk_ref[...]).astype(bf16)
        kaug[h, :, :HEAD] = k_low.T
        kaug[h, :, HEAD:] = onek_ref[...]
        qaug_t[h, :HEAD, :] = (q_low.astype(f32) * HEAD ** (-0.5)).astype(bf16)
        qaug_t[h, HEAD:, :] = penq_ref[...]
        vaug_t[h, :HEAD, :] = v_t[rows]
        vaug_t[h, HEAD:, :] = jnp.ones((16, length), bf16)
        terms_ref[h] = jnp.exp(nn(kaug[h], qaug_t[h])).astype(bf16)
        summed = nn(vaug_t[h], terms_ref[h])
        inverse_sum = 1.0 / summed[HEAD : HEAD + 1]
        sum_ref[0, h : h + 1, :] = inverse_sum
        attended = summed[:HEAD] * inverse_sum
        exact_ref[rows, :] = attended
        parts.append(attended)
    attended = jnp.concatenate(parts, 0).astype(bf16)
    halves(nn(attended, gy_ref[...]).astype(bf16), core_ref, keep_ref, send_ref)
    att_ref[...] = attended.T


def attention_forward(joined, ids, q_gain, k_gain, grad_y, core):
    length = joined.shape[0]
    pairs = D // pair
    image = jnp.where(ids < 0, 4, ids)
    number = jnp.arange(16)
    onek = (image[:, None] == number[None, :]).astype(bf16)
    penq = jnp.where(image[None, :] == number[:, None], 0.0, -penalty).astype(bf16)

    def block(part):
        return pl.BlockSpec((length, pair), lambda p: (0, part * pairs + p))

    def whole(shape):
        return pl.BlockSpec(shape, lambda p: (0, 0))

    return pl.pallas_call(
        forward_kernel,
        grid=(pairs,),
        in_specs=[
            block(0), block(1), block(2),
            whole((length, 16)), whole((16, length)), whole((HEAD, 1)), whole((HEAD, 1)),
            whole((length, D)), core_spec,
        ],
        out_specs=[
            block(0),
            pl.BlockSpec((2, length, length), lambda p: (p, 0, 0)),
            pl.BlockSpec((pair, length), lambda p: (p, 0)),
            pl.BlockSpec((1, 8, length), lambda p: (p, 0, 0)),
            *[pl.BlockSpec((pair, D // 2), lambda p: (p, 0))] * 2,
        ],
        out_shape=[
            jax.ShapeDtypeStruct((length, D), bf16),
            jax.ShapeDtypeStruct((HEADS, length, length), bf16),
            jax.ShapeDtypeStruct((D, length), f32),
            jax.ShapeDtypeStruct((pairs, 8, length), f32),
            *[jax.ShapeDtypeStruct((D, D // 2), bf16)] * 2,
        ],
        scratch_shapes=[
            pltpu.VMEM((2, length, HEAD + 16), bf16),
            pltpu.VMEM((2, HEAD + 16, length), bf16),
            pltpu.VMEM((2, HEAD + 16, length), bf16),
        ],
        compiler_params=pltpu.CompilerParams(vmem_limit_bytes=vmem_bytes),
        cost_estimate=pl.CostEstimate(
            flops=HEADS * 4 * length * length * 256,
            bytes_accessed=16 * length * D + 2 * HEADS * length * length,
            transcendentals=HEADS * length * length,
        ),
        name="attention_forward",
    )(
        joined, joined, joined, onek, penq, q_gain.reshape(HEAD, 1), k_gain.reshape(HEAD, 1), grad_y, core
    )


def backward_kernel(
    q_ref, k_ref, v_ref, do_ref, terms_ref, exact_ref, sum_ref, gq_ref, gk_ref, x_ref, core_ref,
    dq_ref, dk_ref, dv_ref, keep_ref, send_ref, ggq_ref, ggk_ref,
    vaug, qnat, klow_t, doaug_t, donat,
):
    length = q_ref.shape[0]
    step = pl.program_id(0)
    q_t = q_ref[...].T
    k_t = k_ref[...].T
    v_t = v_ref[...].T
    do_t = do_ref[...].T
    q_gain = gq_ref[...]
    k_gain = gk_ref[...]
    dq_parts, dk_parts, dv_parts = [], [], []
    q_gain_grad = jnp.zeros((HEAD, 1), f32)
    k_gain_grad = jnp.zeros((HEAD, 1), f32)
    for h in range(2):
        rows = slice(HEAD * h, HEAD * (h + 1))
        q_hat, q_inverse = normalize_columns(q_t[rows].astype(f32))
        k_hat, k_inverse = normalize_columns(k_t[rows].astype(f32))
        klow_t[h] = (k_hat * k_gain).astype(bf16)
        qnat[h] = (q_hat * q_gain).astype(bf16).T
        vaug[h, :, :HEAD] = v_t[rows].T
        vaug[h, :, HEAD:] = jnp.ones((length, 16), bf16)
        inverse_sum = sum_ref[0, h : h + 1, :]
        do_head = do_t[rows].astype(f32)
        inner = -jnp.sum(do_head * exact_ref[rows, :], axis=0, keepdims=True) * inverse_sum
        do_low = (do_head * inverse_sum).astype(bf16)
        inner_high = inner.astype(bf16).astype(f32)
        extra = lax.broadcasted_iota(jnp.int32, (16, length), 0)
        extra = jnp.where(extra == 0, inner_high, jnp.where(extra == 1, inner - inner_high, 0.0))
        doaug_t[h, :HEAD, :] = do_low
        doaug_t[h, HEAD:, :] = extra.astype(bf16)
        donat[h] = do_low.T
        terms = terms_ref[h]
        dscores = (terms.astype(f32) * nn(vaug[h], doaug_t[h])).astype(bf16)
        dvalue = nn(terms, donat[h])
        dkey = nn(dscores, qnat[h]).T * HEAD ** (-0.5)
        dquery = nn(klow_t[h], dscores) * HEAD ** (-0.5)
        q_gain_grad += jnp.sum(dquery * q_hat, axis=1, keepdims=True)
        k_gain_grad += jnp.sum(dkey * k_hat, axis=1, keepdims=True)
        dq_parts.append(norm_backward(dquery * q_gain, q_hat, q_inverse, 0))
        dk_parts.append(norm_backward(dkey * k_gain, k_hat, k_inverse, 0))
        dv_parts.append(dvalue.T)
    grads = jnp.concatenate(dq_parts + dk_parts + dv_parts, 0).astype(bf16)
    halves(nn(grads, x_ref[...]).astype(bf16), core_ref, keep_ref, send_ref)
    dq_ref[...] = grads[:pair].T
    dk_ref[...] = grads[pair : 2 * pair].T
    dv_ref[...] = grads[2 * pair :].T

    @pl.when(step == 0)
    def _():
        ggq_ref[...] = jnp.zeros_like(ggq_ref)
        ggk_ref[...] = jnp.zeros_like(ggk_ref)

    ggq_ref[...] += jnp.broadcast_to(q_gain_grad, ggq_ref.shape)
    ggk_ref[...] += jnp.broadcast_to(k_gain_grad, ggk_ref.shape)


def attention_backward(joined, dattended, terms, exact, inverse_sum, q_gain, k_gain, x_low, core, first, count):
    length = joined.shape[0]
    pairs = D // pair

    def block(part, offset=first):
        return pl.BlockSpec((length, pair), lambda p: (0, part * pairs + offset + p))

    def whole(shape):
        return pl.BlockSpec(shape, lambda p: (0, 0))

    out = jax.ShapeDtypeStruct((length, count * pair), bf16)
    gain = jax.ShapeDtypeStruct((HEAD, 128), f32)
    outs = pl.pallas_call(
        backward_kernel,
        grid=(count,),
        in_specs=[
            block(0), block(1), block(2), block(0),
            pl.BlockSpec((2, length, length), lambda p: (first + p, 0, 0)),
            pl.BlockSpec((pair, length), lambda p: (first + p, 0)),
            pl.BlockSpec((1, 8, length), lambda p: (first + p, 0, 0)),
            whole((HEAD, 1)), whole((HEAD, 1)), whole((length, D)), core_spec,
        ],
        out_specs=[block(0, 0)] * 3
        + [pl.BlockSpec((3, pair, D // 2), lambda p: (0, p, 0))] * 2
        + [whole((HEAD, 128))] * 2,
        out_shape=[out] * 3 + [jax.ShapeDtypeStruct((3, count * pair, D // 2), bf16)] * 2 + [gain] * 2,
        scratch_shapes=[
            pltpu.VMEM((2, length, HEAD + 16), bf16),
            pltpu.VMEM((2, length, HEAD), bf16),
            pltpu.VMEM((2, HEAD, length), bf16),
            pltpu.VMEM((2, HEAD + 16, length), bf16),
            pltpu.VMEM((2, length, HEAD), bf16),
        ],
        compiler_params=pltpu.CompilerParams(vmem_limit_bytes=vmem_bytes),
        cost_estimate=pl.CostEstimate(
            flops=2 * count * 8 * length * length * 256,
            bytes_accessed=24 * length * count * pair + 4 * count * length * length,
            transcendentals=0,
        ),
        name="attention_backward",
    )(
        joined, joined, joined, dattended, terms, exact, inverse_sum,
        q_gain.reshape(HEAD, 1), k_gain.reshape(HEAD, 1), x_low, core,
    )
    return (outs[:3], outs[3], outs[4], outs[5][:, 0], outs[6][:, 0])


def gelu_pair(u):
    z = jnp.abs(u) * 0.7071067811865476
    t = 1.0 / (1.0 + 0.3275911 * z)
    e = jnp.exp(-z * z)
    poly = t * (0.127414796 + t * (-0.142248368 + t * (0.7107068705 + t * (-0.7265760135 + t * 0.5307027145))))
    half = poly * e
    phi = jnp.where(u >= 0, 1.0 - half, half)
    return (u * phi, phi + u * (0.3989422804014327 * e))


def mlp_kernel(
    x_ref, gy_ref, wu_ref, wd_ref, core_ref, res_ref, gn_ref, keep_up, send_up, keep_down, send_down
):
    @pl.when(pl.program_id(0) == 0)
    def _():
        res_ref[...] = jnp.zeros_like(res_ref)
        gn_ref[...] = jnp.zeros_like(gn_ref)

    x, grad_y, wu, wd = x_ref[...], gy_ref[...], wu_ref[...], wd_ref[...]
    upward = contract(x, wu, 1, 1).astype(bf16).astype(f32)
    grad_hidden = contract(grad_y, wd, 1, 1)
    active, slope = gelu_pair(upward)
    active = active.astype(bf16)
    dupward = (grad_hidden * slope).astype(bf16)
    res_ref[...] += contract(active, wd, 1, 0)
    gn_ref[...] += contract(dupward, wu, 1, 0)
    halves(contract(dupward, x, 0, 0).astype(bf16), core_ref, keep_up, send_up)
    halves(contract(active, grad_y, 0, 0).astype(bf16), core_ref, keep_down, send_down)


def mlp(x_low, grad_y, w_in_all, w_out_all, core):
    length = x_low.shape[0]
    hidden = w_in_all.shape[0] - QKV
    tile = D
    whole = pl.BlockSpec((length, D), lambda t: (0, 0))
    total = jax.ShapeDtypeStruct((length, D), f32)
    grad = jax.ShapeDtypeStruct((hidden, D // 2), bf16)
    return pl.pallas_call(
        mlp_kernel,
        grid=(hidden // tile,),
        in_specs=[
            whole,
            whole,
            pl.BlockSpec((tile, D), lambda t: (t + QKV // tile, 0)),
            pl.BlockSpec((tile, D), lambda t: (t + D // tile, 0)),
            core_spec,
        ],
        out_specs=[whole, whole] + [pl.BlockSpec((tile, D // 2), lambda t: (t, 0))] * 4,
        out_shape=[total, total] + [grad] * 4,
        compiler_params=pltpu.CompilerParams(vmem_limit_bytes=vmem_bytes),
        cost_estimate=pl.CostEstimate(
            flops=18 * length * D * hidden,
            bytes_accessed=12 * length * D + 8 * hidden * D,
            transcendentals=length * hidden,
        ),
        name="mlp",
    )(x_low, grad_y, w_in_all, w_out_all, core)


def split(values):
    high = values.astype(bf16)
    return (high, (values - high.astype(f32)).astype(bf16))


def newton_kernel(g_ref, x_ref, *refs, sweeps, opening, closing, rate):
    if closing:
        w_ref, o_ref, gh, gl, sh, sl, ph, pw, g32, x32 = refs
    else:
        g32, x32, gh, gl, sh, sl, ph, pw = refs
    count = D // tile_rows

    def span(i):
        return slice(i * tile_rows, (i + 1) * tile_rows)

    def store(high_ref, low_ref, i, j, value):
        high_ref[span(i), span(j)], low_ref[span(i), span(j)] = split(value)
        if i != j:
            high_ref[span(j), span(i)], low_ref[span(j), span(i)] = split(value.T)

    def symmetric(ah, al, bh, bl, post):
        for i in range(count):
            for j in range(i, count):
                rows, columns = span(i), span(j)
                post(
                    i,
                    j,
                    nn(ah[rows, :], bh[:, columns])
                    + (nn(ah[rows, :], bl[:, columns]) + nn(al[rows, :], bh[:, columns])),
                )

    def sweep(last):
        def keep_factor(i, j, value):
            value = ns_cubic * g32[span(i), span(j)] + ns_quintic * value
            if i == j:
                shape = (tile_rows, tile_rows)
                diagonal = lax.broadcasted_iota(jnp.int32, shape, 0) == lax.broadcasted_iota(jnp.int32, shape, 1)
                value = value + jnp.where(diagonal, ns_linear, 0.0)
            store(ph, pw, i, j, value)

        def keep_gram(i, j, value):
            g32[span(i), span(j)] = value
            if i != j:
                g32[span(j), span(i)] = value.T
            store(gh, gl, i, j, value)

        symmetric(gh, gl, gh, gl, keep_factor)
        xh, xl = split(x32[...])
        x32[...] = nn(xh, ph[...]) + (nn(xh, pw[...]) + nn(xl, ph[...]))
        if not last:
            symmetric(gh, gl, ph, pw, partial(store, sh, sl))
            symmetric(sh, sl, ph, pw, keep_gram)

    if opening:
        half = D // 2
        corner, side = g_ref[:half, :half], g_ref[:half, half:]
        i = lax.broadcasted_iota(jnp.int32, (half, half), 0)
        j = lax.broadcasted_iota(jnp.int32, (half, half), 1)
        corner_t = corner.T
        first = jnp.where(i <= j, corner, corner_t)
        last = jnp.where(i > j, corner, jnp.where(i == j, g_ref[half : half + 1, :half], corner_t))
        trace = jnp.sum(jnp.where(i == j, first + last, 0.0), axis=0, keepdims=True)
        trace = jnp.sum(trace, axis=1, keepdims=True)
        inverse = 1.0 / (jnp.sqrt(trace) + 1e-07)
        square = inverse * inverse
        g32[:half, :half] = first * square
        g32[half:, half:] = last * square
        g32[:half, half:] = side * square
        g32[half:, :half] = side.T * square
        x32[...] = x_ref[...] * inverse
    else:
        g32[...] = g_ref[...]
        x32[...] = x_ref[...]
    gh[...], gl[...] = split(g32[...])
    plain = sweeps - 1 if closing else sweeps
    if plain > 1:
        pl.loop(0, plain)(lambda k: sweep(False))
    elif plain == 1:
        sweep(False)
    if closing:
        sweep(True)
        o_ref[...] = w_ref[...].astype(f32) * (1 - muon_rate * muon_decay) - rate * x32[...]


def newton(gram, momentum, sweeps, opening=False, weights=None, rate=None):
    rows = momentum.shape[0]
    whole = pl.BlockSpec(memory_space=pltpu.VMEM)
    state = [pltpu.VMEM((D, D), f32), pltpu.VMEM((rows, D), f32)]
    parts = [pltpu.VMEM((D, D), bf16)] * 6
    closing = weights is not None
    moved = jax.ShapeDtypeStruct((rows, D), f32)
    return pl.pallas_call(
        partial(newton_kernel, sweeps=sweeps, opening=opening, closing=closing, rate=rate),
        in_specs=[whole] * (3 if closing else 2),
        out_specs=whole if closing else [whole] * 2,
        out_shape=moved if closing else [jax.ShapeDtypeStruct((D, D), f32), moved],
        scratch_shapes=parts + state if closing else parts,
        compiler_params=pltpu.CompilerParams(vmem_limit_bytes=vmem_bytes),
        cost_estimate=pl.CostEstimate(
            flops=6 * D * D * (2 * D + rows) * sweeps, bytes_accessed=8 * D * D + 10 * rows * D, transcendentals=0
        ),
        name="newton",
    )(gram, momentum, *([weights] if closing else []))


def gram_kernel(m_ref, extra_ref, core_ref, o_ref):
    half = D // 2
    left, right = slice(0, half), slice(half, D)

    def product(a, b):
        ah, al = split(m_ref[:, a])
        bh, bl = split(m_ref[:, b])
        return contract(ah, bh, 0, 0) + (contract(ah, bl, 0, 0) + contract(al, bh, 0, 0))

    o_ref[half:, :] = extra_ref[...]

    @pl.when(core_ref[0] == 0)
    def _():
        i = lax.broadcasted_iota(jnp.int32, (half, half), 0)
        j = lax.broadcasted_iota(jnp.int32, (half, half), 1)
        last = product(right, right)
        o_ref[:half, :] = jnp.where(i <= j, product(left, left), last)
        o_ref[half : half + 1, :] = jnp.sum(jnp.where(i == j, last, 0.0), axis=0, keepdims=True)

    @pl.when(core_ref[0] != 0)
    def _():
        o_ref[:half, :] = product(left, right)


def folded_gram(rows, extra, core):
    rows = jnp.pad(rows, ((0, -rows.shape[0] % 16), (0, 0)))
    whole = pl.BlockSpec(memory_space=pltpu.VMEM)
    return pl.pallas_call(
        gram_kernel,
        in_specs=[whole, whole, core_spec],
        out_specs=whole,
        out_shape=jax.ShapeDtypeStruct((D // 2 + extra_rows, D // 2), f32),
        compiler_params=pltpu.CompilerParams(vmem_limit_bytes=vmem_bytes),
        cost_estimate=pl.CostEstimate(
            flops=4 * rows.shape[0] * D * D, bytes_accessed=8 * rows.shape[0] * D, transcendentals=0
        ),
        name="gram",
    )(rows, extra, core)


def swap(values, axis, bit):
    size = lax.axis_size(axis)
    return lax.ppermute(values, axis, [(i, i ^ bit) for i in range(size)])


def bits(size):
    return [1 << b for b in range(size.bit_length() - 1)]


def take(values, index, axis):
    return lax.dynamic_index_in_dim(values, index, axis, keepdims=False)


def after(value, *others):
    return lax.optimization_barrier((value, *others))[0]


def exchange(values, axis, bit, fill=()):
    return after(swap(values, axis, bit), *fill)


def sum_over(values, halving, full, fills=()):
    fills = list(fills)

    def step(sent, axis, bit):
        fill = fills.pop(0)(sent) if fills else ()
        return exchange(sent, axis, bit, fill)

    sides = []
    for axis, bit in halving:
        side = (lax.axis_index(axis) // bit) % 2
        pieces = values.reshape(2, values.shape[0] // 2, values.shape[1])
        values = take(pieces, side, 0) + step(take(pieces, 1 - side, 0), axis, bit)
        sides.append(side)
    for axis, bit in full:
        values = values + step(values, axis, bit)
    for (axis, bit), side in zip(reversed(halving), reversed(sides), strict=True):
        values = join(values, step(values, axis, bit), side, 0).reshape(-1, values.shape[1])
    return join(values, step(values, "nar", 1), lax.axis_index("nar") % 2, 1).reshape(values.shape[0], -1)


def halve(values, axis, name, bit, fill):
    side = (lax.axis_index(name) // bit) % 2
    other = exchange(take(values, 1 - side, axis), name, bit, fill)
    return (take(values, side, axis).astype(f32) + other.astype(f32)).astype(bf16)


def scatter_stages(values):
    wide = lax.axis_size("wide")
    far = wide // 2
    rows, columns = values.shape[0] // (2 * wide), values.shape[1]
    cut = rows // 32 * 16
    place = lax.axis_index("wide") // 2
    values = values.reshape(far, 2, 2, rows, columns)

    def one(*fill):
        return (
            halve(values[:, :, :, :cut], 1, "wide", 1, fill),
            halve(values[:, :, :, cut:], 2, "nar", 2, fill),
        )

    def two(held, *fill):
        return jnp.concatenate(
            [halve(held[0], 1, "nar", 2, fill), halve(held[1], 1, "wide", 1, fill)], axis=1
        )

    def rest(held, *fill):
        total = take(held, place, 0).astype(f32)
        for shift in range(1, far):
            pairs = [(i, (i // 2 + shift) % far * 2 + i % 2) for i in range(wide)]
            sent = take(held, (place + shift) % far, 0)
            total = total + after(lax.ppermute(sent, "wide", pairs), *fill).astype(f32)
        return total.astype(bf16)

    return one, two, rest


def both_cores(values):
    other = swap(values, "nar", 1)
    return join(values, other, lax.axis_index("nar") % 2, 1).reshape(values.shape[0], D)


def both_chips(values):
    return join(values, swap(values, "nar", 2), lax.axis_index("nar") // 2, 0).reshape(-1, D)


def join(values, other, side, axis):
    ordered = [jnp.where(side == 0, values, other), jnp.where(side == 0, other, values)]
    return jnp.stack(ordered, axis)


def gather(values):
    wide = lax.axis_size("wide")
    rows = values.shape[0]
    far = wide // 2
    place, side = lax.axis_index("wide") // 2, lax.axis_index("wide") % 2
    chip, core = lax.axis_index("nar") // 2, lax.axis_index("nar") % 2
    held = lax.dynamic_update_index_in_dim(jnp.zeros((far, rows, D), values.dtype), values, place, 0)
    for shift in range(1, far):
        pairs = [(i, (i // 2 + shift) % far * 2 + i % 2) for i in range(wide)]
        held = lax.dynamic_update_index_in_dim(
            held, lax.ppermute(values, "wide", pairs), (place - shift) % far, 0
        )
    cut = rows // 32 * 16
    first, second = held[:, :cut], held[:, cut:]
    first = join(first, swap(first, "wide", 1), side, 1)
    second = join(second, swap(second, "nar", 2), chip, 1)
    first = join(first, swap(first, "nar", 2), chip, 2)
    second = join(second, swap(second, "wide", 1), side, 1)
    held = jnp.concatenate([first, second], axis=3)
    return join(held, swap(held, "nar", 1), core, 3).reshape(-1, D)


def on_device(tokens, cotangent, image_ids, w_in, w_out, gains, mom_in, mom_out, gain_m, gain_v):
    row_count = tokens.shape[0]
    rows_in = w_in.shape[0]
    rows_out = w_out.shape[0]
    nar_count = lax.axis_size("nar")
    wide_count = lax.axis_size("wide")
    nar_place = lax.axis_index("nar")
    share_in = rows_in // nar_count
    share_out = rows_out // nar_count
    everyone = ("wide", "nar")

    def share(rows, size):
        return lax.dynamic_slice_in_dim(rows, nar_place * size, size, 0)

    w_in_all = lax.all_gather(share(w_in, share_in), everyone, axis=0, tiled=True)
    w_out_all = gather(share(w_out, share_out))

    x_float = tokens.astype(f32)
    ln_gain = gains[:D]
    x_hat, x_inverse = normalize(x_float)
    x_low = (x_hat * ln_gain).astype(bf16)
    live = (image_ids.reshape(row_count) >= 0)[:, None]
    grad_y = jnp.where(live, cotangent, jnp.zeros_like(cotangent))

    core = (nar_place % 2).reshape(1)
    chip = nar_place // 2
    w_qkv = w_in_all[:QKV]
    w_att = w_out_all[:D]
    joined = contract(x_low, w_qkv, 1, 1).astype(bf16)
    dattended = contract(grad_y, w_att, 1, 1).astype(bf16)
    q_gain, k_gain = gains[D : D + HEAD], gains[D + HEAD :]
    attended, terms, exact, inverse_sum, keep_att, send_att = attention_forward(
        joined, image_ids.reshape(row_count), q_gain, k_gain, grad_y, core
    )
    mlp_result, mlp_normed, keep_up, send_up, keep_down, send_down = mlp(
        after(x_low, keep_att), grad_y, w_in_all, w_out_all, core
    )

    def backward(begin, count, *earlier):
        return attention_backward(
            joined, dattended, terms, exact, inverse_sum, q_gain, k_gain, after(x_low, *earlier), core, begin, count
        )

    def cores(keep, send, *fill):
        other = exchange(send, "nar", 1, fill)
        return (keep.astype(f32) + other.astype(f32)).astype(bf16).reshape(-1, D // 2)

    pairs = D // pair
    first = rows_in * 4 // 7
    second = rows_in - first
    parted = wide_count == 8 and first == D // 2 and rows_in == 672
    start = 96 * jnp.minimum(lax.axis_index("wide"), 3)
    row = lax.broadcasted_iota(jnp.int32, (rows_in, 1), 0)
    hidden = keep_up.shape[0]
    if parted:
        grads_a, keep_a, send_a, q_grad_a, k_grad_a = backward(0, pairs // 2, keep_up)
        up = cores(keep_up, send_up, keep_a)
        out = jnp.concatenate([cores(keep_att, send_att, keep_a), cores(keep_down, send_down, keep_a)], axis=0)
        out_one, out_two, out_rest = scatter_stages(out)
        grads_b, keep_b, send_b, q_grad_b, k_grad_b = backward(pairs // 2, pairs // 2, keep_a, out)
        held_a = cores(keep_a, send_a, keep_b)
        held_a = [held_a, up[:first]] + [up[rows_in * i : rows_in * i + first] for i in range(1, 5)]
        a_one, a_two, a_rest = scatter_stages(jnp.concatenate(held_a, axis=0))
        held_out = out_one(keep_b)
        held_b = cores(keep_b, send_b)
        held_b = [held_b] + [up[rows_in * i + first : rows_in * (i + 1)] for i in range(4)]
        b_one, b_two, b_rest = scatter_stages(jnp.concatenate(held_b, axis=0))
        held_out = out_two(held_out)
        held_a = a_one()
        part_out = out_rest(held_out)
        part_a = a_rest(a_two(held_a))
        part_b = b_rest(b_two(b_one()))
        q_gain_grad, k_gain_grad = q_grad_a + q_grad_b, k_grad_a + k_grad_b
        grad_qkv = [a for pieces in zip(grads_a, grads_b, strict=True) for a in pieces]
        part_in = jnp.concatenate([part_a, part_b], axis=0)

        def halved(rows):
            inside = lax.dynamic_slice_in_dim(rows, start, first, 0)
            others = jnp.where(row[:second] < start, rows[:second], rows[first:])
            return jnp.concatenate(
                [
                    lax.dynamic_slice_in_dim(inside, chip * (first // 2), first // 2, 0),
                    lax.dynamic_slice_in_dim(others, chip * (second // 2), second // 2, 0),
                ],
                axis=0,
            )

        def rejoined(rows):
            a, b = both_chips(rows[: first // 2]), both_chips(rows[first // 2 :])
            a = lax.dynamic_update_slice_in_dim(jnp.zeros((rows_in, D), a.dtype), a, start, 0)
            empty = jnp.zeros((first, D), b.dtype)
            below = jnp.concatenate([b, empty], axis=0)
            above = jnp.concatenate([empty, b], axis=0)
            inside = (row >= start) & (row < start + first)
            return jnp.where(inside, a, jnp.where(row < start, below, above))

    else:
        grad_qkv, keep_a, send_a, q_gain_grad, k_gain_grad = backward(0, pairs, keep_up)
        out = jnp.concatenate([cores(keep_att, send_att), cores(keep_down, send_down)], axis=0)
        out_one, out_two, out_rest = scatter_stages(out)
        part_out = out_rest(out_two(out_one()))
        both = jnp.concatenate([cores(keep_a, send_a), cores(keep_up, send_up)], axis=0)
        in_one, in_two, in_rest = scatter_stages(both)
        part_in = in_rest(in_two(in_one()))

        def halved(rows):
            return lax.dynamic_slice_in_dim(rows, chip * (rows_in // 2), rows_in // 2, 0)

        rejoined = both_chips

    grad_qkv = jnp.concatenate(grad_qkv, axis=1)
    result = (x_float + (mlp_result + nn(attended, w_att))).astype(bf16)
    grad_normed = mlp_normed + nn(grad_qkv, w_qkv)
    ln_grad = jnp.sum(grad_normed * x_hat, axis=0)
    grad_tokens = (
        grad_y.astype(f32) + norm_backward(grad_normed * ln_gain, x_hat, x_inverse)
    ).astype(bf16)

    wide_bits = bits(wide_count)
    halving = [("wide", wide_bits[0]), ("nar", 2)]
    full = [("wide", bit) for bit in wide_bits[1:]]
    gain_terms = jnp.concatenate([ln_grad, q_gain_grad, k_gain_grad])
    count = gain_terms.shape[0]
    half = D // 2
    extra = jnp.pad(gain_terms, (half, (extra_rows - 1) * half - count)).reshape(extra_rows, half)

    part_out = both_cores(part_out)
    half_out = lax.dynamic_slice_in_dim(mom_out, chip * (rows_out // 2), rows_out // 2, 0)
    folded_out = sum_over(
        folded_gram(muon_beta * half_out + part_out.astype(f32), jnp.zeros_like(extra), core), halving, full
    )
    grad_w_out = both_chips(part_out).astype(f32)
    mom_out_new = muon_beta * mom_out + grad_w_out

    part_in = both_cores(part_in)
    state = [folded_out, mom_out_new]

    def sweeps_out(opening):
        def fill(sent):
            state[:] = newton(after(state[0], sent), state[1], 1, opening=opening)
            return (state[1],)

        return fill

    folded_in = sum_over(
        folded_gram(muon_beta * halved(mom_in) + part_in.astype(f32), extra, core),
        halving,
        full,
        [sweeps_out(i == 0) for i in range(4)],
    )
    grad_w_in = rejoined(part_in).astype(f32)
    mom_in_new = muon_beta * mom_in + grad_w_in
    extra = (folded_in[half:, :half] + folded_in[half:, half:]).reshape(extra_rows * half)
    grad_gains = extra[half : half + count]
    w_out_new = newton(*state, 1, weights=w_out, rate=muon_rate * (FOUT / D) ** 0.5)
    w_in_new = newton(
        folded_in, mom_in_new, 5, opening=True, weights=w_in, rate=muon_rate * (FIN / D) ** 0.5
    )
    gain_m_new = adam_first * gain_m + (1 - adam_first) * grad_gains
    gain_v_new = adam_second * gain_v + (1 - adam_second) * grad_gains * grad_gains
    gains_new = gains - adam_rate * (gain_m_new / (1 - adam_first**STEP)) / (
        jnp.sqrt(gain_v_new / (1 - adam_second**STEP)) + adam_eps
    )
    return (
        result,
        grad_tokens,
        grad_w_in,
        grad_w_out,
        grad_gains,
        mom_in_new,
        mom_out_new,
        gain_m_new,
        gain_v_new,
        w_in_new,
        w_out_new,
        gains_new,
    )


def solution(mesh):
    rows = P(("nar", "wide"), None)
    wide = P("wide", None)
    return jax.shard_map(
        on_device,
        mesh=mesh,
        in_specs=(rows, rows, rows, wide, wide, P(), wide, wide, P(), P()),
        out_specs=(rows, rows, wide, wide, P(), wide, wide, P(), P(), wide, wide, P()),
        check_vma=False,
    )
```

```python
from functools import partial

import jax
import jax.numpy as jnp
from jax import lax
from jax.experimental import pallas as pl
from jax.experimental.pallas import tpu as pltpu
from jax.sharding import PartitionSpec as P

D = 768
HEADS = 12
HEAD = 64
LEN = 1024
STEP = 10
FIN = 5376
FOUT = 3840
QKV = 3 * D

f32 = jnp.float32
bf16 = jnp.bfloat16
ns_linear = 3.4445
ns_cubic = -4.775
ns_quintic = 2.0315
muon_beta = 0.5
muon_rate = 0.8
muon_decay = 0.1
adam_rate = 0.8
adam_first = 0.9
adam_second = 0.95
adam_eps = 1e-08
norm_eps = 1e-06
penalty = 16384.0
vmem_bytes = 60 * 1024 * 1024
tile_rows = 256
extra_rows = 32
pair = 2 * HEAD


def normalize(values):
    center = values - jnp.mean(values, axis=-1, keepdims=True)
    variance = jnp.mean(center * center, axis=-1, keepdims=True)
    inverse = lax.rsqrt(variance + norm_eps)
    return (center * inverse, inverse)


def norm_backward(grad_scaled, normed, inverse, axis=-1):
    mean_grad = jnp.mean(grad_scaled, axis=axis, keepdims=True)
    mean_cross = jnp.mean(grad_scaled * normed, axis=axis, keepdims=True)
    return inverse * (grad_scaled - mean_grad - normed * mean_cross)


def nn(a, b):
    return jnp.dot(a, b, preferred_element_type=f32)


def contract(a, b, dim_a, dim_b):
    return lax.dot_general(a, b, (((dim_a,), (dim_b,)), ((), ())), preferred_element_type=f32)


def normalize_columns(columns):
    center = columns - jnp.mean(columns, axis=0, keepdims=True)
    variance = jnp.mean(center * center, axis=0, keepdims=True)
    inverse = lax.rsqrt(variance + norm_eps)
    return (center * inverse, inverse)


core_spec = pl.BlockSpec(memory_space=pltpu.SMEM)


def halves(values, core_ref, keep_ref, send_ref):
    half = D // 2
    left, right = values[:, :half], values[:, half:]
    first = core_ref[0] == 0
    keep_ref[...] = jnp.where(first, left, right).reshape(keep_ref.shape)
    send_ref[...] = jnp.where(first, right, left).reshape(send_ref.shape)


def forward_kernel(
    q_ref, k_ref, v_ref, onek_ref, penq_ref, gq_ref, gk_ref, gy_ref, core_ref,
    att_ref, terms_ref, exact_ref, sum_ref, keep_ref, send_ref, kaug, qaug_t, vaug_t,
):
    length = q_ref.shape[0]
    q_t = q_ref[...].T
    k_t = k_ref[...].T
    v_t = v_ref[...].T
    parts = []
    for h in range(2):
        rows = slice(HEAD * h, HEAD * (h + 1))
        q_hat, _ = normalize_columns(q_t[rows].astype(f32))
        k_hat, _ = normalize_columns(k_t[rows].astype(f32))
        q_low = (q_hat * gq_ref[...]).astype(bf16)
        k_low = (k_hat * gk_ref[...]).astype(bf16)
        kaug[h, :, :HEAD] = k_low.T
        kaug[h, :, HEAD:] = onek_ref[...]
        qaug_t[h, :HEAD, :] = (q_low.astype(f32) * HEAD ** (-0.5)).astype(bf16)
        qaug_t[h, HEAD:, :] = penq_ref[...]
        vaug_t[h, :HEAD, :] = v_t[rows]
        vaug_t[h, HEAD:, :] = jnp.ones((16, length), bf16)
        terms_ref[h] = jnp.exp(nn(kaug[h], qaug_t[h])).astype(bf16)
        summed = nn(vaug_t[h], terms_ref[h])
        inverse_sum = 1.0 / summed[HEAD : HEAD + 1]
        sum_ref[0, h : h + 1, :] = inverse_sum
        attended = summed[:HEAD] * inverse_sum
        exact_ref[rows, :] = attended
        parts.append(attended)
    attended = jnp.concatenate(parts, 0).astype(bf16)
    halves(nn(attended, gy_ref[...]).astype(bf16), core_ref, keep_ref, send_ref)
    att_ref[...] = attended.T


def attention_forward(joined, ids, q_gain, k_gain, grad_y, core):
    length = joined.shape[0]
    pairs = D // pair
    image = jnp.where(ids < 0, 4, ids)
    number = jnp.arange(16)
    onek = (image[:, None] == number[None, :]).astype(bf16)
    penq = jnp.where(image[None, :] == number[:, None], 0.0, -penalty).astype(bf16)

    def block(part):
        return pl.BlockSpec((length, pair), lambda p: (0, part * pairs + p))

    def whole(shape):
        return pl.BlockSpec(shape, lambda p: (0, 0))

    call = pl.pallas_call(
        forward_kernel,
        grid=(pairs,),
        in_specs=[
            block(0), block(1), block(2),
            whole((length, 16)), whole((16, length)), whole((HEAD, 1)), whole((HEAD, 1)),
            whole((length, D)), core_spec,
        ],
        out_specs=[
            block(0),
            pl.BlockSpec((2, length, length), lambda p: (p, 0, 0)),
            pl.BlockSpec((pair, length), lambda p: (p, 0)),
            pl.BlockSpec((1, 8, length), lambda p: (p, 0, 0)),
            *[pl.BlockSpec((pair, D // 2), lambda p: (p, 0))] * 2,
        ],
        out_shape=[
            jax.ShapeDtypeStruct((length, D), bf16),
            jax.ShapeDtypeStruct((HEADS, length, length), bf16),
            jax.ShapeDtypeStruct((D, length), f32),
            jax.ShapeDtypeStruct((pairs, 8, length), f32),
            *[jax.ShapeDtypeStruct((D, D // 2), bf16)] * 2,
        ],
        scratch_shapes=[
            pltpu.VMEM((2, length, HEAD + 16), bf16),
            pltpu.VMEM((2, HEAD + 16, length), bf16),
            pltpu.VMEM((2, HEAD + 16, length), bf16),
        ],
        compiler_params=pltpu.CompilerParams(vmem_limit_bytes=vmem_bytes),
        cost_estimate=pl.CostEstimate(
            flops=HEADS * 4 * length * length * 256,
            bytes_accessed=16 * length * D + 2 * HEADS * length * length,
            transcendentals=HEADS * length * length,
        ),
        name="attention_forward",
    )
    return call(joined, joined, joined, onek, penq, q_gain.reshape(HEAD, 1), k_gain.reshape(HEAD, 1), grad_y, core)


def backward_kernel(
    q_ref, k_ref, v_ref, do_ref, terms_ref, exact_ref, sum_ref, gq_ref, gk_ref, x_ref,
    core_ref, *refs,
):
    grads_ref, keep_ref, send_ref, ggq_ref, ggk_ref, vaug, qnat, klow_t, doaug_t, donat = refs[-10:]
    length = q_ref.shape[0]
    step = pl.program_id(0)
    q_t = q_ref[...].T
    k_t = k_ref[...].T
    v_t = v_ref[...].T
    do_t = do_ref[...].T
    q_gain = gq_ref[...]
    k_gain = gk_ref[...]
    dq_parts, dk_parts, dv_parts = [], [], []
    q_gain_grad = jnp.zeros((HEAD, 1), f32)
    k_gain_grad = jnp.zeros((HEAD, 1), f32)
    for h in range(2):
        rows = slice(HEAD * h, HEAD * (h + 1))
        q_hat, q_inverse = normalize_columns(q_t[rows].astype(f32))
        k_hat, k_inverse = normalize_columns(k_t[rows].astype(f32))
        klow_t[h] = (k_hat * k_gain).astype(bf16)
        qnat[h] = (q_hat * q_gain).astype(bf16).T
        vaug[h, :, :HEAD] = v_t[rows].T
        vaug[h, :, HEAD:] = jnp.ones((length, 16), bf16)
        inverse_sum = sum_ref[0, h : h + 1, :]
        do_head = do_t[rows].astype(f32)
        inner = -jnp.sum(do_head * exact_ref[rows, :], axis=0, keepdims=True) * inverse_sum
        do_low = (do_head * inverse_sum).astype(bf16)
        inner_high = inner.astype(bf16).astype(f32)
        extra = lax.broadcasted_iota(jnp.int32, (16, length), 0)
        extra = jnp.where(extra == 0, inner_high, jnp.where(extra == 1, inner - inner_high, 0.0))
        doaug_t[h, :HEAD, :] = do_low
        doaug_t[h, HEAD:, :] = extra.astype(bf16)
        donat[h] = do_low.T
        terms = terms_ref[h]
        dscores = (terms.astype(f32) * nn(vaug[h], doaug_t[h])).astype(bf16)
        dvalue = nn(terms, donat[h])
        dkey = nn(dscores, qnat[h]).T * HEAD ** (-0.5)
        dquery = nn(klow_t[h], dscores) * HEAD ** (-0.5)
        q_gain_grad += jnp.sum(dquery * q_hat, axis=1, keepdims=True)
        k_gain_grad += jnp.sum(dkey * k_hat, axis=1, keepdims=True)
        dq_parts.append(norm_backward(dquery * q_gain, q_hat, q_inverse, 0))
        dk_parts.append(norm_backward(dkey * k_gain, k_hat, k_inverse, 0))
        dv_parts.append(dvalue.T)
    grads = jnp.concatenate(dq_parts + dk_parts + dv_parts, 0).astype(bf16)
    halves(nn(grads, x_ref[...]).astype(bf16), core_ref, keep_ref, send_ref)
    grads_ref[0] = grads[:pair].T
    grads_ref[1] = grads[pair : 2 * pair].T
    grads_ref[2] = grads[2 * pair :].T

    @pl.when(step == 0)
    def _():
        ggq_ref[...] = jnp.zeros_like(ggq_ref)
        ggk_ref[...] = jnp.zeros_like(ggk_ref)

    ggq_ref[...] += jnp.broadcast_to(q_gain_grad, ggq_ref.shape)
    ggk_ref[...] += jnp.broadcast_to(k_gain_grad, ggk_ref.shape)


def attention_backward(
    joined, dattended, terms, exact, inverse_sum, q_gain, k_gain, x_low, core, first, count, room, place=0, into=()
):
    length = joined.shape[0]
    pairs = D // pair

    def block(part):
        return pl.BlockSpec((length, pair), lambda p: (0, part * pairs + first + p))

    def whole(shape):
        return pl.BlockSpec(shape, lambda p: (0, 0))

    gain = jax.ShapeDtypeStruct((HEAD, 128), f32)
    call = pl.pallas_call(
        backward_kernel,
        grid=(count,),
        in_specs=[
            block(0), block(1), block(2), block(0),
            pl.BlockSpec((2, length, length), lambda p: (first + p, 0, 0)),
            pl.BlockSpec((pair, length), lambda p: (first + p, 0)),
            pl.BlockSpec((1, 8, length), lambda p: (first + p, 0, 0)),
            whole((HEAD, 1)), whole((HEAD, 1)), whole((length, D)), core_spec,
            *[pl.BlockSpec(memory_space=pl.ANY)] * len(into),
        ],
        out_specs=[pl.BlockSpec((3, length, pair), lambda p: (0, 0, p))]
        + [pl.BlockSpec((3, pair, D // 2), lambda p: (0, place + p, 0))] * 2
        + [whole((HEAD, 128))] * 2,
        out_shape=[jax.ShapeDtypeStruct((3, length, count * pair), bf16)]
        + [jax.ShapeDtypeStruct((3, room * pair, D // 2), bf16)] * 2 + [gain] * 2,
        input_output_aliases={11 + i: 1 + i for i in range(len(into))},
        scratch_shapes=[
            pltpu.VMEM((2, length, HEAD + 16), bf16),
            pltpu.VMEM((2, length, HEAD), bf16),
            pltpu.VMEM((2, HEAD, length), bf16),
            pltpu.VMEM((2, HEAD + 16, length), bf16),
            pltpu.VMEM((2, length, HEAD), bf16),
        ],
        compiler_params=pltpu.CompilerParams(vmem_limit_bytes=vmem_bytes),
        cost_estimate=pl.CostEstimate(
            flops=2 * count * 8 * length * length * 256,
            bytes_accessed=24 * length * count * pair + 4 * count * length * length,
            transcendentals=0,
        ),
        name="attention_backward",
    )
    outs = call(joined, joined, joined, dattended, terms, exact, inverse_sum, q_gain.reshape(HEAD, 1), k_gain.reshape(HEAD, 1), x_low, core, *into)
    return (*outs[:3], outs[3][:, 0], outs[4][:, 0])


def gelu_pair(u):
    z = jnp.abs(u) * 0.7071067811865476
    t = 1.0 / (1.0 + 0.3275911 * z)
    e = jnp.exp(-z * z)
    poly = t * (0.127414796 + t * (-0.142248368 + t * (0.7107068705 + t * (-0.7265760135 + t * 0.5307027145))))
    half = poly * e
    phi = jnp.where(u >= 0, 1.0 - half, half)
    return (u * phi, phi + u * (0.3989422804014327 * e))


def mlp_kernel(x_ref, gy_ref, wu_ref, wd_ref, core_ref, res_ref, gn_ref, keep_down, send_down, *refs, segments):
    step = pl.program_id(0)
    act_ref, dup_ref = refs[-2:]
    tile = wu_ref.shape[0]

    @pl.when(step == 0)
    def _():
        res_ref[...] = jnp.zeros_like(res_ref)
        gn_ref[...] = jnp.zeros_like(gn_ref)

    for begin in range(0, tile, tile_rows):
        units = slice(begin, begin + tile_rows)
        upward = contract(x_ref[...], wu_ref[units], 1, 1).astype(bf16).astype(f32)
        grad_hidden = contract(gy_ref[...], wd_ref[units], 1, 1)
        active, slope = gelu_pair(upward)
        act_ref[:, units] = active.astype(bf16)
        dup_ref[:, units] = (grad_hidden * slope).astype(bf16)
    active, dupward = act_ref[...], dup_ref[...]
    res_ref[...] += nn(active, wd_ref[...])
    gn_ref[...] += nn(dupward, wu_ref[...])
    halves(contract(active, gy_ref[...], 0, 0).astype(bf16), core_ref, keep_down, send_down)
    grad = contract(dupward, x_ref[...], 0, 0).astype(bf16)

    def place(index):
        filled = [0, 0]
        for begin, end, array in segments:
            low, high = max(begin, index * tile), min(end, (index + 1) * tile)
            if low < high:
                rows = slice(filled[array] + low - begin, filled[array] + high - begin)
                keep_ref, send_ref = refs[2 * array], refs[2 * array + 1]
                halves(
                    grad[low - index * tile : high - index * tile], core_ref, keep_ref.at[rows], send_ref.at[rows]
                )
            filled[array] += end - begin

    for index in range(segments[-1][1] // tile):
        pl.when(step == index)(partial(place, index))


def mlp(x_low, grad_y, w_in_all, w_out_all, core, segments):
    length = x_low.shape[0]
    hidden = w_in_all.shape[0] - QKV
    tile = D
    whole = pl.BlockSpec((length, D), lambda t: (0, 0))
    total = jax.ShapeDtypeStruct((length, D), f32)
    sizes = [sum(end - begin for begin, end, array in segments if array == i) for i in range(2)]
    sizes = [(size, D // 2) for size in sizes if size for _ in range(2)]
    call = pl.pallas_call(
        partial(mlp_kernel, segments=segments),
        grid=(hidden // tile,),
        in_specs=[
            whole,
            whole,
            pl.BlockSpec((tile, D), lambda t: (t + QKV // tile, 0)),
            pl.BlockSpec((tile, D), lambda t: (t + D // tile, 0)),
            core_spec,
        ],
        out_specs=[whole, whole]
        + [pl.BlockSpec((tile, D // 2), lambda t: (t, 0))] * 2
        + [pl.BlockSpec(size, lambda t: (0, 0)) for size in sizes],
        out_shape=[total, total]
        + [jax.ShapeDtypeStruct((hidden, D // 2), bf16)] * 2
        + [jax.ShapeDtypeStruct(size, bf16) for size in sizes],
        scratch_shapes=[pltpu.VMEM((length, tile), bf16)] * 2,
        compiler_params=pltpu.CompilerParams(vmem_limit_bytes=vmem_bytes),
        cost_estimate=pl.CostEstimate(
            flops=18 * length * D * hidden,
            bytes_accessed=12 * length * D + 8 * hidden * D,
            transcendentals=length * hidden,
        ),
        name="mlp",
    )
    return call(x_low, grad_y, w_in_all, w_out_all, core)


def input_kernel(*refs, calls):
    grads = refs[:calls]
    w_ref, normed_ref, tokens_ref, gy_ref, gain_ref, out_ref, ln_ref, total = refs[calls:]
    step = pl.program_id(0)

    @pl.when(step == 0)
    def _():
        total[...] = normed_ref[...]

    begin = 0
    sums = []
    for ref in grads:
        sums.append(nn(ref[0], w_ref[begin : begin + ref.shape[2], :]))
        begin += ref.shape[2]
    total[...] += sum(sums)

    @pl.when(step == pl.num_programs(0) - 1)
    def _():
        x_hat, x_inverse = normalize(tokens_ref[...].astype(f32))
        grad_normed = total[...]
        ln_ref[...] = jnp.sum(grad_normed * x_hat, axis=0, keepdims=True)
        back = norm_backward(grad_normed * gain_ref[...], x_hat, x_inverse)
        out_ref[...] = (gy_ref[...].astype(f32) + back).astype(bf16)


def input_gradient(grads, w_in_all, normed, tokens, grad_y, gain):
    length = tokens.shape[0]
    whole = pl.BlockSpec((length, D), lambda p: (0, 0))
    row = pl.BlockSpec((1, D), lambda p: (0, 0))
    call = pl.pallas_call(
        partial(input_kernel, calls=len(grads)),
        grid=(3,),
        in_specs=[pl.BlockSpec((1, length, grad.shape[2]), lambda p: (p, 0, 0)) for grad in grads]
        + [pl.BlockSpec((D, D), lambda p: (p, 0)), whole, whole, whole, row],
        out_specs=[whole, row],
        out_shape=[jax.ShapeDtypeStruct((length, D), bf16), jax.ShapeDtypeStruct((1, D), f32)],
        scratch_shapes=[pltpu.VMEM((length, D), f32)],
        compiler_params=pltpu.CompilerParams(vmem_limit_bytes=vmem_bytes),
        cost_estimate=pl.CostEstimate(
            flops=2 * length * D * QKV, bytes_accessed=20 * length * D, transcendentals=length
        ),
        name="input_gradient",
    )
    out, ln_grad = call(*grads, w_in_all, normed, tokens, grad_y, gain.reshape(1, D))
    return (out, ln_grad[0])


def split(values):
    high = values.astype(bf16)
    return (high, (values - high.astype(f32)).astype(bf16))


def newton_kernel(g_ref, x_ref, o_ref, gh, gl, sh, sl, ph, pw, g32, x32):
    count = D // tile_rows

    def span(i):
        return slice(i * tile_rows, (i + 1) * tile_rows)

    def store(high_ref, low_ref, i, j, value):
        high_ref[span(i), span(j)], low_ref[span(i), span(j)] = split(value)
        if i != j:
            high_ref[span(j), span(i)], low_ref[span(j), span(i)] = split(value.T)

    def symmetric(ah, al, bh, bl, post):
        for i in range(count):
            for j in range(i, count):
                rows, columns = span(i), span(j)
                post(
                    i,
                    j,
                    nn(ah[rows, :], bh[:, columns])
                    + (nn(ah[rows, :], bl[:, columns]) + nn(al[rows, :], bh[:, columns])),
                )

    def sweep(last):
        def keep_factor(i, j, value):
            value = ns_cubic * g32[span(i), span(j)] + ns_quintic * value
            if i == j:
                shape = (tile_rows, tile_rows)
                diagonal = lax.broadcasted_iota(jnp.int32, shape, 0) == lax.broadcasted_iota(jnp.int32, shape, 1)
                value = value + jnp.where(diagonal, ns_linear, 0.0)
            store(ph, pw, i, j, value)

        def keep_gram(i, j, value):
            g32[span(i), span(j)] = value
            store(gh, gl, i, j, value)

        symmetric(gh, gl, gh, gl, keep_factor)
        xh, xl = split(x32[...])
        x32[...] = nn(xh, ph[...]) + (nn(xh, pw[...]) + nn(xl, ph[...]))
        if not last:
            symmetric(gh, gl, ph, pw, partial(store, sh, sl))
            symmetric(sh, sl, ph, pw, keep_gram)

    half = D // 2
    corner, side = g_ref[:half, :half], g_ref[:half, half:]
    i = lax.broadcasted_iota(jnp.int32, (half, half), 0)
    j = lax.broadcasted_iota(jnp.int32, (half, half), 1)
    corner_t = corner.T
    first = jnp.where(i <= j, corner, corner_t)
    last = jnp.where(i > j, corner, jnp.where(i == j, g_ref[half : half + 1, :half], corner_t))
    trace = jnp.sum(jnp.where(i == j, first + last, 0.0), axis=0, keepdims=True)
    trace = jnp.sum(trace, axis=1, keepdims=True)
    inverse = 1.0 / (jnp.sqrt(trace) + 1e-07)
    square = inverse * inverse
    g32[:half, :half] = first * square
    g32[half:, half:] = last * square
    g32[:half, half:] = side * square
    g32[half:, :half] = side.T * square
    x32[...] = x_ref[...] * inverse
    gh[...], gl[...] = split(g32[...])

    @pl.loop(0, 4)
    def _(k):
        sweep(False)

    sweep(True)
    o_ref[...] = x32[...].astype(bf16)


def newton(folded, momentum):
    rows = momentum.shape[0]
    whole = pl.BlockSpec(memory_space=pltpu.VMEM)
    call = pl.pallas_call(
        newton_kernel,
        in_specs=[whole] * 2,
        out_specs=whole,
        out_shape=jax.ShapeDtypeStruct((rows, D), bf16),
        scratch_shapes=[pltpu.VMEM((D, D), bf16)] * 6 + [pltpu.VMEM((D, D), f32), pltpu.VMEM((rows, D), f32)],
        compiler_params=pltpu.CompilerParams(vmem_limit_bytes=vmem_bytes),
        cost_estimate=pl.CostEstimate(
            flops=30 * D * D * (2 * D + rows), bytes_accessed=4 * D * D + 6 * rows * D, transcendentals=0
        ),
        name="newton",
    )
    return call(folded, momentum)


def gram_kernel(m_ref, extra_ref, core_ref, o_ref):
    half = D // 2
    left, right = slice(0, half), slice(half, D)

    def product(a, b):
        ah, al = split(m_ref[:, a])
        bh, bl = split(m_ref[:, b])
        return contract(ah, bh, 0, 0) + (contract(ah, bl, 0, 0) + contract(al, bh, 0, 0))

    o_ref[half:, :] = extra_ref[...]

    @pl.when(core_ref[0] == 0)
    def _():
        i = lax.broadcasted_iota(jnp.int32, (half, half), 0)
        j = lax.broadcasted_iota(jnp.int32, (half, half), 1)
        last = product(right, right)
        o_ref[:half, :] = jnp.where(i <= j, product(left, left), last)
        o_ref[half : half + 1, :] = jnp.sum(jnp.where(i == j, last, 0.0), axis=0, keepdims=True)

    @pl.when(core_ref[0] != 0)
    def _():
        o_ref[:half, :] = product(left, right)


def folded_gram(rows, extra, core):
    rows = jnp.pad(rows, ((0, -rows.shape[0] % 16), (0, 0)))
    whole = pl.BlockSpec(memory_space=pltpu.VMEM)
    call = pl.pallas_call(
        gram_kernel,
        in_specs=[whole, whole, core_spec],
        out_specs=whole,
        out_shape=jax.ShapeDtypeStruct((D // 2 + extra_rows, D // 2), f32),
        compiler_params=pltpu.CompilerParams(vmem_limit_bytes=vmem_bytes),
        cost_estimate=pl.CostEstimate(
            flops=4 * rows.shape[0] * D * D, bytes_accessed=8 * rows.shape[0] * D, transcendentals=0
        ),
        name="gram",
    )
    return call(rows, extra, core)


def bits(size):
    return [1 << b for b in range(size.bit_length() - 1)]


def take(values, index, axis):
    return lax.dynamic_index_in_dim(values, index, axis, keepdims=False)


def after(value, *others):
    return lax.optimization_barrier((value, *others))[0]


def exchange(values, axis, bit, fill=()):
    size = lax.axis_size(axis)
    return after(lax.ppermute(values, axis, [(i, i ^ bit) for i in range(size)]), *fill)


def sum_steps(values, halving, full):
    columns = values.shape[1]
    fill = yield values
    sides = []
    for axis, bit in halving:
        side = (lax.axis_index(axis) // bit) % 2
        pieces = values.reshape(2, values.shape[0] // 2, columns)
        values = take(pieces, side, 0) + exchange(take(pieces, 1 - side, 0), axis, bit, fill)
        sides.append(side)
        fill = yield values
    for axis, bit in full:
        values = values + exchange(values, axis, bit, fill)
        fill = yield values
    for (axis, bit), side in zip(reversed(halving), reversed(sides), strict=True):
        values = join(values, exchange(values, axis, bit, fill), side, 0).reshape(-1, columns)
        fill = yield values
    other = exchange(values, "nar", 1, fill)
    yield join(values, other, lax.axis_index("nar") % 2, 1).reshape(values.shape[0], -1)


def halve(parts, axis, name, bit):
    side = (lax.axis_index(name) // bit) % 2
    sent = [take(part, 1 - side, axis) for part in parts]

    def receive(*fill):
        kept = jnp.concatenate([take(part, side, axis) for part in parts], axis=0)
        return (kept, exchange(jnp.concatenate(sent, axis=0), name, bit, fill))

    return sent, receive


def added(kept, other):
    return (kept.astype(f32) + other.astype(f32)).astype(bf16)


def scatter_one(*parts):
    wide = lax.axis_size("wide")
    columns = parts[0].shape[-1]
    rows = sum(part.size for part in parts) // (2 * wide * columns)
    cut = rows // 32 * 16
    parts = [part.reshape(-1, 2, 2, rows, columns) for part in parts]
    sent_a, receive_a = halve([part[:, :, :, :cut] for part in parts], 1, "wide", 1)
    sent_b, receive_b = halve([part[:, :, :, cut:] for part in parts], 2, "nar", 2)
    return sent_a + sent_b, lambda *fill: (added(*receive_a(*fill)), added(*receive_b(*fill)))


def scatter_two(held):
    sent_a, receive_a = halve(held[:1], 1, "nar", 2)
    sent_b, receive_b = halve(held[1:], 1, "wide", 1)

    def receive(*fill):
        kept, other = zip(receive_a(*fill), receive_b(*fill), strict=True)
        return added(jnp.concatenate(kept, axis=1), jnp.concatenate(other, axis=1))

    return sent_a + sent_b, receive


def scatter_rest(held):
    wide = lax.axis_size("wide")
    far = wide // 2
    place = lax.axis_index("wide") // 2
    sent = [take(held, (place + shift) % far, 0) for shift in range(1, far)]

    def receive(*fill):
        total = take(held, place, 0).astype(f32)
        for shift in range(1, far):
            pairs = [(i, (i // 2 + shift) % far * 2 + i % 2) for i in range(wide)]
            total = total + after(lax.ppermute(sent[shift - 1], "wide", pairs), *fill).astype(f32)
        return total.astype(bf16)

    return sent, receive


def both_cores(values, *fill):
    other = exchange(values, "nar", 1, fill)
    return join(values, other, lax.axis_index("nar") % 2, 1).reshape(values.shape[0], D)


def both_chips(values):
    return join(values, exchange(values, "nar", 2), lax.axis_index("nar") // 2, 0).reshape(-1, D)


def join(values, other, side, axis):
    ordered = [jnp.where(side == 0, values, other), jnp.where(side == 0, other, values)]
    return jnp.stack(ordered, axis)


def gather(values):
    wide = lax.axis_size("wide")
    rows = values.shape[0]
    far = wide // 2
    place, side = lax.axis_index("wide") // 2, lax.axis_index("wide") % 2
    chip, core = lax.axis_index("nar") // 2, lax.axis_index("nar") % 2
    held = lax.dynamic_update_index_in_dim(jnp.zeros((far, rows, D), values.dtype), values, place, 0)
    for shift in range(1, far):
        pairs = [(i, (i // 2 + shift) % far * 2 + i % 2) for i in range(wide)]
        held = lax.dynamic_update_index_in_dim(
            held, lax.ppermute(values, "wide", pairs), (place - shift) % far, 0
        )
    cut = rows // 32 * 16
    first, second = held[:, :cut], held[:, cut:]
    first = join(first, exchange(first, "wide", 1), side, 1)
    second = join(second, exchange(second, "nar", 2), chip, 1)
    first = join(first, exchange(first, "nar", 2), chip, 2)
    second = join(second, exchange(second, "wide", 1), side, 1)
    held = jnp.concatenate([first, second], axis=3)
    return join(held, exchange(held, "nar", 1), core, 3).reshape(-1, D)


def on_device(tokens, cotangent, image_ids, w_in, w_out, gains, mom_in, mom_out, gain_m, gain_v):
    row_count = tokens.shape[0]
    rows_in = w_in.shape[0]
    rows_out = w_out.shape[0]
    nar_count = lax.axis_size("nar")
    wide_count = lax.axis_size("wide")
    nar_place = lax.axis_index("nar")
    share_in = rows_in // nar_count
    share_out = rows_out // nar_count
    everyone = ("wide", "nar")

    def share(rows, size):
        return lax.dynamic_slice_in_dim(rows, nar_place * size, size, 0)

    w_in_all = lax.all_gather(share(w_in, share_in), everyone, axis=0, tiled=True)
    w_out_all = gather(share(w_out, share_out))

    x_float = tokens.astype(f32)
    ln_gain = gains[:D]
    x_hat, x_inverse = normalize(x_float)
    x_low = (x_hat * ln_gain).astype(bf16)
    live = (image_ids.reshape(row_count) >= 0)[:, None]
    grad_y = jnp.where(live, cotangent, jnp.zeros_like(cotangent))

    core = (nar_place % 2).reshape(1)
    chip = nar_place // 2
    half = D // 2
    pairs = D // pair
    q_gain, k_gain = gains[D : D + HEAD], gains[D + HEAD :]
    dattended = contract(grad_y, w_out_all[:D], 1, 1).astype(bf16)
    w_in_all = after(w_in_all, dattended)
    joined = contract(x_low, w_in_all[:QKV], 1, 1).astype(bf16)
    first = rows_in * 4 // 7
    second = rows_in - first
    parted = wide_count == 8 and first == half and rows_in == 672
    segments = [(0, FIN - QKV, 0)]
    if parted:
        segments = [(0, first, 0)]
        for i in range(4):
            segments += [(rows_in * i + first, rows_in * (i + 1), 1), (rows_in * (i + 1), rows_in * (i + 1) + first, 0)]
    mlp_result, mlp_normed, keep_down, send_down, *up_parts = mlp(
        x_low, grad_y, w_in_all, w_out_all, core, segments
    )
    attended, terms, exact, inverse_sum, keep_att, send_att = attention_forward(
        after(joined, keep_down), image_ids.reshape(row_count), q_gain, k_gain, grad_y, core
    )

    def backward(begin, count, earlier=(), **buffers):
        return attention_backward(
            joined, dattended, terms, exact, inverse_sum, q_gain, k_gain, after(x_low, *earlier), core, begin, count,
            **buffers,
        )

    def cores(keep, send, *fill):
        return added(keep, exchange(send, "nar", 1, fill)).reshape(-1, half)

    start = 96 * jnp.minimum(lax.axis_index("wide"), 3)
    row = lax.broadcasted_iota(jnp.int32, (rows_in, 1), 0)
    half_out = lax.dynamic_slice_in_dim(mom_out, chip * (rows_out // 2), rows_out // 2, 0)
    wide_bits = bits(wide_count)
    halving = [("wide", wide_bits[0]), ("nar", 2)]
    full = [("wide", bit) for bit in wide_bits[1:]]

    def begin_out(part):
        zeros = jnp.zeros((extra_rows, half), f32)
        steps = sum_steps(folded_gram(muon_beta * half_out + part.astype(f32), zeros, core), halving, full)
        return (steps, next(steps))

    if parted:
        keep_up_a, send_up_a, keep_up_b, send_up_b = up_parts
        down = cores(keep_down, send_down, keep_att)
        up_a = cores(keep_up_a, send_up_a, keep_att)
        up_b = cores(keep_up_b, send_up_b, keep_att)
        att = cores(keep_att, send_att)
        sent, receive = scatter_one(jnp.concatenate([att, down], axis=0))
        dqkv_a, keep_a, send_a, q_grad_a, k_grad_a = backward(0, 3, [up_a, up_b, *sent], room=3)
        sent, receive = scatter_two(receive(keep_a))
        dqkv_b, keep_b, send_b, q_grad_b, k_grad_b = backward(3, 1, [keep_a, *sent], room=3)
        sent_o, receive_o = scatter_rest(receive(keep_b))
        added_a = cores(keep_a, send_a, keep_b)
        sent_a, receive_a = scatter_one(jnp.concatenate([added_a, up_a], axis=0))
        dqkv_c, keep_b, send_b, q_grad_c, k_grad_c = backward(
            4, 2, [*sent_a, *sent_o], room=3, place=1, into=(keep_b, send_b)
        )
        sent_a, receive_a = scatter_two(receive_a(keep_b))
        added_b = cores(keep_b, send_b, *sent_a)
        sent_b, receive_b = scatter_one(added_b, up_b)
        sent_a, receive_a = scatter_rest(receive_a(*sent_b))
        part_out = both_cores(receive_o(*sent_a), *sent_a)
        sent_b, receive_b = scatter_two(receive_b(*sent_a))
        steps_out, folded_out = begin_out(after(part_out, *sent_b))
        sent_b, receive_b = scatter_rest(receive_b(folded_out))
        dqkv = [dqkv_a, dqkv_b, dqkv_c]
        grad_tokens, ln_grad = input_gradient(dqkv, w_in_all, after(mlp_normed, *sent_b), tokens, grad_y, ln_gain)
        part_a = receive_a(grad_tokens)
        part_b = receive_b(grad_tokens)
        folded_out = steps_out.send((part_b,))
        q_gain_grad, k_gain_grad = q_grad_a + q_grad_b + q_grad_c, k_grad_a + k_grad_b + k_grad_c
        part_in = jnp.concatenate([part_a, part_b], axis=0)

        def halved(rows):
            inside = lax.dynamic_slice_in_dim(rows, start, first, 0)
            others = jnp.where(row[:second] < start, rows[:second], rows[first:])
            return jnp.concatenate(
                [
                    lax.dynamic_slice_in_dim(inside, chip * (first // 2), first // 2, 0),
                    lax.dynamic_slice_in_dim(others, chip * (second // 2), second // 2, 0),
                ],
                axis=0,
            )

        def rejoined(rows):
            a, b = both_chips(rows[: first // 2]), both_chips(rows[first // 2 :])
            a = lax.dynamic_update_slice_in_dim(jnp.zeros((rows_in, D), a.dtype), a, start, 0)
            empty = jnp.zeros((first, D), b.dtype)
            below = jnp.concatenate([b, empty], axis=0)
            above = jnp.concatenate([empty, b], axis=0)
            inside = (row >= start) & (row < start + first)
            return jnp.where(inside, a, jnp.where(row < start, below, above))

    else:
        keep_up, send_up = up_parts
        dqkv, keep_a, send_a, q_gain_grad, k_gain_grad = backward(0, pairs, room=pairs)
        grad_tokens, ln_grad = input_gradient([dqkv], w_in_all, mlp_normed, tokens, grad_y, ln_gain)

        def scattered(*parts):
            held = scatter_one(jnp.concatenate(parts, axis=0))[1]()
            return scatter_rest(scatter_two(held)[1]())[1]()

        part_out = both_cores(scattered(cores(keep_att, send_att), cores(keep_down, send_down)))
        steps_out, folded_out = begin_out(part_out)
        part_in = scattered(cores(keep_a, send_a), cores(keep_up, send_up))

        def halved(rows):
            return lax.dynamic_slice_in_dim(rows, chip * (rows_in // 2), rows_in // 2, 0)

        rejoined = both_chips

    part_in = both_cores(part_in)
    gain_terms = jnp.concatenate([ln_grad, q_gain_grad, k_gain_grad])
    count = gain_terms.shape[0]
    extra = jnp.pad(gain_terms, (half, (extra_rows - 1) * half - count)).reshape(extra_rows, half)
    steps_in = sum_steps(folded_gram(muon_beta * halved(mom_in) + part_in.astype(f32), extra, core), halving, full)
    folded_in = next(steps_in)
    summed = []
    while folded_in.shape[1] < D:
        folded_in = steps_in.send(())
        summed.append(folded_in)
        if folded_out.shape[1] < D:
            folded_out = steps_out.send((folded_in,))
    grad_w_out = both_chips(after(part_out, summed[0])).astype(f32)
    mom_out_new = muon_beta * mom_out + grad_w_out
    grad_w_in = rejoined(after(part_in, summed[1])).astype(f32)
    mom_in_new = muon_beta * mom_in + grad_w_in
    extra = (folded_in[half:, :half] + folded_in[half:, half:]).reshape(extra_rows * half)
    grad_gains = extra[half : half + count]

    half_in, half_out = rows_in // 2, rows_out // 2
    rows = jnp.where(
        chip == 0,
        lax.dynamic_slice_in_dim(mom_in_new, core[0] * half_in, half_in, 0),
        jnp.pad(
            lax.dynamic_slice_in_dim(mom_out_new, core[0] * half_out, half_out, 0), ((0, half_in - half_out), (0, 0))
        ),
    )
    ortho = newton(jnp.where(chip == 0, folded_in, folded_out), rows)
    branch = mlp_result + nn(after(attended, ortho), w_out_all[:D])
    result = (tokens.astype(f32) + branch).astype(bf16)
    other = exchange(ortho, "nar", 2, (result,))
    ortho_in = jnp.where(chip == 0, ortho, other)
    ortho_out = jnp.where(chip == 0, other, ortho)[:half_out]
    ortho = jnp.concatenate([ortho_in, ortho_out], axis=0)
    other = exchange(ortho, "nar", 1)
    ortho_in = join(ortho[:half_in], other[:half_in], core[0], 0).reshape(rows_in, D)
    ortho_out = join(ortho[half_in:], other[half_in:], core[0], 0).reshape(rows_out, D)

    def updated(weights, ortho, size):
        rate = muon_rate * (size / D) ** 0.5
        return weights.astype(f32) * (1 - muon_rate * muon_decay) - rate * ortho.astype(f32)

    w_in_new = updated(w_in, ortho_in, FIN)
    w_out_new = updated(w_out, ortho_out, FOUT)
    gain_m_new = adam_first * gain_m + (1 - adam_first) * grad_gains
    gain_v_new = adam_second * gain_v + (1 - adam_second) * grad_gains * grad_gains
    gains_new = gains - adam_rate * (gain_m_new / (1 - adam_first**STEP)) / (
        jnp.sqrt(gain_v_new / (1 - adam_second**STEP)) + adam_eps
    )
    return (
        result,
        grad_tokens,
        grad_w_in,
        grad_w_out,
        grad_gains,
        mom_in_new,
        mom_out_new,
        gain_m_new,
        gain_v_new,
        w_in_new,
        w_out_new,
        gains_new,
    )


def solution(mesh):
    rows = P(("nar", "wide"), None)
    wide = P("wide", None)
    return jax.shard_map(
        on_device,
        mesh=mesh,
        in_specs=(rows, rows, rows, wide, wide, P(), wide, wide, P(), P()),
        out_specs=(rows, rows, wide, wide, P(), wide, wide, P(), P(), wide, wide, P()),
        check_vma=False,
    )
```

```python
from functools import partial

import jax
import jax.numpy as jnp
from jax import lax
from jax.experimental import pallas as pl
from jax.experimental.pallas import tpu as pltpu
from jax.sharding import PartitionSpec as P

D = 768
HEADS = 12
HEAD = 64
LEN = 1024
STEP = 10
FIN = 5376
FOUT = 3840
QKV = 3 * D

f32 = jnp.float32
bf16 = jnp.bfloat16
ns_linear = 3.4445
ns_cubic = -4.775
ns_quintic = 2.0315
muon_beta = 0.5
muon_rate = 0.8
muon_decay = 0.1
adam_rate = 0.8
adam_first = 0.9
adam_second = 0.95
adam_eps = 1e-08
norm_eps = 1e-06
penalty = 16384.0
vmem_bytes = 60 * 1024 * 1024
tile_rows = 256
extra_rows = 32
pair = 2 * HEAD


def normalize(values):
    center = values - jnp.mean(values, axis=-1, keepdims=True)
    variance = jnp.mean(center * center, axis=-1, keepdims=True)
    inverse = lax.rsqrt(variance + norm_eps)
    return (center * inverse, inverse)


def norm_backward(grad_scaled, normed, inverse, axis=-1):
    mean_grad = jnp.mean(grad_scaled, axis=axis, keepdims=True)
    mean_cross = jnp.mean(grad_scaled * normed, axis=axis, keepdims=True)
    return inverse * (grad_scaled - mean_grad - normed * mean_cross)


def nn(a, b):
    return jnp.dot(a, b, preferred_element_type=f32)


def contract(a, b, dim_a, dim_b):
    return lax.dot_general(a, b, (((dim_a,), (dim_b,)), ((), ())), preferred_element_type=f32)


def normalize_columns(columns):
    center = columns - jnp.mean(columns, axis=0, keepdims=True)
    variance = jnp.mean(center * center, axis=0, keepdims=True)
    inverse = lax.rsqrt(variance + norm_eps)
    return (center * inverse, inverse)


core_spec = pl.BlockSpec(memory_space=pltpu.SMEM)


def halves(values, core_ref, keep_ref, send_ref):
    half = D // 2
    left, right = values[:, :half], values[:, half:]
    first = core_ref[0] == 0
    keep_ref[...] = jnp.where(first, left, right).reshape(keep_ref.shape)
    send_ref[...] = jnp.where(first, right, left).reshape(send_ref.shape)


def forward_kernel(
    x_ref, gy_ref, wq_ref, wk_ref, wv_ref, wa_ref, onek_ref, penq_ref, gq_ref, gk_ref, core_ref,
    joined_ref, do_ref, att_ref, terms_ref, exact_ref, sum_ref, keep_ref, send_ref, kaug, qaug_t, vaug_t,
):
    length = x_ref.shape[0]
    weights = jnp.concatenate([wq_ref[...], wk_ref[...], wv_ref[...]], axis=0)
    joined = contract(weights, x_ref[...], 1, 1).astype(bf16)
    for i in range(3):
        joined_ref[i] = joined[i * pair : (i + 1) * pair]
    do_ref[...] = contract(wa_ref[...], gy_ref[...], 1, 1).astype(bf16)
    parts = []
    for h in range(2):
        rows = slice(HEAD * h, HEAD * (h + 1))
        q_hat, _ = normalize_columns(joined_ref[0, rows, :].astype(f32))
        k_hat, _ = normalize_columns(joined_ref[1, rows, :].astype(f32))
        q_low = (q_hat * gq_ref[...]).astype(bf16)
        k_low = (k_hat * gk_ref[...]).astype(bf16)
        kaug[h, :, :HEAD] = k_low.T
        kaug[h, :, HEAD:] = onek_ref[...]
        qaug_t[h, :HEAD, :] = (q_low.astype(f32) * HEAD ** (-0.5)).astype(bf16)
        qaug_t[h, HEAD:, :] = penq_ref[...]
        vaug_t[h, :HEAD, :] = joined_ref[2, rows, :]
        vaug_t[h, HEAD:, :] = jnp.ones((16, length), bf16)
        terms_ref[h] = jnp.exp(nn(kaug[h], qaug_t[h])).astype(bf16)
        summed = nn(vaug_t[h], terms_ref[h])
        inverse_sum = 1.0 / summed[HEAD : HEAD + 1]
        sum_ref[0, h : h + 1, :] = inverse_sum
        attended = summed[:HEAD] * inverse_sum
        exact_ref[rows, :] = attended
        parts.append(attended)
    attended = jnp.concatenate(parts, 0).astype(bf16)
    halves(nn(attended, gy_ref[...]).astype(bf16), core_ref, keep_ref, send_ref)
    att_ref[...] = attended.T


def attention_forward(x_low, grad_y, w_in_all, w_out_all, ids, q_gain, k_gain, core):
    length = x_low.shape[0]
    pairs = D // pair
    image = jnp.where(ids < 0, 4, ids)
    number = jnp.arange(16)
    onek = (image[:, None] == number[None, :]).astype(bf16)
    penq = jnp.where(image[None, :] == number[:, None], 0.0, -penalty).astype(bf16)

    def rows(part):
        return pl.BlockSpec((pair, D), lambda p: (part * pairs + p, 0))

    def whole(shape):
        return pl.BlockSpec(shape, lambda p: (0, 0))

    call = pl.pallas_call(
        forward_kernel,
        grid=(pairs,),
        in_specs=[
            whole((length, D)), whole((length, D)), rows(0), rows(1), rows(2), rows(0),
            whole((length, 16)), whole((16, length)), whole((HEAD, 1)), whole((HEAD, 1)), core_spec,
        ],
        out_specs=[
            pl.BlockSpec((3, pair, length), lambda p: (0, p, 0)),
            pl.BlockSpec((pair, length), lambda p: (p, 0)),
            pl.BlockSpec((length, pair), lambda p: (0, p)),
            pl.BlockSpec((2, length, length), lambda p: (p, 0, 0)),
            pl.BlockSpec((pair, length), lambda p: (p, 0)),
            pl.BlockSpec((1, 8, length), lambda p: (p, 0, 0)),
            *[pl.BlockSpec((pair, D // 2), lambda p: (p, 0))] * 2,
        ],
        out_shape=[
            jax.ShapeDtypeStruct((3, D, length), bf16),
            jax.ShapeDtypeStruct((D, length), bf16),
            jax.ShapeDtypeStruct((length, D), bf16),
            jax.ShapeDtypeStruct((HEADS, length, length), bf16),
            jax.ShapeDtypeStruct((D, length), f32),
            jax.ShapeDtypeStruct((pairs, 8, length), f32),
            *[jax.ShapeDtypeStruct((D, D // 2), bf16)] * 2,
        ],
        scratch_shapes=[
            pltpu.VMEM((2, length, HEAD + 16), bf16),
            pltpu.VMEM((2, HEAD + 16, length), bf16),
            pltpu.VMEM((2, HEAD + 16, length), bf16),
        ],
        compiler_params=pltpu.CompilerParams(vmem_limit_bytes=vmem_bytes),
        cost_estimate=pl.CostEstimate(
            flops=HEADS * 4 * length * length * 256,
            bytes_accessed=16 * length * D + 2 * HEADS * length * length,
            transcendentals=HEADS * length * length,
        ),
        name="attention_forward",
    )
    return call(
        x_low, grad_y, w_in_all, w_in_all, w_in_all, w_out_all, onek, penq,
        q_gain.reshape(HEAD, 1), k_gain.reshape(HEAD, 1), core,
    )


def backward_kernel(
    joined_ref, do_ref, terms_ref, exact_ref, sum_ref, gq_ref, gk_ref, x_ref, core_ref, *refs,
):
    grads_ref, keep_ref, send_ref, ggq_ref, ggk_ref, vaug, qnat, klow_t, doaug_t, donat = refs[-10:]
    length = x_ref.shape[0]
    step = pl.program_id(0)
    q_gain = gq_ref[...]
    k_gain = gk_ref[...]
    dq_parts, dk_parts, dv_parts = [], [], []
    q_gain_grad = jnp.zeros((HEAD, 1), f32)
    k_gain_grad = jnp.zeros((HEAD, 1), f32)
    for h in range(2):
        rows = slice(HEAD * h, HEAD * (h + 1))
        q_hat, q_inverse = normalize_columns(joined_ref[0, rows, :].astype(f32))
        k_hat, k_inverse = normalize_columns(joined_ref[1, rows, :].astype(f32))
        klow_t[h] = (k_hat * k_gain).astype(bf16)
        qnat[h] = (q_hat * q_gain).astype(bf16).T
        vaug[h, :, :HEAD] = joined_ref[2, rows, :].T
        vaug[h, :, HEAD:] = jnp.ones((length, 16), bf16)
        inverse_sum = sum_ref[0, h : h + 1, :]
        do_head = do_ref[rows, :].astype(f32)
        inner = -jnp.sum(do_head * exact_ref[rows, :], axis=0, keepdims=True) * inverse_sum
        do_low = (do_head * inverse_sum).astype(bf16)
        inner_high = inner.astype(bf16).astype(f32)
        extra = lax.broadcasted_iota(jnp.int32, (16, length), 0)
        extra = jnp.where(extra == 0, inner_high, jnp.where(extra == 1, inner - inner_high, 0.0))
        doaug_t[h, :HEAD, :] = do_low
        doaug_t[h, HEAD:, :] = extra.astype(bf16)
        donat[h] = do_low.T
        terms = terms_ref[h]
        dscores = (terms.astype(f32) * nn(vaug[h], doaug_t[h])).astype(bf16)
        dvalue = nn(terms, donat[h])
        dkey = nn(dscores, qnat[h]).T * HEAD ** (-0.5)
        dquery = nn(klow_t[h], dscores) * HEAD ** (-0.5)
        q_gain_grad += jnp.sum(dquery * q_hat, axis=1, keepdims=True)
        k_gain_grad += jnp.sum(dkey * k_hat, axis=1, keepdims=True)
        dq_parts.append(norm_backward(dquery * q_gain, q_hat, q_inverse, 0))
        dk_parts.append(norm_backward(dkey * k_gain, k_hat, k_inverse, 0))
        dv_parts.append(dvalue.T)
    grads = jnp.concatenate(dq_parts + dk_parts + dv_parts, 0).astype(bf16)
    halves(nn(grads, x_ref[...]).astype(bf16), core_ref, keep_ref, send_ref)
    grads_ref[0] = grads[:pair].T
    grads_ref[1] = grads[pair : 2 * pair].T
    grads_ref[2] = grads[2 * pair :].T

    @pl.when(step == 0)
    def _():
        ggq_ref[...] = jnp.zeros_like(ggq_ref)
        ggk_ref[...] = jnp.zeros_like(ggk_ref)

    ggq_ref[...] += jnp.broadcast_to(q_gain_grad, ggq_ref.shape)
    ggk_ref[...] += jnp.broadcast_to(k_gain_grad, ggk_ref.shape)


def attention_backward(
    joined, dattended, terms, exact, inverse_sum, q_gain, k_gain, x_low, core, first, count, room, place=0, into=()
):
    length = x_low.shape[0]

    def whole(shape):
        return pl.BlockSpec(shape, lambda p: (0, 0))

    gain = jax.ShapeDtypeStruct((HEAD, 128), f32)
    call = pl.pallas_call(
        backward_kernel,
        grid=(count,),
        in_specs=[
            pl.BlockSpec((3, pair, length), lambda p: (0, first + p, 0)),
            pl.BlockSpec((pair, length), lambda p: (first + p, 0)),
            pl.BlockSpec((2, length, length), lambda p: (first + p, 0, 0)),
            pl.BlockSpec((pair, length), lambda p: (first + p, 0)),
            pl.BlockSpec((1, 8, length), lambda p: (first + p, 0, 0)),
            whole((HEAD, 1)), whole((HEAD, 1)), whole((length, D)), core_spec,
            *[pl.BlockSpec(memory_space=pl.ANY)] * len(into),
        ],
        out_specs=[pl.BlockSpec((3, length, pair), lambda p: (0, 0, p))]
        + [pl.BlockSpec((3, pair, D // 2), lambda p: (0, place + p, 0))] * 2
        + [whole((HEAD, 128))] * 2,
        out_shape=[jax.ShapeDtypeStruct((3, length, count * pair), bf16)]
        + [jax.ShapeDtypeStruct((3, room * pair, D // 2), bf16)] * 2 + [gain] * 2,
        input_output_aliases={9 + i: 1 + i for i in range(len(into))},
        scratch_shapes=[
            pltpu.VMEM((2, length, HEAD + 16), bf16),
            pltpu.VMEM((2, length, HEAD), bf16),
            pltpu.VMEM((2, HEAD, length), bf16),
            pltpu.VMEM((2, HEAD + 16, length), bf16),
            pltpu.VMEM((2, length, HEAD), bf16),
        ],
        compiler_params=pltpu.CompilerParams(vmem_limit_bytes=vmem_bytes),
        cost_estimate=pl.CostEstimate(
            flops=2 * count * 8 * length * length * 256,
            bytes_accessed=24 * length * count * pair + 4 * count * length * length,
            transcendentals=0,
        ),
        name="attention_backward",
    )
    outs = call(joined, dattended, terms, exact, inverse_sum, q_gain.reshape(HEAD, 1), k_gain.reshape(HEAD, 1), x_low, core, *into)
    return (*outs[:3], outs[3][:, 0], outs[4][:, 0])


def gelu_pair(u):
    z = jnp.abs(u) * 0.7071067811865476
    t = 1.0 / (1.0 + 0.3275911 * z)
    e = jnp.exp(-z * z)
    poly = t * (0.127414796 + t * (-0.142248368 + t * (0.7107068705 + t * (-0.7265760135 + t * 0.5307027145))))
    half = poly * e
    phi = jnp.where(u >= 0, 1.0 - half, half)
    return (u * phi, phi + u * (0.3989422804014327 * e))


def mlp_kernel(x_ref, gy_ref, wu_ref, wd_ref, core_ref, res_ref, gn_ref, keep_down, send_down, *refs, segments):
    step = pl.program_id(0)
    act_ref, dup_ref = refs[-2:]
    tile = wu_ref.shape[0]

    @pl.when(step == 0)
    def _():
        res_ref[...] = jnp.zeros_like(res_ref)
        gn_ref[...] = jnp.zeros_like(gn_ref)

    for begin in range(0, tile, tile_rows):
        units = slice(begin, begin + tile_rows)
        upward = contract(x_ref[...], wu_ref[units], 1, 1).astype(bf16).astype(f32)
        grad_hidden = contract(gy_ref[...], wd_ref[units], 1, 1)
        active, slope = gelu_pair(upward)
        act_ref[:, units] = active.astype(bf16)
        dup_ref[:, units] = (grad_hidden * slope).astype(bf16)
    active, dupward = act_ref[...], dup_ref[...]
    res_ref[...] += nn(active, wd_ref[...])
    gn_ref[...] += nn(dupward, wu_ref[...])
    halves(contract(active, gy_ref[...], 0, 0).astype(bf16), core_ref, keep_down, send_down)
    grad = contract(dupward, x_ref[...], 0, 0).astype(bf16)

    def place(index):
        filled = [0, 0]
        for begin, end, array in segments:
            low, high = max(begin, index * tile), min(end, (index + 1) * tile)
            if low < high:
                rows = slice(filled[array] + low - begin, filled[array] + high - begin)
                keep_ref, send_ref = refs[2 * array], refs[2 * array + 1]
                halves(
                    grad[low - index * tile : high - index * tile], core_ref, keep_ref.at[rows], send_ref.at[rows]
                )
            filled[array] += end - begin

    for index in range(segments[-1][1] // tile):
        pl.when(step == index)(partial(place, index))


def mlp(x_low, grad_y, w_in_all, w_out_all, core, segments):
    length = x_low.shape[0]
    hidden = w_in_all.shape[0] - QKV
    tile = D
    whole = pl.BlockSpec((length, D), lambda t: (0, 0))
    total = jax.ShapeDtypeStruct((length, D), f32)
    sizes = [sum(end - begin for begin, end, array in segments if array == i) for i in range(2)]
    sizes = [(size, D // 2) for size in sizes if size for _ in range(2)]
    call = pl.pallas_call(
        partial(mlp_kernel, segments=segments),
        grid=(hidden // tile,),
        in_specs=[
            whole,
            whole,
            pl.BlockSpec((tile, D), lambda t: (t + QKV // tile, 0)),
            pl.BlockSpec((tile, D), lambda t: (t + D // tile, 0)),
            core_spec,
        ],
        out_specs=[whole, whole]
        + [pl.BlockSpec((tile, D // 2), lambda t: (t, 0))] * 2
        + [pl.BlockSpec(size, lambda t: (0, 0)) for size in sizes],
        out_shape=[total, total]
        + [jax.ShapeDtypeStruct((hidden, D // 2), bf16)] * 2
        + [jax.ShapeDtypeStruct(size, bf16) for size in sizes],
        scratch_shapes=[pltpu.VMEM((length, tile), bf16)] * 2,
        compiler_params=pltpu.CompilerParams(vmem_limit_bytes=vmem_bytes),
        cost_estimate=pl.CostEstimate(
            flops=18 * length * D * hidden,
            bytes_accessed=12 * length * D + 8 * hidden * D,
            transcendentals=length * hidden,
        ),
        name="mlp",
    )
    return call(x_low, grad_y, w_in_all, w_out_all, core)


def input_kernel(*refs, calls):
    grads = refs[:calls]
    w_ref, normed_ref, tokens_ref, gy_ref, gain_ref, out_ref, ln_ref, total = refs[calls:]
    step = pl.program_id(0)

    @pl.when(step == 0)
    def _():
        total[...] = normed_ref[...]

    begin = 0
    sums = []
    for ref in grads:
        sums.append(nn(ref[0], w_ref[begin : begin + ref.shape[2], :]))
        begin += ref.shape[2]
    total[...] += sum(sums)

    @pl.when(step == pl.num_programs(0) - 1)
    def _():
        x_hat, x_inverse = normalize(tokens_ref[...].astype(f32))
        grad_normed = total[...]
        ln_ref[...] = jnp.sum(grad_normed * x_hat, axis=0, keepdims=True)
        back = norm_backward(grad_normed * gain_ref[...], x_hat, x_inverse)
        out_ref[...] = (gy_ref[...].astype(f32) + back).astype(bf16)


def input_gradient(grads, w_in_all, normed, tokens, grad_y, gain):
    length = tokens.shape[0]
    whole = pl.BlockSpec((length, D), lambda p: (0, 0))
    row = pl.BlockSpec((1, D), lambda p: (0, 0))
    call = pl.pallas_call(
        partial(input_kernel, calls=len(grads)),
        grid=(3,),
        in_specs=[pl.BlockSpec((1, length, grad.shape[2]), lambda p: (p, 0, 0)) for grad in grads]
        + [pl.BlockSpec((D, D), lambda p: (p, 0)), whole, whole, whole, row],
        out_specs=[whole, row],
        out_shape=[jax.ShapeDtypeStruct((length, D), bf16), jax.ShapeDtypeStruct((1, D), f32)],
        scratch_shapes=[pltpu.VMEM((length, D), f32)],
        compiler_params=pltpu.CompilerParams(vmem_limit_bytes=vmem_bytes),
        cost_estimate=pl.CostEstimate(
            flops=2 * length * D * QKV, bytes_accessed=20 * length * D, transcendentals=length
        ),
        name="input_gradient",
    )
    out, ln_grad = call(*grads, w_in_all, normed, tokens, grad_y, gain.reshape(1, D))
    return (out, ln_grad[0])


def split(values):
    high = values.astype(bf16)
    return (high, (values - high.astype(f32)).astype(bf16))


def newton_kernel(
    in_ref, in_far_ref, out_ref, out_far_ref, own_ref, far_ref, place_ref, o_ref, gh, gl, sh, sl, ph, pw, g32, x32
):
    count = D // tile_rows

    def span(i):
        return slice(i * tile_rows, (i + 1) * tile_rows)

    def store(high_ref, low_ref, i, j, value):
        high_ref[span(i), span(j)], low_ref[span(i), span(j)] = split(value)
        if i != j:
            high_ref[span(j), span(i)], low_ref[span(j), span(i)] = split(value.T)

    def symmetric(ah, al, bh, bl, post):
        for i in range(count):
            for j in range(i, count):
                rows, columns = span(i), span(j)
                post(
                    i,
                    j,
                    nn(ah[rows, :], bh[:, columns])
                    + (nn(ah[rows, :], bl[:, columns]) + nn(al[rows, :], bh[:, columns])),
                )

    def sweep(last):
        def keep_factor(i, j, value):
            value = ns_cubic * g32[span(i), span(j)] + ns_quintic * value
            if i == j:
                shape = (tile_rows, tile_rows)
                diagonal = lax.broadcasted_iota(jnp.int32, shape, 0) == lax.broadcasted_iota(jnp.int32, shape, 1)
                value = value + jnp.where(diagonal, ns_linear, 0.0)
            store(ph, pw, i, j, value)

        def keep_gram(i, j, value):
            g32[span(i), span(j)] = value
            store(gh, gl, i, j, value)

        symmetric(gh, gl, gh, gl, keep_factor)
        xh, xl = split(x32[...])
        x32[...] = nn(xh, ph[...]) + (nn(xh, pw[...]) + nn(xl, ph[...]))
        if not last:
            symmetric(gh, gl, ph, pw, partial(store, sh, sl))
            symmetric(sh, sl, ph, pw, keep_gram)

    half = D // 2
    first_core, first_chip = place_ref[0] == 0, place_ref[1] == 0
    near = jnp.where(first_chip, in_ref[...], out_ref[...])
    far = jnp.where(first_chip, in_far_ref[...], out_far_ref[...])
    left, side = jnp.where(first_core, near, far), jnp.where(first_core, far, near)[:half]
    corner = left[:half]
    i = lax.broadcasted_iota(jnp.int32, (half, half), 0)
    j = lax.broadcasted_iota(jnp.int32, (half, half), 1)
    corner_t = corner.T
    first = jnp.where(i <= j, corner, corner_t)
    last = jnp.where(i > j, corner, jnp.where(i == j, left[half : half + 1], corner_t))
    trace = jnp.sum(jnp.where(i == j, first + last, 0.0), axis=0, keepdims=True)
    trace = jnp.sum(trace, axis=1, keepdims=True)
    inverse = 1.0 / (jnp.sqrt(trace) + 1e-07)
    square = inverse * inverse
    g32[:half, :half] = first * square
    g32[half:, half:] = last * square
    g32[:half, half:] = side * square
    g32[half:, :half] = side.T * square
    rows = own_ref.shape[0]
    x32[:rows] = own_ref[...] * inverse
    x32[rows:] = far_ref[...] * inverse
    gh[...], gl[...] = split(g32[...])

    @pl.loop(0, 4)
    def _(k):
        sweep(False)

    sweep(True)
    o_ref[...] = x32[...].astype(bf16)


def newton(folded_in, folded_out, own_rows, far_rows, place):
    rows = own_rows.shape[0] + far_rows.shape[0]
    whole = pl.BlockSpec(memory_space=pltpu.VMEM)
    call = pl.pallas_call(
        newton_kernel,
        in_specs=[whole] * 6 + [core_spec],
        out_specs=whole,
        out_shape=jax.ShapeDtypeStruct((rows, D), bf16),
        scratch_shapes=[pltpu.VMEM((D, D), bf16)] * 6 + [pltpu.VMEM((D, D), f32), pltpu.VMEM((rows, D), f32)],
        compiler_params=pltpu.CompilerParams(vmem_limit_bytes=vmem_bytes),
        cost_estimate=pl.CostEstimate(
            flops=30 * D * D * (2 * D + rows), bytes_accessed=4 * D * D + 6 * rows * D, transcendentals=0
        ),
        name="newton",
    )
    return call(*folded_in, *folded_out, own_rows, far_rows, place)


def update_kernel(in_ref, in_far_ref, out_ref, out_far_ref, wi_ref, wo_ref, place_ref, in_new, out_new, held, *, first):
    def new(weights, ortho, size):
        rate = muon_rate * (size / D) ** 0.5
        return weights.astype(f32) * (1 - muon_rate * muon_decay) - rate * ortho.astype(f32)

    first_core = place_ref[0] == 0
    for near_ref, far_ref, total in ((in_ref, in_far_ref, None), (out_ref, out_far_ref, out_new)):
        size = far_ref.shape[0] // 2
        all_near, all_far, weights = near_ref[...].astype(f32), far_ref[...].astype(f32), wo_ref[...].astype(f32)
        for chip in range(2):
            rows = slice(chip * size, (chip + 1) * size)
            near, far = all_near[rows], all_far[rows]
            begin = 2 * chip * size
            both = (jnp.where(first_core, near, far), jnp.where(first_core, far, near))
            for i in range(2):
                spot = slice(begin + i * size, begin + (i + 1) * size)
                if total is None:
                    held[spot] = both[i]
                else:
                    total[spot] = new(weights[spot], both[i], FOUT)
    rows = in_new.shape[0]
    if first == rows:
        in_new[...] = new(wi_ref[...], held[...], FIN)
        return
    start = pl.multiple_of(place_ref[1], 32)
    cut, rest = first // 2, (rows - first) // 2
    pieces = jnp.concatenate([held[cut : cut + rest], held[rows // 2 + cut :]], axis=0)
    in_new[: rows - first] = new(wi_ref[: rows - first], pieces, FIN)
    in_new[first:] = jnp.where(
        lax.broadcasted_iota(jnp.int32, (rows - first, 1), 0) < start, in_new[first:], new(wi_ref[first:], pieces, FIN)
    )
    spot = pl.ds(start, first)
    pieces = jnp.concatenate([held[:cut], held[rows // 2 : rows // 2 + cut]], axis=0)
    in_new[spot] = new(wi_ref[spot], pieces, FIN)


def update(ortho_in, far_in, ortho_out, far_out, w_in, w_out, place, first):
    whole = pl.BlockSpec(memory_space=pltpu.VMEM)
    call = pl.pallas_call(
        partial(update_kernel, first=first),
        in_specs=[whole] * 6 + [core_spec],
        out_specs=[whole] * 2,
        out_shape=[jax.ShapeDtypeStruct(w.shape, f32) for w in (w_in, w_out)],
        scratch_shapes=[pltpu.VMEM(w_in.shape, f32)],
        compiler_params=pltpu.CompilerParams(vmem_limit_bytes=vmem_bytes),
        cost_estimate=pl.CostEstimate(flops=4 * w_in.size, bytes_accessed=14 * w_in.size, transcendentals=0),
        name="update",
    )
    return call(ortho_in, far_in, ortho_out, far_out, w_in, w_out, place)


def gram_kernel(m_ref, extra_ref, core_ref, o_ref):
    half = D // 2
    left, right = slice(0, half), slice(half, D)

    def product(a, b):
        ah, al = split(m_ref[:, a])
        bh, bl = split(m_ref[:, b])
        return contract(ah, bh, 0, 0) + (contract(ah, bl, 0, 0) + contract(al, bh, 0, 0))

    o_ref[half:, :] = extra_ref[...]

    @pl.when(core_ref[0] == 0)
    def _():
        i = lax.broadcasted_iota(jnp.int32, (half, half), 0)
        j = lax.broadcasted_iota(jnp.int32, (half, half), 1)
        last = product(right, right)
        o_ref[:half, :] = jnp.where(i <= j, product(left, left), last)
        o_ref[half : half + 1, :] = jnp.sum(jnp.where(i == j, last, 0.0), axis=0, keepdims=True)

    @pl.when(core_ref[0] != 0)
    def _():
        o_ref[:half, :] = product(left, right)


def folded_gram(rows, extra, core):
    rows = jnp.pad(rows, ((0, -rows.shape[0] % 16), (0, 0)))
    whole = pl.BlockSpec(memory_space=pltpu.VMEM)
    call = pl.pallas_call(
        gram_kernel,
        in_specs=[whole, whole, core_spec],
        out_specs=whole,
        out_shape=jax.ShapeDtypeStruct((D // 2 + extra_rows, D // 2), f32),
        compiler_params=pltpu.CompilerParams(vmem_limit_bytes=vmem_bytes),
        cost_estimate=pl.CostEstimate(
            flops=4 * rows.shape[0] * D * D, bytes_accessed=8 * rows.shape[0] * D, transcendentals=0
        ),
        name="gram",
    )
    return call(rows, extra, core)


def bits(size):
    return [1 << b for b in range(size.bit_length() - 1)]


def take(values, index, axis):
    return lax.dynamic_index_in_dim(values, index, axis, keepdims=False)


def after(value, *others):
    return lax.optimization_barrier((value, *others))[0]


def exchange(values, axis, bit, fill=()):
    size = lax.axis_size(axis)
    return after(lax.ppermute(values, axis, [(i, i ^ bit) for i in range(size)]), *fill)


def sum_steps(values, halving, full):
    columns = values.shape[1]
    fill = yield values
    sides = []
    for axis, bit in halving:
        side = (lax.axis_index(axis) // bit) % 2
        pieces = values.reshape(2, values.shape[0] // 2, columns)
        values = take(pieces, side, 0) + exchange(take(pieces, 1 - side, 0), axis, bit, fill)
        sides.append(side)
        fill = yield values
    for axis, bit in full:
        values = values + exchange(values, axis, bit, fill)
        fill = yield values
    for (axis, bit), side in zip(reversed(halving), reversed(sides), strict=True):
        values = join(values, exchange(values, axis, bit, fill), side, 0).reshape(-1, columns)
        fill = yield values
    yield values, exchange(values, "nar", 1, fill)


def halve(parts, axis, name, bit):
    side = (lax.axis_index(name) // bit) % 2
    sent = [take(part, 1 - side, axis) for part in parts]

    def receive(*fill):
        kept = jnp.concatenate([take(part, side, axis) for part in parts], axis=0)
        return (kept, exchange(jnp.concatenate(sent, axis=0), name, bit, fill))

    return sent, receive


def added(kept, other):
    return (kept.astype(f32) + other.astype(f32)).astype(bf16)


def scatter_one(*parts):
    wide = lax.axis_size("wide")
    columns = parts[0].shape[-1]
    rows = sum(part.size for part in parts) // (2 * wide * columns)
    cut = rows // 16 * 8
    parts = [part.reshape(-1, 2, 2, rows, columns) for part in parts]
    sent_a, receive_a = halve([part[:, :, :, :cut] for part in parts], 1, "wide", 1)
    sent_b, receive_b = halve([part[:, :, :, cut:] for part in parts], 2, "nar", 2)
    return sent_a + sent_b, lambda *fill: (added(*receive_a(*fill)), added(*receive_b(*fill)))


def scatter_two(held):
    sent_a, receive_a = halve(held[:1], 1, "nar", 2)
    sent_b, receive_b = halve(held[1:], 1, "wide", 1)

    def receive(*fill):
        kept, other = zip(receive_a(*fill), receive_b(*fill), strict=True)
        return added(jnp.concatenate(kept, axis=1), jnp.concatenate(other, axis=1))

    return sent_a + sent_b, receive


def scatter_rest(held):
    wide = lax.axis_size("wide")
    far = wide // 2
    place = lax.axis_index("wide") // 2
    sent = [take(held, (place + shift) % far, 0) for shift in range(1, far)]

    def receive(*fill):
        total = take(held, place, 0).astype(f32)
        for shift in range(1, far):
            pairs = [(i, (i // 2 + shift) % far * 2 + i % 2) for i in range(wide)]
            total = total + after(lax.ppermute(sent[shift - 1], "wide", pairs), *fill).astype(f32)
        return total.astype(bf16)

    return sent, receive


def both_cores(values, *fill):
    other = exchange(values, "nar", 1, fill)
    return join(values, other, lax.axis_index("nar") % 2, 1).reshape(values.shape[0], D)


def ordered(values, other, side):
    return (jnp.where(side == 0, values, other), jnp.where(side == 0, other, values))


def join(values, other, side, axis):
    return jnp.stack(ordered(values, other, side), axis)


def gather(values):
    wide = lax.axis_size("wide")
    rows = values.shape[0]
    far = wide // 2
    place, side = lax.axis_index("wide") // 2, lax.axis_index("wide") % 2
    chip, core = lax.axis_index("nar") // 2, lax.axis_index("nar") % 2
    held = lax.dynamic_update_index_in_dim(jnp.zeros((far, rows, D), values.dtype), values, place, 0)
    for shift in range(1, far):
        pairs = [(i, (i // 2 + shift) % far * 2 + i % 2) for i in range(wide)]
        held = lax.dynamic_update_index_in_dim(
            held, lax.ppermute(values, "wide", pairs), (place - shift) % far, 0
        )
    cut = rows // 32 * 16
    first, second = held[:, :cut], held[:, cut:]
    first = join(first, exchange(first, "wide", 1), side, 1)
    second = join(second, exchange(second, "nar", 2), chip, 1)
    first = join(first, exchange(first, "nar", 2), chip, 2)
    second = join(second, exchange(second, "wide", 1), side, 1)
    held = jnp.concatenate([first, second], axis=3)
    return join(held, exchange(held, "nar", 1), core, 3).reshape(-1, D)


def on_device(tokens, cotangent, image_ids, w_in, w_out, gains, mom_in, mom_out, gain_m, gain_v):
    row_count = tokens.shape[0]
    rows_in = w_in.shape[0]
    rows_out = w_out.shape[0]
    nar_count = lax.axis_size("nar")
    wide_count = lax.axis_size("wide")
    nar_place = lax.axis_index("nar")
    share_in = rows_in // nar_count
    share_out = rows_out // nar_count
    everyone = ("wide", "nar")

    def share(rows, size):
        return lax.dynamic_slice_in_dim(rows, nar_place * size, size, 0)

    w_in_all = lax.all_gather(share(w_in, share_in), everyone, axis=0, tiled=True)
    w_out_all = gather(share(w_out, share_out))

    x_float = tokens.astype(f32)
    ln_gain = gains[:D]
    x_hat, x_inverse = normalize(x_float)
    x_low = (x_hat * ln_gain).astype(bf16)
    live = (image_ids.reshape(row_count) >= 0)[:, None]
    grad_y = jnp.where(live, cotangent, jnp.zeros_like(cotangent))

    core = (nar_place % 2).reshape(1)
    chip = nar_place // 2
    half = D // 2
    pairs = D // pair
    q_gain, k_gain = gains[D : D + HEAD], gains[D + HEAD :]
    first = rows_in * 4 // 7
    second = rows_in - first
    parted = wide_count == 8 and first == half and rows_in == 672
    segments = [(0, FIN - QKV, 0)]
    if parted:
        segments = [(0, first, 0)]
        for i in range(4):
            segments += [(rows_in * i + first, rows_in * (i + 1), 1), (rows_in * (i + 1), rows_in * (i + 1) + first, 0)]
    mlp_result, mlp_normed, keep_down, send_down, *up_parts = mlp(
        x_low, grad_y, w_in_all, w_out_all, core, segments
    )
    joined, dattended, attended, terms, exact, inverse_sum, keep_att, send_att = attention_forward(
        after(x_low, keep_down), grad_y, w_in_all, w_out_all, image_ids.reshape(row_count), q_gain, k_gain, core
    )

    def backward(begin, count, earlier=(), **buffers):
        return attention_backward(
            joined, dattended, terms, exact, inverse_sum, q_gain, k_gain, after(x_low, *earlier), core, begin, count,
            **buffers,
        )

    def cores(keep, send, *fill):
        return added(keep, exchange(send, "nar", 1, fill)).reshape(-1, half)

    start = 96 * jnp.minimum(lax.axis_index("wide"), 3)
    row = lax.broadcasted_iota(jnp.int32, (rows_in, 1), 0)
    half_mom_out = lax.dynamic_slice_in_dim(mom_out, chip * (rows_out // 2), rows_out // 2, 0)
    wide_bits = bits(wide_count)
    halving = [("wide", wide_bits[0]), ("nar", 2)]
    full = [("wide", bit) for bit in wide_bits[1:]]

    def begin_out(part):
        zeros = jnp.zeros((extra_rows, half), f32)
        steps = sum_steps(folded_gram(muon_beta * half_mom_out + part.astype(f32), zeros, core), halving, full)
        return (steps, next(steps))

    if parted:
        keep_up_a, send_up_a, keep_up_b, send_up_b = up_parts
        down = cores(keep_down, send_down, keep_att)
        up_a = cores(keep_up_a, send_up_a, keep_att)
        att = cores(keep_att, send_att)
        sent, receive = scatter_one(jnp.concatenate([att, down], axis=0))
        dqkv_a, keep_a, send_a, q_grad_a, k_grad_a = backward(0, 3, [up_a, *sent], room=3)
        sent, receive = scatter_two(receive(keep_a))
        dqkv_b, keep_b, send_b, q_grad_b, k_grad_b = backward(3, 1, [keep_a, *sent], room=3)
        sent_o, receive_o = scatter_rest(receive(dqkv_b))
        added_a = cores(keep_a, send_a, dqkv_b)
        up_b = cores(keep_up_b, send_up_b, dqkv_b)
        sent_a, receive_a = scatter_one(jnp.concatenate([added_a, up_a], axis=0))
        dqkv_c, keep_b, send_b, q_grad_c, k_grad_c = backward(
            4, 2, [up_b, *sent_a, *sent_o], room=3, place=1, into=(keep_b, send_b)
        )
        part_out = receive_o(dqkv_c)
        sent_a, receive_a = scatter_two(receive_a(dqkv_c))
        added_b = cores(keep_b, send_b, part_out, *sent_a)
        sent_b, receive_b = scatter_one(added_b, up_b)
        held_b = receive_b(*sent_b)
        sent_b, receive_b = scatter_two(held_b)
        part_out = both_cores(part_out, *sent_b)
        steps_out, folded_out = begin_out(after(part_out, *sent_b))
        held_a = receive_a(*sent_b)
        held_b = receive_b(held_a, folded_out)
        sent, receive = scatter_rest(jnp.concatenate([held_a, held_b], axis=1))
        grad_tokens, ln_grad = input_gradient(
            [dqkv_a, dqkv_b, dqkv_c], w_in_all, after(mlp_normed, *sent), tokens, grad_y, ln_gain
        )
        far_out = exchange(after(part_out, *sent), "nar", 2, (grad_tokens,))
        part_in = receive(grad_tokens, far_out)
        folded_out = steps_out.send((part_in,))
        q_gain_grad, k_gain_grad = q_grad_a + q_grad_b + q_grad_c, k_grad_a + k_grad_b + k_grad_c

        def halved(rows, chip):
            inside = lax.dynamic_slice_in_dim(rows, start, first, 0)
            others = jnp.where(row[:second] < start, rows[:second], rows[first:])
            return jnp.concatenate(
                [
                    lax.dynamic_slice_in_dim(inside, chip * (first // 2), first // 2, 0),
                    lax.dynamic_slice_in_dim(others, chip * (second // 2), second // 2, 0),
                ],
                axis=0,
            )

        def rejoined(near, far):
            cut = first // 2
            a, b = jnp.concatenate([near[:cut], far[:cut]], 0), jnp.concatenate([near[cut:], far[cut:]], 0)
            a = lax.dynamic_update_slice_in_dim(jnp.zeros((rows_in, D), a.dtype), a, start, 0)
            empty = jnp.zeros((first, D), b.dtype)
            below = jnp.concatenate([b, empty], axis=0)
            above = jnp.concatenate([empty, b], axis=0)
            inside = (row >= start) & (row < start + first)
            return jnp.where(inside, a, jnp.where(row < start, below, above))

    else:
        keep_up, send_up = up_parts
        dqkv, keep_a, send_a, q_gain_grad, k_gain_grad = backward(0, pairs, room=pairs)
        grad_tokens, ln_grad = input_gradient([dqkv], w_in_all, mlp_normed, tokens, grad_y, ln_gain)

        def scattered(*parts):
            held = scatter_one(jnp.concatenate(parts, axis=0))[1]()
            return scatter_rest(scatter_two(held)[1]())[1]()

        part_out = both_cores(scattered(cores(keep_att, send_att), cores(keep_down, send_down)))
        steps_out, folded_out = begin_out(part_out)
        far_out = exchange(part_out, "nar", 2)
        part_in = scattered(cores(keep_a, send_a), cores(keep_up, send_up))

        def halved(rows, chip):
            return lax.dynamic_slice_in_dim(rows, chip * (rows_in // 2), rows_in // 2, 0)

        def rejoined(near, far):
            return jnp.concatenate([near, far], axis=0)

    part_in = both_cores(part_in)
    gain_terms = jnp.concatenate([ln_grad, q_gain_grad, k_gain_grad])
    count = gain_terms.shape[0]
    extra = jnp.pad(gain_terms, (half, (extra_rows - 1) * half - count)).reshape(extra_rows, half)
    momenta_in = muon_beta * halved(mom_in, chip) + part_in.astype(f32)
    steps_in = sum_steps(folded_gram(momenta_in, extra, core), halving, full)
    folded_in = next(steps_in)

    half_in, half_out = rows_in // 4, rows_out // 4

    def mine(rows, size):
        return lax.dynamic_slice_in_dim(rows, core[0] * size, size, 0)

    def fitted(rows):
        return jnp.pad(rows, ((0, half_in - half_out), (0, 0)))

    far_in = exchange(part_in, "nar", 2)
    own_rows = jnp.where(
        chip == 0,
        mine(momenta_in, half_in),
        fitted(mine(muon_beta * half_mom_out + part_out.astype(f32), half_out)),
    )
    far_mom = jnp.where(
        chip == 0,
        mine(halved(mom_in, 1 - chip), half_in),
        fitted(mine(lax.dynamic_slice_in_dim(mom_out, (1 - chip) * (rows_out // 2), rows_out // 2, 0), half_out)),
    )
    far_rows = jnp.where(chip == 0, mine(far_in, half_in), fitted(mine(far_out, half_out)))
    far_rows = muon_beta * far_mom + far_rows.astype(f32)
    summed = []
    result = None
    while not isinstance(folded_in, tuple):
        fill = () if summed else (far_in,)
        if len(summed) == len(halving):
            fill = (own_rows, far_rows)
        if len(summed) == len(halving) + len(full) + 1:
            branch = mlp_result + nn(after(attended, folded_in), w_out_all[:D])
            result = (tokens.astype(f32) + branch).astype(bf16)
            fill = (result,)
        folded_in = steps_in.send(fill)
        summed.append(folded_in)
        if not isinstance(folded_out, tuple):
            folded_out = steps_out.send(folded_in if isinstance(folded_in, tuple) else (folded_in,))
    extra = (folded_in[0][half:] + folded_in[1][half:]).reshape(extra_rows * half)
    grad_gains = extra[half : half + count]
    ortho = newton(folded_in, folded_out, own_rows, far_rows, jnp.stack([core[0], chip]))
    far_out, far_in = after(far_out, ortho), after(far_in, ortho)
    grad_w_out = join(part_out, far_out, chip, 0).reshape(rows_out, D).astype(f32)
    mom_out_new = muon_beta * mom_out + grad_w_out
    grad_w_in = after(rejoined(*ordered(part_in, far_in, chip))).astype(f32)
    mom_in_new = muon_beta * mom_in + grad_w_in

    other = exchange(ortho, "nar", 2, (mom_in_new, mom_out_new))
    ortho_in, ortho_out = ordered(ortho, other, chip)
    ortho_out = jnp.concatenate([ortho_out[half_in : half_in + half_out], ortho_out[:half_out]], axis=0)
    far_in, far_out = (exchange(rows, "nar", 1) for rows in (ortho_in, ortho_out))
    w_in_new, w_out_new = update(
        ortho_in, far_in, ortho_out, far_out, w_in, w_out, jnp.stack([core[0], start]), first if parted else rows_in
    )
    gain_m_new = adam_first * gain_m + (1 - adam_first) * grad_gains
    gain_v_new = adam_second * gain_v + (1 - adam_second) * grad_gains * grad_gains
    gains_new = gains - adam_rate * (gain_m_new / (1 - adam_first**STEP)) / (
        jnp.sqrt(gain_v_new / (1 - adam_second**STEP)) + adam_eps
    )
    return (
        result,
        grad_tokens,
        grad_w_in,
        grad_w_out,
        grad_gains,
        mom_in_new,
        mom_out_new,
        gain_m_new,
        gain_v_new,
        w_in_new,
        w_out_new,
        gains_new,
    )


def solution(mesh):
    rows = P(("nar", "wide"), None)
    wide = P("wide", None)
    return jax.shard_map(
        on_device,
        mesh=mesh,
        in_specs=(rows, rows, rows, wide, wide, P(), wide, wide, P(), P()),
        out_specs=(rows, rows, wide, wide, P(), wide, wide, P(), P(), wide, wide, P()),
        check_vma=False,
    )
```

```python
from functools import partial

import jax
import jax.numpy as jnp
from jax import lax
from jax.experimental import pallas as pl
from jax.experimental.pallas import tpu as pltpu
from jax.sharding import PartitionSpec as P

D = 768
HEADS = 12
HEAD = 64
LEN = 1024
STEP = 10
FIN = 5376
FOUT = 3840
QKV = 3 * D

f32 = jnp.float32
bf16 = jnp.bfloat16
ns_linear = 3.4445
ns_cubic = -4.775
ns_quintic = 2.0315
muon_beta = 0.5
muon_rate = 0.8
muon_decay = 0.1
adam_rate = 0.8
adam_first = 0.9
adam_second = 0.95
adam_eps = 1e-08
norm_eps = 1e-06
penalty = 16384.0
vmem_bytes = 60 * 1024 * 1024
tile_rows = 256
extra_rows = 32
pair = 2 * HEAD


def normalize(values):
    center = values - jnp.mean(values, axis=-1, keepdims=True)
    variance = jnp.mean(center * center, axis=-1, keepdims=True)
    inverse = lax.rsqrt(variance + norm_eps)
    return (center * inverse, inverse)


def norm_backward(grad_scaled, normed, inverse, axis=-1):
    mean_grad = jnp.mean(grad_scaled, axis=axis, keepdims=True)
    mean_cross = jnp.mean(grad_scaled * normed, axis=axis, keepdims=True)
    return inverse * (grad_scaled - mean_grad - normed * mean_cross)


def nn(a, b):
    return jnp.dot(a, b, preferred_element_type=f32)


def contract(a, b, dim_a, dim_b):
    return lax.dot_general(a, b, (((dim_a,), (dim_b,)), ((), ())), preferred_element_type=f32)


def normalize_columns(columns):
    center = columns - jnp.mean(columns, axis=0, keepdims=True)
    variance = jnp.mean(center * center, axis=0, keepdims=True)
    inverse = lax.rsqrt(variance + norm_eps)
    return (center * inverse, inverse)


core_spec = pl.BlockSpec(memory_space=pltpu.SMEM)


def halves(values, core_ref, keep_ref, send_ref):
    half = D // 2
    left, right = values[:, :half], values[:, half:]
    first = core_ref[0] == 0
    keep_ref[...] = jnp.where(first, left, right).reshape(keep_ref.shape)
    send_ref[...] = jnp.where(first, right, left).reshape(send_ref.shape)


def forward_kernel(
    x_ref, gy_ref, wq_ref, wk_ref, wv_ref, wa_ref, onek_ref, penq_ref, gq_ref, gk_ref, core_ref,
    joined_ref, do_ref, att_ref, terms_ref, exact_ref, sum_ref, keep_ref, send_ref, kaug, qaug_t, vaug_t,
):
    length = x_ref.shape[0]
    weights = jnp.concatenate([wq_ref[...], wk_ref[...], wv_ref[...]], axis=0)
    joined = contract(weights, x_ref[...], 1, 1).astype(bf16)
    for i in range(3):
        joined_ref[i] = joined[i * pair : (i + 1) * pair]
    do_ref[...] = contract(wa_ref[...], gy_ref[...], 1, 1).astype(bf16)
    parts = []
    for h in range(2):
        rows = slice(HEAD * h, HEAD * (h + 1))
        q_hat, _ = normalize_columns(joined_ref[0, rows, :].astype(f32))
        k_hat, _ = normalize_columns(joined_ref[1, rows, :].astype(f32))
        q_low = (q_hat * gq_ref[...]).astype(bf16)
        k_low = (k_hat * gk_ref[...]).astype(bf16)
        kaug[h, :, :HEAD] = k_low.T
        kaug[h, :, HEAD:] = onek_ref[...]
        qaug_t[h, :HEAD, :] = (q_low.astype(f32) * HEAD ** (-0.5)).astype(bf16)
        qaug_t[h, HEAD:, :] = penq_ref[...]
        vaug_t[h, :HEAD, :] = joined_ref[2, rows, :]
        vaug_t[h, HEAD:, :] = jnp.ones((16, length), bf16)
        terms_ref[h] = jnp.exp(nn(kaug[h], qaug_t[h])).astype(bf16)
        summed = nn(vaug_t[h], terms_ref[h])
        inverse_sum = 1.0 / summed[HEAD : HEAD + 1]
        sum_ref[0, h : h + 1, :] = inverse_sum
        attended = summed[:HEAD] * inverse_sum
        exact_ref[rows, :] = attended
        parts.append(attended)
    attended = jnp.concatenate(parts, 0).astype(bf16)
    halves(nn(attended, gy_ref[...]).astype(bf16), core_ref, keep_ref, send_ref)
    att_ref[...] = attended.T


def attention_forward(x_low, grad_y, w_in_all, w_out_all, ids, q_gain, k_gain, core):
    length = x_low.shape[0]
    pairs = D // pair
    image = jnp.where(ids < 0, 4, ids)
    number = jnp.arange(16)
    onek = (image[:, None] == number[None, :]).astype(bf16)
    penq = jnp.where(image[None, :] == number[:, None], 0.0, -penalty).astype(bf16)

    def rows(part):
        return pl.BlockSpec((pair, D), lambda p: (part * pairs + p, 0))

    def whole(shape):
        return pl.BlockSpec(shape, lambda p: (0, 0))

    call = pl.pallas_call(
        forward_kernel,
        grid=(pairs,),
        in_specs=[
            whole((length, D)), whole((length, D)), rows(0), rows(1), rows(2), rows(0),
            whole((length, 16)), whole((16, length)), whole((HEAD, 1)), whole((HEAD, 1)), core_spec,
        ],
        out_specs=[
            pl.BlockSpec((3, pair, length), lambda p: (0, p, 0)),
            pl.BlockSpec((pair, length), lambda p: (p, 0)),
            pl.BlockSpec((length, pair), lambda p: (0, p)),
            pl.BlockSpec((2, length, length), lambda p: (p, 0, 0)),
            pl.BlockSpec((pair, length), lambda p: (p, 0)),
            pl.BlockSpec((1, 8, length), lambda p: (p, 0, 0)),
            *[pl.BlockSpec((pair, D // 2), lambda p: (p, 0))] * 2,
        ],
        out_shape=[
            jax.ShapeDtypeStruct((3, D, length), bf16),
            jax.ShapeDtypeStruct((D, length), bf16),
            jax.ShapeDtypeStruct((length, D), bf16),
            jax.ShapeDtypeStruct((HEADS, length, length), bf16),
            jax.ShapeDtypeStruct((D, length), f32),
            jax.ShapeDtypeStruct((pairs, 8, length), f32),
            *[jax.ShapeDtypeStruct((D, D // 2), bf16)] * 2,
        ],
        scratch_shapes=[
            pltpu.VMEM((2, length, HEAD + 16), bf16),
            pltpu.VMEM((2, HEAD + 16, length), bf16),
            pltpu.VMEM((2, HEAD + 16, length), bf16),
        ],
        compiler_params=pltpu.CompilerParams(vmem_limit_bytes=vmem_bytes),
        cost_estimate=pl.CostEstimate(
            flops=HEADS * 4 * length * length * 256,
            bytes_accessed=16 * length * D + 2 * HEADS * length * length,
            transcendentals=HEADS * length * length,
        ),
        name="attention_forward",
    )
    return call(
        x_low, grad_y, w_in_all, w_in_all, w_in_all, w_out_all, onek, penq,
        q_gain.reshape(HEAD, 1), k_gain.reshape(HEAD, 1), core,
    )


def backward_kernel(
    joined_ref, do_ref, terms_ref, exact_ref, sum_ref, gq_ref, gk_ref, x_ref, core_ref, *refs, folds,
):
    *refs, vaug, qlow_t, klow_t, doaug_t = refs
    if folds:
        *refs, folded_ref = refs
    *refs, grads_ref, keep_ref, send_ref, ggq_ref, ggk_ref = refs
    if folds:
        size = folded_ref.shape[0] // 2
        for i in range(2):
            near_ref, far_ref = refs[-4 + 2 * i], refs[-3 + 2 * i]
            folded_ref[i * size : (i + 1) * size, :] = added(near_ref[...], far_ref[...])
    length = x_ref.shape[0]
    step = pl.program_id(0)
    q_gain = gq_ref[...]
    k_gain = gk_ref[...]
    dq_parts, dk_parts, dv_parts = [], [], []
    q_gain_grad = jnp.zeros((HEAD, 1), f32)
    k_gain_grad = jnp.zeros((HEAD, 1), f32)
    kept = []
    for h in range(2):
        rows = slice(HEAD * h, HEAD * (h + 1))
        q_hat, q_inverse = normalize_columns(joined_ref[0, rows, :].astype(f32))
        k_hat, k_inverse = normalize_columns(joined_ref[1, rows, :].astype(f32))
        klow_t[h] = (k_hat * k_gain).astype(bf16)
        qlow_t[h] = (q_hat * q_gain).astype(bf16)
        vaug[h, :, :HEAD] = joined_ref[2, rows, :].T
        vaug[h, :, HEAD:] = jnp.ones((length, 16), bf16)
        inverse_sum = sum_ref[0, h : h + 1, :]
        do_head = do_ref[rows, :].astype(f32)
        inner = -jnp.sum(do_head * exact_ref[rows, :], axis=0, keepdims=True) * inverse_sum
        do_low = (do_head * inverse_sum).astype(bf16)
        inner_high = inner.astype(bf16).astype(f32)
        extra = lax.broadcasted_iota(jnp.int32, (16, length), 0)
        extra = jnp.where(extra == 0, inner_high, jnp.where(extra == 1, inner - inner_high, 0.0))
        doaug_t[h, :HEAD, :] = do_low
        doaug_t[h, HEAD:, :] = extra.astype(bf16)
        kept.append((q_hat, q_inverse, k_hat, k_inverse))
    sums = [[None] * 3 for _ in range(2)]
    for k in range(0, length, tile_rows):
        for h in range(2):
            span = slice(k, k + tile_rows)
            terms = terms_ref[h, span, :]
            dscores = (terms.astype(f32) * nn(vaug[h, span, :], doaug_t[h])).astype(bf16)
            dv = contract(doaug_t[h, :HEAD, :], terms, 1, 1)
            dk = contract(qlow_t[h], dscores, 1, 1)
            dq = nn(klow_t[h, :, span], dscores)
            sums[h][0] = dq if sums[h][0] is None else sums[h][0] + dq
            sums[h][1] = [dk] if sums[h][1] is None else sums[h][1] + [dk]
            sums[h][2] = [dv] if sums[h][2] is None else sums[h][2] + [dv]
    for h in range(2):
        q_hat, q_inverse, k_hat, k_inverse = kept[h]
        dquery = sums[h][0] * HEAD ** (-0.5)
        dkey = jnp.concatenate(sums[h][1], axis=1) * HEAD ** (-0.5)
        dvalue = jnp.concatenate(sums[h][2], axis=1)
        q_gain_grad += jnp.sum(dquery * q_hat, axis=1, keepdims=True)
        k_gain_grad += jnp.sum(dkey * k_hat, axis=1, keepdims=True)
        dq_parts.append(norm_backward(dquery * q_gain, q_hat, q_inverse, 0))
        dk_parts.append(norm_backward(dkey * k_gain, k_hat, k_inverse, 0))
        dv_parts.append(dvalue)
    grads = jnp.concatenate(dq_parts + dk_parts + dv_parts, 0).astype(bf16)
    halves(nn(grads, x_ref[...]).astype(bf16), core_ref, keep_ref, send_ref)
    grads_ref[0] = grads[:pair].T
    grads_ref[1] = grads[pair : 2 * pair].T
    grads_ref[2] = grads[2 * pair :].T

    @pl.when(step == 0)
    def _():
        ggq_ref[...] = jnp.zeros_like(ggq_ref)
        ggk_ref[...] = jnp.zeros_like(ggk_ref)

    ggq_ref[...] += jnp.broadcast_to(q_gain_grad, ggq_ref.shape)
    ggk_ref[...] += jnp.broadcast_to(k_gain_grad, ggk_ref.shape)


def attention_backward(
    joined, dattended, terms, exact, inverse_sum, q_gain, k_gain, x_low, core, first, count, room,
    place=0, into=(), fold=(), origin=0, size=0,
):
    length = x_low.shape[0]

    def whole(shape):
        return pl.BlockSpec(shape, lambda p: (0, 0))

    last = (fold[0].shape[0] - origin - size) // (FIN // 8) if fold else 0

    def segment(i):
        return pl.BlockSpec(
            (pl.Element(size), pl.Element(D // 2)),
            lambda p: (pl.multiple_of(origin + FIN // 8 * jnp.minimum(2 * p + i, last), 32), 0),
        )

    gain = jax.ShapeDtypeStruct((HEAD, 128), f32)
    call = pl.pallas_call(
        partial(backward_kernel, folds=bool(fold)),
        grid=(count,),
        in_specs=[
            pl.BlockSpec((3, pair, length), lambda p: (0, first + p, 0)),
            pl.BlockSpec((pair, length), lambda p: (first + p, 0)),
            pl.BlockSpec((2, length, length), lambda p: (first + p, 0, 0)),
            pl.BlockSpec((pair, length), lambda p: (first + p, 0)),
            pl.BlockSpec((1, 8, length), lambda p: (first + p, 0, 0)),
            whole((HEAD, 1)), whole((HEAD, 1)), whole((length, D)), core_spec,
            *[pl.BlockSpec(memory_space=pl.ANY)] * len(into),
            *[segment(i) for i in range(2) for _ in fold],
        ],
        out_specs=[pl.BlockSpec((3, length, pair), lambda p: (0, 0, p))]
        + [pl.BlockSpec((3, pair, D // 2), lambda p: (0, place + p, 0))] * 2
        + [whole((HEAD, 128))] * 2
        + [pl.BlockSpec((2 * size, D // 2), lambda p: (p, 0))] * bool(fold),
        out_shape=[jax.ShapeDtypeStruct((3, length, count * pair), bf16)]
        + [jax.ShapeDtypeStruct((3, room * pair, D // 2), bf16)] * 2 + [gain] * 2
        + [jax.ShapeDtypeStruct(((last + 1) * size, D // 2), bf16)] * bool(fold),
        input_output_aliases={9 + i: 1 + i for i in range(len(into))},
        scratch_shapes=[
            pltpu.VMEM((2, length, HEAD + 16), bf16),
            pltpu.VMEM((2, HEAD, length), bf16),
            pltpu.VMEM((2, HEAD, length), bf16),
            pltpu.VMEM((2, HEAD + 16, length), bf16),
        ],
        compiler_params=pltpu.CompilerParams(vmem_limit_bytes=vmem_bytes),
        cost_estimate=pl.CostEstimate(
            flops=2 * count * 8 * length * length * 256,
            bytes_accessed=24 * length * count * pair + 4 * count * length * length,
            transcendentals=0,
        ),
        name="attention_backward",
    )
    outs = call(joined, dattended, terms, exact, inverse_sum, q_gain.reshape(HEAD, 1), k_gain.reshape(HEAD, 1), x_low, core, *into, *fold, *fold)
    return (*outs[:3], outs[3][:, 0], outs[4][:, 0], *outs[5:])


def gelu_pair(u):
    z = jnp.abs(u) * 0.7071067811865476
    t = 1.0 / (1.0 + 0.3275911 * z)
    e = jnp.exp(-z * z)
    poly = t * (0.127414796 + t * (-0.142248368 + t * (0.7107068705 + t * (-0.7265760135 + t * 0.5307027145))))
    half = poly * e
    phi = jnp.where(u >= 0, 1.0 - half, half)
    return (u * phi, phi + u * (0.3989422804014327 * e))


def mlp_kernel(
    x_ref, gy_ref, wu_ref, wd_ref, core_ref,
    res_ref, gn_ref, keep_up, send_up, keep_down, send_down, act_ref, dup_ref,
):
    @pl.when(pl.program_id(0) == 0)
    def _():
        res_ref[...] = jnp.zeros_like(res_ref)
        gn_ref[...] = jnp.zeros_like(gn_ref)

    for begin in range(0, wu_ref.shape[0], tile_rows):
        units = slice(begin, begin + tile_rows)
        upward = contract(x_ref[...], wu_ref[units], 1, 1).astype(bf16).astype(f32)
        grad_hidden = contract(gy_ref[...], wd_ref[units], 1, 1)
        active, slope = gelu_pair(upward)
        act_ref[:, units] = active.astype(bf16)
        dup_ref[:, units] = (grad_hidden * slope).astype(bf16)
    active, dupward = act_ref[...], dup_ref[...]
    res_ref[...] += nn(active, wd_ref[...])
    gn_ref[...] += nn(dupward, wu_ref[...])
    halves(contract(active, gy_ref[...], 0, 0).astype(bf16), core_ref, keep_down, send_down)
    halves(contract(dupward, x_ref[...], 0, 0).astype(bf16), core_ref, keep_up, send_up)


def mlp(x_low, grad_y, w_in_all, w_out_all, core):
    length = x_low.shape[0]
    hidden = w_in_all.shape[0] - QKV
    tile = D
    whole = pl.BlockSpec((length, D), lambda t: (0, 0))
    total = jax.ShapeDtypeStruct((length, D), f32)
    grad = jax.ShapeDtypeStruct((hidden, D // 2), bf16)
    call = pl.pallas_call(
        mlp_kernel,
        grid=(hidden // tile,),
        in_specs=[
            whole,
            whole,
            pl.BlockSpec((tile, D), lambda t: (t + QKV // tile, 0)),
            pl.BlockSpec((tile, D), lambda t: (t + D // tile, 0)),
            core_spec,
        ],
        out_specs=[whole, whole] + [pl.BlockSpec((tile, D // 2), lambda t: (t, 0))] * 4,
        out_shape=[total, total] + [grad] * 4,
        scratch_shapes=[pltpu.VMEM((length, tile), bf16)] * 2,
        compiler_params=pltpu.CompilerParams(vmem_limit_bytes=vmem_bytes),
        cost_estimate=pl.CostEstimate(
            flops=18 * length * D * hidden,
            bytes_accessed=12 * length * D + 8 * hidden * D,
            transcendentals=length * hidden,
        ),
        name="mlp",
    )
    return call(x_low, grad_y, w_in_all, w_out_all, core)


def input_kernel(*refs, calls):
    grads = refs[:calls]
    w_ref, normed_ref, tokens_ref, gy_ref, gain_ref, out_ref, ln_ref, total = refs[calls:]
    step = pl.program_id(0)

    @pl.when(step == 0)
    def _():
        total[...] = normed_ref[...]

    begin = 0
    sums = []
    for ref in grads:
        sums.append(nn(ref[0], w_ref[begin : begin + ref.shape[2], :]))
        begin += ref.shape[2]
    total[...] += sum(sums)

    @pl.when(step == pl.num_programs(0) - 1)
    def _():
        x_hat, x_inverse = normalize(tokens_ref[...].astype(f32))
        grad_normed = total[...]
        ln_ref[...] = jnp.sum(grad_normed * x_hat, axis=0, keepdims=True)
        back = norm_backward(grad_normed * gain_ref[...], x_hat, x_inverse)
        out_ref[...] = (gy_ref[...].astype(f32) + back).astype(bf16)


def input_gradient(grads, w_in_all, normed, tokens, grad_y, gain):
    length = tokens.shape[0]
    whole = pl.BlockSpec((length, D), lambda p: (0, 0))
    row = pl.BlockSpec((1, D), lambda p: (0, 0))
    call = pl.pallas_call(
        partial(input_kernel, calls=len(grads)),
        grid=(3,),
        in_specs=[pl.BlockSpec((1, length, grad.shape[2]), lambda p: (p, 0, 0)) for grad in grads]
        + [pl.BlockSpec((D, D), lambda p: (p, 0)), whole, whole, whole, row],
        out_specs=[whole, row],
        out_shape=[jax.ShapeDtypeStruct((length, D), bf16), jax.ShapeDtypeStruct((1, D), f32)],
        scratch_shapes=[pltpu.VMEM((length, D), f32)],
        compiler_params=pltpu.CompilerParams(vmem_limit_bytes=vmem_bytes),
        cost_estimate=pl.CostEstimate(
            flops=2 * length * D * QKV, bytes_accessed=20 * length * D, transcendentals=length
        ),
        name="input_gradient",
    )
    out, ln_grad = call(*grads, w_in_all, normed, tokens, grad_y, gain.reshape(1, D))
    return (out, ln_grad[0])


def split(values):
    high = values.astype(bf16)
    return (high, (values - high.astype(f32)).astype(bf16))


def newton_kernel(
    in_ref, in_far_ref, out_ref, out_far_ref, own_ref, far_ref, place_ref, o_ref, gh, gl, sh, sl, ph, pw, g32, x32
):
    count = D // tile_rows

    def span(i):
        return slice(i * tile_rows, (i + 1) * tile_rows)

    def store(high_ref, low_ref, i, j, value):
        high_ref[span(i), span(j)], low_ref[span(i), span(j)] = split(value)
        if i != j:
            high_ref[span(j), span(i)], low_ref[span(j), span(i)] = split(value.T)

    def symmetric(ah, al, bh, bl, post):
        for i in range(count):
            for j in range(i, count):
                rows, columns = span(i), span(j)
                post(
                    i,
                    j,
                    nn(ah[rows, :], bh[:, columns])
                    + (nn(ah[rows, :], bl[:, columns]) + nn(al[rows, :], bh[:, columns])),
                )

    def squared(ah, al, post):
        for i in range(count):
            for j in range(i, count):
                rows, columns = span(i), span(j)
                mixed = nn(ah[rows, :], al[:, columns])
                other = mixed if i == j else nn(ah[columns, :], al[:, rows])
                post(i, j, nn(ah[rows, :], ah[:, columns]) + (mixed + other.T))

    def sweep(last):
        def keep_factor(i, j, value):
            value = ns_cubic * g32[span(i), span(j)] + ns_quintic * value
            if i == j:
                shape = (tile_rows, tile_rows)
                diagonal = lax.broadcasted_iota(jnp.int32, shape, 0) == lax.broadcasted_iota(jnp.int32, shape, 1)
                value = value + jnp.where(diagonal, ns_linear, 0.0)
            store(ph, pw, i, j, value)

        def keep_gram(i, j, value):
            g32[span(i), span(j)] = value
            store(gh, gl, i, j, value)

        squared(gh, gl, keep_factor)
        xh, xl = split(x32[...])
        x32[...] = nn(xh, ph[...]) + (nn(xh, pw[...]) + nn(xl, ph[...]))
        if not last:
            symmetric(gh, gl, ph, pw, partial(store, sh, sl))
            symmetric(sh, sl, ph, pw, keep_gram)

    half = D // 2
    first_core, first_chip = place_ref[0] == 0, place_ref[1] == 0
    near = jnp.where(first_chip, in_ref[...], out_ref[...])
    far = jnp.where(first_chip, in_far_ref[...], out_far_ref[...])
    left, side = jnp.where(first_core, near, far), jnp.where(first_core, far, near)[:half]
    corner = left[:half]
    i = lax.broadcasted_iota(jnp.int32, (half, half), 0)
    j = lax.broadcasted_iota(jnp.int32, (half, half), 1)
    corner_t = corner.T
    first = jnp.where(i <= j, corner, corner_t)
    last = jnp.where(i > j, corner, jnp.where(i == j, left[half : half + 1], corner_t))
    trace = jnp.sum(jnp.where(i == j, first + last, 0.0), axis=0, keepdims=True)
    trace = jnp.sum(trace, axis=1, keepdims=True)
    inverse = 1.0 / (jnp.sqrt(trace) + 1e-07)
    square = inverse * inverse
    g32[:half, :half] = first * square
    g32[half:, half:] = last * square
    g32[:half, half:] = side * square
    g32[half:, :half] = side.T * square
    rows = own_ref.shape[0]
    x32[:rows] = own_ref[...] * inverse
    x32[rows:] = far_ref[...] * inverse
    gh[...], gl[...] = split(g32[...])

    @pl.loop(0, 4)
    def _(k):
        sweep(False)

    sweep(True)
    o_ref[...] = x32[...].astype(bf16)


def newton(folded_in, folded_out, own_rows, far_rows, place):
    rows = own_rows.shape[0] + far_rows.shape[0]
    whole = pl.BlockSpec(memory_space=pltpu.VMEM)
    call = pl.pallas_call(
        newton_kernel,
        in_specs=[whole] * 6 + [core_spec],
        out_specs=whole,
        out_shape=jax.ShapeDtypeStruct((rows, D), bf16),
        scratch_shapes=[pltpu.VMEM((D, D), bf16)] * 6 + [pltpu.VMEM((D, D), f32), pltpu.VMEM((rows, D), f32)],
        compiler_params=pltpu.CompilerParams(vmem_limit_bytes=vmem_bytes),
        cost_estimate=pl.CostEstimate(
            flops=30 * D * D * (2 * D + rows), bytes_accessed=4 * D * D + 6 * rows * D, transcendentals=0
        ),
        name="newton",
    )
    return call(*folded_in, *folded_out, own_rows, far_rows, place)


def update_kernel(in_ref, in_far_ref, out_ref, out_far_ref, wi_ref, wo_ref, place_ref, in_new, out_new, held, *, first):
    def new(weights, ortho, size):
        rate = muon_rate * (size / D) ** 0.5
        return weights.astype(f32) * (1 - muon_rate * muon_decay) - rate * ortho.astype(f32)

    first_core = place_ref[0] == 0
    for near_ref, far_ref, total in ((in_ref, in_far_ref, None), (out_ref, out_far_ref, out_new)):
        size = far_ref.shape[0] // 2
        all_near, all_far, weights = near_ref[...].astype(f32), far_ref[...].astype(f32), wo_ref[...].astype(f32)
        for chip in range(2):
            rows = slice(chip * size, (chip + 1) * size)
            near, far = all_near[rows], all_far[rows]
            begin = 2 * chip * size
            both = (jnp.where(first_core, near, far), jnp.where(first_core, far, near))
            for i in range(2):
                spot = slice(begin + i * size, begin + (i + 1) * size)
                if total is None:
                    held[spot] = both[i]
                else:
                    total[spot] = new(weights[spot], both[i], FOUT)
    rows = in_new.shape[0]
    if first == rows:
        in_new[...] = new(wi_ref[...], held[...], FIN)
        return
    start = pl.multiple_of(place_ref[1], 32)
    cut, rest = first // 2, (rows - first) // 2
    pieces = jnp.concatenate([held[cut : cut + rest], held[rows // 2 + cut :]], axis=0)
    in_new[: rows - first] = new(wi_ref[: rows - first], pieces, FIN)
    in_new[first:] = jnp.where(
        lax.broadcasted_iota(jnp.int32, (rows - first, 1), 0) < start, in_new[first:], new(wi_ref[first:], pieces, FIN)
    )
    spot = pl.ds(start, first)
    pieces = jnp.concatenate([held[:cut], held[rows // 2 : rows // 2 + cut]], axis=0)
    in_new[spot] = new(wi_ref[spot], pieces, FIN)


def update(ortho_in, far_in, ortho_out, far_out, w_in, w_out, place, first):
    whole = pl.BlockSpec(memory_space=pltpu.VMEM)
    call = pl.pallas_call(
        partial(update_kernel, first=first),
        in_specs=[whole] * 6 + [core_spec],
        out_specs=[whole] * 2,
        out_shape=[jax.ShapeDtypeStruct(w.shape, f32) for w in (w_in, w_out)],
        scratch_shapes=[pltpu.VMEM(w_in.shape, f32)],
        compiler_params=pltpu.CompilerParams(vmem_limit_bytes=vmem_bytes),
        cost_estimate=pl.CostEstimate(flops=4 * w_in.size, bytes_accessed=14 * w_in.size, transcendentals=0),
        name="update",
    )
    return call(ortho_in, far_in, ortho_out, far_out, w_in, w_out, place)


def gram_kernel(m_ref, extra_ref, core_ref, o_ref):
    half = D // 2
    left, right = slice(0, half), slice(half, D)

    def product(a, b):
        ah, al = split(m_ref[:, a])
        bh, bl = split(m_ref[:, b])
        return contract(ah, bh, 0, 0) + (contract(ah, bl, 0, 0) + contract(al, bh, 0, 0))

    o_ref[half:, :] = extra_ref[...]

    @pl.when(core_ref[0] == 0)
    def _():
        i = lax.broadcasted_iota(jnp.int32, (half, half), 0)
        j = lax.broadcasted_iota(jnp.int32, (half, half), 1)
        last = product(right, right)
        o_ref[:half, :] = jnp.where(i <= j, product(left, left), last)
        o_ref[half : half + 1, :] = jnp.sum(jnp.where(i == j, last, 0.0), axis=0, keepdims=True)

    @pl.when(core_ref[0] != 0)
    def _():
        o_ref[:half, :] = product(left, right)


def folded_gram(rows, extra, core):
    rows = jnp.pad(rows, ((0, -rows.shape[0] % 16), (0, 0)))
    whole = pl.BlockSpec(memory_space=pltpu.VMEM)
    call = pl.pallas_call(
        gram_kernel,
        in_specs=[whole, whole, core_spec],
        out_specs=whole,
        out_shape=jax.ShapeDtypeStruct((D // 2 + extra_rows, D // 2), f32),
        compiler_params=pltpu.CompilerParams(vmem_limit_bytes=vmem_bytes),
        cost_estimate=pl.CostEstimate(
            flops=4 * rows.shape[0] * D * D, bytes_accessed=8 * rows.shape[0] * D, transcendentals=0
        ),
        name="gram",
    )
    return call(rows, extra, core)


def bits(size):
    return [1 << b for b in range(size.bit_length() - 1)]


def take(values, index, axis):
    return lax.dynamic_index_in_dim(values, index, axis, keepdims=False)


def after(value, *others):
    return lax.optimization_barrier((value, *others))[0]


def exchange(values, axis, bit, fill=()):
    size = lax.axis_size(axis)
    return after(lax.ppermute(values, axis, [(i, i ^ bit) for i in range(size)]), *fill)


def sum_steps(values, halving, full):
    columns = values.shape[1]
    fill = yield values
    sides = []
    for axis, bit in halving:
        side = (lax.axis_index(axis) // bit) % 2
        pieces = values.reshape(2, values.shape[0] // 2, columns)
        values = take(pieces, side, 0) + exchange(take(pieces, 1 - side, 0), axis, bit, fill)
        sides.append(side)
        fill = yield values
    for axis, bit in full:
        values = values + exchange(values, axis, bit, fill)
        fill = yield values
    for (axis, bit), side in zip(reversed(halving), reversed(sides), strict=True):
        values = join(values, exchange(values, axis, bit, fill), side, 0).reshape(-1, columns)
        fill = yield values
    yield values, exchange(values, "nar", 1, fill)


def halve(parts, axis, name, bit):
    side = (lax.axis_index(name) // bit) % 2
    sent = [take(part, 1 - side, axis) for part in parts]

    def receive(*fill):
        kept = jnp.concatenate([take(part, side, axis) for part in parts], axis=0)
        return (kept, exchange(jnp.concatenate(sent, axis=0), name, bit, fill))

    return sent, receive


def added(kept, other):
    return (kept.astype(f32) + other.astype(f32)).astype(bf16)


def scatter_one(*parts):
    wide = lax.axis_size("wide")
    columns = parts[0].shape[-1]
    rows = sum(part.size for part in parts) // (2 * wide * columns)
    cut = rows // 16 * 8
    parts = [part.reshape(-1, 2, 2, rows, columns) for part in parts]
    sent_a, receive_a = halve([part[:, :, :, :cut] for part in parts], 1, "wide", 1)
    sent_b, receive_b = halve([part[:, :, :, cut:] for part in parts], 2, "nar", 2)
    return sent_a + sent_b, lambda *fill: (added(*receive_a(*fill)), added(*receive_b(*fill)))


def scatter_two(held):
    sent_a, receive_a = halve(held[:1], 1, "nar", 2)
    sent_b, receive_b = halve(held[1:], 1, "wide", 1)

    def receive(*fill):
        kept, other = zip(receive_a(*fill), receive_b(*fill), strict=True)
        return added(jnp.concatenate(kept, axis=1), jnp.concatenate(other, axis=1))

    return sent_a + sent_b, receive


def scatter_rest(held):
    wide = lax.axis_size("wide")
    far = wide // 2
    place = lax.axis_index("wide") // 2
    sent = [take(held, (place + shift) % far, 0) for shift in range(1, far)]

    def receive(*fill):
        total = take(held, place, 0).astype(f32)
        for shift in range(1, far):
            pairs = [(i, (i // 2 + shift) % far * 2 + i % 2) for i in range(wide)]
            total = total + after(lax.ppermute(sent[shift - 1], "wide", pairs), *fill).astype(f32)
        return total.astype(bf16)

    return sent, receive


def both_cores(values, *fill):
    other = exchange(values, "nar", 1, fill)
    return join(values, other, lax.axis_index("nar") % 2, 1).reshape(values.shape[0], D)


def ordered(values, other, side):
    return (jnp.where(side == 0, values, other), jnp.where(side == 0, other, values))


def join(values, other, side, axis):
    return jnp.stack(ordered(values, other, side), axis)


def gather(values):
    wide = lax.axis_size("wide")
    rows = values.shape[0]
    far = wide // 2
    place, side = lax.axis_index("wide") // 2, lax.axis_index("wide") % 2
    chip, core = lax.axis_index("nar") // 2, lax.axis_index("nar") % 2
    held = lax.dynamic_update_index_in_dim(jnp.zeros((far, rows, D), values.dtype), values, place, 0)
    for shift in range(1, far):
        pairs = [(i, (i // 2 + shift) % far * 2 + i % 2) for i in range(wide)]
        held = lax.dynamic_update_index_in_dim(
            held, lax.ppermute(values, "wide", pairs), (place - shift) % far, 0
        )
    cut = rows // 32 * 16
    first, second = held[:, :cut], held[:, cut:]
    first = join(first, exchange(first, "wide", 1), side, 1)
    second = join(second, exchange(second, "nar", 2), chip, 1)
    first = join(first, exchange(first, "nar", 2), chip, 2)
    second = join(second, exchange(second, "wide", 1), side, 1)
    held = jnp.concatenate([first, second], axis=3)
    return join(held, exchange(held, "nar", 1), core, 3).reshape(-1, D)


def on_device(tokens, cotangent, image_ids, w_in, w_out, gains, mom_in, mom_out, gain_m, gain_v):
    row_count = tokens.shape[0]
    rows_in = w_in.shape[0]
    rows_out = w_out.shape[0]
    nar_count = lax.axis_size("nar")
    wide_count = lax.axis_size("wide")
    nar_place = lax.axis_index("nar")
    share_in = rows_in // nar_count
    share_out = rows_out // nar_count
    everyone = ("wide", "nar")

    def share(rows, size):
        return lax.dynamic_slice_in_dim(rows, nar_place * size, size, 0)

    w_in_all = lax.all_gather(share(w_in, share_in), everyone, axis=0, tiled=True)
    w_out_all = gather(share(w_out, share_out))

    x_float = tokens.astype(f32)
    ln_gain = gains[:D]
    x_hat, x_inverse = normalize(x_float)
    x_low = (x_hat * ln_gain).astype(bf16)
    live = (image_ids.reshape(row_count) >= 0)[:, None]
    grad_y = jnp.where(live, cotangent, jnp.zeros_like(cotangent))

    core = (nar_place % 2).reshape(1)
    chip = nar_place // 2
    half = D // 2
    pairs = D // pair
    q_gain, k_gain = gains[D : D + HEAD], gains[D + HEAD :]
    first = rows_in * 4 // 7
    second = rows_in - first
    parted = wide_count == 8 and first == half and rows_in == 672
    mlp_result, mlp_normed, keep_up, send_up, keep_down, send_down = mlp(x_low, grad_y, w_in_all, w_out_all, core)
    joined, dattended, attended, terms, exact, inverse_sum, keep_att, send_att = attention_forward(
        after(x_low, keep_down), grad_y, w_in_all, w_out_all, image_ids.reshape(row_count), q_gain, k_gain, core
    )

    def backward(begin, count, earlier=(), **buffers):
        return attention_backward(
            joined, dattended, terms, exact, inverse_sum, q_gain, k_gain, after(x_low, *earlier), core, begin, count,
            **buffers,
        )

    def cores(keep, send, *fill):
        return added(keep, exchange(send, "nar", 1, fill)).reshape(-1, half)

    start = 96 * jnp.minimum(lax.axis_index("wide"), 3)
    row = lax.broadcasted_iota(jnp.int32, (rows_in, 1), 0)
    half_mom_out = lax.dynamic_slice_in_dim(mom_out, chip * (rows_out // 2), rows_out // 2, 0)
    wide_bits = bits(wide_count)
    halving = [("wide", wide_bits[0]), ("nar", 2)]
    full = [("wide", bit) for bit in wide_bits[1:]]

    def begin_out(part):
        zeros = jnp.zeros((extra_rows, half), f32)
        steps = sum_steps(folded_gram(muon_beta * half_mom_out + part.astype(f32), zeros, core), halving, full)
        return (steps, next(steps))

    if parted:
        down = cores(keep_down, send_down, keep_att)
        up = (keep_up, exchange(send_up, "nar", 1, (keep_att,)))
        att = cores(keep_att, send_att)
        sent, receive = scatter_one(jnp.concatenate([att, down], axis=0))
        dqkv_a, keep_a, send_a, q_grad_a, k_grad_a, up_a = backward(0, 3, sent, room=3, fold=up, size=first)
        sent, receive = scatter_two(receive(keep_a))
        dqkv_b, keep_b, send_b, q_grad_b, k_grad_b = backward(3, 1, [keep_a, *sent], room=3)
        sent_o, receive_o = scatter_rest(receive(dqkv_b))
        added_a = cores(keep_a, send_a, dqkv_b)
        sent_a, receive_a = scatter_one(jnp.concatenate([added_a, up_a], axis=0))
        dqkv_c, keep_b, send_b, q_grad_c, k_grad_c, up_b = backward(
            4, 2, [*sent_a, *sent_o], room=3, place=1, into=(keep_b, send_b), fold=up, origin=first, size=second
        )
        part_out = receive_o(dqkv_c)
        sent_a, receive_a = scatter_two(receive_a(dqkv_c))
        added_b = cores(keep_b, send_b, part_out, *sent_a)
        sent_b, receive_b = scatter_one(added_b, up_b)
        held_b = receive_b(*sent_b)
        sent_b, receive_b = scatter_two(held_b)
        part_out = both_cores(part_out, *sent_b)
        steps_out, folded_out = begin_out(after(part_out, *sent_b))
        held_a = receive_a(*sent_b)
        held_b = receive_b(held_a, folded_out)
        sent, receive = scatter_rest(jnp.concatenate([held_a, held_b], axis=1))
        grad_tokens, ln_grad = input_gradient(
            [dqkv_a, dqkv_b, dqkv_c], w_in_all, after(mlp_normed, *sent), tokens, grad_y, ln_gain
        )
        far_out = exchange(after(part_out, *sent), "nar", 2, (grad_tokens,))
        part_in = receive(grad_tokens, far_out)
        folded_out = steps_out.send((part_in,))
        q_gain_grad, k_gain_grad = q_grad_a + q_grad_b + q_grad_c, k_grad_a + k_grad_b + k_grad_c

        def halved(rows, chip):
            inside = lax.dynamic_slice_in_dim(rows, start, first, 0)
            others = jnp.where(row[:second] < start, rows[:second], rows[first:])
            return jnp.concatenate(
                [
                    lax.dynamic_slice_in_dim(inside, chip * (first // 2), first // 2, 0),
                    lax.dynamic_slice_in_dim(others, chip * (second // 2), second // 2, 0),
                ],
                axis=0,
            )

        def rejoined(near, far):
            cut = first // 2
            a, b = jnp.concatenate([near[:cut], far[:cut]], 0), jnp.concatenate([near[cut:], far[cut:]], 0)
            a = lax.dynamic_update_slice_in_dim(jnp.zeros((rows_in, D), a.dtype), a, start, 0)
            empty = jnp.zeros((first, D), b.dtype)
            below = jnp.concatenate([b, empty], axis=0)
            above = jnp.concatenate([empty, b], axis=0)
            inside = (row >= start) & (row < start + first)
            return jnp.where(inside, a, jnp.where(row < start, below, above))

    else:
        dqkv, keep_a, send_a, q_gain_grad, k_gain_grad = backward(0, pairs, room=pairs)
        grad_tokens, ln_grad = input_gradient([dqkv], w_in_all, mlp_normed, tokens, grad_y, ln_gain)

        def scattered(*parts):
            held = scatter_one(jnp.concatenate(parts, axis=0))[1]()
            return scatter_rest(scatter_two(held)[1]())[1]()

        part_out = both_cores(scattered(cores(keep_att, send_att), cores(keep_down, send_down)))
        steps_out, folded_out = begin_out(part_out)
        far_out = exchange(part_out, "nar", 2)
        part_in = scattered(cores(keep_a, send_a), cores(keep_up, send_up))

        def halved(rows, chip):
            return lax.dynamic_slice_in_dim(rows, chip * (rows_in // 2), rows_in // 2, 0)

        def rejoined(near, far):
            return jnp.concatenate([near, far], axis=0)

    part_in = both_cores(part_in)
    gain_terms = jnp.concatenate([ln_grad, q_gain_grad, k_gain_grad])
    count = gain_terms.shape[0]
    extra = jnp.pad(gain_terms, (half, (extra_rows - 1) * half - count)).reshape(extra_rows, half)
    momenta_in = muon_beta * halved(mom_in, chip) + part_in.astype(f32)
    steps_in = sum_steps(folded_gram(momenta_in, extra, core), halving, full)
    folded_in = next(steps_in)

    half_in, half_out = rows_in // 4, rows_out // 4

    def mine(rows, size):
        return lax.dynamic_slice_in_dim(rows, core[0] * size, size, 0)

    def fitted(rows):
        return jnp.pad(rows, ((0, half_in - half_out), (0, 0)))

    far_in = exchange(part_in, "nar", 2)
    own_rows = jnp.where(
        chip == 0,
        mine(momenta_in, half_in),
        fitted(mine(muon_beta * half_mom_out + part_out.astype(f32), half_out)),
    )
    far_mom = jnp.where(
        chip == 0,
        mine(halved(mom_in, 1 - chip), half_in),
        fitted(mine(lax.dynamic_slice_in_dim(mom_out, (1 - chip) * (rows_out // 2), rows_out // 2, 0), half_out)),
    )
    far_rows = jnp.where(chip == 0, mine(far_in, half_in), fitted(mine(far_out, half_out)))
    far_rows = muon_beta * far_mom + far_rows.astype(f32)
    summed = []
    result = None
    while not isinstance(folded_in, tuple):
        fill = () if summed else (far_in,)
        if len(summed) == len(halving):
            fill = (own_rows, far_rows)
        if len(summed) == len(halving) + len(full) + 1:
            branch = mlp_result + nn(after(attended, folded_in), w_out_all[:D])
            result = (tokens.astype(f32) + branch).astype(bf16)
            fill = (result,)
        folded_in = steps_in.send(fill)
        summed.append(folded_in)
        if not isinstance(folded_out, tuple):
            folded_out = steps_out.send(folded_in if isinstance(folded_in, tuple) else (folded_in,))
    extra = (folded_in[0][half:] + folded_in[1][half:]).reshape(extra_rows * half)
    grad_gains = extra[half : half + count]
    ortho = newton(folded_in, folded_out, own_rows, far_rows, jnp.stack([core[0], chip]))
    far_out, far_in = after(far_out, ortho), after(far_in, ortho)
    grad_w_out = join(part_out, far_out, chip, 0).reshape(rows_out, D).astype(f32)
    mom_out_new = muon_beta * mom_out + grad_w_out
    grad_w_in = after(rejoined(*ordered(part_in, far_in, chip))).astype(f32)
    mom_in_new = muon_beta * mom_in + grad_w_in

    other = exchange(ortho, "nar", 2, (mom_in_new, mom_out_new))
    ortho_in, ortho_out = ordered(ortho, other, chip)
    ortho_out = jnp.concatenate([ortho_out[half_in : half_in + half_out], ortho_out[:half_out]], axis=0)
    far_in, far_out = (exchange(rows, "nar", 1) for rows in (ortho_in, ortho_out))
    w_in_new, w_out_new = update(
        ortho_in, far_in, ortho_out, far_out, w_in, w_out, jnp.stack([core[0], start]), first if parted else rows_in
    )
    gain_m_new = adam_first * gain_m + (1 - adam_first) * grad_gains
    gain_v_new = adam_second * gain_v + (1 - adam_second) * grad_gains * grad_gains
    gains_new = gains - adam_rate * (gain_m_new / (1 - adam_first**STEP)) / (
        jnp.sqrt(gain_v_new / (1 - adam_second**STEP)) + adam_eps
    )
    return (
        result,
        grad_tokens,
        grad_w_in,
        grad_w_out,
        grad_gains,
        mom_in_new,
        mom_out_new,
        gain_m_new,
        gain_v_new,
        w_in_new,
        w_out_new,
        gains_new,
    )


def solution(mesh):
    rows = P(("nar", "wide"), None)
    wide = P("wide", None)
    return jax.shard_map(
        on_device,
        mesh=mesh,
        in_specs=(rows, rows, rows, wide, wide, P(), wide, wide, P(), P()),
        out_specs=(rows, rows, wide, wide, P(), wide, wide, P(), P(), wide, wide, P()),
        check_vma=False,
    )
```

```python
from functools import partial

import jax
import jax.numpy as jnp
from jax import lax
from jax.experimental import pallas as pl
from jax.experimental.pallas import tpu as pltpu
from jax.sharding import PartitionSpec as P

D = 768
HEADS = 12
HEAD = 64
LEN = 1024
STEP = 10
FIN = 5376
FOUT = 3840
QKV = 3 * D

f32 = jnp.float32
bf16 = jnp.bfloat16
ns_linear = 3.4445
ns_cubic = -4.775
ns_quintic = 2.0315
muon_beta = 0.5
muon_rate = 0.8
muon_decay = 0.1
adam_rate = 0.8
adam_first = 0.9
adam_second = 0.95
adam_eps = 1e-08
norm_eps = 1e-06
penalty = 16384.0
vmem_bytes = 60 * 1024 * 1024
tile_rows = 256
extra_rows = 32
pair = 2 * HEAD


def normalize(values):
    center = values - jnp.mean(values, axis=-1, keepdims=True)
    variance = jnp.mean(center * center, axis=-1, keepdims=True)
    inverse = lax.rsqrt(variance + norm_eps)
    return (center * inverse, inverse)


def norm_backward(grad_scaled, normed, inverse, axis=-1):
    mean_grad = jnp.mean(grad_scaled, axis=axis, keepdims=True)
    mean_cross = jnp.mean(grad_scaled * normed, axis=axis, keepdims=True)
    return inverse * (grad_scaled - mean_grad - normed * mean_cross)


def nn(a, b):
    return jnp.dot(a, b, preferred_element_type=f32)


def contract(a, b, dim_a, dim_b):
    return lax.dot_general(a, b, (((dim_a,), (dim_b,)), ((), ())), preferred_element_type=f32)


def normalize_columns(columns):
    center = columns - jnp.mean(columns, axis=0, keepdims=True)
    variance = jnp.mean(center * center, axis=0, keepdims=True)
    inverse = lax.rsqrt(variance + norm_eps)
    return (center * inverse, inverse)


core_spec = pl.BlockSpec(memory_space=pltpu.SMEM)


def halves(values, core_ref, keep_ref, send_ref):
    half = D // 2
    left, right = values[:, :half], values[:, half:]
    first = core_ref[0] == 0
    keep_ref[...] = jnp.where(first, left, right).reshape(keep_ref.shape)
    send_ref[...] = jnp.where(first, right, left).reshape(send_ref.shape)


def forward_kernel(
    x_ref, gy_ref, wq_ref, wk_ref, wv_ref, wa_ref, onek_ref, penq_ref, gq_ref, gk_ref, core_ref,
    joined_ref, do_ref, att_ref, terms_ref, exact_ref, sum_ref, keep_ref, send_ref, kaug, qaug_t, vaug_t,
):
    length = x_ref.shape[0]
    weights = jnp.concatenate([wq_ref[...], wk_ref[...], wv_ref[...]], axis=0)
    joined = contract(weights, x_ref[...], 1, 1).astype(bf16)
    for i in range(3):
        joined_ref[i] = joined[i * pair : (i + 1) * pair]
    do_ref[...] = contract(wa_ref[...], gy_ref[...], 1, 1).astype(bf16)
    parts = []
    for h in range(2):
        rows = slice(HEAD * h, HEAD * (h + 1))
        q_hat, _ = normalize_columns(joined_ref[0, rows, :].astype(f32))
        k_hat, _ = normalize_columns(joined_ref[1, rows, :].astype(f32))
        q_low = (q_hat * gq_ref[...]).astype(bf16)
        k_low = (k_hat * gk_ref[...]).astype(bf16)
        kaug[h, :, :HEAD] = k_low.T
        kaug[h, :, HEAD:] = onek_ref[...]
        qaug_t[h, :HEAD, :] = (q_low.astype(f32) * HEAD ** (-0.5)).astype(bf16)
        qaug_t[h, HEAD:, :] = penq_ref[...]
        vaug_t[h, :HEAD, :] = joined_ref[2, rows, :]
        vaug_t[h, HEAD:, :] = jnp.ones((16, length), bf16)
        terms_ref[h] = jnp.exp(nn(kaug[h], qaug_t[h])).astype(bf16)
        summed = nn(vaug_t[h], terms_ref[h])
        inverse_sum = 1.0 / summed[HEAD : HEAD + 1]
        sum_ref[0, h : h + 1, :] = inverse_sum
        attended = summed[:HEAD] * inverse_sum
        exact_ref[rows, :] = attended
        parts.append(attended)
    attended = jnp.concatenate(parts, 0).astype(bf16)
    halves(nn(attended, gy_ref[...]).astype(bf16), core_ref, keep_ref, send_ref)
    att_ref[...] = attended.T


def attention_forward(x_low, grad_y, w_in_all, w_out_all, ids, q_gain, k_gain, core):
    length = x_low.shape[0]
    pairs = D // pair
    image = jnp.where(ids < 0, 4, ids)
    number = jnp.arange(16)
    onek = (image[:, None] == number[None, :]).astype(bf16)
    penq = jnp.where(image[None, :] == number[:, None], 0.0, -penalty).astype(bf16)

    def rows(part):
        return pl.BlockSpec((pair, D), lambda p: (part * pairs + p, 0))

    def whole(shape):
        return pl.BlockSpec(shape, lambda p: (0, 0))

    call = pl.pallas_call(
        forward_kernel,
        grid=(pairs,),
        in_specs=[
            whole((length, D)), whole((length, D)), rows(0), rows(1), rows(2), rows(0),
            whole((length, 16)), whole((16, length)), whole((HEAD, 1)), whole((HEAD, 1)), core_spec,
        ],
        out_specs=[
            pl.BlockSpec((3, pair, length), lambda p: (0, p, 0)),
            pl.BlockSpec((pair, length), lambda p: (p, 0)),
            pl.BlockSpec((length, pair), lambda p: (0, p)),
            pl.BlockSpec((2, length, length), lambda p: (p, 0, 0)),
            pl.BlockSpec((pair, length), lambda p: (p, 0)),
            pl.BlockSpec((1, 8, length), lambda p: (p, 0, 0)),
            *[pl.BlockSpec((pair, D // 2), lambda p: (p, 0))] * 2,
        ],
        out_shape=[
            jax.ShapeDtypeStruct((3, D, length), bf16),
            jax.ShapeDtypeStruct((D, length), bf16),
            jax.ShapeDtypeStruct((length, D), bf16),
            jax.ShapeDtypeStruct((HEADS, length, length), bf16),
            jax.ShapeDtypeStruct((D, length), f32),
            jax.ShapeDtypeStruct((pairs, 8, length), f32),
            *[jax.ShapeDtypeStruct((D, D // 2), bf16)] * 2,
        ],
        scratch_shapes=[
            pltpu.VMEM((2, length, HEAD + 16), bf16),
            pltpu.VMEM((2, HEAD + 16, length), bf16),
            pltpu.VMEM((2, HEAD + 16, length), bf16),
        ],
        compiler_params=pltpu.CompilerParams(vmem_limit_bytes=vmem_bytes),
        cost_estimate=pl.CostEstimate(
            flops=HEADS * 4 * length * length * 256,
            bytes_accessed=16 * length * D + 2 * HEADS * length * length,
            transcendentals=HEADS * length * length,
        ),
        name="attention_forward",
    )
    return call(
        x_low, grad_y, w_in_all, w_in_all, w_in_all, w_out_all, onek, penq,
        q_gain.reshape(HEAD, 1), k_gain.reshape(HEAD, 1), core,
    )


def backward_kernel(
    joined_ref, do_ref, terms_ref, exact_ref, sum_ref, gq_ref, gk_ref, x_ref, core_ref, *refs, folds,
):
    *refs, vaug, qlow_t, klow_t, doaug_t = refs
    if folds:
        *refs, folded_ref = refs
    *refs, grads_ref, keep_ref, send_ref, ggq_ref, ggk_ref = refs
    if folds:
        size = folded_ref.shape[0] // 2
        for i in range(2):
            near_ref, far_ref = refs[-4 + 2 * i], refs[-3 + 2 * i]
            folded_ref[i * size : (i + 1) * size, :] = added(near_ref[...], far_ref[...])
    length = x_ref.shape[0]
    step = pl.program_id(0)
    q_gain = gq_ref[...]
    k_gain = gk_ref[...]
    dq_parts, dk_parts, dv_parts = [], [], []
    q_gain_grad = jnp.zeros((HEAD, 1), f32)
    k_gain_grad = jnp.zeros((HEAD, 1), f32)
    kept = []
    for h in range(2):
        rows = slice(HEAD * h, HEAD * (h + 1))
        q_hat, q_inverse = normalize_columns(joined_ref[0, rows, :].astype(f32))
        k_hat, k_inverse = normalize_columns(joined_ref[1, rows, :].astype(f32))
        klow_t[h] = (k_hat * k_gain).astype(bf16)
        qlow_t[h] = (q_hat * q_gain).astype(bf16)
        vaug[h, :, :HEAD] = joined_ref[2, rows, :].T
        vaug[h, :, HEAD:] = jnp.ones((length, 16), bf16)
        inverse_sum = sum_ref[0, h : h + 1, :]
        do_head = do_ref[rows, :].astype(f32)
        inner = -jnp.sum(do_head * exact_ref[rows, :], axis=0, keepdims=True) * inverse_sum
        do_low = (do_head * inverse_sum).astype(bf16)
        inner_high = inner.astype(bf16).astype(f32)
        extra = lax.broadcasted_iota(jnp.int32, (16, length), 0)
        extra = jnp.where(extra == 0, inner_high, jnp.where(extra == 1, inner - inner_high, 0.0))
        doaug_t[h, :HEAD, :] = do_low
        doaug_t[h, HEAD:, :] = extra.astype(bf16)
        kept.append((q_hat, q_inverse, k_hat, k_inverse))
    sums = [[None] * 3 for _ in range(2)]
    for k in range(0, length, tile_rows):
        for h in range(2):
            span = slice(k, k + tile_rows)
            terms = terms_ref[h, span, :]
            dscores = (terms.astype(f32) * nn(vaug[h, span, :], doaug_t[h])).astype(bf16)
            dv = contract(doaug_t[h, :HEAD, :], terms, 1, 1)
            dk = contract(qlow_t[h], dscores, 1, 1)
            dq = nn(klow_t[h, :, span], dscores)
            sums[h][0] = dq if sums[h][0] is None else sums[h][0] + dq
            sums[h][1] = [dk] if sums[h][1] is None else sums[h][1] + [dk]
            sums[h][2] = [dv] if sums[h][2] is None else sums[h][2] + [dv]
    for h in range(2):
        q_hat, q_inverse, k_hat, k_inverse = kept[h]
        dquery = sums[h][0] * HEAD ** (-0.5)
        dkey = jnp.concatenate(sums[h][1], axis=1) * HEAD ** (-0.5)
        dvalue = jnp.concatenate(sums[h][2], axis=1)
        q_gain_grad += jnp.sum(dquery * q_hat, axis=1, keepdims=True)
        k_gain_grad += jnp.sum(dkey * k_hat, axis=1, keepdims=True)
        dq_parts.append(norm_backward(dquery * q_gain, q_hat, q_inverse, 0))
        dk_parts.append(norm_backward(dkey * k_gain, k_hat, k_inverse, 0))
        dv_parts.append(dvalue)
    grads = jnp.concatenate(dq_parts + dk_parts + dv_parts, 0).astype(bf16)
    halves(nn(grads, x_ref[...]).astype(bf16), core_ref, keep_ref, send_ref)
    grads_ref[0] = grads[:pair].T
    grads_ref[1] = grads[pair : 2 * pair].T
    grads_ref[2] = grads[2 * pair :].T

    @pl.when(step == 0)
    def _():
        ggq_ref[...] = jnp.zeros_like(ggq_ref)
        ggk_ref[...] = jnp.zeros_like(ggk_ref)

    ggq_ref[...] += jnp.broadcast_to(q_gain_grad, ggq_ref.shape)
    ggk_ref[...] += jnp.broadcast_to(k_gain_grad, ggk_ref.shape)


def attention_backward(
    joined, dattended, terms, exact, inverse_sum, q_gain, k_gain, x_low, core, first, count, room,
    place=0, into=(), fold=(), origin=0, size=0,
):
    length = x_low.shape[0]

    def whole(shape):
        return pl.BlockSpec(shape, lambda p: (0, 0))

    last = (fold[0].shape[0] - origin - size) // (FIN // 8) if fold else 0

    def segment(i):
        return pl.BlockSpec(
            (pl.Element(size), pl.Element(D // 2)),
            lambda p: (pl.multiple_of(origin + FIN // 8 * jnp.minimum(2 * p + i, last), 32), 0),
        )

    gain = jax.ShapeDtypeStruct((HEAD, 128), f32)
    call = pl.pallas_call(
        partial(backward_kernel, folds=bool(fold)),
        grid=(count,),
        in_specs=[
            pl.BlockSpec((3, pair, length), lambda p: (0, first + p, 0)),
            pl.BlockSpec((pair, length), lambda p: (first + p, 0)),
            pl.BlockSpec((2, length, length), lambda p: (first + p, 0, 0)),
            pl.BlockSpec((pair, length), lambda p: (first + p, 0)),
            pl.BlockSpec((1, 8, length), lambda p: (first + p, 0, 0)),
            whole((HEAD, 1)), whole((HEAD, 1)), whole((length, D)), core_spec,
            *[pl.BlockSpec(memory_space=pl.ANY)] * len(into),
            *[segment(i) for i in range(2) for _ in fold],
        ],
        out_specs=[pl.BlockSpec((3, length, pair), lambda p: (0, 0, p))]
        + [pl.BlockSpec((3, pair, D // 2), lambda p: (0, place + p, 0))] * 2
        + [whole((HEAD, 128))] * 2
        + [pl.BlockSpec((2 * size, D // 2), lambda p: (p, 0))] * bool(fold),
        out_shape=[jax.ShapeDtypeStruct((3, length, count * pair), bf16)]
        + [jax.ShapeDtypeStruct((3, room * pair, D // 2), bf16)] * 2 + [gain] * 2
        + [jax.ShapeDtypeStruct(((last + 1) * size, D // 2), bf16)] * bool(fold),
        input_output_aliases={9 + i: 1 + i for i in range(len(into))},
        scratch_shapes=[
            pltpu.VMEM((2, length, HEAD + 16), bf16),
            pltpu.VMEM((2, HEAD, length), bf16),
            pltpu.VMEM((2, HEAD, length), bf16),
            pltpu.VMEM((2, HEAD + 16, length), bf16),
        ],
        compiler_params=pltpu.CompilerParams(vmem_limit_bytes=vmem_bytes),
        cost_estimate=pl.CostEstimate(
            flops=2 * count * 8 * length * length * 256,
            bytes_accessed=24 * length * count * pair + 4 * count * length * length,
            transcendentals=0,
        ),
        name="attention_backward",
    )
    outs = call(joined, dattended, terms, exact, inverse_sum, q_gain.reshape(HEAD, 1), k_gain.reshape(HEAD, 1), x_low, core, *into, *fold, *fold)
    return (*outs[:3], outs[3][:, 0], outs[4][:, 0], *outs[5:])


def gelu_pair(u):
    z = jnp.abs(u) * 0.7071067811865476
    t = 1.0 / (1.0 + 0.3275911 * z)
    e = jnp.exp(-z * z)
    poly = t * (0.127414796 + t * (-0.142248368 + t * (0.7107068705 + t * (-0.7265760135 + t * 0.5307027145))))
    half = poly * e
    phi = jnp.where(u >= 0, 1.0 - half, half)
    return (u * phi, phi + u * (0.3989422804014327 * e))


def mlp_kernel(
    x_ref, gy_ref, wu_ref, wd_ref, core_ref,
    res_ref, gn_ref, keep_up, send_up, keep_down, send_down, act_ref, dup_ref,
):
    @pl.when(pl.program_id(0) == 0)
    def _():
        res_ref[...] = jnp.zeros_like(res_ref)
        gn_ref[...] = jnp.zeros_like(gn_ref)

    for begin in range(0, wu_ref.shape[0], tile_rows):
        units = slice(begin, begin + tile_rows)
        upward = contract(x_ref[...], wu_ref[units], 1, 1).astype(bf16).astype(f32)
        grad_hidden = contract(gy_ref[...], wd_ref[units], 1, 1)
        active, slope = gelu_pair(upward)
        act_ref[:, units] = active.astype(bf16)
        dup_ref[:, units] = (grad_hidden * slope).astype(bf16)
    active, dupward = act_ref[...], dup_ref[...]
    res_ref[...] += nn(active, wd_ref[...])
    gn_ref[...] += nn(dupward, wu_ref[...])
    halves(contract(active, gy_ref[...], 0, 0).astype(bf16), core_ref, keep_down, send_down)
    halves(contract(dupward, x_ref[...], 0, 0).astype(bf16), core_ref, keep_up, send_up)


def mlp(x_low, grad_y, w_in_all, w_out_all, core):
    length = x_low.shape[0]
    hidden = w_in_all.shape[0] - QKV
    tile = D
    whole = pl.BlockSpec((length, D), lambda t: (0, 0))
    total = jax.ShapeDtypeStruct((length, D), f32)
    grad = jax.ShapeDtypeStruct((hidden, D // 2), bf16)
    call = pl.pallas_call(
        mlp_kernel,
        grid=(hidden // tile,),
        in_specs=[
            whole,
            whole,
            pl.BlockSpec((tile, D), lambda t: (t + QKV // tile, 0)),
            pl.BlockSpec((tile, D), lambda t: (t + D // tile, 0)),
            core_spec,
        ],
        out_specs=[whole, whole] + [pl.BlockSpec((tile, D // 2), lambda t: (t, 0))] * 4,
        out_shape=[total, total] + [grad] * 4,
        scratch_shapes=[pltpu.VMEM((length, tile), bf16)] * 2,
        compiler_params=pltpu.CompilerParams(vmem_limit_bytes=vmem_bytes),
        cost_estimate=pl.CostEstimate(
            flops=18 * length * D * hidden,
            bytes_accessed=12 * length * D + 8 * hidden * D,
            transcendentals=length * hidden,
        ),
        name="mlp",
    )
    return call(x_low, grad_y, w_in_all, w_out_all, core)


def input_kernel(*refs, calls):
    grads = refs[:calls]
    w_ref, normed_ref, tokens_ref, gy_ref, gain_ref, out_ref, ln_ref, total = refs[calls:]
    step = pl.program_id(0)

    @pl.when(step == 0)
    def _():
        total[...] = normed_ref[...]

    begin = 0
    sums = []
    for ref in grads:
        sums.append(nn(ref[0], w_ref[begin : begin + ref.shape[2], :]))
        begin += ref.shape[2]
    total[...] += sum(sums)

    @pl.when(step == pl.num_programs(0) - 1)
    def _():
        x_hat, x_inverse = normalize(tokens_ref[...].astype(f32))
        grad_normed = total[...]
        ln_ref[...] = jnp.sum(grad_normed * x_hat, axis=0, keepdims=True)
        back = norm_backward(grad_normed * gain_ref[...], x_hat, x_inverse)
        out_ref[...] = (gy_ref[...].astype(f32) + back).astype(bf16)


def input_gradient(grads, w_in_all, normed, tokens, grad_y, gain):
    length = tokens.shape[0]
    whole = pl.BlockSpec((length, D), lambda p: (0, 0))
    row = pl.BlockSpec((1, D), lambda p: (0, 0))
    call = pl.pallas_call(
        partial(input_kernel, calls=len(grads)),
        grid=(3,),
        in_specs=[pl.BlockSpec((1, length, grad.shape[2]), lambda p: (p, 0, 0)) for grad in grads]
        + [pl.BlockSpec((D, D), lambda p: (p, 0)), whole, whole, whole, row],
        out_specs=[whole, row],
        out_shape=[jax.ShapeDtypeStruct((length, D), bf16), jax.ShapeDtypeStruct((1, D), f32)],
        scratch_shapes=[pltpu.VMEM((length, D), f32)],
        compiler_params=pltpu.CompilerParams(vmem_limit_bytes=vmem_bytes),
        cost_estimate=pl.CostEstimate(
            flops=2 * length * D * QKV, bytes_accessed=20 * length * D, transcendentals=length
        ),
        name="input_gradient",
    )
    out, ln_grad = call(*grads, w_in_all, normed, tokens, grad_y, gain.reshape(1, D))
    return (out, ln_grad[0])


def split(values):
    high = values.astype(bf16)
    return (high, (values - high.astype(f32)).astype(bf16))


def newton_kernel(
    near_ref, other_ref, own_ref, far_ref, core_ref, o_ref, gh, gl, sh, sl, ph, pw, g32, x32
):
    count = D // tile_rows

    def span(i):
        return slice(i * tile_rows, (i + 1) * tile_rows)

    def store(high_ref, low_ref, i, j, value):
        high_ref[span(i), span(j)], low_ref[span(i), span(j)] = split(value)
        if i != j:
            high_ref[span(j), span(i)], low_ref[span(j), span(i)] = split(value.T)

    def symmetric(ah, al, bh, bl, post):
        for i in range(count):
            for j in range(i, count):
                rows, columns = span(i), span(j)
                post(
                    i,
                    j,
                    nn(ah[rows, :], bh[:, columns])
                    + (nn(ah[rows, :], bl[:, columns]) + nn(al[rows, :], bh[:, columns])),
                )

    def squared(ah, al, post):
        for i in range(count):
            for j in range(i, count):
                rows, columns = span(i), span(j)
                mixed = nn(ah[rows, :], al[:, columns])
                other = mixed if i == j else nn(ah[columns, :], al[:, rows])
                post(i, j, nn(ah[rows, :], ah[:, columns]) + (mixed + other.T))

    def sweep(last):
        def keep_factor(i, j, value):
            value = ns_cubic * g32[span(i), span(j)] + ns_quintic * value
            if i == j:
                shape = (tile_rows, tile_rows)
                diagonal = lax.broadcasted_iota(jnp.int32, shape, 0) == lax.broadcasted_iota(jnp.int32, shape, 1)
                value = value + jnp.where(diagonal, ns_linear, 0.0)
            store(ph, pw, i, j, value)

        def keep_gram(i, j, value):
            g32[span(i), span(j)] = value
            store(gh, gl, i, j, value)

        squared(gh, gl, keep_factor)
        xh, xl = split(x32[...])
        x32[...] = nn(xh, ph[...]) + (nn(xh, pw[...]) + nn(xl, ph[...]))
        if not last:
            symmetric(gh, gl, ph, pw, partial(store, sh, sl))
            symmetric(sh, sl, ph, pw, keep_gram)

    half = D // 2
    first_core = core_ref[0] == 0
    left = jnp.where(first_core, near_ref[...], other_ref[...])
    side = jnp.where(first_core, other_ref[:half], near_ref[:half])
    corner = left[:half]
    i = lax.broadcasted_iota(jnp.int32, (half, half), 0)
    j = lax.broadcasted_iota(jnp.int32, (half, half), 1)
    corner_t = corner.T
    first = jnp.where(i <= j, corner, corner_t)
    last = jnp.where(i > j, corner, jnp.where(i == j, left[half : half + 1], corner_t))
    trace = jnp.sum(jnp.where(i == j, first + last, 0.0), axis=0, keepdims=True)
    trace = jnp.sum(trace, axis=1, keepdims=True)
    inverse = 1.0 / (jnp.sqrt(trace) + 1e-07)
    square = inverse * inverse
    g32[:half, :half] = first * square
    g32[half:, half:] = last * square
    g32[:half, half:] = side * square
    g32[half:, :half] = side.T * square
    rows = own_ref.shape[0]
    x32[:rows] = own_ref[...] * inverse
    x32[rows:] = far_ref[...] * inverse
    gh[...], gl[...] = split(g32[...])

    @pl.loop(0, 4)
    def _(k):
        sweep(False)

    sweep(True)
    o_ref[...] = x32[...].astype(bf16)


def newton(folded, far_folded, own_rows, far_rows, core):
    rows = own_rows.shape[0] + far_rows.shape[0]
    whole = pl.BlockSpec(memory_space=pltpu.VMEM)
    call = pl.pallas_call(
        newton_kernel,
        in_specs=[whole] * 4 + [core_spec],
        out_specs=whole,
        out_shape=jax.ShapeDtypeStruct((rows, D), bf16),
        scratch_shapes=[pltpu.VMEM((D, D), bf16)] * 6 + [pltpu.VMEM((D, D), f32), pltpu.VMEM((rows, D), f32)],
        compiler_params=pltpu.CompilerParams(vmem_limit_bytes=vmem_bytes),
        cost_estimate=pl.CostEstimate(
            flops=30 * D * D * (2 * D + rows), bytes_accessed=4 * D * D + 6 * rows * D, transcendentals=0
        ),
        name="newton",
    )
    return call(folded, far_folded, own_rows, far_rows, core)


def update_kernel(in_ref, in_far_ref, out_ref, out_far_ref, wi_ref, wo_ref, place_ref, in_new, out_new, held, *, first):
    def new(weights, ortho, size):
        rate = muon_rate * (size / D) ** 0.5
        return weights.astype(f32) * (1 - muon_rate * muon_decay) - rate * ortho.astype(f32)

    first_core = place_ref[0] == 0
    for near_ref, far_ref, total in ((in_ref, in_far_ref, None), (out_ref, out_far_ref, out_new)):
        size = far_ref.shape[0] // 2
        all_near, all_far, weights = near_ref[...].astype(f32), far_ref[...].astype(f32), wo_ref[...].astype(f32)
        for chip in range(2):
            rows = slice(chip * size, (chip + 1) * size)
            near, far = all_near[rows], all_far[rows]
            begin = 2 * chip * size
            both = (jnp.where(first_core, near, far), jnp.where(first_core, far, near))
            for i in range(2):
                spot = slice(begin + i * size, begin + (i + 1) * size)
                if total is None:
                    held[spot] = both[i]
                else:
                    total[spot] = new(weights[spot], both[i], FOUT)
    rows = in_new.shape[0]
    if first == rows:
        in_new[...] = new(wi_ref[...], held[...], FIN)
        return
    start = pl.multiple_of(place_ref[1], 32)
    cut, rest = first // 2, (rows - first) // 2
    pieces = jnp.concatenate([held[cut : cut + rest], held[rows // 2 + cut :]], axis=0)
    in_new[: rows - first] = new(wi_ref[: rows - first], pieces, FIN)
    in_new[first:] = jnp.where(
        lax.broadcasted_iota(jnp.int32, (rows - first, 1), 0) < start, in_new[first:], new(wi_ref[first:], pieces, FIN)
    )
    spot = pl.ds(start, first)
    pieces = jnp.concatenate([held[:cut], held[rows // 2 : rows // 2 + cut]], axis=0)
    in_new[spot] = new(wi_ref[spot], pieces, FIN)


def update(ortho_in, far_in, ortho_out, far_out, w_in, w_out, place, first):
    whole = pl.BlockSpec(memory_space=pltpu.VMEM)
    call = pl.pallas_call(
        partial(update_kernel, first=first),
        in_specs=[whole] * 6 + [core_spec],
        out_specs=[whole] * 2,
        out_shape=[jax.ShapeDtypeStruct(w.shape, f32) for w in (w_in, w_out)],
        scratch_shapes=[pltpu.VMEM(w_in.shape, f32)],
        compiler_params=pltpu.CompilerParams(vmem_limit_bytes=vmem_bytes),
        cost_estimate=pl.CostEstimate(flops=4 * w_in.size, bytes_accessed=14 * w_in.size, transcendentals=0),
        name="update",
    )
    return call(ortho_in, far_in, ortho_out, far_out, w_in, w_out, place)


def gram_kernel(m_ref, extra_ref, core_ref, o_ref):
    half = D // 2
    left, right = slice(0, half), slice(half, D)

    def product(a, b):
        ah, al = split(m_ref[:, a])
        bh, bl = split(m_ref[:, b])
        return contract(ah, bh, 0, 0) + (contract(ah, bl, 0, 0) + contract(al, bh, 0, 0))

    o_ref[half:, :] = extra_ref[...]

    @pl.when(core_ref[0] == 0)
    def _():
        i = lax.broadcasted_iota(jnp.int32, (half, half), 0)
        j = lax.broadcasted_iota(jnp.int32, (half, half), 1)
        last = product(right, right)
        o_ref[:half, :] = jnp.where(i <= j, product(left, left), last)
        o_ref[half : half + 1, :] = jnp.sum(jnp.where(i == j, last, 0.0), axis=0, keepdims=True)

    @pl.when(core_ref[0] != 0)
    def _():
        o_ref[:half, :] = product(left, right)


def folded_gram(rows, extra, core):
    rows = jnp.pad(rows, ((0, -rows.shape[0] % 16), (0, 0)))
    whole = pl.BlockSpec(memory_space=pltpu.VMEM)
    call = pl.pallas_call(
        gram_kernel,
        in_specs=[whole, whole, core_spec],
        out_specs=whole,
        out_shape=jax.ShapeDtypeStruct((D // 2 + extra_rows, D // 2), f32),
        compiler_params=pltpu.CompilerParams(vmem_limit_bytes=vmem_bytes),
        cost_estimate=pl.CostEstimate(
            flops=4 * rows.shape[0] * D * D, bytes_accessed=8 * rows.shape[0] * D, transcendentals=0
        ),
        name="gram",
    )
    return call(rows, extra, core)


def bits(size):
    return [1 << b for b in range(size.bit_length() - 1)]


def take(values, index, axis):
    return lax.dynamic_index_in_dim(values, index, axis, keepdims=False)


def after(value, *others):
    return lax.optimization_barrier((value, *others))[0]


def exchange(values, axis, bit, fill=()):
    size = lax.axis_size(axis)
    return after(lax.ppermute(values, axis, [(i, i ^ bit) for i in range(size)]), *fill)


def sum_steps(values, halving, full):
    fill = yield values
    for axis, bit in halving:
        side = (lax.axis_index(axis) // bit) % 2
        pieces = values.reshape(2, values.shape[0] // 2, values.shape[1])
        values = take(pieces, side, 0) + exchange(take(pieces, 1 - side, 0), axis, bit, fill)
        fill = yield values
    for axis, bit in full:
        values = values + exchange(values, axis, bit, fill)
        fill = yield values


def halve(parts, axis, name, bit):
    side = (lax.axis_index(name) // bit) % 2
    sent = [take(part, 1 - side, axis) for part in parts]

    def receive(*fill):
        kept = jnp.concatenate([take(part, side, axis) for part in parts], axis=0)
        return (kept, exchange(jnp.concatenate(sent, axis=0), name, bit, fill))

    return sent, receive


def added(kept, other):
    return (kept.astype(f32) + other.astype(f32)).astype(bf16)


def scatter_one(*parts):
    wide = lax.axis_size("wide")
    columns = parts[0].shape[-1]
    rows = sum(part.size for part in parts) // (2 * wide * columns)
    cut = rows // 16 * 8
    parts = [part.reshape(-1, 2, 2, rows, columns) for part in parts]
    sent_a, receive_a = halve([part[:, :, :, :cut] for part in parts], 1, "wide", 1)
    sent_b, receive_b = halve([part[:, :, :, cut:] for part in parts], 2, "nar", 2)
    return sent_a + sent_b, lambda *fill: (added(*receive_a(*fill)), added(*receive_b(*fill)))


def split_kernel(*refs, pairs, rows):
    *parts, place_ref, sent_y, kept_y, sent_x, kept_x, held = refs
    begin = 0
    for paired in pairs:
        values = parts.pop(0)[...].astype(f32)
        if paired:
            values = values + parts.pop(0)[...].astype(f32)
        held[begin : begin + values.shape[0]] = values
        begin += values.shape[0]
    cut = kept_y.shape[2]
    for z in range(kept_y.shape[0]):
        for j in range(2):
            for near, out_y, out_x in ((True, kept_y, kept_x), (False, sent_y, sent_x)):
                y = place_ref[0] if near else 1 - place_ref[0]
                x = place_ref[1] if near else 1 - place_ref[1]
                first = pl.ds(pl.multiple_of(((2 * z + y) * 2 + j) * rows, 8), cut)
                out_y[z, j] = held[first].astype(bf16)
                second = pl.ds(pl.multiple_of(((2 * z + j) * 2 + x) * rows + cut, 8), rows - cut)
                out_x[z, j] = held[second].astype(bf16)


def split_one(rows, *parts):
    half = D // 2
    cut = rows // 16 * 8
    far = lax.axis_size("wide") // 2
    place = jnp.stack([lax.axis_index("wide") % 2, lax.axis_index("nar") // 2])
    terms = [term.reshape(-1, half) for part in parts for term in (part if isinstance(part, tuple) else (part,))]
    whole = pl.BlockSpec(memory_space=pltpu.VMEM)
    shapes = [(far, 2, cut, half)] * 2 + [(far, 2, rows - cut, half)] * 2
    call = pl.pallas_call(
        partial(split_kernel, pairs=[isinstance(part, tuple) for part in parts], rows=rows),
        in_specs=[whole] * len(terms) + [core_spec],
        out_specs=[whole] * 4,
        out_shape=[jax.ShapeDtypeStruct(shape, bf16) for shape in shapes],
        scratch_shapes=[pltpu.VMEM((4 * far * rows, half), f32)],
        compiler_params=pltpu.CompilerParams(vmem_limit_bytes=vmem_bytes),
        cost_estimate=pl.CostEstimate(
            flops=8 * far * rows * half, bytes_accessed=24 * far * rows * half, transcendentals=0
        ),
        name="split",
    )
    sent_y, kept_y, sent_x, kept_x = call(*terms, place)

    def arrive(*fill):
        return (exchange(sent_y, "wide", 1, fill), exchange(sent_x, "nar", 2, fill))

    return [sent_y, sent_x], arrive, lambda other_y, other_x: (added(kept_y, other_y), added(kept_x, other_x))


def scatter_two(held):
    sent_a, receive_a = halve(held[:1], 1, "nar", 2)
    sent_b, receive_b = halve(held[1:], 1, "wide", 1)

    def receive(*fill):
        kept, other = zip(receive_a(*fill), receive_b(*fill), strict=True)
        return added(jnp.concatenate(kept, axis=1), jnp.concatenate(other, axis=1))

    return sent_a + sent_b, receive


def scatter_rest(held):
    wide = lax.axis_size("wide")
    far = wide // 2
    place = lax.axis_index("wide") // 2
    sent = [take(held, place ^ shift, 0) for shift in range(1, far)]

    def receive(*fill):
        total = take(held, place, 0).astype(f32)
        for shift in reversed(range(1, far)):
            pairs = [(i, i ^ (2 * shift)) for i in range(wide)]
            total = total + after(lax.ppermute(sent[shift - 1], "wide", pairs), *fill).astype(f32)
        return total.astype(bf16)

    return sent, receive


def both_cores(values, *fill):
    other = exchange(values, "nar", 1, fill)
    return join(values, other, lax.axis_index("nar") % 2, 1).reshape(values.shape[0], D)


def ordered(values, other, side):
    return (jnp.where(side == 0, values, other), jnp.where(side == 0, other, values))


def join(values, other, side, axis):
    return jnp.stack(ordered(values, other, side), axis)


def gather(values):
    wide = lax.axis_size("wide")
    rows = values.shape[0]
    far = wide // 2
    place, side = lax.axis_index("wide") // 2, lax.axis_index("wide") % 2
    chip, core = lax.axis_index("nar") // 2, lax.axis_index("nar") % 2
    held = lax.dynamic_update_index_in_dim(jnp.zeros((far, rows, D), values.dtype), values, place, 0)
    for shift in range(1, far):
        pairs = [(i, i ^ (2 * shift)) for i in range(wide)]
        held = lax.dynamic_update_index_in_dim(held, lax.ppermute(values, "wide", pairs), place ^ shift, 0)
    cut = rows // 32 * 16
    first, second = held[:, :cut], held[:, cut:]
    first = join(first, exchange(first, "wide", 1), side, 1)
    second = join(second, exchange(second, "nar", 2), chip, 1)
    first = join(first, exchange(first, "nar", 2), chip, 2)
    second = join(second, exchange(second, "wide", 1), side, 1)
    held = jnp.concatenate([first, second], axis=3)
    return join(held, exchange(held, "nar", 1), core, 3).reshape(-1, D)


def on_device(tokens, cotangent, image_ids, w_in, w_out, gains, mom_in, mom_out, gain_m, gain_v):
    row_count = tokens.shape[0]
    rows_in = w_in.shape[0]
    rows_out = w_out.shape[0]
    nar_count = lax.axis_size("nar")
    wide_count = lax.axis_size("wide")
    nar_place = lax.axis_index("nar")
    share_in = rows_in // nar_count
    share_out = rows_out // nar_count
    everyone = ("wide", "nar")

    def share(rows, size):
        return lax.dynamic_slice_in_dim(rows, nar_place * size, size, 0)

    w_in_all = lax.all_gather(share(w_in, share_in), everyone, axis=0, tiled=True)
    w_out_all = gather(share(w_out, share_out))

    x_float = tokens.astype(f32)
    ln_gain = gains[:D]
    x_hat, x_inverse = normalize(x_float)
    x_low = (x_hat * ln_gain).astype(bf16)
    live = (image_ids.reshape(row_count) >= 0)[:, None]
    grad_y = jnp.where(live, cotangent, jnp.zeros_like(cotangent))

    core = (nar_place % 2).reshape(1)
    chip = nar_place // 2
    half = D // 2
    pairs = D // pair
    q_gain, k_gain = gains[D : D + HEAD], gains[D + HEAD :]
    first = rows_in * 4 // 7
    second = rows_in - first
    parted = wide_count == 8 and first == half and rows_in == 672
    mlp_result, mlp_normed, keep_up, send_up, keep_down, send_down = mlp(x_low, grad_y, w_in_all, w_out_all, core)
    joined, dattended, attended, terms, exact, inverse_sum, keep_att, send_att = attention_forward(
        after(x_low, keep_down), grad_y, w_in_all, w_out_all, image_ids.reshape(row_count), q_gain, k_gain, core
    )

    def backward(begin, count, earlier=(), **buffers):
        return attention_backward(
            joined, dattended, terms, exact, inverse_sum, q_gain, k_gain, after(x_low, *earlier), core, begin, count,
            **buffers,
        )

    def cores(keep, send, *fill):
        return added(keep, exchange(send, "nar", 1, fill)).reshape(-1, half)

    start = 96 * jnp.minimum(lax.axis_index("wide"), 3)
    row = lax.broadcasted_iota(jnp.int32, (rows_in, 1), 0)
    half_mom_out = lax.dynamic_slice_in_dim(mom_out, chip * (rows_out // 2), rows_out // 2, 0)
    wide_bits = bits(wide_count)
    halving = [("wide", wide_bits[0]), ("nar", 2)]
    full = [("wide", bit) for bit in wide_bits[1:]]

    def begin_out(part):
        zeros = jnp.zeros((extra_rows, half), f32)
        steps = sum_steps(folded_gram(muon_beta * half_mom_out + part.astype(f32), zeros, core), halving, full)
        return (steps, next(steps))

    if parted:
        def pair_of(keep, send, *fill):
            return (keep, exchange(send, "nar", 1, fill))

        down = pair_of(keep_down, send_down, keep_att)
        up = pair_of(keep_up, send_up, keep_att)
        sent, arrive, combine = split_one(rows_out // 2, pair_of(keep_att, send_att), down)
        dqkv_a, keep_a, send_a, q_grad_a, k_grad_a, up_a = backward(0, 3, sent, room=3, fold=up, size=first)
        sent, receive = scatter_two(combine(*arrive(keep_a)))
        dqkv_b, keep_b, send_b, q_grad_b, k_grad_b = backward(3, 1, [keep_a, *sent], room=3)
        sent_o, receive_o = scatter_rest(receive(dqkv_b))
        sent_a, arrive_a, combine_a = split_one(first // 2, pair_of(keep_a, send_a, dqkv_b), up_a)
        dqkv_c, keep_b, send_b, q_grad_c, k_grad_c, up_b = backward(
            4, 2, [*sent_a, *sent_o], room=3, place=1, into=(keep_b, send_b), fold=up, origin=first, size=second
        )
        part_out = receive_o(dqkv_c)
        sent_a, receive_a = scatter_two(combine_a(*arrive_a(dqkv_c)))
        sent_b, arrive_b, combine_b = split_one(second // 2, pair_of(keep_b, send_b, part_out, *sent_a), up_b)
        held_b = combine_b(*arrive_b(*sent_b))
        sent_b, receive_b = scatter_two(held_b)
        part_out = both_cores(part_out, *sent_b)
        steps_out, folded_out = begin_out(after(part_out, *sent_b))
        held_a = receive_a(*sent_b)
        held_b = receive_b(held_a, folded_out)
        sent, receive = scatter_rest(jnp.concatenate([held_a, held_b], axis=1))
        grad_tokens, ln_grad = input_gradient(
            [dqkv_a, dqkv_b, dqkv_c], w_in_all, after(mlp_normed, *sent), tokens, grad_y, ln_gain
        )
        far_out = exchange(after(part_out, *sent), "nar", 2, (grad_tokens,))
        part_in = receive(grad_tokens, far_out)
        folded_out = steps_out.send((part_in,))
        steps_done = 1
        q_gain_grad, k_gain_grad = q_grad_a + q_grad_b + q_grad_c, k_grad_a + k_grad_b + k_grad_c

        def halved(rows, chip):
            inside = lax.dynamic_slice_in_dim(rows, start, first, 0)
            others = jnp.where(row[:second] < start, rows[:second], rows[first:])
            return jnp.concatenate(
                [
                    lax.dynamic_slice_in_dim(inside, chip * (first // 2), first // 2, 0),
                    lax.dynamic_slice_in_dim(others, chip * (second // 2), second // 2, 0),
                ],
                axis=0,
            )

        def rejoined(near, far):
            cut = first // 2
            a, b = jnp.concatenate([near[:cut], far[:cut]], 0), jnp.concatenate([near[cut:], far[cut:]], 0)
            a = lax.dynamic_update_slice_in_dim(jnp.zeros((rows_in, D), a.dtype), a, start, 0)
            empty = jnp.zeros((first, D), b.dtype)
            below = jnp.concatenate([b, empty], axis=0)
            above = jnp.concatenate([empty, b], axis=0)
            inside = (row >= start) & (row < start + first)
            return jnp.where(inside, a, jnp.where(row < start, below, above))

    else:
        dqkv, keep_a, send_a, q_gain_grad, k_gain_grad = backward(0, pairs, room=pairs)
        grad_tokens, ln_grad = input_gradient([dqkv], w_in_all, mlp_normed, tokens, grad_y, ln_gain)

        def scattered(*parts):
            held = scatter_one(jnp.concatenate(parts, axis=0))[1]()
            return scatter_rest(scatter_two(held)[1]())[1]()

        part_out = both_cores(scattered(cores(keep_att, send_att), cores(keep_down, send_down)))
        steps_out, folded_out = begin_out(part_out)
        steps_done = 0
        far_out = exchange(part_out, "nar", 2)
        part_in = scattered(cores(keep_a, send_a), cores(keep_up, send_up))

        def halved(rows, chip):
            return lax.dynamic_slice_in_dim(rows, chip * (rows_in // 2), rows_in // 2, 0)

        def rejoined(near, far):
            return jnp.concatenate([near, far], axis=0)

    part_in = both_cores(part_in)
    gain_terms = jnp.concatenate([ln_grad, q_gain_grad, k_gain_grad])
    count = gain_terms.shape[0]
    extra = jnp.pad(gain_terms, (half, (extra_rows - 1) * half - count)).reshape(extra_rows, half)
    momenta_in = muon_beta * halved(mom_in, chip) + part_in.astype(f32)
    steps_in = sum_steps(folded_gram(momenta_in, extra, core), halving, full)
    folded_in = next(steps_in)

    half_in, half_out = rows_in // 4, rows_out // 4

    def mine(rows, size):
        return lax.dynamic_slice_in_dim(rows, core[0] * size, size, 0)

    def fitted(rows):
        return jnp.pad(rows, ((0, half_in - half_out), (0, 0)))

    far_in = exchange(part_in, "nar", 2)
    own_rows = jnp.where(
        chip == 0,
        mine(momenta_in, half_in),
        fitted(mine(muon_beta * half_mom_out + part_out.astype(f32), half_out)),
    )
    far_mom = jnp.where(
        chip == 0,
        mine(halved(mom_in, 1 - chip), half_in),
        fitted(mine(lax.dynamic_slice_in_dim(mom_out, (1 - chip) * (rows_out // 2), rows_out // 2, 0), half_out)),
    )
    far_rows = jnp.where(chip == 0, mine(far_in, half_in), fitted(mine(far_out, half_out)))
    far_rows = muon_beta * far_mom + far_rows.astype(f32)
    steps = len(halving) + len(full)
    for step in range(steps):
        fill = {0: (far_in,), len(halving): (own_rows, far_rows)}.get(step, ())
        folded_in = steps_in.send(fill)
        if steps_done < steps:
            folded_out = steps_out.send((folded_in,))
            steps_done += 1
    own, far = ordered(folded_in, folded_out, chip)
    folded = join(own, exchange(far, "nar", 2), chip, 0).reshape(-1, half)
    branch = mlp_result + nn(after(attended, folded), w_out_all[:D])
    result = (tokens.astype(f32) + branch).astype(bf16)
    side = lax.axis_index("wide") % 2
    folded = join(folded, exchange(folded, "wide", 1, (result,)), side, 0).reshape(-1, half)
    far_folded = exchange(folded, "nar", 1)
    ortho = newton(folded, far_folded, own_rows, far_rows, core)
    extra = folded[half : half + 8] + far_folded[half : half + 8]
    extra = ordered(extra, exchange(after(extra, ortho), "nar", 2), chip)[0].reshape(8 * half)
    grad_gains = extra[half : half + count]
    far_out, far_in = after(far_out, ortho), after(far_in, ortho)
    grad_w_out = join(part_out, far_out, chip, 0).reshape(rows_out, D).astype(f32)
    mom_out_new = muon_beta * mom_out + grad_w_out
    grad_w_in = after(rejoined(*ordered(part_in, far_in, chip))).astype(f32)
    mom_in_new = muon_beta * mom_in + grad_w_in

    other = exchange(ortho, "nar", 2, (mom_in_new, mom_out_new, grad_gains))
    ortho_in, ortho_out = ordered(ortho, other, chip)
    ortho_out = jnp.concatenate([ortho_out[half_in : half_in + half_out], ortho_out[:half_out]], axis=0)
    far_in, far_out = (exchange(rows, "nar", 1) for rows in (ortho_in, ortho_out))
    w_in_new, w_out_new = update(
        ortho_in, far_in, ortho_out, far_out, w_in, w_out, jnp.stack([core[0], start]), first if parted else rows_in
    )
    gain_m_new = adam_first * gain_m + (1 - adam_first) * grad_gains
    gain_v_new = adam_second * gain_v + (1 - adam_second) * grad_gains * grad_gains
    gains_new = gains - adam_rate * (gain_m_new / (1 - adam_first**STEP)) / (
        jnp.sqrt(gain_v_new / (1 - adam_second**STEP)) + adam_eps
    )
    return (
        result,
        grad_tokens,
        grad_w_in,
        grad_w_out,
        grad_gains,
        mom_in_new,
        mom_out_new,
        gain_m_new,
        gain_v_new,
        w_in_new,
        w_out_new,
        gains_new,
    )


def solution(mesh):
    rows = P(("nar", "wide"), None)
    wide = P("wide", None)
    return jax.shard_map(
        on_device,
        mesh=mesh,
        in_specs=(rows, rows, rows, wide, wide, P(), wide, wide, P(), P()),
        out_specs=(rows, rows, wide, wide, P(), wide, wide, P(), P(), wide, wide, P()),
        check_vma=False,
    )
```

```python
from functools import partial

import jax
import jax.numpy as jnp
from jax import lax
from jax.experimental import pallas as pl
from jax.experimental.pallas import tpu as pltpu
from jax.sharding import PartitionSpec as P

D = 768
HEADS = 12
HEAD = 64
LEN = 1024
STEP = 10
FIN = 5376
FOUT = 3840
QKV = 3 * D

f32 = jnp.float32
bf16 = jnp.bfloat16
ns_linear = 3.4445
ns_cubic = -4.775
ns_quintic = 2.0315
muon_beta = 0.5
muon_rate = 0.8
muon_decay = 0.1
adam_rate = 0.8
adam_first = 0.9
adam_second = 0.95
adam_eps = 1e-08
norm_eps = 1e-06
penalty = 16384.0
vmem_bytes = 60 * 1024 * 1024
tile_rows = 256
extra_rows = 32
pair = 2 * HEAD


def normalize(values):
    center = values - jnp.mean(values, axis=-1, keepdims=True)
    variance = jnp.mean(center * center, axis=-1, keepdims=True)
    inverse = lax.rsqrt(variance + norm_eps)
    return (center * inverse, inverse)


def norm_backward(grad_scaled, normed, inverse, axis=-1):
    mean_grad = jnp.mean(grad_scaled, axis=axis, keepdims=True)
    mean_cross = jnp.mean(grad_scaled * normed, axis=axis, keepdims=True)
    return inverse * (grad_scaled - mean_grad - normed * mean_cross)


def nn(a, b):
    return jnp.dot(a, b, preferred_element_type=f32)


def contract(a, b, dim_a, dim_b):
    return lax.dot_general(a, b, (((dim_a,), (dim_b,)), ((), ())), preferred_element_type=f32)


def normalize_columns(columns):
    center = columns - jnp.mean(columns, axis=0, keepdims=True)
    variance = jnp.mean(center * center, axis=0, keepdims=True)
    inverse = lax.rsqrt(variance + norm_eps)
    return (center * inverse, inverse)


core_spec = pl.BlockSpec(memory_space=pltpu.SMEM)


def halves(values, core_ref, keep_ref, send_ref):
    half = D // 2
    left, right = values[:, :half], values[:, half:]
    first = core_ref[0] == 0
    keep_ref[...] = jnp.where(first, left, right).reshape(keep_ref.shape)
    send_ref[...] = jnp.where(first, right, left).reshape(send_ref.shape)


def forward_kernel(
    x_ref, gy_ref, wq_ref, wk_ref, wv_ref, wa_ref, onek_ref, penq_ref, gq_ref, gk_ref, core_ref,
    joined_ref, do_ref, att_ref, terms_ref, exact_ref, sum_ref, keep_ref, send_ref, kaug, qaug_t, vaug_t,
):
    length = x_ref.shape[0]
    weights = jnp.concatenate([wq_ref[...], wk_ref[...], wv_ref[...]], axis=0)
    joined = contract(weights, x_ref[...], 1, 1).astype(bf16)
    for i in range(3):
        joined_ref[i] = joined[i * pair : (i + 1) * pair]
    do_ref[...] = contract(wa_ref[...], gy_ref[...], 1, 1).astype(bf16)
    parts = []
    for h in range(2):
        rows = slice(HEAD * h, HEAD * (h + 1))
        q_hat, _ = normalize_columns(joined_ref[0, rows, :].astype(f32))
        k_hat, _ = normalize_columns(joined_ref[1, rows, :].astype(f32))
        q_low = (q_hat * gq_ref[...]).astype(bf16)
        k_low = (k_hat * gk_ref[...]).astype(bf16)
        kaug[h, :, :HEAD] = k_low.T
        kaug[h, :, HEAD:] = onek_ref[...]
        qaug_t[h, :HEAD, :] = (q_low.astype(f32) * HEAD ** (-0.5)).astype(bf16)
        qaug_t[h, HEAD:, :] = penq_ref[...]
        vaug_t[h, :HEAD, :] = joined_ref[2, rows, :]
        vaug_t[h, HEAD:, :] = jnp.ones((16, length), bf16)
        terms_ref[h] = jnp.exp(nn(kaug[h], qaug_t[h])).astype(bf16)
        summed = nn(vaug_t[h], terms_ref[h])
        inverse_sum = 1.0 / summed[HEAD : HEAD + 1]
        sum_ref[0, h : h + 1, :] = inverse_sum
        attended = summed[:HEAD] * inverse_sum
        exact_ref[rows, :] = attended
        parts.append(attended)
    attended = jnp.concatenate(parts, 0).astype(bf16)
    halves(nn(attended, gy_ref[...]).astype(bf16), core_ref, keep_ref, send_ref)
    att_ref[...] = attended.T


def attention_forward(x_low, grad_y, w_in_all, w_out_all, ids, q_gain, k_gain, core):
    length = x_low.shape[0]
    pairs = D // pair
    image = jnp.where(ids < 0, 4, ids)
    number = jnp.arange(16)
    onek = (image[:, None] == number[None, :]).astype(bf16)
    penq = jnp.where(image[None, :] == number[:, None], 0.0, -penalty).astype(bf16)

    def rows(part):
        return pl.BlockSpec((pair, D), lambda p: (part * pairs + p, 0))

    def whole(shape):
        return pl.BlockSpec(shape, lambda p: (0, 0))

    call = pl.pallas_call(
        forward_kernel,
        grid=(pairs,),
        in_specs=[
            whole((length, D)), whole((length, D)), rows(0), rows(1), rows(2), rows(0),
            whole((length, 16)), whole((16, length)), whole((HEAD, 1)), whole((HEAD, 1)), core_spec,
        ],
        out_specs=[
            pl.BlockSpec((3, pair, length), lambda p: (0, p, 0)),
            pl.BlockSpec((pair, length), lambda p: (p, 0)),
            pl.BlockSpec((length, pair), lambda p: (0, p)),
            pl.BlockSpec((2, length, length), lambda p: (p, 0, 0)),
            pl.BlockSpec((pair, length), lambda p: (p, 0)),
            pl.BlockSpec((1, 8, length), lambda p: (p, 0, 0)),
            *[pl.BlockSpec((pair, D // 2), lambda p: (p, 0))] * 2,
        ],
        out_shape=[
            jax.ShapeDtypeStruct((3, D, length), bf16),
            jax.ShapeDtypeStruct((D, length), bf16),
            jax.ShapeDtypeStruct((length, D), bf16),
            jax.ShapeDtypeStruct((HEADS, length, length), bf16),
            jax.ShapeDtypeStruct((D, length), f32),
            jax.ShapeDtypeStruct((pairs, 8, length), f32),
            *[jax.ShapeDtypeStruct((D, D // 2), bf16)] * 2,
        ],
        scratch_shapes=[
            pltpu.VMEM((2, length, HEAD + 16), bf16),
            pltpu.VMEM((2, HEAD + 16, length), bf16),
            pltpu.VMEM((2, HEAD + 16, length), bf16),
        ],
        compiler_params=pltpu.CompilerParams(vmem_limit_bytes=vmem_bytes),
        cost_estimate=pl.CostEstimate(
            flops=HEADS * 4 * length * length * 256,
            bytes_accessed=16 * length * D + 2 * HEADS * length * length,
            transcendentals=HEADS * length * length,
        ),
        name="attention_forward",
    )
    return call(
        x_low, grad_y, w_in_all, w_in_all, w_in_all, w_out_all, onek, penq,
        q_gain.reshape(HEAD, 1), k_gain.reshape(HEAD, 1), core,
    )


def backward_kernel(
    joined_ref, do_ref, terms_ref, exact_ref, sum_ref, gq_ref, gk_ref, x_ref, core_ref, *refs, folds,
):
    *refs, vaug, qlow_t, klow_t, doaug_t = refs
    if folds:
        *refs, folded_ref = refs
    *refs, grads_ref, keep_ref, send_ref, ggq_ref, ggk_ref = refs
    if folds:
        size = folded_ref.shape[0] // 2
        for i in range(2):
            near_ref, far_ref = refs[-4 + 2 * i], refs[-3 + 2 * i]
            folded_ref[i * size : (i + 1) * size, :] = added(near_ref[...], far_ref[...])
    length = x_ref.shape[0]
    step = pl.program_id(0)
    q_gain = gq_ref[...]
    k_gain = gk_ref[...]
    dq_parts, dk_parts, dv_parts = [], [], []
    q_gain_grad = jnp.zeros((HEAD, 1), f32)
    k_gain_grad = jnp.zeros((HEAD, 1), f32)
    kept = []
    for h in range(2):
        rows = slice(HEAD * h, HEAD * (h + 1))
        q_hat, q_inverse = normalize_columns(joined_ref[0, rows, :].astype(f32))
        k_hat, k_inverse = normalize_columns(joined_ref[1, rows, :].astype(f32))
        klow_t[h] = (k_hat * k_gain).astype(bf16)
        qlow_t[h] = (q_hat * q_gain).astype(bf16)
        vaug[h, :, :HEAD] = joined_ref[2, rows, :].T
        vaug[h, :, HEAD:] = jnp.ones((length, 16), bf16)
        inverse_sum = sum_ref[0, h : h + 1, :]
        do_head = do_ref[rows, :].astype(f32)
        inner = -jnp.sum(do_head * exact_ref[rows, :], axis=0, keepdims=True) * inverse_sum
        do_low = (do_head * inverse_sum).astype(bf16)
        inner_high = inner.astype(bf16).astype(f32)
        extra = lax.broadcasted_iota(jnp.int32, (16, length), 0)
        extra = jnp.where(extra == 0, inner_high, jnp.where(extra == 1, inner - inner_high, 0.0))
        doaug_t[h, :HEAD, :] = do_low
        doaug_t[h, HEAD:, :] = extra.astype(bf16)
        kept.append((q_hat, q_inverse, k_hat, k_inverse))
    sums = [[None] * 3 for _ in range(2)]
    for k in range(0, length, tile_rows):
        for h in range(2):
            span = slice(k, k + tile_rows)
            terms = terms_ref[h, span, :]
            dscores = (terms.astype(f32) * nn(vaug[h, span, :], doaug_t[h])).astype(bf16)
            dv = contract(doaug_t[h, :HEAD, :], terms, 1, 1)
            dk = contract(qlow_t[h], dscores, 1, 1)
            dq = nn(klow_t[h, :, span], dscores)
            sums[h][0] = dq if sums[h][0] is None else sums[h][0] + dq
            sums[h][1] = [dk] if sums[h][1] is None else sums[h][1] + [dk]
            sums[h][2] = [dv] if sums[h][2] is None else sums[h][2] + [dv]
    for h in range(2):
        q_hat, q_inverse, k_hat, k_inverse = kept[h]
        dquery = sums[h][0] * HEAD ** (-0.5)
        dkey = jnp.concatenate(sums[h][1], axis=1) * HEAD ** (-0.5)
        dvalue = jnp.concatenate(sums[h][2], axis=1)
        q_gain_grad += jnp.sum(dquery * q_hat, axis=1, keepdims=True)
        k_gain_grad += jnp.sum(dkey * k_hat, axis=1, keepdims=True)
        dq_parts.append(norm_backward(dquery * q_gain, q_hat, q_inverse, 0))
        dk_parts.append(norm_backward(dkey * k_gain, k_hat, k_inverse, 0))
        dv_parts.append(dvalue)
    grads = jnp.concatenate(dq_parts + dk_parts + dv_parts, 0).astype(bf16)
    halves(nn(grads, x_ref[...]).astype(bf16), core_ref, keep_ref, send_ref)
    grads_ref[0] = grads[:pair].T
    grads_ref[1] = grads[pair : 2 * pair].T
    grads_ref[2] = grads[2 * pair :].T

    @pl.when(step == 0)
    def _():
        ggq_ref[...] = jnp.zeros_like(ggq_ref)
        ggk_ref[...] = jnp.zeros_like(ggk_ref)

    ggq_ref[...] += jnp.broadcast_to(q_gain_grad, ggq_ref.shape)
    ggk_ref[...] += jnp.broadcast_to(k_gain_grad, ggk_ref.shape)


def attention_backward(
    joined, dattended, terms, exact, inverse_sum, q_gain, k_gain, x_low, core, first, count, room,
    place=0, into=(), fold=(), origin=0, size=0,
):
    length = x_low.shape[0]

    def whole(shape):
        return pl.BlockSpec(shape, lambda p: (0, 0))

    last = (fold[0].shape[0] - origin - size) // (FIN // 8) if fold else 0

    def segment(i):
        return pl.BlockSpec(
            (pl.Element(size), pl.Element(D // 2)),
            lambda p: (pl.multiple_of(origin + FIN // 8 * jnp.minimum(2 * p + i, last), 32), 0),
        )

    gain = jax.ShapeDtypeStruct((HEAD, 128), f32)
    call = pl.pallas_call(
        partial(backward_kernel, folds=bool(fold)),
        grid=(count,),
        in_specs=[
            pl.BlockSpec((3, pair, length), lambda p: (0, first + p, 0)),
            pl.BlockSpec((pair, length), lambda p: (first + p, 0)),
            pl.BlockSpec((2, length, length), lambda p: (first + p, 0, 0)),
            pl.BlockSpec((pair, length), lambda p: (first + p, 0)),
            pl.BlockSpec((1, 8, length), lambda p: (first + p, 0, 0)),
            whole((HEAD, 1)), whole((HEAD, 1)), whole((length, D)), core_spec,
            *[pl.BlockSpec(memory_space=pl.ANY)] * len(into),
            *[segment(i) for i in range(2) for _ in fold],
        ],
        out_specs=[pl.BlockSpec((3, length, pair), lambda p: (0, 0, p))]
        + [pl.BlockSpec((3, pair, D // 2), lambda p: (0, place + p, 0))] * 2
        + [whole((HEAD, 128))] * 2
        + [pl.BlockSpec((2 * size, D // 2), lambda p: (p, 0))] * bool(fold),
        out_shape=[jax.ShapeDtypeStruct((3, length, count * pair), bf16)]
        + [jax.ShapeDtypeStruct((3, room * pair, D // 2), bf16)] * 2 + [gain] * 2
        + [jax.ShapeDtypeStruct(((last + 1) * size, D // 2), bf16)] * bool(fold),
        input_output_aliases={9 + i: 1 + i for i in range(len(into))},
        scratch_shapes=[
            pltpu.VMEM((2, length, HEAD + 16), bf16),
            pltpu.VMEM((2, HEAD, length), bf16),
            pltpu.VMEM((2, HEAD, length), bf16),
            pltpu.VMEM((2, HEAD + 16, length), bf16),
        ],
        compiler_params=pltpu.CompilerParams(vmem_limit_bytes=vmem_bytes),
        cost_estimate=pl.CostEstimate(
            flops=2 * count * 8 * length * length * 256,
            bytes_accessed=24 * length * count * pair + 4 * count * length * length,
            transcendentals=0,
        ),
        name="attention_backward",
    )
    outs = call(joined, dattended, terms, exact, inverse_sum, q_gain.reshape(HEAD, 1), k_gain.reshape(HEAD, 1), x_low, core, *into, *fold, *fold)
    return (*outs[:3], outs[3][:, 0], outs[4][:, 0], *outs[5:])


def gelu_pair(u):
    z = jnp.abs(u) * 0.7071067811865476
    t = 1.0 / (1.0 + 0.3275911 * z)
    e = jnp.exp(-z * z)
    poly = t * (0.127414796 + t * (-0.142248368 + t * (0.7107068705 + t * (-0.7265760135 + t * 0.5307027145))))
    half = poly * e
    phi = jnp.where(u >= 0, 1.0 - half, half)
    return (u * phi, phi + u * (0.3989422804014327 * e))


def mlp_kernel(
    x_ref, gy_ref, wu_ref, wd_ref, core_ref,
    res_ref, gn_ref, keep_up, send_up, keep_down, send_down, act_ref, dup_ref,
):
    @pl.when(pl.program_id(0) == 0)
    def _():
        res_ref[...] = jnp.zeros_like(res_ref)
        gn_ref[...] = jnp.zeros_like(gn_ref)

    for begin in range(0, wu_ref.shape[0], tile_rows):
        units = slice(begin, begin + tile_rows)
        upward = contract(x_ref[...], wu_ref[units], 1, 1).astype(bf16).astype(f32)
        grad_hidden = contract(gy_ref[...], wd_ref[units], 1, 1)
        active, slope = gelu_pair(upward)
        act_ref[:, units] = active.astype(bf16)
        dup_ref[:, units] = (grad_hidden * slope).astype(bf16)
    active, dupward = act_ref[...], dup_ref[...]
    res_ref[...] += nn(active, wd_ref[...])
    gn_ref[...] += nn(dupward, wu_ref[...])
    halves(contract(active, gy_ref[...], 0, 0).astype(bf16), core_ref, keep_down, send_down)
    halves(contract(dupward, x_ref[...], 0, 0).astype(bf16), core_ref, keep_up, send_up)


def mlp(x_low, grad_y, w_in_all, w_out_all, core):
    length = x_low.shape[0]
    hidden = w_in_all.shape[0] - QKV
    tile = D
    whole = pl.BlockSpec((length, D), lambda t: (0, 0))
    total = jax.ShapeDtypeStruct((length, D), f32)
    grad = jax.ShapeDtypeStruct((hidden, D // 2), bf16)
    call = pl.pallas_call(
        mlp_kernel,
        grid=(hidden // tile,),
        in_specs=[
            whole,
            whole,
            pl.BlockSpec((tile, D), lambda t: (t + QKV // tile, 0)),
            pl.BlockSpec((tile, D), lambda t: (t + D // tile, 0)),
            core_spec,
        ],
        out_specs=[whole, whole] + [pl.BlockSpec((tile, D // 2), lambda t: (t, 0))] * 4,
        out_shape=[total, total] + [grad] * 4,
        scratch_shapes=[pltpu.VMEM((length, tile), bf16)] * 2,
        compiler_params=pltpu.CompilerParams(vmem_limit_bytes=vmem_bytes),
        cost_estimate=pl.CostEstimate(
            flops=18 * length * D * hidden,
            bytes_accessed=12 * length * D + 8 * hidden * D,
            transcendentals=length * hidden,
        ),
        name="mlp",
    )
    return call(x_low, grad_y, w_in_all, w_out_all, core)


def input_kernel(*refs, calls):
    grads = refs[:calls]
    w_ref, normed_ref, tokens_ref, gy_ref, gain_ref, out_ref, ln_ref, total = refs[calls:]
    step = pl.program_id(0)

    @pl.when(step == 0)
    def _():
        total[...] = normed_ref[...]

    begin = 0
    sums = []
    for ref in grads:
        sums.append(nn(ref[0], w_ref[begin : begin + ref.shape[2], :]))
        begin += ref.shape[2]
    total[...] += sum(sums)

    @pl.when(step == pl.num_programs(0) - 1)
    def _():
        x_hat, x_inverse = normalize(tokens_ref[...].astype(f32))
        grad_normed = total[...]
        ln_ref[...] = jnp.sum(grad_normed * x_hat, axis=0, keepdims=True)
        back = norm_backward(grad_normed * gain_ref[...], x_hat, x_inverse)
        out_ref[...] = (gy_ref[...].astype(f32) + back).astype(bf16)


def input_gradient(grads, w_in_all, normed, tokens, grad_y, gain):
    length = tokens.shape[0]
    whole = pl.BlockSpec((length, D), lambda p: (0, 0))
    row = pl.BlockSpec((1, D), lambda p: (0, 0))
    call = pl.pallas_call(
        partial(input_kernel, calls=len(grads)),
        grid=(3,),
        in_specs=[pl.BlockSpec((1, length, grad.shape[2]), lambda p: (p, 0, 0)) for grad in grads]
        + [pl.BlockSpec((D, D), lambda p: (p, 0)), whole, whole, whole, row],
        out_specs=[whole, row],
        out_shape=[jax.ShapeDtypeStruct((length, D), bf16), jax.ShapeDtypeStruct((1, D), f32)],
        scratch_shapes=[pltpu.VMEM((length, D), f32)],
        compiler_params=pltpu.CompilerParams(vmem_limit_bytes=vmem_bytes),
        cost_estimate=pl.CostEstimate(
            flops=2 * length * D * QKV, bytes_accessed=20 * length * D, transcendentals=length
        ),
        name="input_gradient",
    )
    out, ln_grad = call(*grads, w_in_all, normed, tokens, grad_y, gain.reshape(1, D))
    return (out, ln_grad[0])


def split(values):
    high = values.astype(bf16)
    return (high, (values - high.astype(f32)).astype(bf16))


def newton_kernel(
    near_ref, other_ref, own_ref, far_ref, core_ref, o_ref, gh, gl, sh, sl, ph, pw, g32, x32
):
    count = D // tile_rows

    def span(i):
        return slice(i * tile_rows, (i + 1) * tile_rows)

    def store(high_ref, low_ref, i, j, value):
        high_ref[span(i), span(j)], low_ref[span(i), span(j)] = split(value)
        if i != j:
            high_ref[span(j), span(i)], low_ref[span(j), span(i)] = split(value.T)

    def symmetric(ah, al, bh, bl, post):
        for i in range(count):
            for j in range(i, count):
                rows, columns = span(i), span(j)
                post(
                    i,
                    j,
                    nn(ah[rows, :], bh[:, columns])
                    + (nn(ah[rows, :], bl[:, columns]) + nn(al[rows, :], bh[:, columns])),
                )

    def squared(ah, al, post):
        for i in range(count):
            for j in range(i, count):
                rows, columns = span(i), span(j)
                mixed = nn(ah[rows, :], al[:, columns])
                other = mixed if i == j else nn(ah[columns, :], al[:, rows])
                post(i, j, nn(ah[rows, :], ah[:, columns]) + (mixed + other.T))

    def sweep(last):
        def keep_factor(i, j, value):
            value = ns_cubic * g32[span(i), span(j)] + ns_quintic * value
            if i == j:
                shape = (tile_rows, tile_rows)
                diagonal = lax.broadcasted_iota(jnp.int32, shape, 0) == lax.broadcasted_iota(jnp.int32, shape, 1)
                value = value + jnp.where(diagonal, ns_linear, 0.0)
            store(ph, pw, i, j, value)

        def keep_gram(i, j, value):
            g32[span(i), span(j)] = value
            store(gh, gl, i, j, value)

        squared(gh, gl, keep_factor)
        xh, xl = split(x32[...])
        x32[...] = nn(xh, ph[...]) + (nn(xh, pw[...]) + nn(xl, ph[...]))
        if not last:
            symmetric(gh, gl, ph, pw, partial(store, sh, sl))
            symmetric(sh, sl, ph, pw, keep_gram)

    half = D // 2
    first_core = core_ref[0] == 0
    left = jnp.where(first_core, near_ref[...], other_ref[...])
    side = jnp.where(first_core, other_ref[:half], near_ref[:half])
    corner = left[:half]
    i = lax.broadcasted_iota(jnp.int32, (half, half), 0)
    j = lax.broadcasted_iota(jnp.int32, (half, half), 1)
    corner_t = corner.T
    first = jnp.where(i <= j, corner, corner_t)
    last = jnp.where(i > j, corner, jnp.where(i == j, left[half : half + 1], corner_t))
    trace = jnp.sum(jnp.where(i == j, first + last, 0.0), axis=0, keepdims=True)
    trace = jnp.sum(trace, axis=1, keepdims=True)
    inverse = 1.0 / (jnp.sqrt(trace) + 1e-07)
    square = inverse * inverse
    g32[:half, :half] = first * square
    g32[half:, half:] = last * square
    g32[:half, half:] = side * square
    g32[half:, :half] = side.T * square
    rows = own_ref.shape[0]
    x32[:rows] = own_ref[...] * inverse
    x32[rows:] = far_ref[...] * inverse
    gh[...], gl[...] = split(g32[...])

    @pl.loop(0, 4)
    def _(k):
        sweep(False)

    sweep(True)
    o_ref[...] = x32[...].astype(bf16)


def newton(folded, far_folded, own_rows, far_rows, core):
    rows = own_rows.shape[0] + far_rows.shape[0]
    whole = pl.BlockSpec(memory_space=pltpu.VMEM)
    call = pl.pallas_call(
        newton_kernel,
        in_specs=[whole] * 4 + [core_spec],
        out_specs=whole,
        out_shape=jax.ShapeDtypeStruct((rows, D), bf16),
        scratch_shapes=[pltpu.VMEM((D, D), bf16)] * 6 + [pltpu.VMEM((D, D), f32), pltpu.VMEM((rows, D), f32)],
        compiler_params=pltpu.CompilerParams(vmem_limit_bytes=vmem_bytes),
        cost_estimate=pl.CostEstimate(
            flops=30 * D * D * (2 * D + rows), bytes_accessed=4 * D * D + 6 * rows * D, transcendentals=0
        ),
        name="newton",
    )
    return call(folded, far_folded, own_rows, far_rows, core)


def update_kernel(in_ref, in_far_ref, out_ref, out_far_ref, wi_ref, wo_ref, place_ref, in_new, out_new, held, *, first):
    def new(weights, ortho, size):
        rate = muon_rate * (size / D) ** 0.5
        return weights.astype(f32) * (1 - muon_rate * muon_decay) - rate * ortho.astype(f32)

    first_core = place_ref[0] == 0
    for near_ref, far_ref, total in ((in_ref, in_far_ref, None), (out_ref, out_far_ref, out_new)):
        size = far_ref.shape[0] // 2
        all_near, all_far, weights = near_ref[...].astype(f32), far_ref[...].astype(f32), wo_ref[...].astype(f32)
        for chip in range(2):
            rows = slice(chip * size, (chip + 1) * size)
            near, far = all_near[rows], all_far[rows]
            begin = 2 * chip * size
            both = (jnp.where(first_core, near, far), jnp.where(first_core, far, near))
            for i in range(2):
                spot = slice(begin + i * size, begin + (i + 1) * size)
                if total is None:
                    held[spot] = both[i]
                else:
                    total[spot] = new(weights[spot], both[i], FOUT)
    rows = in_new.shape[0]
    if first == rows:
        in_new[...] = new(wi_ref[...], held[...], FIN)
        return
    start = pl.multiple_of(place_ref[1], 32)
    cut, rest = first // 2, (rows - first) // 2
    pieces = jnp.concatenate([held[cut : cut + rest], held[rows // 2 + cut :]], axis=0)
    in_new[: rows - first] = new(wi_ref[: rows - first], pieces, FIN)
    in_new[first:] = jnp.where(
        lax.broadcasted_iota(jnp.int32, (rows - first, 1), 0) < start, in_new[first:], new(wi_ref[first:], pieces, FIN)
    )
    spot = pl.ds(start, first)
    pieces = jnp.concatenate([held[:cut], held[rows // 2 : rows // 2 + cut]], axis=0)
    in_new[spot] = new(wi_ref[spot], pieces, FIN)


def update(ortho_in, far_in, ortho_out, far_out, w_in, w_out, place, first):
    whole = pl.BlockSpec(memory_space=pltpu.VMEM)
    call = pl.pallas_call(
        partial(update_kernel, first=first),
        in_specs=[whole] * 6 + [core_spec],
        out_specs=[whole] * 2,
        out_shape=[jax.ShapeDtypeStruct(w.shape, f32) for w in (w_in, w_out)],
        scratch_shapes=[pltpu.VMEM(w_in.shape, f32)],
        compiler_params=pltpu.CompilerParams(vmem_limit_bytes=vmem_bytes),
        cost_estimate=pl.CostEstimate(flops=4 * w_in.size, bytes_accessed=14 * w_in.size, transcendentals=0),
        name="update",
    )
    return call(ortho_in, far_in, ortho_out, far_out, w_in, w_out, place)


def gram_kernel(m_ref, extra_ref, core_ref, o_ref):
    half = D // 2
    left, right = slice(0, half), slice(half, D)

    def product(a, b):
        ah, al = split(m_ref[:, a])
        bh, bl = split(m_ref[:, b])
        return contract(ah, bh, 0, 0) + (contract(ah, bl, 0, 0) + contract(al, bh, 0, 0))

    o_ref[half:, :] = extra_ref[...]

    @pl.when(core_ref[0] == 0)
    def _():
        i = lax.broadcasted_iota(jnp.int32, (half, half), 0)
        j = lax.broadcasted_iota(jnp.int32, (half, half), 1)
        last = product(right, right)
        o_ref[:half, :] = jnp.where(i <= j, product(left, left), last)
        o_ref[half : half + 1, :] = jnp.sum(jnp.where(i == j, last, 0.0), axis=0, keepdims=True)

    @pl.when(core_ref[0] != 0)
    def _():
        o_ref[:half, :] = product(left, right)


def folded_gram(rows, extra, core):
    rows = jnp.pad(rows, ((0, -rows.shape[0] % 16), (0, 0)))
    whole = pl.BlockSpec(memory_space=pltpu.VMEM)
    call = pl.pallas_call(
        gram_kernel,
        in_specs=[whole, whole, core_spec],
        out_specs=whole,
        out_shape=jax.ShapeDtypeStruct((D // 2 + extra_rows, D // 2), f32),
        compiler_params=pltpu.CompilerParams(vmem_limit_bytes=vmem_bytes),
        cost_estimate=pl.CostEstimate(
            flops=4 * rows.shape[0] * D * D, bytes_accessed=8 * rows.shape[0] * D, transcendentals=0
        ),
        name="gram",
    )
    return call(rows, extra, core)


def bits(size):
    return [1 << b for b in range(size.bit_length() - 1)]


def take(values, index, axis):
    return lax.dynamic_index_in_dim(values, index, axis, keepdims=False)


def after(value, *others):
    return lax.optimization_barrier((value, *others))[0]


def exchange(values, axis, bit, fill=()):
    size = lax.axis_size(axis)
    return after(lax.ppermute(values, axis, [(i, i ^ bit) for i in range(size)]), *fill)


def sum_steps(values, halving, full):
    fill = yield values
    for axis, bit in halving:
        side = (lax.axis_index(axis) // bit) % 2
        pieces = values.reshape(2, values.shape[0] // 2, values.shape[1])
        values = take(pieces, side, 0) + exchange(take(pieces, 1 - side, 0), axis, bit, fill)
        fill = yield values
    for axis, bit in full:
        values = values + exchange(values, axis, bit, fill)
        fill = yield values


def halve(parts, axis, name, bit):
    side = (lax.axis_index(name) // bit) % 2
    sent = [take(part, 1 - side, axis) for part in parts]

    def receive(*fill):
        kept = jnp.concatenate([take(part, side, axis) for part in parts], axis=0)
        return (kept, exchange(jnp.concatenate(sent, axis=0), name, bit, fill))

    return sent, receive


def added(kept, other):
    return (kept.astype(f32) + other.astype(f32)).astype(bf16)


def scatter_one(*parts):
    wide = lax.axis_size("wide")
    columns = parts[0].shape[-1]
    rows = sum(part.size for part in parts) // (2 * wide * columns)
    cut = rows // 16 * 8
    parts = [part.reshape(-1, 2, 2, rows, columns) for part in parts]
    sent_a, receive_a = halve([part[:, :, :, :cut] for part in parts], 1, "wide", 1)
    sent_b, receive_b = halve([part[:, :, :, cut:] for part in parts], 2, "nar", 2)
    return sent_a + sent_b, lambda *fill: (added(*receive_a(*fill)), added(*receive_b(*fill)))


def split_kernel(*refs, pairs, rows):
    *parts, place_ref, sent_y, kept_y, sent_x, kept_x, held = refs
    begin = 0
    for paired in pairs:
        values = parts.pop(0)[...].astype(f32)
        if paired:
            values = values + parts.pop(0)[...].astype(f32)
        held[begin : begin + values.shape[0]] = values
        begin += values.shape[0]
    cut = kept_y.shape[2]
    for z in range(kept_y.shape[0]):
        for j in range(2):
            for near, out_y, out_x in ((True, kept_y, kept_x), (False, sent_y, sent_x)):
                y = place_ref[0] if near else 1 - place_ref[0]
                x = place_ref[1] if near else 1 - place_ref[1]
                first = pl.ds(pl.multiple_of(((2 * z + y) * 2 + j) * rows, 8), cut)
                out_y[z, j] = held[first].astype(bf16)
                second = pl.ds(pl.multiple_of(((2 * z + j) * 2 + x) * rows + cut, 8), rows - cut)
                out_x[z, j] = held[second].astype(bf16)


def split_one(rows, *parts):
    half = D // 2
    cut = rows // 16 * 8
    far = lax.axis_size("wide") // 2
    place = jnp.stack([lax.axis_index("wide") % 2, lax.axis_index("nar") // 2])
    terms = [term.reshape(-1, half) for part in parts for term in (part if isinstance(part, tuple) else (part,))]
    whole = pl.BlockSpec(memory_space=pltpu.VMEM)
    shapes = [(far, 2, cut, half)] * 2 + [(far, 2, rows - cut, half)] * 2
    call = pl.pallas_call(
        partial(split_kernel, pairs=[isinstance(part, tuple) for part in parts], rows=rows),
        in_specs=[whole] * len(terms) + [core_spec],
        out_specs=[whole] * 4,
        out_shape=[jax.ShapeDtypeStruct(shape, bf16) for shape in shapes],
        scratch_shapes=[pltpu.VMEM((4 * far * rows, half), f32)],
        compiler_params=pltpu.CompilerParams(vmem_limit_bytes=vmem_bytes),
        cost_estimate=pl.CostEstimate(
            flops=8 * far * rows * half, bytes_accessed=24 * far * rows * half, transcendentals=0
        ),
        name="split",
    )
    sent_y, kept_y, sent_x, kept_x = call(*terms, place)

    def arrive(*fill):
        return (exchange(sent_y, "wide", 1, fill), exchange(sent_x, "nar", 2, fill))

    return [sent_y, sent_x], arrive, lambda other_y, other_x: (added(kept_y, other_y), added(kept_x, other_x))


def scatter_two(held):
    sent_a, receive_a = halve(held[:1], 1, "nar", 2)
    sent_b, receive_b = halve(held[1:], 1, "wide", 1)

    def receive(*fill):
        kept, other = zip(receive_a(*fill), receive_b(*fill), strict=True)
        return added(jnp.concatenate(kept, axis=1), jnp.concatenate(other, axis=1))

    return sent_a + sent_b, receive


def scatter_rest(held):
    wide = lax.axis_size("wide")
    far = wide // 2
    place = lax.axis_index("wide") // 2
    sent = [take(held, place ^ shift, 0) for shift in range(1, far)]

    def receive(*fill):
        total = take(held, place, 0).astype(f32)
        for shift in reversed(range(1, far)):
            pairs = [(i, i ^ (2 * shift)) for i in range(wide)]
            total = total + after(lax.ppermute(sent[shift - 1], "wide", pairs), *fill).astype(f32)
        return total.astype(bf16)

    return sent, receive


def both_cores(values, *fill):
    other = exchange(values, "nar", 1, fill)
    return join(values, other, lax.axis_index("nar") % 2, 1).reshape(values.shape[0], D)


def ordered(values, other, side):
    return (jnp.where(side == 0, values, other), jnp.where(side == 0, other, values))


def join(values, other, side, axis):
    return jnp.stack(ordered(values, other, side), axis)


def gather(values):
    wide = lax.axis_size("wide")
    rows = values.shape[0]
    far = wide // 2
    place, side = lax.axis_index("wide") // 2, lax.axis_index("wide") % 2
    chip, core = lax.axis_index("nar") // 2, lax.axis_index("nar") % 2
    held = lax.dynamic_update_index_in_dim(jnp.zeros((far, rows, D), values.dtype), values, place, 0)
    for shift in range(1, far):
        pairs = [(i, i ^ (2 * shift)) for i in range(wide)]
        held = lax.dynamic_update_index_in_dim(held, lax.ppermute(values, "wide", pairs), place ^ shift, 0)
    cut = rows // 32 * 16
    first, second = held[:, :cut], held[:, cut:]
    first = join(first, exchange(first, "wide", 1), side, 1)
    second = join(second, exchange(second, "nar", 2), chip, 1)
    first = join(first, exchange(first, "nar", 2), chip, 2)
    second = join(second, exchange(second, "wide", 1), side, 1)
    held = jnp.concatenate([first, second], axis=3)
    return join(held, exchange(held, "nar", 1), core, 3).reshape(-1, D)


def on_device(tokens, cotangent, image_ids, w_in, w_out, gains, mom_in, mom_out, gain_m, gain_v):
    row_count = tokens.shape[0]
    rows_in = w_in.shape[0]
    rows_out = w_out.shape[0]
    nar_count = lax.axis_size("nar")
    wide_count = lax.axis_size("wide")
    nar_place = lax.axis_index("nar")
    share_in = rows_in // nar_count
    share_out = rows_out // nar_count
    everyone = ("wide", "nar")

    def share(rows, size):
        return lax.dynamic_slice_in_dim(rows, nar_place * size, size, 0)

    w_in_all = lax.all_gather(share(w_in, share_in), everyone, axis=0, tiled=True)
    w_out_all = gather(share(w_out, share_out))

    x_float = tokens.astype(f32)
    ln_gain = gains[:D]
    x_hat, x_inverse = normalize(x_float)
    x_low = (x_hat * ln_gain).astype(bf16)
    live = (image_ids.reshape(row_count) >= 0)[:, None]
    grad_y = jnp.where(live, cotangent, jnp.zeros_like(cotangent))

    core = (nar_place % 2).reshape(1)
    chip = nar_place // 2
    half = D // 2
    pairs = D // pair
    q_gain, k_gain = gains[D : D + HEAD], gains[D + HEAD :]
    first = rows_in * 4 // 7
    second = rows_in - first
    parted = wide_count == 8 and first == half and rows_in == 672
    mlp_result, mlp_normed, keep_up, send_up, keep_down, send_down = mlp(x_low, grad_y, w_in_all, w_out_all, core)
    joined, dattended, attended, terms, exact, inverse_sum, keep_att, send_att = attention_forward(
        after(x_low, keep_down), grad_y, w_in_all, w_out_all, image_ids.reshape(row_count), q_gain, k_gain, core
    )

    def backward(begin, count, earlier=(), **buffers):
        return attention_backward(
            joined, dattended, terms, exact, inverse_sum, q_gain, k_gain, after(x_low, *earlier), core, begin, count,
            **buffers,
        )

    def cores(keep, send, *fill):
        return added(keep, exchange(send, "nar", 1, fill)).reshape(-1, half)

    start = 96 * jnp.minimum(lax.axis_index("wide"), 3)
    row = lax.broadcasted_iota(jnp.int32, (rows_in, 1), 0)
    half_mom_out = lax.dynamic_slice_in_dim(mom_out, chip * (rows_out // 2), rows_out // 2, 0)
    wide_bits = bits(wide_count)
    halving = [("wide", wide_bits[0]), ("nar", 2)]
    full = [("wide", bit) for bit in wide_bits[1:]]

    def begin_out(part):
        zeros = jnp.zeros((extra_rows, half), f32)
        steps = sum_steps(folded_gram(muon_beta * half_mom_out + part.astype(f32), zeros, core), halving, full)
        return (steps, next(steps))

    if parted:
        def pair_of(keep, send, *fill):
            return (keep, exchange(send, "nar", 1, fill))

        down = pair_of(keep_down, send_down, keep_att)
        up = pair_of(keep_up, send_up, keep_att)
        sent, arrive, combine = split_one(rows_out // 2, pair_of(keep_att, send_att), down)
        dqkv_a, keep_a, send_a, q_grad_a, k_grad_a, up_a = backward(0, 3, sent, room=3, fold=up, size=first)
        sent, receive = scatter_two(combine(*arrive(keep_a)))
        dqkv_b, keep_b, send_b, q_grad_b, k_grad_b = backward(3, 1, [keep_a, *sent], room=3)
        sent_o, receive_o = scatter_rest(receive(dqkv_b))
        sent_a, arrive_a, combine_a = split_one(first // 2, pair_of(keep_a, send_a, dqkv_b), up_a)
        dqkv_c, keep_b, send_b, q_grad_c, k_grad_c, up_b = backward(
            4, 2, [*sent_a, *sent_o], room=3, place=1, into=(keep_b, send_b), fold=up, origin=first, size=second
        )
        part_out = receive_o(dqkv_c)
        sent_a, receive_a = scatter_two(combine_a(*arrive_a(dqkv_c)))
        sent_b, arrive_b, combine_b = split_one(second // 2, pair_of(keep_b, send_b, part_out, *sent_a), up_b)
        part_out = both_cores(part_out, *sent_b)
        steps_out, folded_out = begin_out(after(part_out, *sent_b))
        held_b = combine_b(*arrive_b(folded_out))
        sent_b, receive_b = scatter_two(held_b)
        folded_out = steps_out.send(sent_b)
        held_a = receive_a(*sent_b)
        held_b = receive_b(held_a, folded_out)
        sent, receive = scatter_rest(jnp.concatenate([held_a, held_b], axis=1))
        grad_tokens, ln_grad = input_gradient(
            [dqkv_a, dqkv_b, dqkv_c], w_in_all, after(mlp_normed, *sent), tokens, grad_y, ln_gain
        )
        far_out = exchange(after(part_out, *sent), "nar", 2, (grad_tokens,))
        folded_out = steps_out.send((grad_tokens,))
        part_in = receive(grad_tokens, far_out, folded_out)
        steps_done = 2
        q_gain_grad, k_gain_grad = q_grad_a + q_grad_b + q_grad_c, k_grad_a + k_grad_b + k_grad_c

        def halved(rows, chip):
            inside = lax.dynamic_slice_in_dim(rows, start, first, 0)
            others = jnp.where(row[:second] < start, rows[:second], rows[first:])
            return jnp.concatenate(
                [
                    lax.dynamic_slice_in_dim(inside, chip * (first // 2), first // 2, 0),
                    lax.dynamic_slice_in_dim(others, chip * (second // 2), second // 2, 0),
                ],
                axis=0,
            )

        def rejoined(near, far):
            cut = first // 2
            a, b = jnp.concatenate([near[:cut], far[:cut]], 0), jnp.concatenate([near[cut:], far[cut:]], 0)
            a = lax.dynamic_update_slice_in_dim(jnp.zeros((rows_in, D), a.dtype), a, start, 0)
            empty = jnp.zeros((first, D), b.dtype)
            below = jnp.concatenate([b, empty], axis=0)
            above = jnp.concatenate([empty, b], axis=0)
            inside = (row >= start) & (row < start + first)
            return jnp.where(inside, a, jnp.where(row < start, below, above))

    else:
        dqkv, keep_a, send_a, q_gain_grad, k_gain_grad = backward(0, pairs, room=pairs)
        grad_tokens, ln_grad = input_gradient([dqkv], w_in_all, mlp_normed, tokens, grad_y, ln_gain)

        def scattered(*parts):
            held = scatter_one(jnp.concatenate(parts, axis=0))[1]()
            return scatter_rest(scatter_two(held)[1]())[1]()

        part_out = both_cores(scattered(cores(keep_att, send_att), cores(keep_down, send_down)))
        steps_out, folded_out = begin_out(part_out)
        steps_done = 0
        far_out = exchange(part_out, "nar", 2)
        part_in = scattered(cores(keep_a, send_a), cores(keep_up, send_up))

        def halved(rows, chip):
            return lax.dynamic_slice_in_dim(rows, chip * (rows_in // 2), rows_in // 2, 0)

        def rejoined(near, far):
            return jnp.concatenate([near, far], axis=0)

    part_in = both_cores(part_in)
    gain_terms = jnp.concatenate([ln_grad, q_gain_grad, k_gain_grad])
    count = gain_terms.shape[0]
    extra = jnp.pad(gain_terms, (half, (extra_rows - 1) * half - count)).reshape(extra_rows, half)
    momenta_in = muon_beta * halved(mom_in, chip) + part_in.astype(f32)
    steps_in = sum_steps(folded_gram(momenta_in, extra, core), halving, full)
    folded_in = next(steps_in)

    half_in, half_out = rows_in // 4, rows_out // 4

    def mine(rows, size):
        return lax.dynamic_slice_in_dim(rows, core[0] * size, size, 0)

    def fitted(rows):
        return jnp.pad(rows, ((0, half_in - half_out), (0, 0)))

    far_in = exchange(part_in, "nar", 2)
    own_rows = jnp.where(
        chip == 0,
        mine(momenta_in, half_in),
        fitted(mine(muon_beta * half_mom_out + part_out.astype(f32), half_out)),
    )
    far_mom = jnp.where(
        chip == 0,
        mine(halved(mom_in, 1 - chip), half_in),
        fitted(mine(lax.dynamic_slice_in_dim(mom_out, (1 - chip) * (rows_out // 2), rows_out // 2, 0), half_out)),
    )
    far_rows = jnp.where(chip == 0, mine(far_in, half_in), fitted(mine(far_out, half_out)))
    far_rows = muon_beta * far_mom + far_rows.astype(f32)
    steps = len(halving) + len(full)
    folded_out = steps_out.send((folded_in,))
    steps_done += 1
    for step in range(steps):
        fill = {0: (far_in, folded_out), len(halving): (own_rows, far_rows)}.get(step, ())
        folded_in = steps_in.send(fill)
        if steps_done < steps:
            folded_out = steps_out.send((folded_in,))
            steps_done += 1
    own, far = ordered(folded_in, folded_out, chip)
    folded = join(own, exchange(far, "nar", 2), chip, 0).reshape(-1, half)
    branch = mlp_result + nn(after(attended, folded), w_out_all[:D])
    result = (tokens.astype(f32) + branch).astype(bf16)
    side = lax.axis_index("wide") % 2
    folded = join(folded, exchange(folded, "wide", 1, (result,)), side, 0).reshape(-1, half)
    far_folded = exchange(folded, "nar", 1)
    ortho = newton(folded, far_folded, own_rows, far_rows, core)
    extra = folded[half : half + 8] + far_folded[half : half + 8]
    extra = ordered(extra, exchange(after(extra, ortho), "nar", 2), chip)[0].reshape(8 * half)
    grad_gains = extra[half : half + count]
    far_out, far_in = after(far_out, ortho), after(far_in, ortho)
    grad_w_out = join(part_out, far_out, chip, 0).reshape(rows_out, D).astype(f32)
    mom_out_new = muon_beta * mom_out + grad_w_out
    grad_w_in = after(rejoined(*ordered(part_in, far_in, chip))).astype(f32)
    mom_in_new = muon_beta * mom_in + grad_w_in

    other = exchange(ortho, "nar", 2, (mom_in_new, mom_out_new, grad_gains))
    ortho_in, ortho_out = ordered(ortho, other, chip)
    ortho_out = jnp.concatenate([ortho_out[half_in : half_in + half_out], ortho_out[:half_out]], axis=0)
    far_in, far_out = (exchange(rows, "nar", 1) for rows in (ortho_in, ortho_out))
    w_in_new, w_out_new = update(
        ortho_in, far_in, ortho_out, far_out, w_in, w_out, jnp.stack([core[0], start]), first if parted else rows_in
    )
    gain_m_new = adam_first * gain_m + (1 - adam_first) * grad_gains
    gain_v_new = adam_second * gain_v + (1 - adam_second) * grad_gains * grad_gains
    gains_new = gains - adam_rate * (gain_m_new / (1 - adam_first**STEP)) / (
        jnp.sqrt(gain_v_new / (1 - adam_second**STEP)) + adam_eps
    )
    return (
        result,
        grad_tokens,
        grad_w_in,
        grad_w_out,
        grad_gains,
        mom_in_new,
        mom_out_new,
        gain_m_new,
        gain_v_new,
        w_in_new,
        w_out_new,
        gains_new,
    )


def solution(mesh):
    rows = P(("nar", "wide"), None)
    wide = P("wide", None)
    return jax.shard_map(
        on_device,
        mesh=mesh,
        in_specs=(rows, rows, rows, wide, wide, P(), wide, wide, P(), P()),
        out_specs=(rows, rows, wide, wide, P(), wide, wide, P(), P(), wide, wide, P()),
        check_vma=False,
    )
```

```python
from functools import partial

import jax
import jax.numpy as jnp
from jax import lax
from jax.experimental import pallas as pl
from jax.experimental.pallas import tpu as pltpu
from jax.sharding import PartitionSpec as P

D = 768
HEADS = 12
HEAD = 64
LEN = 1024
STEP = 10
FIN = 5376
FOUT = 3840
QKV = 3 * D

f32 = jnp.float32
bf16 = jnp.bfloat16
ns_linear = 3.4445
ns_cubic = -4.775
ns_quintic = 2.0315
muon_beta = 0.5
muon_rate = 0.8
muon_decay = 0.1
adam_rate = 0.8
adam_first = 0.9
adam_second = 0.95
adam_eps = 1e-08
norm_eps = 1e-06
penalty = 16384.0
vmem_bytes = 60 * 1024 * 1024
tile_rows = 256
extra_rows = 32
pair = 2 * HEAD


def normalize(values):
    center = values - jnp.mean(values, axis=-1, keepdims=True)
    variance = jnp.mean(center * center, axis=-1, keepdims=True)
    inverse = lax.rsqrt(variance + norm_eps)
    return (center * inverse, inverse)


def norm_backward(grad_scaled, normed, inverse, axis=-1):
    mean_grad = jnp.mean(grad_scaled, axis=axis, keepdims=True)
    mean_cross = jnp.mean(grad_scaled * normed, axis=axis, keepdims=True)
    return inverse * (grad_scaled - mean_grad - normed * mean_cross)


def nn(a, b):
    return jnp.dot(a, b, preferred_element_type=f32)


def contract(a, b, dim_a, dim_b):
    return lax.dot_general(a, b, (((dim_a,), (dim_b,)), ((), ())), preferred_element_type=f32)


def normalize_columns(columns):
    center = columns - jnp.mean(columns, axis=0, keepdims=True)
    variance = jnp.mean(center * center, axis=0, keepdims=True)
    inverse = lax.rsqrt(variance + norm_eps)
    return (center * inverse, inverse)


core_spec = pl.BlockSpec(memory_space=pltpu.SMEM)


def halves(values, core_ref, keep_ref, send_ref):
    half = D // 2
    left, right = values[:, :half], values[:, half:]
    first = core_ref[0] == 0
    keep_ref[...] = jnp.where(first, left, right).reshape(keep_ref.shape)
    send_ref[...] = jnp.where(first, right, left).reshape(send_ref.shape)


def forward_kernel(
    x_ref, gy_ref, wq_ref, wk_ref, wv_ref, wa_ref, onek_ref, penq_ref, gq_ref, gk_ref, core_ref,
    joined_ref, do_ref, att_ref, terms_ref, exact_ref, sum_ref, keep_ref, send_ref, kaug, qaug_t, vaug_t,
):
    length = x_ref.shape[0]
    weights = jnp.concatenate([wq_ref[...], wk_ref[...], wv_ref[...]], axis=0)
    joined = contract(weights, x_ref[...], 1, 1).astype(bf16)
    for i in range(3):
        joined_ref[i] = joined[i * pair : (i + 1) * pair]
    do_ref[...] = contract(wa_ref[...], gy_ref[...], 1, 1).astype(bf16)
    parts = []
    for h in range(2):
        rows = slice(HEAD * h, HEAD * (h + 1))
        q_hat, _ = normalize_columns(joined_ref[0, rows, :].astype(f32))
        k_hat, _ = normalize_columns(joined_ref[1, rows, :].astype(f32))
        q_low = (q_hat * gq_ref[...]).astype(bf16)
        k_low = (k_hat * gk_ref[...]).astype(bf16)
        kaug[h, :, :HEAD] = k_low.T
        kaug[h, :, HEAD:] = onek_ref[...]
        qaug_t[h, :HEAD, :] = (q_low.astype(f32) * HEAD ** (-0.5)).astype(bf16)
        qaug_t[h, HEAD:, :] = penq_ref[...]
        vaug_t[h, :HEAD, :] = joined_ref[2, rows, :]
        vaug_t[h, HEAD:, :] = jnp.ones((16, length), bf16)
        terms_ref[h] = jnp.exp(nn(kaug[h], qaug_t[h])).astype(bf16)
        summed = nn(vaug_t[h], terms_ref[h])
        inverse_sum = 1.0 / summed[HEAD : HEAD + 1]
        sum_ref[0, h : h + 1, :] = inverse_sum
        attended = summed[:HEAD] * inverse_sum
        exact_ref[rows, :] = attended
        parts.append(attended)
    attended = jnp.concatenate(parts, 0).astype(bf16)
    halves(nn(attended, gy_ref[...]).astype(bf16), core_ref, keep_ref, send_ref)
    att_ref[...] = attended.T


def image_columns(ids):
    image = jnp.where(ids < 0, 4, ids)
    number = jnp.arange(16)
    onek = (image[:, None] == number[None, :]).astype(bf16)
    penq = jnp.where(image[None, :] == number[:, None], 0.0, -penalty).astype(bf16)
    return (onek, penq)


def attention_forward(x_low, grad_y, w_in_all, w_out_all, onek, penq, q_gain, k_gain, core):
    length = x_low.shape[0]
    pairs = D // pair

    def rows(part):
        return pl.BlockSpec((pair, D), lambda p: (part * pairs + p, 0))

    def whole(shape):
        return pl.BlockSpec(shape, lambda p: (0, 0))

    call = pl.pallas_call(
        forward_kernel,
        grid=(pairs,),
        in_specs=[
            whole((length, D)), whole((length, D)), rows(0), rows(1), rows(2), rows(0),
            whole((length, 16)), whole((16, length)), whole((HEAD, 1)), whole((HEAD, 1)), core_spec,
        ],
        out_specs=[
            pl.BlockSpec((3, pair, length), lambda p: (0, p, 0)),
            pl.BlockSpec((pair, length), lambda p: (p, 0)),
            pl.BlockSpec((length, pair), lambda p: (0, p)),
            pl.BlockSpec((2, length, length), lambda p: (p, 0, 0)),
            pl.BlockSpec((pair, length), lambda p: (p, 0)),
            pl.BlockSpec((1, 8, length), lambda p: (p, 0, 0)),
            *[pl.BlockSpec((pair, D // 2), lambda p: (p, 0))] * 2,
        ],
        out_shape=[
            jax.ShapeDtypeStruct((3, D, length), bf16),
            jax.ShapeDtypeStruct((D, length), bf16),
            jax.ShapeDtypeStruct((length, D), bf16),
            jax.ShapeDtypeStruct((HEADS, length, length), bf16),
            jax.ShapeDtypeStruct((D, length), f32),
            jax.ShapeDtypeStruct((pairs, 8, length), f32),
            *[jax.ShapeDtypeStruct((D, D // 2), bf16)] * 2,
        ],
        scratch_shapes=[
            pltpu.VMEM((2, length, HEAD + 16), bf16),
            pltpu.VMEM((2, HEAD + 16, length), bf16),
            pltpu.VMEM((2, HEAD + 16, length), bf16),
        ],
        compiler_params=pltpu.CompilerParams(vmem_limit_bytes=vmem_bytes),
        cost_estimate=pl.CostEstimate(
            flops=HEADS * 4 * length * length * 256,
            bytes_accessed=16 * length * D + 2 * HEADS * length * length,
            transcendentals=HEADS * length * length,
        ),
        name="attention_forward",
    )
    return call(
        x_low, grad_y, w_in_all, w_in_all, w_in_all, w_out_all, onek, penq,
        q_gain, k_gain, core,
    )


def backward_kernel(
    joined_ref, do_ref, terms_ref, exact_ref, sum_ref, gq_ref, gk_ref, x_ref, core_ref, *refs, folds,
):
    *refs, vaug, qlow_t, klow_t, doaug_t = refs
    if folds:
        *refs, folded_ref = refs
    *refs, grads_ref, keep_ref, send_ref, ggq_ref, ggk_ref = refs
    if folds:
        size = folded_ref.shape[0] // 2
        for i in range(2):
            near_ref, far_ref = refs[-4 + 2 * i], refs[-3 + 2 * i]
            folded_ref[i * size : (i + 1) * size, :] = added(near_ref[...], far_ref[...])
    length = x_ref.shape[0]
    step = pl.program_id(0)
    q_gain = gq_ref[...]
    k_gain = gk_ref[...]
    dq_parts, dk_parts, dv_parts = [], [], []
    q_gain_grad = jnp.zeros((HEAD, 1), f32)
    k_gain_grad = jnp.zeros((HEAD, 1), f32)
    kept = []
    for h in range(2):
        rows = slice(HEAD * h, HEAD * (h + 1))
        q_hat, q_inverse = normalize_columns(joined_ref[0, rows, :].astype(f32))
        k_hat, k_inverse = normalize_columns(joined_ref[1, rows, :].astype(f32))
        klow_t[h] = (k_hat * k_gain).astype(bf16)
        qlow_t[h] = (q_hat * q_gain).astype(bf16)
        vaug[h, :, :HEAD] = joined_ref[2, rows, :].T
        vaug[h, :, HEAD:] = jnp.ones((length, 16), bf16)
        inverse_sum = sum_ref[0, h : h + 1, :]
        do_head = do_ref[rows, :].astype(f32)
        inner = -jnp.sum(do_head * exact_ref[rows, :], axis=0, keepdims=True) * inverse_sum
        do_low = (do_head * inverse_sum).astype(bf16)
        inner_high = inner.astype(bf16).astype(f32)
        extra = lax.broadcasted_iota(jnp.int32, (16, length), 0)
        extra = jnp.where(extra == 0, inner_high, jnp.where(extra == 1, inner - inner_high, 0.0))
        doaug_t[h, :HEAD, :] = do_low
        doaug_t[h, HEAD:, :] = extra.astype(bf16)
        kept.append((q_hat, q_inverse, k_hat, k_inverse))
    sums = [[None] * 3 for _ in range(2)]
    for k in range(0, length, tile_rows):
        for h in range(2):
            span = slice(k, k + tile_rows)
            terms = terms_ref[h, span, :]
            dscores = (terms.astype(f32) * nn(vaug[h, span, :], doaug_t[h])).astype(bf16)
            dv = contract(doaug_t[h, :HEAD, :], terms, 1, 1)
            dk = contract(qlow_t[h], dscores, 1, 1)
            dq = nn(klow_t[h, :, span], dscores)
            sums[h][0] = dq if sums[h][0] is None else sums[h][0] + dq
            sums[h][1] = [dk] if sums[h][1] is None else sums[h][1] + [dk]
            sums[h][2] = [dv] if sums[h][2] is None else sums[h][2] + [dv]
    for h in range(2):
        q_hat, q_inverse, k_hat, k_inverse = kept[h]
        dquery = sums[h][0] * HEAD ** (-0.5)
        dkey = jnp.concatenate(sums[h][1], axis=1) * HEAD ** (-0.5)
        dvalue = jnp.concatenate(sums[h][2], axis=1)
        q_gain_grad += jnp.sum(dquery * q_hat, axis=1, keepdims=True)
        k_gain_grad += jnp.sum(dkey * k_hat, axis=1, keepdims=True)
        dq_parts.append(norm_backward(dquery * q_gain, q_hat, q_inverse, 0))
        dk_parts.append(norm_backward(dkey * k_gain, k_hat, k_inverse, 0))
        dv_parts.append(dvalue)
    grads = jnp.concatenate(dq_parts + dk_parts + dv_parts, 0).astype(bf16)
    halves(nn(grads, x_ref[...]).astype(bf16), core_ref, keep_ref, send_ref)
    grads_ref[0] = grads[:pair].T
    grads_ref[1] = grads[pair : 2 * pair].T
    grads_ref[2] = grads[2 * pair :].T

    @pl.when(step == 0)
    def _():
        ggq_ref[...] = jnp.zeros_like(ggq_ref)
        ggk_ref[...] = jnp.zeros_like(ggk_ref)

    ggq_ref[...] += jnp.broadcast_to(q_gain_grad, ggq_ref.shape)
    ggk_ref[...] += jnp.broadcast_to(k_gain_grad, ggk_ref.shape)


def attention_backward(
    joined, dattended, terms, exact, inverse_sum, q_gain, k_gain, x_low, core, first, count, room,
    place=0, into=(), fold=(), origin=0, size=0,
):
    length = x_low.shape[0]

    def whole(shape):
        return pl.BlockSpec(shape, lambda p: (0, 0))

    last = (fold[0].shape[0] - origin - size) // (FIN // 8) if fold else 0

    def segment(i):
        return pl.BlockSpec(
            (pl.Element(size), pl.Element(D // 2)),
            lambda p: (pl.multiple_of(origin + FIN // 8 * jnp.minimum(2 * p + i, last), 32), 0),
        )

    gain = jax.ShapeDtypeStruct((HEAD, 128), f32)
    call = pl.pallas_call(
        partial(backward_kernel, folds=bool(fold)),
        grid=(count,),
        in_specs=[
            pl.BlockSpec((3, pair, length), lambda p: (0, first + p, 0)),
            pl.BlockSpec((pair, length), lambda p: (first + p, 0)),
            pl.BlockSpec((2, length, length), lambda p: (first + p, 0, 0)),
            pl.BlockSpec((pair, length), lambda p: (first + p, 0)),
            pl.BlockSpec((1, 8, length), lambda p: (first + p, 0, 0)),
            whole((HEAD, 1)), whole((HEAD, 1)), whole((length, D)), core_spec,
            *[pl.BlockSpec(memory_space=pl.ANY)] * len(into),
            *[segment(i) for i in range(2) for _ in fold],
        ],
        out_specs=[pl.BlockSpec((3, length, pair), lambda p: (0, 0, p))]
        + [pl.BlockSpec((3, pair, D // 2), lambda p: (0, place + p, 0))] * 2
        + [whole((HEAD, 128))] * 2
        + [pl.BlockSpec((2 * size, D // 2), lambda p: (p, 0))] * bool(fold),
        out_shape=[jax.ShapeDtypeStruct((3, length, count * pair), bf16)]
        + [jax.ShapeDtypeStruct((3, room * pair, D // 2), bf16)] * 2 + [gain] * 2
        + [jax.ShapeDtypeStruct(((last + 1) * size, D // 2), bf16)] * bool(fold),
        input_output_aliases={9 + i: 1 + i for i in range(len(into))},
        scratch_shapes=[
            pltpu.VMEM((2, length, HEAD + 16), bf16),
            pltpu.VMEM((2, HEAD, length), bf16),
            pltpu.VMEM((2, HEAD, length), bf16),
            pltpu.VMEM((2, HEAD + 16, length), bf16),
        ],
        compiler_params=pltpu.CompilerParams(vmem_limit_bytes=vmem_bytes),
        cost_estimate=pl.CostEstimate(
            flops=2 * count * 8 * length * length * 256,
            bytes_accessed=24 * length * count * pair + 4 * count * length * length,
            transcendentals=0,
        ),
        name="attention_backward",
    )
    outs = call(joined, dattended, terms, exact, inverse_sum, q_gain, k_gain, x_low, core, *into, *fold, *fold)
    return (*outs[:3], outs[3][:, 0], outs[4][:, 0], *outs[5:])


def gelu_pair(u):
    z = jnp.abs(u) * 0.7071067811865476
    t = 1.0 / (1.0 + 0.3275911 * z)
    e = jnp.exp(-z * z)
    poly = t * (0.127414796 + t * (-0.142248368 + t * (0.7107068705 + t * (-0.7265760135 + t * 0.5307027145))))
    half = poly * e
    phi = jnp.where(u >= 0, 1.0 - half, half)
    return (u * phi, phi + u * (0.3989422804014327 * e))


def mlp_kernel(
    x_ref, gy_ref, wu_ref, wd_ref, core_ref,
    res_ref, gn_ref, keep_up, send_up, keep_down, send_down, act_ref, dup_ref,
):
    @pl.when(pl.program_id(0) == 0)
    def _():
        res_ref[...] = jnp.zeros_like(res_ref)
        gn_ref[...] = jnp.zeros_like(gn_ref)

    for begin in range(0, wu_ref.shape[0], tile_rows):
        units = slice(begin, begin + tile_rows)
        upward = contract(x_ref[...], wu_ref[units], 1, 1).astype(bf16).astype(f32)
        grad_hidden = contract(gy_ref[...], wd_ref[units], 1, 1)
        active, slope = gelu_pair(upward)
        act_ref[:, units] = active.astype(bf16)
        dup_ref[:, units] = (grad_hidden * slope).astype(bf16)
    active, dupward = act_ref[...], dup_ref[...]
    res_ref[...] += nn(active, wd_ref[...])
    gn_ref[...] += nn(dupward, wu_ref[...])
    halves(contract(active, gy_ref[...], 0, 0).astype(bf16), core_ref, keep_down, send_down)
    halves(contract(dupward, x_ref[...], 0, 0).astype(bf16), core_ref, keep_up, send_up)


def mlp(x_low, grad_y, w_in_all, w_out_all, core):
    length = x_low.shape[0]
    hidden = w_in_all.shape[0] - QKV
    tile = D
    whole = pl.BlockSpec((length, D), lambda t: (0, 0))
    total = jax.ShapeDtypeStruct((length, D), f32)
    grad = jax.ShapeDtypeStruct((hidden, D // 2), bf16)
    call = pl.pallas_call(
        mlp_kernel,
        grid=(hidden // tile,),
        in_specs=[
            whole,
            whole,
            pl.BlockSpec((tile, D), lambda t: (t + QKV // tile, 0)),
            pl.BlockSpec((tile, D), lambda t: (t + D // tile, 0)),
            core_spec,
        ],
        out_specs=[whole, whole] + [pl.BlockSpec((tile, D // 2), lambda t: (t, 0))] * 4,
        out_shape=[total, total] + [grad] * 4,
        scratch_shapes=[pltpu.VMEM((length, tile), bf16)] * 2,
        compiler_params=pltpu.CompilerParams(vmem_limit_bytes=vmem_bytes),
        cost_estimate=pl.CostEstimate(
            flops=18 * length * D * hidden,
            bytes_accessed=12 * length * D + 8 * hidden * D,
            transcendentals=length * hidden,
        ),
        name="mlp",
    )
    return call(x_low, grad_y, w_in_all, w_out_all, core)


def input_kernel(*refs, calls):
    grads = refs[:calls]
    w_ref, normed_ref, tokens_ref, gy_ref, gain_ref, out_ref, ln_ref, total = refs[calls:]
    step = pl.program_id(0)

    @pl.when(step == 0)
    def _():
        total[...] = normed_ref[...]

    begin = 0
    sums = []
    for ref in grads:
        sums.append(nn(ref[0], w_ref[begin : begin + ref.shape[2], :]))
        begin += ref.shape[2]
    total[...] += sum(sums)

    @pl.when(step == pl.num_programs(0) - 1)
    def _():
        x_hat, x_inverse = normalize(tokens_ref[...].astype(f32))
        grad_normed = total[...]
        ln_ref[...] = jnp.sum(grad_normed * x_hat, axis=0, keepdims=True)
        back = norm_backward(grad_normed * gain_ref[...], x_hat, x_inverse)
        out_ref[...] = (gy_ref[...].astype(f32) + back).astype(bf16)


def input_gradient(grads, w_in_all, normed, tokens, grad_y, gain):
    length = tokens.shape[0]
    whole = pl.BlockSpec((length, D), lambda p: (0, 0))
    row = pl.BlockSpec((1, D), lambda p: (0, 0))
    call = pl.pallas_call(
        partial(input_kernel, calls=len(grads)),
        grid=(3,),
        in_specs=[pl.BlockSpec((1, length, grad.shape[2]), lambda p: (p, 0, 0)) for grad in grads]
        + [pl.BlockSpec((D, D), lambda p: (p, 0)), whole, whole, whole, row],
        out_specs=[whole, row],
        out_shape=[jax.ShapeDtypeStruct((length, D), bf16), jax.ShapeDtypeStruct((1, D), f32)],
        scratch_shapes=[pltpu.VMEM((length, D), f32)],
        compiler_params=pltpu.CompilerParams(vmem_limit_bytes=vmem_bytes),
        cost_estimate=pl.CostEstimate(
            flops=2 * length * D * QKV, bytes_accessed=20 * length * D, transcendentals=length
        ),
        name="input_gradient",
    )
    out, ln_grad = call(*grads, w_in_all, normed, tokens, grad_y, gain.reshape(1, D))
    return (out, ln_grad[0])


def split(values):
    high = values.astype(bf16)
    return (high, (values - high.astype(f32)).astype(bf16))


def newton_kernel(
    near_ref, other_ref, own_ref, far_ref, core_ref, o_ref, gh, gl, sh, sl, ph, pw, g32, x32
):
    count = D // tile_rows

    def span(i):
        return slice(i * tile_rows, (i + 1) * tile_rows)

    def store(high_ref, low_ref, i, j, value):
        high_ref[span(i), span(j)], low_ref[span(i), span(j)] = split(value)
        if i != j:
            high_ref[span(j), span(i)], low_ref[span(j), span(i)] = split(value.T)

    def symmetric(ah, al, bh, bl, post):
        for i in range(count):
            for j in range(i, count):
                rows, columns = span(i), span(j)
                post(
                    i,
                    j,
                    nn(ah[rows, :], bh[:, columns])
                    + (nn(ah[rows, :], bl[:, columns]) + nn(al[rows, :], bh[:, columns])),
                )

    def squared(ah, al, post):
        for i in range(count):
            for j in range(i, count):
                rows, columns = span(i), span(j)
                mixed = nn(ah[rows, :], al[:, columns])
                other = mixed if i == j else nn(ah[columns, :], al[:, rows])
                post(i, j, nn(ah[rows, :], ah[:, columns]) + (mixed + other.T))

    def sweep(last):
        def keep_factor(i, j, value):
            value = ns_cubic * g32[span(i), span(j)] + ns_quintic * value
            if i == j:
                shape = (tile_rows, tile_rows)
                diagonal = lax.broadcasted_iota(jnp.int32, shape, 0) == lax.broadcasted_iota(jnp.int32, shape, 1)
                value = value + jnp.where(diagonal, ns_linear, 0.0)
            store(ph, pw, i, j, value)

        def keep_gram(i, j, value):
            g32[span(i), span(j)] = value
            store(gh, gl, i, j, value)

        squared(gh, gl, keep_factor)
        xh, xl = split(x32[...])
        x32[...] = nn(xh, ph[...]) + (nn(xh, pw[...]) + nn(xl, ph[...]))
        if not last:
            symmetric(gh, gl, ph, pw, partial(store, sh, sl))
            symmetric(sh, sl, ph, pw, keep_gram)

    half = D // 2
    first_core = core_ref[0] == 0
    left = jnp.where(first_core, near_ref[...], other_ref[...])
    side = jnp.where(first_core, other_ref[:half], near_ref[:half])
    corner = left[:half]
    i = lax.broadcasted_iota(jnp.int32, (half, half), 0)
    j = lax.broadcasted_iota(jnp.int32, (half, half), 1)
    corner_t = corner.T
    first = jnp.where(i <= j, corner, corner_t)
    last = jnp.where(i > j, corner, jnp.where(i == j, left[half : half + 1], corner_t))
    trace = jnp.sum(jnp.where(i == j, first + last, 0.0), axis=0, keepdims=True)
    trace = jnp.sum(trace, axis=1, keepdims=True)
    inverse = 1.0 / (jnp.sqrt(trace) + 1e-07)
    square = inverse * inverse
    g32[:half, :half] = first * square
    g32[half:, half:] = last * square
    g32[:half, half:] = side * square
    g32[half:, :half] = side.T * square
    rows = own_ref.shape[0]
    x32[:rows] = own_ref[...] * inverse
    x32[rows:] = far_ref[...] * inverse
    gh[...], gl[...] = split(g32[...])

    @pl.loop(0, 4)
    def _(k):
        sweep(False)

    sweep(True)
    o_ref[...] = x32[...].astype(bf16)


def newton(folded, far_folded, own_rows, far_rows, core):
    rows = own_rows.shape[0] + far_rows.shape[0]
    whole = pl.BlockSpec(memory_space=pltpu.VMEM)
    call = pl.pallas_call(
        newton_kernel,
        in_specs=[whole] * 4 + [core_spec],
        out_specs=whole,
        out_shape=jax.ShapeDtypeStruct((rows, D), bf16),
        scratch_shapes=[pltpu.VMEM((D, D), bf16)] * 6 + [pltpu.VMEM((D, D), f32), pltpu.VMEM((rows, D), f32)],
        compiler_params=pltpu.CompilerParams(vmem_limit_bytes=vmem_bytes),
        cost_estimate=pl.CostEstimate(
            flops=30 * D * D * (2 * D + rows), bytes_accessed=4 * D * D + 6 * rows * D, transcendentals=0
        ),
        name="newton",
    )
    return call(folded, far_folded, own_rows, far_rows, core)


def update_kernel(in_ref, in_far_ref, out_ref, out_far_ref, wi_ref, wo_ref, place_ref, in_new, out_new, held, *, first):
    def new(weights, ortho, size):
        rate = muon_rate * (size / D) ** 0.5
        return weights.astype(f32) * (1 - muon_rate * muon_decay) - rate * ortho.astype(f32)

    first_core = place_ref[0] == 0
    for near_ref, far_ref, total in ((in_ref, in_far_ref, None), (out_ref, out_far_ref, out_new)):
        size = far_ref.shape[0] // 2
        all_near, all_far, weights = near_ref[...].astype(f32), far_ref[...].astype(f32), wo_ref[...].astype(f32)
        for chip in range(2):
            rows = slice(chip * size, (chip + 1) * size)
            near, far = all_near[rows], all_far[rows]
            begin = 2 * chip * size
            both = (jnp.where(first_core, near, far), jnp.where(first_core, far, near))
            for i in range(2):
                spot = slice(begin + i * size, begin + (i + 1) * size)
                if total is None:
                    held[spot] = both[i]
                else:
                    total[spot] = new(weights[spot], both[i], FOUT)
    rows = in_new.shape[0]
    if first == rows:
        in_new[...] = new(wi_ref[...], held[...], FIN)
        return
    start = pl.multiple_of(place_ref[1], 32)
    cut, rest = first // 2, (rows - first) // 2
    pieces = jnp.concatenate([held[cut : cut + rest], held[rows // 2 + cut :]], axis=0)
    in_new[: rows - first] = new(wi_ref[: rows - first], pieces, FIN)
    in_new[first:] = jnp.where(
        lax.broadcasted_iota(jnp.int32, (rows - first, 1), 0) < start, in_new[first:], new(wi_ref[first:], pieces, FIN)
    )
    spot = pl.ds(start, first)
    pieces = jnp.concatenate([held[:cut], held[rows // 2 : rows // 2 + cut]], axis=0)
    in_new[spot] = new(wi_ref[spot], pieces, FIN)


def update(ortho_in, far_in, ortho_out, far_out, w_in, w_out, place, first):
    whole = pl.BlockSpec(memory_space=pltpu.VMEM)
    call = pl.pallas_call(
        partial(update_kernel, first=first),
        in_specs=[whole] * 6 + [core_spec],
        out_specs=[whole] * 2,
        out_shape=[jax.ShapeDtypeStruct(w.shape, f32) for w in (w_in, w_out)],
        scratch_shapes=[pltpu.VMEM(w_in.shape, f32)],
        compiler_params=pltpu.CompilerParams(vmem_limit_bytes=vmem_bytes),
        cost_estimate=pl.CostEstimate(flops=4 * w_in.size, bytes_accessed=14 * w_in.size, transcendentals=0),
        name="update",
    )
    return call(ortho_in, far_in, ortho_out, far_out, w_in, w_out, place)


def gram_kernel(m_ref, extra_ref, core_ref, o_ref):
    half = D // 2
    left, right = slice(0, half), slice(half, D)

    def product(a, b):
        ah, al = split(m_ref[:, a])
        bh, bl = split(m_ref[:, b])
        return contract(ah, bh, 0, 0) + (contract(ah, bl, 0, 0) + contract(al, bh, 0, 0))

    o_ref[half:, :] = extra_ref[...]

    @pl.when(core_ref[0] == 0)
    def _():
        i = lax.broadcasted_iota(jnp.int32, (half, half), 0)
        j = lax.broadcasted_iota(jnp.int32, (half, half), 1)
        last = product(right, right)
        o_ref[:half, :] = jnp.where(i <= j, product(left, left), last)
        o_ref[half : half + 1, :] = jnp.sum(jnp.where(i == j, last, 0.0), axis=0, keepdims=True)

    @pl.when(core_ref[0] != 0)
    def _():
        o_ref[:half, :] = product(left, right)


def folded_gram(rows, extra, core):
    rows = jnp.pad(rows, ((0, -rows.shape[0] % 16), (0, 0)))
    whole = pl.BlockSpec(memory_space=pltpu.VMEM)
    call = pl.pallas_call(
        gram_kernel,
        in_specs=[whole, whole, core_spec],
        out_specs=whole,
        out_shape=jax.ShapeDtypeStruct((D // 2 + extra_rows, D // 2), f32),
        compiler_params=pltpu.CompilerParams(vmem_limit_bytes=vmem_bytes),
        cost_estimate=pl.CostEstimate(
            flops=4 * rows.shape[0] * D * D, bytes_accessed=8 * rows.shape[0] * D, transcendentals=0
        ),
        name="gram",
    )
    return call(rows, extra, core)


def bits(size):
    return [1 << b for b in range(size.bit_length() - 1)]


def take(values, index, axis):
    return lax.dynamic_index_in_dim(values, index, axis, keepdims=False)


def after(value, *others):
    return lax.optimization_barrier((value, *others))[0]


def exchange(values, axis, bit, fill=()):
    size = lax.axis_size(axis)
    return after(lax.ppermute(values, axis, [(i, i ^ bit) for i in range(size)]), *fill)


def sum_steps(values, halving, full):
    fill = yield values
    for axis, bit in halving:
        side = (lax.axis_index(axis) // bit) % 2
        pieces = values.reshape(2, values.shape[0] // 2, values.shape[1])
        values = take(pieces, side, 0) + exchange(take(pieces, 1 - side, 0), axis, bit, fill)
        fill = yield values
    for axis, bit in full:
        values = values + exchange(values, axis, bit, fill)
        fill = yield values


def halve(parts, axis, name, bit):
    side = (lax.axis_index(name) // bit) % 2
    sent = [take(part, 1 - side, axis) for part in parts]

    def receive(*fill):
        kept = jnp.concatenate([take(part, side, axis) for part in parts], axis=0)
        return (kept, exchange(jnp.concatenate(sent, axis=0), name, bit, fill))

    return sent, receive


def added(kept, other):
    return (kept.astype(f32) + other.astype(f32)).astype(bf16)


def scatter_one(*parts):
    wide = lax.axis_size("wide")
    columns = parts[0].shape[-1]
    rows = sum(part.size for part in parts) // (2 * wide * columns)
    cut = rows // 16 * 8
    parts = [part.reshape(-1, 2, 2, rows, columns) for part in parts]
    sent_a, receive_a = halve([part[:, :, :, :cut] for part in parts], 1, "wide", 1)
    sent_b, receive_b = halve([part[:, :, :, cut:] for part in parts], 2, "nar", 2)
    return sent_a + sent_b, lambda *fill: (added(*receive_a(*fill)), added(*receive_b(*fill)))


def split_kernel(*refs, pairs, rows):
    *parts, place_ref, sent_y, kept_y, sent_x, kept_x, held = refs
    begin = 0
    for paired in pairs:
        values = parts.pop(0)[...].astype(f32)
        if paired:
            values = values + parts.pop(0)[...].astype(f32)
        held[begin : begin + values.shape[0]] = values
        begin += values.shape[0]
    cut = kept_y.shape[2]
    for z in range(kept_y.shape[0]):
        for j in range(2):
            for near, out_y, out_x in ((True, kept_y, kept_x), (False, sent_y, sent_x)):
                y = place_ref[0] if near else 1 - place_ref[0]
                x = place_ref[1] if near else 1 - place_ref[1]
                first = pl.ds(pl.multiple_of(((2 * z + y) * 2 + j) * rows, 8), cut)
                out_y[z, j] = held[first].astype(bf16)
                second = pl.ds(pl.multiple_of(((2 * z + j) * 2 + x) * rows + cut, 8), rows - cut)
                out_x[z, j] = held[second].astype(bf16)


def split_one(rows, *parts):
    half = D // 2
    cut = rows // 16 * 8
    far = lax.axis_size("wide") // 2
    place = jnp.stack([lax.axis_index("wide") % 2, lax.axis_index("nar") // 2])
    terms = [term.reshape(-1, half) for part in parts for term in (part if isinstance(part, tuple) else (part,))]
    whole = pl.BlockSpec(memory_space=pltpu.VMEM)
    shapes = [(far, 2, cut, half)] * 2 + [(far, 2, rows - cut, half)] * 2
    call = pl.pallas_call(
        partial(split_kernel, pairs=[isinstance(part, tuple) for part in parts], rows=rows),
        in_specs=[whole] * len(terms) + [core_spec],
        out_specs=[whole] * 4,
        out_shape=[jax.ShapeDtypeStruct(shape, bf16) for shape in shapes],
        scratch_shapes=[pltpu.VMEM((4 * far * rows, half), f32)],
        compiler_params=pltpu.CompilerParams(vmem_limit_bytes=vmem_bytes),
        cost_estimate=pl.CostEstimate(
            flops=8 * far * rows * half, bytes_accessed=24 * far * rows * half, transcendentals=0
        ),
        name="split",
    )
    sent_y, kept_y, sent_x, kept_x = call(*terms, place)

    def arrive(*fill):
        return (exchange(sent_y, "wide", 1, fill), exchange(sent_x, "nar", 2, fill))

    return [sent_y, sent_x], arrive, lambda other_y, other_x: (added(kept_y, other_y), added(kept_x, other_x))


def scatter_two(held):
    sent_a, receive_a = halve(held[:1], 1, "nar", 2)
    sent_b, receive_b = halve(held[1:], 1, "wide", 1)

    def receive(*fill):
        kept, other = zip(receive_a(*fill), receive_b(*fill), strict=True)
        return added(jnp.concatenate(kept, axis=1), jnp.concatenate(other, axis=1))

    return sent_a + sent_b, receive


def scatter_rest(held):
    wide = lax.axis_size("wide")
    far = wide // 2
    place = lax.axis_index("wide") // 2
    sent = [take(held, place ^ shift, 0) for shift in range(1, far)]

    def receive(*fill):
        total = take(held, place, 0).astype(f32)
        for shift in reversed(range(1, far)):
            pairs = [(i, i ^ (2 * shift)) for i in range(wide)]
            total = total + after(lax.ppermute(sent[shift - 1], "wide", pairs), *fill).astype(f32)
        return total.astype(bf16)

    return sent, receive


def both_cores(values, *fill):
    other = exchange(values, "nar", 1, fill)
    return join(values, other, lax.axis_index("nar") % 2, 1).reshape(values.shape[0], D)


def ordered(values, other, side):
    return (jnp.where(side == 0, values, other), jnp.where(side == 0, other, values))


def join(values, other, side, axis):
    return jnp.stack(ordered(values, other, side), axis)


def gather(values):
    wide = lax.axis_size("wide")
    rows = values.shape[0]
    far = wide // 2
    place, side = lax.axis_index("wide") // 2, lax.axis_index("wide") % 2
    chip, core = lax.axis_index("nar") // 2, lax.axis_index("nar") % 2
    held = lax.dynamic_update_index_in_dim(jnp.zeros((far, rows, D), values.dtype), values, place, 0)
    for shift in range(1, far):
        pairs = [(i, i ^ (2 * shift)) for i in range(wide)]
        held = lax.dynamic_update_index_in_dim(held, lax.ppermute(values, "wide", pairs), place ^ shift, 0)
    cut = rows // 32 * 16
    first, second = held[:, :cut], held[:, cut:]
    first = join(first, exchange(first, "wide", 1), side, 1)
    second = join(second, exchange(second, "nar", 2), chip, 1)
    first = join(first, exchange(first, "nar", 2), chip, 2)
    second = join(second, exchange(second, "wide", 1), side, 1)
    held = jnp.concatenate([first, second], axis=3)
    return join(held, exchange(held, "nar", 1), core, 3).reshape(-1, D)


def on_device(tokens, cotangent, image_ids, w_in, w_out, gains, mom_in, mom_out, gain_m, gain_v):
    row_count = tokens.shape[0]
    rows_in = w_in.shape[0]
    rows_out = w_out.shape[0]
    nar_count = lax.axis_size("nar")
    wide_count = lax.axis_size("wide")
    nar_place = lax.axis_index("nar")
    share_in = rows_in // nar_count
    share_out = rows_out // nar_count
    everyone = ("wide", "nar")

    def share(rows, size):
        return lax.dynamic_slice_in_dim(rows, nar_place * size, size, 0)

    w_in_all = lax.all_gather(share(w_in, share_in), everyone, axis=0, tiled=True)
    w_out_all = gather(share(w_out, share_out))

    x_float = tokens.astype(f32)
    ln_gain = gains[:D]
    x_hat, x_inverse = normalize(x_float)
    x_low = (x_hat * ln_gain).astype(bf16)
    live = (image_ids.reshape(row_count) >= 0)[:, None]
    grad_y = jnp.where(live, cotangent, jnp.zeros_like(cotangent))

    core = (nar_place % 2).reshape(1)
    chip = nar_place // 2
    half = D // 2
    pairs = D // pair
    q_gain, k_gain = gains[D : D + HEAD].reshape(HEAD, 1), gains[D + HEAD :].reshape(HEAD, 1)
    onek, penq = image_columns(image_ids.reshape(row_count))
    x_low = after(x_low, q_gain, k_gain, onek, penq)
    first = rows_in * 4 // 7
    second = rows_in - first
    parted = wide_count == 8 and first == half and rows_in == 672
    mlp_result, mlp_normed, keep_up, send_up, keep_down, send_down = mlp(x_low, grad_y, w_in_all, w_out_all, core)
    joined, dattended, attended, terms, exact, inverse_sum, keep_att, send_att = attention_forward(
        after(x_low, keep_down), grad_y, w_in_all, w_out_all, onek, penq, q_gain, k_gain, core
    )

    def backward(begin, count, earlier=(), **buffers):
        return attention_backward(
            joined, dattended, terms, exact, inverse_sum, q_gain, k_gain, after(x_low, *earlier), core, begin, count,
            **buffers,
        )

    def cores(keep, send, *fill):
        return added(keep, exchange(send, "nar", 1, fill)).reshape(-1, half)

    start = 96 * jnp.minimum(lax.axis_index("wide"), 3)
    row = lax.broadcasted_iota(jnp.int32, (rows_in, 1), 0)
    half_mom_out = lax.dynamic_slice_in_dim(mom_out, chip * (rows_out // 2), rows_out // 2, 0)
    wide_bits = bits(wide_count)
    halving = [("wide", wide_bits[0]), ("nar", 2)]
    full = [("wide", bit) for bit in wide_bits[1:]]

    def begin_out(part):
        zeros = jnp.zeros((extra_rows, half), f32)
        steps = sum_steps(folded_gram(muon_beta * half_mom_out + part.astype(f32), zeros, core), halving, full)
        return (steps, next(steps))

    if parted:
        def pair_of(keep, send, *fill):
            return (keep, exchange(send, "nar", 1, fill))

        down = pair_of(keep_down, send_down, keep_att)
        up = pair_of(keep_up, send_up, keep_att)
        sent, arrive, combine = split_one(rows_out // 2, pair_of(keep_att, send_att), down)
        dqkv_a, keep_a, send_a, q_grad_a, k_grad_a, up_a = backward(0, 3, sent, room=3, fold=up, size=first)
        sent, receive = scatter_two(combine(*arrive(keep_a)))
        dqkv_b, keep_b, send_b, q_grad_b, k_grad_b = backward(3, 1, [keep_a, *sent], room=3)
        sent_o, receive_o = scatter_rest(receive(dqkv_b))
        sent_a, arrive_a, combine_a = split_one(first // 2, pair_of(keep_a, send_a, dqkv_b), up_a)
        dqkv_c, keep_b, send_b, q_grad_c, k_grad_c, up_b = backward(
            4, 2, [*sent_a, *sent_o], room=3, place=1, into=(keep_b, send_b), fold=up, origin=first, size=second
        )
        part_out = receive_o(dqkv_c)
        sent_a, receive_a = scatter_two(combine_a(*arrive_a(dqkv_c)))
        sent_b, arrive_b, combine_b = split_one(second // 2, pair_of(keep_b, send_b, part_out, *sent_a), up_b)
        part_out = both_cores(part_out, *sent_b)
        steps_out, folded_out = begin_out(after(part_out, *sent_b))
        mom_in_late = after(mom_in, folded_out)
        held_b = combine_b(*arrive_b(folded_out))
        sent_b, receive_b = scatter_two(held_b)
        folded_out = steps_out.send(sent_b)
        held_a = receive_a(*sent_b)
        held_b = receive_b(held_a, folded_out)
        sent, receive = scatter_rest(jnp.concatenate([held_a, held_b], axis=1))
        grad_tokens, ln_grad = input_gradient(
            [dqkv_a, dqkv_b, dqkv_c], w_in_all, after(mlp_normed, *sent), tokens, grad_y, ln_gain
        )
        far_out = exchange(after(part_out, *sent), "nar", 2, (grad_tokens,))
        folded_out = steps_out.send((grad_tokens,))
        part_in = receive(grad_tokens, far_out, folded_out)
        steps_done = 2
        q_gain_grad, k_gain_grad = q_grad_a + q_grad_b + q_grad_c, k_grad_a + k_grad_b + k_grad_c

        def halved(rows, chip):
            inside = lax.dynamic_slice_in_dim(rows, start, first, 0)
            others = jnp.where(row[:second] < start, rows[:second], rows[first:])
            return jnp.concatenate(
                [
                    lax.dynamic_slice_in_dim(inside, chip * (first // 2), first // 2, 0),
                    lax.dynamic_slice_in_dim(others, chip * (second // 2), second // 2, 0),
                ],
                axis=0,
            )

        def rejoined(near, far):
            cut = first // 2
            a, b = jnp.concatenate([near[:cut], far[:cut]], 0), jnp.concatenate([near[cut:], far[cut:]], 0)
            a = lax.dynamic_update_slice_in_dim(jnp.zeros((rows_in, D), a.dtype), a, start, 0)
            empty = jnp.zeros((first, D), b.dtype)
            below = jnp.concatenate([b, empty], axis=0)
            above = jnp.concatenate([empty, b], axis=0)
            inside = (row >= start) & (row < start + first)
            return jnp.where(inside, a, jnp.where(row < start, below, above))

    else:
        dqkv, keep_a, send_a, q_gain_grad, k_gain_grad = backward(0, pairs, room=pairs)
        grad_tokens, ln_grad = input_gradient([dqkv], w_in_all, mlp_normed, tokens, grad_y, ln_gain)

        def scattered(*parts):
            held = scatter_one(jnp.concatenate(parts, axis=0))[1]()
            return scatter_rest(scatter_two(held)[1]())[1]()

        part_out = both_cores(scattered(cores(keep_att, send_att), cores(keep_down, send_down)))
        steps_out, folded_out = begin_out(part_out)
        mom_in_late = mom_in
        steps_done = 0
        far_out = exchange(part_out, "nar", 2)
        part_in = scattered(cores(keep_a, send_a), cores(keep_up, send_up))

        def halved(rows, chip):
            return lax.dynamic_slice_in_dim(rows, chip * (rows_in // 2), rows_in // 2, 0)

        def rejoined(near, far):
            return jnp.concatenate([near, far], axis=0)

    part_in = both_cores(part_in)
    gain_terms = jnp.concatenate([ln_grad, q_gain_grad, k_gain_grad])
    count = gain_terms.shape[0]
    extra = jnp.pad(gain_terms, (half, (extra_rows - 1) * half - count)).reshape(extra_rows, half)
    momenta_in = muon_beta * halved(mom_in_late, chip) + part_in.astype(f32)
    steps_in = sum_steps(folded_gram(momenta_in, extra, core), halving, full)
    folded_in = next(steps_in)

    half_in, half_out = rows_in // 4, rows_out // 4

    def mine(rows, size):
        return lax.dynamic_slice_in_dim(rows, core[0] * size, size, 0)

    def fitted(rows):
        return jnp.pad(rows, ((0, half_in - half_out), (0, 0)))

    far_in = exchange(part_in, "nar", 2)
    own_rows = jnp.where(
        chip == 0,
        mine(momenta_in, half_in),
        fitted(mine(muon_beta * half_mom_out + part_out.astype(f32), half_out)),
    )
    far_mom = jnp.where(
        chip == 0,
        mine(halved(mom_in_late, 1 - chip), half_in),
        fitted(mine(lax.dynamic_slice_in_dim(mom_out, (1 - chip) * (rows_out // 2), rows_out // 2, 0), half_out)),
    )
    far_rows = jnp.where(chip == 0, mine(far_in, half_in), fitted(mine(far_out, half_out)))
    far_rows = muon_beta * far_mom + far_rows.astype(f32)
    steps = len(halving) + len(full)
    folded_out = steps_out.send((folded_in,))
    steps_done += 1
    for step in range(steps):
        fill = {0: (far_in, folded_out), len(halving): (own_rows, far_rows)}.get(step, ())
        folded_in = steps_in.send(fill)
        if steps_done < steps:
            folded_out = steps_out.send((folded_in,))
            steps_done += 1
    own, far = ordered(folded_in, folded_out, chip)
    folded = join(own, exchange(far, "nar", 2), chip, 0).reshape(-1, half)
    branch = mlp_result + nn(after(attended, folded), w_out_all[:D])
    result = (tokens.astype(f32) + branch).astype(bf16)
    side = lax.axis_index("wide") % 2
    folded = join(folded, exchange(folded, "wide", 1, (result,)), side, 0).reshape(-1, half)
    far_folded = exchange(folded, "nar", 1)
    ortho = newton(folded, far_folded, own_rows, far_rows, core)
    extra = folded[half : half + 8] + far_folded[half : half + 8]
    extra = ordered(extra, exchange(after(extra, ortho), "nar", 2), chip)[0].reshape(8 * half)
    grad_gains = extra[half : half + count]
    far_out, far_in = after(far_out, ortho), after(far_in, ortho)
    grad_w_out = join(part_out, far_out, chip, 0).reshape(rows_out, D).astype(f32)
    mom_out_new = muon_beta * mom_out + grad_w_out
    grad_w_in = after(rejoined(*ordered(part_in, far_in, chip))).astype(f32)
    mom_in_new = muon_beta * mom_in + grad_w_in

    other = exchange(ortho, "nar", 2, (mom_in_new, mom_out_new, grad_gains))
    ortho_in, ortho_out = ordered(ortho, other, chip)
    ortho_out = jnp.concatenate([ortho_out[half_in : half_in + half_out], ortho_out[:half_out]], axis=0)
    far_in, far_out = (exchange(rows, "nar", 1) for rows in (ortho_in, ortho_out))
    w_in_new, w_out_new = update(
        ortho_in, far_in, ortho_out, far_out, w_in, w_out, jnp.stack([core[0], start]), first if parted else rows_in
    )
    gain_m_new = adam_first * gain_m + (1 - adam_first) * grad_gains
    gain_v_new = adam_second * gain_v + (1 - adam_second) * grad_gains * grad_gains
    gains_new = gains - adam_rate * (gain_m_new / (1 - adam_first**STEP)) / (
        jnp.sqrt(gain_v_new / (1 - adam_second**STEP)) + adam_eps
    )
    return (
        result,
        grad_tokens,
        grad_w_in,
        grad_w_out,
        grad_gains,
        mom_in_new,
        mom_out_new,
        gain_m_new,
        gain_v_new,
        w_in_new,
        w_out_new,
        gains_new,
    )


def solution(mesh):
    rows = P(("nar", "wide"), None)
    wide = P("wide", None)
    return jax.shard_map(
        on_device,
        mesh=mesh,
        in_specs=(rows, rows, rows, wide, wide, P(), wide, wide, P(), P()),
        out_specs=(rows, rows, wide, wide, P(), wide, wide, P(), P(), wide, wide, P()),
        check_vma=False,
    )
```

```python
from functools import partial

import jax
import jax.numpy as jnp
from jax import lax
from jax.experimental import pallas as pl
from jax.experimental.pallas import tpu as pltpu
from jax.sharding import PartitionSpec as P

D = 768
HEADS = 12
HEAD = 64
LEN = 1024
STEP = 10
FIN = 5376
FOUT = 3840
QKV = 3 * D

f32 = jnp.float32
bf16 = jnp.bfloat16
ns_linear = 3.4445
ns_cubic = -4.775
ns_quintic = 2.0315
muon_beta = 0.5
muon_rate = 0.8
muon_decay = 0.1
adam_rate = 0.8
adam_first = 0.9
adam_second = 0.95
adam_eps = 1e-08
norm_eps = 1e-06
penalty = 16384.0
vmem_bytes = 60 * 1024 * 1024
tile_rows = 256
extra_rows = 32
pair = 2 * HEAD


def normalize(values):
    center = values - jnp.mean(values, axis=-1, keepdims=True)
    variance = jnp.mean(center * center, axis=-1, keepdims=True)
    inverse = lax.rsqrt(variance + norm_eps)
    return (center * inverse, inverse)


def norm_backward(grad_scaled, normed, inverse, axis=-1):
    mean_grad = jnp.mean(grad_scaled, axis=axis, keepdims=True)
    mean_cross = jnp.mean(grad_scaled * normed, axis=axis, keepdims=True)
    return inverse * (grad_scaled - mean_grad - normed * mean_cross)


def nn(a, b):
    return jnp.dot(a, b, preferred_element_type=f32)


def contract(a, b, dim_a, dim_b):
    return lax.dot_general(a, b, (((dim_a,), (dim_b,)), ((), ())), preferred_element_type=f32)


def normalize_columns(columns):
    center = columns - jnp.mean(columns, axis=0, keepdims=True)
    variance = jnp.mean(center * center, axis=0, keepdims=True)
    inverse = lax.rsqrt(variance + norm_eps)
    return (center * inverse, inverse)


core_spec = pl.BlockSpec(memory_space=pltpu.SMEM)


def halves(values, core_ref, keep_ref, send_ref):
    half = D // 2
    left, right = values[:, :half], values[:, half:]
    first = core_ref[0] == 0
    keep_ref[...] = jnp.where(first, left, right).reshape(keep_ref.shape)
    send_ref[...] = jnp.where(first, right, left).reshape(send_ref.shape)


def forward_kernel(
    x_ref, gy_ref, wq_ref, wk_ref, wv_ref, wa_ref, onek_ref, penq_ref, gq_ref, gk_ref, core_ref,
    joined_ref, do_ref, att_ref, terms_ref, exact_ref, sum_ref, keep_ref, send_ref, kaug, qaug_t, vaug_t,
):
    length = x_ref.shape[0]
    weights = jnp.concatenate([wq_ref[...], wk_ref[...], wv_ref[...]], axis=0)
    joined = contract(weights, x_ref[...], 1, 1).astype(bf16)
    for i in range(3):
        joined_ref[i] = joined[i * pair : (i + 1) * pair]
    do_ref[...] = contract(wa_ref[...], gy_ref[...], 1, 1).astype(bf16)
    parts = []
    for h in range(2):
        rows = slice(HEAD * h, HEAD * (h + 1))
        q_hat, _ = normalize_columns(joined_ref[0, rows, :].astype(f32))
        k_hat, _ = normalize_columns(joined_ref[1, rows, :].astype(f32))
        q_low = (q_hat * gq_ref[:, :1]).astype(bf16)
        k_low = (k_hat * gk_ref[:, :1]).astype(bf16)
        kaug[h, :, :HEAD] = k_low.T
        kaug[h, :, HEAD:] = onek_ref[...]
        qaug_t[h, :HEAD, :] = (q_low.astype(f32) * HEAD ** (-0.5)).astype(bf16)
        qaug_t[h, HEAD:, :] = penq_ref[...]
        vaug_t[h, :HEAD, :] = joined_ref[2, rows, :]
        vaug_t[h, HEAD:, :] = jnp.ones((16, length), bf16)
        terms_ref[h] = jnp.exp(nn(kaug[h], qaug_t[h])).astype(bf16)
        summed = nn(vaug_t[h], terms_ref[h])
        inverse_sum = 1.0 / summed[HEAD : HEAD + 1]
        sum_ref[0, h : h + 1, :] = inverse_sum
        attended = summed[:HEAD] * inverse_sum
        exact_ref[rows, :] = attended
        parts.append(attended)
    attended = jnp.concatenate(parts, 0).astype(bf16)
    halves(nn(attended, gy_ref[...]).astype(bf16), core_ref, keep_ref, send_ref)
    att_ref[...] = attended.T


def image_columns(ids):
    image = jnp.where(ids < 0, 4, ids)
    number = jnp.arange(16)
    onek = (image[:, None] == number[None, :]).astype(bf16)
    penq = jnp.where(image[None, :] == number[:, None], 0.0, -penalty).astype(bf16)
    return (onek, penq)


def attention_forward(x_low, grad_y, w_in_all, w_out_all, onek, penq, q_gain, k_gain, core):
    length = x_low.shape[0]
    pairs = D // pair

    def rows(part):
        return pl.BlockSpec((pair, D), lambda p: (part * pairs + p, 0))

    def whole(shape):
        return pl.BlockSpec(shape, lambda p: (0, 0))

    call = pl.pallas_call(
        forward_kernel,
        grid=(pairs,),
        in_specs=[
            whole((length, D)), whole((length, D)), rows(0), rows(1), rows(2), rows(0),
            whole((length, 16)), whole((16, length)), whole((HEAD, 128)), whole((HEAD, 128)), core_spec,
        ],
        out_specs=[
            pl.BlockSpec((3, pair, length), lambda p: (0, p, 0)),
            pl.BlockSpec((pair, length), lambda p: (p, 0)),
            pl.BlockSpec((length, pair), lambda p: (0, p)),
            pl.BlockSpec((2, length, length), lambda p: (p, 0, 0)),
            pl.BlockSpec((pair, length), lambda p: (p, 0)),
            pl.BlockSpec((1, 8, length), lambda p: (p, 0, 0)),
            *[pl.BlockSpec((pair, D // 2), lambda p: (p, 0))] * 2,
        ],
        out_shape=[
            jax.ShapeDtypeStruct((3, D, length), bf16),
            jax.ShapeDtypeStruct((D, length), bf16),
            jax.ShapeDtypeStruct((length, D), bf16),
            jax.ShapeDtypeStruct((HEADS, length, length), bf16),
            jax.ShapeDtypeStruct((D, length), f32),
            jax.ShapeDtypeStruct((pairs, 8, length), f32),
            *[jax.ShapeDtypeStruct((D, D // 2), bf16)] * 2,
        ],
        scratch_shapes=[
            pltpu.VMEM((2, length, HEAD + 16), bf16),
            pltpu.VMEM((2, HEAD + 16, length), bf16),
            pltpu.VMEM((2, HEAD + 16, length), bf16),
        ],
        compiler_params=pltpu.CompilerParams(vmem_limit_bytes=vmem_bytes),
        cost_estimate=pl.CostEstimate(
            flops=HEADS * 4 * length * length * 256,
            bytes_accessed=16 * length * D + 2 * HEADS * length * length,
            transcendentals=HEADS * length * length,
        ),
        name="attention_forward",
    )
    return call(
        x_low, grad_y, w_in_all, w_in_all, w_in_all, w_out_all, onek, penq,
        q_gain, k_gain, core,
    )


def backward_kernel(
    joined_ref, do_ref, terms_ref, exact_ref, sum_ref, gq_ref, gk_ref, x_ref, core_ref, *refs, folds,
):
    *refs, vaug, qlow_t, klow_t, doaug_t = refs
    if folds:
        *refs, folded_ref = refs
    *refs, grads_ref, keep_ref, send_ref, ggq_ref, ggk_ref = refs
    if folds:
        size = folded_ref.shape[0] // 2
        for i in range(2):
            near_ref, far_ref = refs[-4 + 2 * i], refs[-3 + 2 * i]
            folded_ref[i * size : (i + 1) * size, :] = added(near_ref[...], far_ref[...])
    length = x_ref.shape[0]
    step = pl.program_id(0)
    q_gain = gq_ref[:, :1]
    k_gain = gk_ref[:, :1]
    dq_parts, dk_parts, dv_parts = [], [], []
    q_gain_grad = jnp.zeros((HEAD, 1), f32)
    k_gain_grad = jnp.zeros((HEAD, 1), f32)
    kept = []
    for h in range(2):
        rows = slice(HEAD * h, HEAD * (h + 1))
        q_hat, q_inverse = normalize_columns(joined_ref[0, rows, :].astype(f32))
        k_hat, k_inverse = normalize_columns(joined_ref[1, rows, :].astype(f32))
        klow_t[h] = (k_hat * k_gain).astype(bf16)
        qlow_t[h] = (q_hat * q_gain).astype(bf16)
        vaug[h, :, :HEAD] = joined_ref[2, rows, :].T
        vaug[h, :, HEAD:] = jnp.ones((length, 16), bf16)
        inverse_sum = sum_ref[0, h : h + 1, :]
        do_head = do_ref[rows, :].astype(f32)
        inner = -jnp.sum(do_head * exact_ref[rows, :], axis=0, keepdims=True) * inverse_sum
        do_low = (do_head * inverse_sum).astype(bf16)
        inner_high = inner.astype(bf16).astype(f32)
        extra = lax.broadcasted_iota(jnp.int32, (16, length), 0)
        extra = jnp.where(extra == 0, inner_high, jnp.where(extra == 1, inner - inner_high, 0.0))
        doaug_t[h, :HEAD, :] = do_low
        doaug_t[h, HEAD:, :] = extra.astype(bf16)
        kept.append((q_hat, q_inverse, k_hat, k_inverse))
    sums = [[None] * 3 for _ in range(2)]
    for k in range(0, length, tile_rows):
        for h in range(2):
            span = slice(k, k + tile_rows)
            terms = terms_ref[h, span, :]
            dscores = (terms.astype(f32) * nn(vaug[h, span, :], doaug_t[h])).astype(bf16)
            dv = contract(doaug_t[h, :HEAD, :], terms, 1, 1)
            dk = contract(qlow_t[h], dscores, 1, 1)
            dq = nn(klow_t[h, :, span], dscores)
            sums[h][0] = dq if sums[h][0] is None else sums[h][0] + dq
            sums[h][1] = [dk] if sums[h][1] is None else sums[h][1] + [dk]
            sums[h][2] = [dv] if sums[h][2] is None else sums[h][2] + [dv]
    for h in range(2):
        q_hat, q_inverse, k_hat, k_inverse = kept[h]
        dquery = sums[h][0] * HEAD ** (-0.5)
        dkey = jnp.concatenate(sums[h][1], axis=1) * HEAD ** (-0.5)
        dvalue = jnp.concatenate(sums[h][2], axis=1)
        q_gain_grad += jnp.sum(dquery * q_hat, axis=1, keepdims=True)
        k_gain_grad += jnp.sum(dkey * k_hat, axis=1, keepdims=True)
        dq_parts.append(norm_backward(dquery * q_gain, q_hat, q_inverse, 0))
        dk_parts.append(norm_backward(dkey * k_gain, k_hat, k_inverse, 0))
        dv_parts.append(dvalue)
    grads = jnp.concatenate(dq_parts + dk_parts + dv_parts, 0).astype(bf16)
    halves(nn(grads, x_ref[...]).astype(bf16), core_ref, keep_ref, send_ref)
    grads_ref[0] = grads[:pair].T
    grads_ref[1] = grads[pair : 2 * pair].T
    grads_ref[2] = grads[2 * pair :].T

    @pl.when(step == 0)
    def _():
        ggq_ref[...] = jnp.zeros_like(ggq_ref)
        ggk_ref[...] = jnp.zeros_like(ggk_ref)

    ggq_ref[...] += jnp.broadcast_to(q_gain_grad, ggq_ref.shape)
    ggk_ref[...] += jnp.broadcast_to(k_gain_grad, ggk_ref.shape)


def attention_backward(
    joined, dattended, terms, exact, inverse_sum, q_gain, k_gain, x_low, core, first, count, room,
    place=0, into=(), fold=(), origin=0, size=0,
):
    length = x_low.shape[0]

    def whole(shape):
        return pl.BlockSpec(shape, lambda p: (0, 0))

    last = (fold[0].shape[0] - origin - size) // (FIN // 8) if fold else 0

    def segment(i):
        return pl.BlockSpec(
            (pl.Element(size), pl.Element(D // 2)),
            lambda p: (pl.multiple_of(origin + FIN // 8 * jnp.minimum(2 * p + i, last), 32), 0),
        )

    gain = jax.ShapeDtypeStruct((HEAD, 128), f32)
    call = pl.pallas_call(
        partial(backward_kernel, folds=bool(fold)),
        grid=(count,),
        in_specs=[
            pl.BlockSpec((3, pair, length), lambda p: (0, first + p, 0)),
            pl.BlockSpec((pair, length), lambda p: (first + p, 0)),
            pl.BlockSpec((2, length, length), lambda p: (first + p, 0, 0)),
            pl.BlockSpec((pair, length), lambda p: (first + p, 0)),
            pl.BlockSpec((1, 8, length), lambda p: (first + p, 0, 0)),
            whole((HEAD, 128)), whole((HEAD, 128)), whole((length, D)), core_spec,
            *[pl.BlockSpec(memory_space=pl.ANY)] * len(into),
            *[segment(i) for i in range(2) for _ in fold],
        ],
        out_specs=[pl.BlockSpec((3, length, pair), lambda p: (0, 0, p))]
        + [pl.BlockSpec((3, pair, D // 2), lambda p: (0, place + p, 0))] * 2
        + [whole((HEAD, 128))] * 2
        + [pl.BlockSpec((2 * size, D // 2), lambda p: (p, 0))] * bool(fold),
        out_shape=[jax.ShapeDtypeStruct((3, length, count * pair), bf16)]
        + [jax.ShapeDtypeStruct((3, room * pair, D // 2), bf16)] * 2 + [gain] * 2
        + [jax.ShapeDtypeStruct(((last + 1) * size, D // 2), bf16)] * bool(fold),
        input_output_aliases={9 + i: 1 + i for i in range(len(into))},
        scratch_shapes=[
            pltpu.VMEM((2, length, HEAD + 16), bf16),
            pltpu.VMEM((2, HEAD, length), bf16),
            pltpu.VMEM((2, HEAD, length), bf16),
            pltpu.VMEM((2, HEAD + 16, length), bf16),
        ],
        compiler_params=pltpu.CompilerParams(vmem_limit_bytes=vmem_bytes),
        cost_estimate=pl.CostEstimate(
            flops=2 * count * 8 * length * length * 256,
            bytes_accessed=24 * length * count * pair + 4 * count * length * length,
            transcendentals=0,
        ),
        name="attention_backward",
    )
    outs = call(joined, dattended, terms, exact, inverse_sum, q_gain, k_gain, x_low, core, *into, *fold, *fold)
    return outs


def gelu_pair(u):
    z = jnp.abs(u) * 0.7071067811865476
    t = 1.0 / (1.0 + 0.3275911 * z)
    e = jnp.exp(-z * z)
    poly = t * (0.127414796 + t * (-0.142248368 + t * (0.7107068705 + t * (-0.7265760135 + t * 0.5307027145))))
    half = poly * e
    phi = jnp.where(u >= 0, 1.0 - half, half)
    return (u * phi, phi + u * (0.3989422804014327 * e))


def mlp_kernel(
    x_ref, gy_ref, wu_ref, wd_ref, core_ref,
    res_ref, gn_ref, keep_up, send_up, keep_down, send_down, act_ref, dup_ref,
):
    @pl.when(pl.program_id(0) == 0)
    def _():
        res_ref[...] = jnp.zeros_like(res_ref)
        gn_ref[...] = jnp.zeros_like(gn_ref)

    for begin in range(0, wu_ref.shape[0], tile_rows):
        units = slice(begin, begin + tile_rows)
        upward = contract(x_ref[...], wu_ref[units], 1, 1).astype(bf16).astype(f32)
        grad_hidden = contract(gy_ref[...], wd_ref[units], 1, 1)
        active, slope = gelu_pair(upward)
        act_ref[:, units] = active.astype(bf16)
        dup_ref[:, units] = (grad_hidden * slope).astype(bf16)
    active, dupward = act_ref[...], dup_ref[...]
    res_ref[...] += nn(active, wd_ref[...])
    gn_ref[...] += nn(dupward, wu_ref[...])
    halves(contract(active, gy_ref[...], 0, 0).astype(bf16), core_ref, keep_down, send_down)
    halves(contract(dupward, x_ref[...], 0, 0).astype(bf16), core_ref, keep_up, send_up)


def mlp(x_low, grad_y, w_in_all, w_out_all, core):
    length = x_low.shape[0]
    hidden = w_in_all.shape[0] - QKV
    tile = D
    whole = pl.BlockSpec((length, D), lambda t: (0, 0))
    total = jax.ShapeDtypeStruct((length, D), f32)
    grad = jax.ShapeDtypeStruct((hidden, D // 2), bf16)
    call = pl.pallas_call(
        mlp_kernel,
        grid=(hidden // tile,),
        in_specs=[
            whole,
            whole,
            pl.BlockSpec((tile, D), lambda t: (t + QKV // tile, 0)),
            pl.BlockSpec((tile, D), lambda t: (t + D // tile, 0)),
            core_spec,
        ],
        out_specs=[whole, whole] + [pl.BlockSpec((tile, D // 2), lambda t: (t, 0))] * 4,
        out_shape=[total, total] + [grad] * 4,
        scratch_shapes=[pltpu.VMEM((length, tile), bf16)] * 2,
        compiler_params=pltpu.CompilerParams(vmem_limit_bytes=vmem_bytes),
        cost_estimate=pl.CostEstimate(
            flops=18 * length * D * hidden,
            bytes_accessed=12 * length * D + 8 * hidden * D,
            transcendentals=length * hidden,
        ),
        name="mlp",
    )
    return call(x_low, grad_y, w_in_all, w_out_all, core)


def input_kernel(*refs, calls):
    grads = refs[:calls]
    w_ref, normed_ref, tokens_ref, gy_ref, gain_ref, out_ref, ln_ref, total = refs[calls:]
    step = pl.program_id(0)

    @pl.when(step == 0)
    def _():
        total[...] = normed_ref[...]

    begin = 0
    sums = []
    for ref in grads:
        sums.append(nn(ref[0], w_ref[begin : begin + ref.shape[2], :]))
        begin += ref.shape[2]
    total[...] += sum(sums)

    @pl.when(step == pl.num_programs(0) - 1)
    def _():
        x_hat, x_inverse = normalize(tokens_ref[...].astype(f32))
        grad_normed = total[...]
        ln_ref[...] = jnp.sum(grad_normed * x_hat, axis=0, keepdims=True)
        back = norm_backward(grad_normed * gain_ref[...], x_hat, x_inverse)
        out_ref[...] = (gy_ref[...].astype(f32) + back).astype(bf16)


def input_gradient(grads, w_in_all, normed, tokens, grad_y, gain):
    length = tokens.shape[0]
    whole = pl.BlockSpec((length, D), lambda p: (0, 0))
    row = pl.BlockSpec((1, D), lambda p: (0, 0))
    call = pl.pallas_call(
        partial(input_kernel, calls=len(grads)),
        grid=(3,),
        in_specs=[pl.BlockSpec((1, length, grad.shape[2]), lambda p: (p, 0, 0)) for grad in grads]
        + [pl.BlockSpec((D, D), lambda p: (p, 0)), whole, whole, whole, row],
        out_specs=[whole, row],
        out_shape=[jax.ShapeDtypeStruct((length, D), bf16), jax.ShapeDtypeStruct((1, D), f32)],
        scratch_shapes=[pltpu.VMEM((length, D), f32)],
        compiler_params=pltpu.CompilerParams(vmem_limit_bytes=vmem_bytes),
        cost_estimate=pl.CostEstimate(
            flops=2 * length * D * QKV, bytes_accessed=20 * length * D, transcendentals=length
        ),
        name="input_gradient",
    )
    out, ln_grad = call(*grads, w_in_all, normed, tokens, grad_y, gain.reshape(1, D))
    return (out, ln_grad[0])


def split(values):
    high = values.astype(bf16)
    return (high, (values - high.astype(f32)).astype(bf16))


def newton_kernel(
    near_ref, other_ref, own_ref, far_ref, core_ref, o_ref, gh, gl, sh, sl, ph, pw, g32, x32
):
    count = D // tile_rows

    def span(i):
        return slice(i * tile_rows, (i + 1) * tile_rows)

    def store(high_ref, low_ref, i, j, value):
        high_ref[span(i), span(j)], low_ref[span(i), span(j)] = split(value)
        if i != j:
            high_ref[span(j), span(i)], low_ref[span(j), span(i)] = split(value.T)

    def symmetric(ah, al, bh, bl, post):
        for i in range(count):
            for j in range(i, count):
                rows, columns = span(i), span(j)
                post(
                    i,
                    j,
                    nn(ah[rows, :], bh[:, columns])
                    + (nn(ah[rows, :], bl[:, columns]) + nn(al[rows, :], bh[:, columns])),
                )

    def squared(ah, al, post):
        for i in range(count):
            for j in range(i, count):
                rows, columns = span(i), span(j)
                mixed = nn(ah[rows, :], al[:, columns])
                other = mixed if i == j else nn(ah[columns, :], al[:, rows])
                post(i, j, nn(ah[rows, :], ah[:, columns]) + (mixed + other.T))

    def sweep(last):
        def keep_factor(i, j, value):
            value = ns_cubic * g32[span(i), span(j)] + ns_quintic * value
            if i == j:
                shape = (tile_rows, tile_rows)
                diagonal = lax.broadcasted_iota(jnp.int32, shape, 0) == lax.broadcasted_iota(jnp.int32, shape, 1)
                value = value + jnp.where(diagonal, ns_linear, 0.0)
            store(ph, pw, i, j, value)

        def keep_gram(i, j, value):
            g32[span(i), span(j)] = value
            store(gh, gl, i, j, value)

        squared(gh, gl, keep_factor)
        xh, xl = split(x32[...])
        x32[...] = nn(xh, ph[...]) + (nn(xh, pw[...]) + nn(xl, ph[...]))
        if not last:
            symmetric(gh, gl, ph, pw, partial(store, sh, sl))
            symmetric(sh, sl, ph, pw, keep_gram)

    half = D // 2
    first_core = core_ref[0] == 0
    left = jnp.where(first_core, near_ref[...], other_ref[...])
    side = jnp.where(first_core, other_ref[:half], near_ref[:half])
    corner = left[:half]
    i = lax.broadcasted_iota(jnp.int32, (half, half), 0)
    j = lax.broadcasted_iota(jnp.int32, (half, half), 1)
    corner_t = corner.T
    first = jnp.where(i <= j, corner, corner_t)
    last = jnp.where(i > j, corner, jnp.where(i == j, left[half : half + 1], corner_t))
    trace = jnp.sum(jnp.where(i == j, first + last, 0.0), axis=0, keepdims=True)
    trace = jnp.sum(trace, axis=1, keepdims=True)
    inverse = 1.0 / (jnp.sqrt(trace) + 1e-07)
    square = inverse * inverse
    g32[:half, :half] = first * square
    g32[half:, half:] = last * square
    g32[:half, half:] = side * square
    g32[half:, :half] = side.T * square
    rows = own_ref.shape[0]
    x32[:rows] = own_ref[...] * inverse
    x32[rows:] = far_ref[...] * inverse
    gh[...], gl[...] = split(g32[...])

    @pl.loop(0, 4)
    def _(k):
        sweep(False)

    sweep(True)
    o_ref[...] = x32[...].astype(bf16)


def newton(folded, far_folded, own_rows, far_rows, core):
    rows = own_rows.shape[0] + far_rows.shape[0]
    whole = pl.BlockSpec(memory_space=pltpu.VMEM)
    call = pl.pallas_call(
        newton_kernel,
        in_specs=[whole] * 4 + [core_spec],
        out_specs=whole,
        out_shape=jax.ShapeDtypeStruct((rows, D), bf16),
        scratch_shapes=[pltpu.VMEM((D, D), bf16)] * 6 + [pltpu.VMEM((D, D), f32), pltpu.VMEM((rows, D), f32)],
        compiler_params=pltpu.CompilerParams(vmem_limit_bytes=vmem_bytes),
        cost_estimate=pl.CostEstimate(
            flops=30 * D * D * (2 * D + rows), bytes_accessed=4 * D * D + 6 * rows * D, transcendentals=0
        ),
        name="newton",
    )
    return call(folded, far_folded, own_rows, far_rows, core)


def update_kernel(in_ref, in_far_ref, out_ref, out_far_ref, wi_ref, wo_ref, place_ref, in_new, out_new, held, *, first):
    def new(weights, ortho, size):
        rate = muon_rate * (size / D) ** 0.5
        return weights.astype(f32) * (1 - muon_rate * muon_decay) - rate * ortho.astype(f32)

    first_core = place_ref[0] == 0
    for near_ref, far_ref, total in ((in_ref, in_far_ref, None), (out_ref, out_far_ref, out_new)):
        size = far_ref.shape[0] // 2
        all_near, all_far, weights = near_ref[...].astype(f32), far_ref[...].astype(f32), wo_ref[...].astype(f32)
        for chip in range(2):
            rows = slice(chip * size, (chip + 1) * size)
            near, far = all_near[rows], all_far[rows]
            begin = 2 * chip * size
            both = (jnp.where(first_core, near, far), jnp.where(first_core, far, near))
            for i in range(2):
                spot = slice(begin + i * size, begin + (i + 1) * size)
                if total is None:
                    held[spot] = both[i]
                else:
                    total[spot] = new(weights[spot], both[i], FOUT)
    rows = in_new.shape[0]
    if first == rows:
        in_new[...] = new(wi_ref[...], held[...], FIN)
        return
    start = pl.multiple_of(place_ref[1], 32)
    cut, rest = first // 2, (rows - first) // 2
    pieces = jnp.concatenate([held[cut : cut + rest], held[rows // 2 + cut :]], axis=0)
    in_new[: rows - first] = new(wi_ref[: rows - first], pieces, FIN)
    in_new[first:] = jnp.where(
        lax.broadcasted_iota(jnp.int32, (rows - first, 1), 0) < start, in_new[first:], new(wi_ref[first:], pieces, FIN)
    )
    spot = pl.ds(start, first)
    pieces = jnp.concatenate([held[:cut], held[rows // 2 : rows // 2 + cut]], axis=0)
    in_new[spot] = new(wi_ref[spot], pieces, FIN)


def update(ortho_in, far_in, ortho_out, far_out, w_in, w_out, place, first):
    whole = pl.BlockSpec(memory_space=pltpu.VMEM)
    call = pl.pallas_call(
        partial(update_kernel, first=first),
        in_specs=[whole] * 6 + [core_spec],
        out_specs=[whole] * 2,
        out_shape=[jax.ShapeDtypeStruct(w.shape, f32) for w in (w_in, w_out)],
        scratch_shapes=[pltpu.VMEM(w_in.shape, f32)],
        compiler_params=pltpu.CompilerParams(vmem_limit_bytes=vmem_bytes),
        cost_estimate=pl.CostEstimate(flops=4 * w_in.size, bytes_accessed=14 * w_in.size, transcendentals=0),
        name="update",
    )
    return call(ortho_in, far_in, ortho_out, far_out, w_in, w_out, place)


def gram_kernel(m_ref, extra_ref, core_ref, o_ref):
    half = D // 2
    left, right = slice(0, half), slice(half, D)

    def product(a, b):
        ah, al = split(m_ref[:, a])
        bh, bl = split(m_ref[:, b])
        return contract(ah, bh, 0, 0) + (contract(ah, bl, 0, 0) + contract(al, bh, 0, 0))

    o_ref[half:, :] = extra_ref[...]

    @pl.when(core_ref[0] == 0)
    def _():
        i = lax.broadcasted_iota(jnp.int32, (half, half), 0)
        j = lax.broadcasted_iota(jnp.int32, (half, half), 1)
        last = product(right, right)
        o_ref[:half, :] = jnp.where(i <= j, product(left, left), last)
        o_ref[half : half + 1, :] = jnp.sum(jnp.where(i == j, last, 0.0), axis=0, keepdims=True)

    @pl.when(core_ref[0] != 0)
    def _():
        o_ref[:half, :] = product(left, right)


def folded_gram(rows, extra, core):
    rows = jnp.pad(rows, ((0, -rows.shape[0] % 16), (0, 0)))
    whole = pl.BlockSpec(memory_space=pltpu.VMEM)
    call = pl.pallas_call(
        gram_kernel,
        in_specs=[whole, whole, core_spec],
        out_specs=whole,
        out_shape=jax.ShapeDtypeStruct((D // 2 + extra_rows, D // 2), f32),
        compiler_params=pltpu.CompilerParams(vmem_limit_bytes=vmem_bytes),
        cost_estimate=pl.CostEstimate(
            flops=4 * rows.shape[0] * D * D, bytes_accessed=8 * rows.shape[0] * D, transcendentals=0
        ),
        name="gram",
    )
    return call(rows, extra, core)


def bits(size):
    return [1 << b for b in range(size.bit_length() - 1)]


def take(values, index, axis):
    return lax.dynamic_index_in_dim(values, index, axis, keepdims=False)


def after(value, *others):
    return lax.optimization_barrier((value, *others))[0]


def exchange(values, axis, bit, fill=()):
    size = lax.axis_size(axis)
    return after(lax.ppermute(values, axis, [(i, i ^ bit) for i in range(size)]), *fill)


def sum_steps(values, halving, full):
    fill = yield values
    for axis, bit in halving:
        side = (lax.axis_index(axis) // bit) % 2
        pieces = values.reshape(2, values.shape[0] // 2, values.shape[1])
        values = take(pieces, side, 0) + exchange(take(pieces, 1 - side, 0), axis, bit, fill)
        fill = yield values
    for axis, bit in full:
        values = values + exchange(values, axis, bit, fill)
        fill = yield values


def halve(parts, axis, name, bit):
    side = (lax.axis_index(name) // bit) % 2
    sent = [take(part, 1 - side, axis) for part in parts]

    def receive(*fill):
        kept = jnp.concatenate([take(part, side, axis) for part in parts], axis=0)
        return (kept, exchange(jnp.concatenate(sent, axis=0), name, bit, fill))

    return sent, receive


def added(kept, other):
    return (kept.astype(f32) + other.astype(f32)).astype(bf16)


def scatter_one(*parts):
    wide = lax.axis_size("wide")
    columns = parts[0].shape[-1]
    rows = sum(part.size for part in parts) // (2 * wide * columns)
    cut = rows // 16 * 8
    parts = [part.reshape(-1, 2, 2, rows, columns) for part in parts]
    sent_a, receive_a = halve([part[:, :, :, :cut] for part in parts], 1, "wide", 1)
    sent_b, receive_b = halve([part[:, :, :, cut:] for part in parts], 2, "nar", 2)
    return sent_a + sent_b, lambda *fill: (added(*receive_a(*fill)), added(*receive_b(*fill)))


def split_kernel(*refs, pairs, rows):
    *parts, place_ref, sent_y, kept_y, sent_x, kept_x, held = refs
    begin = 0
    for paired in pairs:
        values = parts.pop(0)[...].astype(f32)
        if paired:
            values = values + parts.pop(0)[...].astype(f32)
        held[begin : begin + values.shape[0]] = values
        begin += values.shape[0]
    cut = kept_y.shape[2]
    for z in range(kept_y.shape[0]):
        for j in range(2):
            for near, out_y, out_x in ((True, kept_y, kept_x), (False, sent_y, sent_x)):
                y = place_ref[0] if near else 1 - place_ref[0]
                x = place_ref[1] if near else 1 - place_ref[1]
                first = pl.ds(pl.multiple_of(((2 * z + y) * 2 + j) * rows, 8), cut)
                out_y[z, j] = held[first].astype(bf16)
                second = pl.ds(pl.multiple_of(((2 * z + j) * 2 + x) * rows + cut, 8), rows - cut)
                out_x[z, j] = held[second].astype(bf16)


def split_one(rows, *parts):
    half = D // 2
    cut = rows // 16 * 8
    far = lax.axis_size("wide") // 2
    place = jnp.stack([lax.axis_index("wide") % 2, lax.axis_index("nar") // 2])
    terms = [term.reshape(-1, half) for part in parts for term in (part if isinstance(part, tuple) else (part,))]
    whole = pl.BlockSpec(memory_space=pltpu.VMEM)
    shapes = [(far, 2, cut, half)] * 2 + [(far, 2, rows - cut, half)] * 2
    call = pl.pallas_call(
        partial(split_kernel, pairs=[isinstance(part, tuple) for part in parts], rows=rows),
        in_specs=[whole] * len(terms) + [core_spec],
        out_specs=[whole] * 4,
        out_shape=[jax.ShapeDtypeStruct(shape, bf16) for shape in shapes],
        scratch_shapes=[pltpu.VMEM((4 * far * rows, half), f32)],
        compiler_params=pltpu.CompilerParams(vmem_limit_bytes=vmem_bytes),
        cost_estimate=pl.CostEstimate(
            flops=8 * far * rows * half, bytes_accessed=24 * far * rows * half, transcendentals=0
        ),
        name="split",
    )
    sent_y, kept_y, sent_x, kept_x = call(*terms, place)

    def arrive(*fill):
        return (exchange(sent_y, "wide", 1, fill), exchange(sent_x, "nar", 2, fill))

    return [sent_y, sent_x], arrive, lambda other_y, other_x: (added(kept_y, other_y), added(kept_x, other_x))


def scatter_two(held):
    sent_a, receive_a = halve(held[:1], 1, "nar", 2)
    sent_b, receive_b = halve(held[1:], 1, "wide", 1)

    def receive(*fill):
        kept, other = zip(receive_a(*fill), receive_b(*fill), strict=True)
        return added(jnp.concatenate(kept, axis=1), jnp.concatenate(other, axis=1))

    return sent_a + sent_b, receive


def scatter_rest(held):
    wide = lax.axis_size("wide")
    far = wide // 2
    place = lax.axis_index("wide") // 2
    sent = [take(held, place ^ shift, 0) for shift in range(1, far)]

    def receive(*fill):
        total = take(held, place, 0).astype(f32)
        for shift in reversed(range(1, far)):
            pairs = [(i, i ^ (2 * shift)) for i in range(wide)]
            total = total + after(lax.ppermute(sent[shift - 1], "wide", pairs), *fill).astype(f32)
        return total.astype(bf16)

    return sent, receive


def both_cores(values, *fill):
    other = exchange(values, "nar", 1, fill)
    return join(values, other, lax.axis_index("nar") % 2, 1).reshape(values.shape[0], D)


def ordered(values, other, side):
    return (jnp.where(side == 0, values, other), jnp.where(side == 0, other, values))


def join(values, other, side, axis):
    return jnp.stack(ordered(values, other, side), axis)


def gather(values):
    wide = lax.axis_size("wide")
    rows = values.shape[0]
    far = wide // 2
    place, side = lax.axis_index("wide") // 2, lax.axis_index("wide") % 2
    chip, core = lax.axis_index("nar") // 2, lax.axis_index("nar") % 2
    held = lax.dynamic_update_index_in_dim(jnp.zeros((far, rows, D), values.dtype), values, place, 0)
    for shift in range(1, far):
        pairs = [(i, i ^ (2 * shift)) for i in range(wide)]
        held = lax.dynamic_update_index_in_dim(held, lax.ppermute(values, "wide", pairs), place ^ shift, 0)
    cut = rows // 32 * 16
    first, second = held[:, :cut], held[:, cut:]
    first = join(first, exchange(first, "wide", 1), side, 1)
    second = join(second, exchange(second, "nar", 2), chip, 1)
    first = join(first, exchange(first, "nar", 2), chip, 2)
    second = join(second, exchange(second, "wide", 1), side, 1)
    held = jnp.concatenate([first, second], axis=3)
    return join(held, exchange(held, "nar", 1), core, 3).reshape(-1, D)


def on_device(tokens, cotangent, image_ids, w_in, w_out, gains, mom_in, mom_out, gain_m, gain_v):
    row_count = tokens.shape[0]
    rows_in = w_in.shape[0]
    rows_out = w_out.shape[0]
    nar_count = lax.axis_size("nar")
    wide_count = lax.axis_size("wide")
    nar_place = lax.axis_index("nar")
    share_in = rows_in // nar_count
    share_out = rows_out // nar_count
    everyone = ("wide", "nar")

    def share(rows, size):
        return lax.dynamic_slice_in_dim(rows, nar_place * size, size, 0)

    w_in_all = lax.all_gather(share(w_in, share_in), everyone, axis=0, tiled=True)
    w_out_all = gather(share(w_out, share_out))

    x_float = tokens.astype(f32)
    ln_gain = gains[:D]
    x_hat, x_inverse = normalize(x_float)
    x_low = (x_hat * ln_gain).astype(bf16)
    live = (image_ids.reshape(row_count) >= 0)[:, None]
    grad_y = jnp.where(live, cotangent, jnp.zeros_like(cotangent))

    core = (nar_place % 2).reshape(1)
    chip = nar_place // 2
    half = D // 2
    pairs = D // pair
    q_gain, k_gain = (
        jnp.broadcast_to(gain[:, None], (HEAD, 128)) for gain in (gains[D : D + HEAD], gains[D + HEAD :])
    )
    onek, penq = image_columns(image_ids.reshape(row_count))
    x_low = after(x_low, q_gain, k_gain, onek, penq)
    first = rows_in * 4 // 7
    second = rows_in - first
    parted = wide_count == 8 and first == half and rows_in == 672
    mlp_result, mlp_normed, keep_up, send_up, keep_down, send_down = mlp(x_low, grad_y, w_in_all, w_out_all, core)
    joined, dattended, attended, terms, exact, inverse_sum, keep_att, send_att = attention_forward(
        after(x_low, keep_down), grad_y, w_in_all, w_out_all, onek, penq, q_gain, k_gain, core
    )

    def backward(begin, count, earlier=(), **buffers):
        return attention_backward(
            joined, dattended, terms, exact, inverse_sum, q_gain, k_gain, after(x_low, *earlier), core, begin, count,
            **buffers,
        )

    def cores(keep, send, *fill):
        return added(keep, exchange(send, "nar", 1, fill)).reshape(-1, half)

    start = 96 * jnp.minimum(lax.axis_index("wide"), 3)
    row = lax.broadcasted_iota(jnp.int32, (rows_in, 1), 0)
    half_mom_out = lax.dynamic_slice_in_dim(mom_out, chip * (rows_out // 2), rows_out // 2, 0)
    wide_bits = bits(wide_count)
    halving = [("wide", wide_bits[0]), ("nar", 2)]
    full = [("wide", bit) for bit in wide_bits[1:]]

    def begin_out(part):
        zeros = jnp.zeros((extra_rows, half), f32)
        steps = sum_steps(folded_gram(muon_beta * half_mom_out + part.astype(f32), zeros, core), halving, full)
        return (steps, next(steps))

    if parted:
        def pair_of(keep, send, *fill):
            return (keep, exchange(send, "nar", 1, fill))

        down = pair_of(keep_down, send_down, keep_att)
        up = pair_of(keep_up, send_up, keep_att)
        sent, arrive, combine = split_one(rows_out // 2, pair_of(keep_att, send_att), down)
        dqkv_a, keep_a, send_a, q_grad_a, k_grad_a, up_a = backward(0, 3, sent, room=3, fold=up, size=first)
        sent, receive = scatter_two(combine(*arrive(keep_a)))
        dqkv_b, keep_b, send_b, q_grad_b, k_grad_b = backward(3, 1, [keep_a, *sent], room=3)
        sent_o, receive_o = scatter_rest(receive(dqkv_b))
        sent_a, arrive_a, combine_a = split_one(first // 2, pair_of(keep_a, send_a, dqkv_b), up_a)
        dqkv_c, keep_b, send_b, q_grad_c, k_grad_c, up_b = backward(
            4, 2, [*sent_a, *sent_o], room=3, place=1, into=(keep_b, send_b), fold=up, origin=first, size=second
        )
        part_out = receive_o(dqkv_c)
        sent_a, receive_a = scatter_two(combine_a(*arrive_a(dqkv_c)))
        sent_b, arrive_b, combine_b = split_one(second // 2, pair_of(keep_b, send_b, part_out, *sent_a), up_b)
        part_out = both_cores(part_out, *sent_b)
        steps_out, folded_out = begin_out(after(part_out, *sent_b))
        mom_in_late = after(mom_in, folded_out)
        held_b = combine_b(*arrive_b(folded_out))
        sent_b, receive_b = scatter_two(held_b)
        folded_out = steps_out.send(sent_b)
        held_a = receive_a(*sent_b)
        held_b = receive_b(held_a, folded_out)
        sent, receive = scatter_rest(jnp.concatenate([held_a, held_b], axis=1))
        grad_tokens, ln_grad = input_gradient(
            [dqkv_a, dqkv_b, dqkv_c], w_in_all, after(mlp_normed, *sent), tokens, grad_y, ln_gain
        )
        far_out = exchange(after(part_out, *sent), "nar", 2, (grad_tokens,))
        folded_out = steps_out.send((grad_tokens,))
        part_in = receive(grad_tokens, far_out, folded_out)
        steps_done = 2
        q_gain_grad = (q_grad_a + q_grad_b + after(q_grad_c, grad_tokens))[:, 0]
        k_gain_grad = (k_grad_a + k_grad_b + after(k_grad_c, grad_tokens))[:, 0]

        def halved(rows, chip):
            inside = lax.dynamic_slice_in_dim(rows, start, first, 0)
            others = jnp.where(row[:second] < start, rows[:second], rows[first:])
            return jnp.concatenate(
                [
                    lax.dynamic_slice_in_dim(inside, chip * (first // 2), first // 2, 0),
                    lax.dynamic_slice_in_dim(others, chip * (second // 2), second // 2, 0),
                ],
                axis=0,
            )

        def rejoined(near, far):
            cut = first // 2
            a, b = jnp.concatenate([near[:cut], far[:cut]], 0), jnp.concatenate([near[cut:], far[cut:]], 0)
            a = lax.dynamic_update_slice_in_dim(jnp.zeros((rows_in, D), a.dtype), a, start, 0)
            empty = jnp.zeros((first, D), b.dtype)
            below = jnp.concatenate([b, empty], axis=0)
            above = jnp.concatenate([empty, b], axis=0)
            inside = (row >= start) & (row < start + first)
            return jnp.where(inside, a, jnp.where(row < start, below, above))

    else:
        dqkv, keep_a, send_a, q_gain_grad, k_gain_grad = backward(0, pairs, room=pairs)
        q_gain_grad, k_gain_grad = q_gain_grad[:, 0], k_gain_grad[:, 0]
        grad_tokens, ln_grad = input_gradient([dqkv], w_in_all, mlp_normed, tokens, grad_y, ln_gain)

        def scattered(*parts):
            held = scatter_one(jnp.concatenate(parts, axis=0))[1]()
            return scatter_rest(scatter_two(held)[1]())[1]()

        part_out = both_cores(scattered(cores(keep_att, send_att), cores(keep_down, send_down)))
        steps_out, folded_out = begin_out(part_out)
        mom_in_late = mom_in
        steps_done = 0
        far_out = exchange(part_out, "nar", 2)
        part_in = scattered(cores(keep_a, send_a), cores(keep_up, send_up))

        def halved(rows, chip):
            return lax.dynamic_slice_in_dim(rows, chip * (rows_in // 2), rows_in // 2, 0)

        def rejoined(near, far):
            return jnp.concatenate([near, far], axis=0)

    part_in = both_cores(part_in)
    gain_terms = jnp.concatenate([ln_grad, q_gain_grad, k_gain_grad])
    count = gain_terms.shape[0]
    extra = jnp.pad(gain_terms, (half, (extra_rows - 1) * half - count)).reshape(extra_rows, half)
    momenta_in = muon_beta * halved(mom_in_late, chip) + part_in.astype(f32)
    steps_in = sum_steps(folded_gram(momenta_in, extra, core), halving, full)
    folded_in = next(steps_in)

    half_in, half_out = rows_in // 4, rows_out // 4

    def mine(rows, size):
        return lax.dynamic_slice_in_dim(rows, core[0] * size, size, 0)

    def fitted(rows):
        return jnp.pad(rows, ((0, half_in - half_out), (0, 0)))

    far_in = exchange(part_in, "nar", 2)
    own_rows = jnp.where(
        chip == 0,
        mine(momenta_in, half_in),
        fitted(mine(muon_beta * half_mom_out + part_out.astype(f32), half_out)),
    )
    far_mom = jnp.where(
        chip == 0,
        mine(halved(mom_in_late, 1 - chip), half_in),
        fitted(mine(lax.dynamic_slice_in_dim(mom_out, (1 - chip) * (rows_out // 2), rows_out // 2, 0), half_out)),
    )
    far_rows = jnp.where(chip == 0, mine(far_in, half_in), fitted(mine(far_out, half_out)))
    far_rows = muon_beta * far_mom + far_rows.astype(f32)
    steps = len(halving) + len(full)
    folded_out = steps_out.send((folded_in,))
    steps_done += 1
    for step in range(steps):
        fill = {0: (far_in, folded_out), len(halving): (own_rows, far_rows)}.get(step, ())
        folded_in = steps_in.send(fill)
        if steps_done < steps:
            folded_out = steps_out.send((folded_in,))
            steps_done += 1
    own, far = ordered(folded_in, folded_out, chip)
    folded = join(own, exchange(far, "nar", 2), chip, 0).reshape(-1, half)
    branch = mlp_result + nn(after(attended, folded), w_out_all[:D])
    result = (tokens.astype(f32) + branch).astype(bf16)
    side = lax.axis_index("wide") % 2
    folded = join(folded, exchange(folded, "wide", 1, (result,)), side, 0).reshape(-1, half)
    far_folded = exchange(folded, "nar", 1)
    ortho = newton(folded, far_folded, own_rows, far_rows, core)
    extra = folded[half : half + 8] + far_folded[half : half + 8]
    extra = ordered(extra, exchange(after(extra, ortho), "nar", 2), chip)[0].reshape(8 * half)
    grad_gains = extra[half : half + count]
    far_out, far_in = after(far_out, ortho), after(far_in, ortho)
    grad_w_out = join(part_out, far_out, chip, 0).reshape(rows_out, D).astype(f32)
    mom_out_new = muon_beta * mom_out + grad_w_out
    grad_w_in = after(rejoined(*ordered(part_in, far_in, chip))).astype(f32)
    mom_in_new = muon_beta * mom_in + grad_w_in

    other = exchange(ortho, "nar", 2, (mom_in_new, mom_out_new, grad_gains))
    ortho_in, ortho_out = ordered(ortho, other, chip)
    ortho_out = jnp.concatenate([ortho_out[half_in : half_in + half_out], ortho_out[:half_out]], axis=0)
    far_in, far_out = (exchange(rows, "nar", 1) for rows in (ortho_in, ortho_out))
    w_in_new, w_out_new = update(
        ortho_in, far_in, ortho_out, far_out, w_in, w_out, jnp.stack([core[0], start]), first if parted else rows_in
    )
    gain_m_new = adam_first * gain_m + (1 - adam_first) * grad_gains
    gain_v_new = adam_second * gain_v + (1 - adam_second) * grad_gains * grad_gains
    gains_new = gains - adam_rate * (gain_m_new / (1 - adam_first**STEP)) / (
        jnp.sqrt(gain_v_new / (1 - adam_second**STEP)) + adam_eps
    )
    return (
        result,
        grad_tokens,
        grad_w_in,
        grad_w_out,
        grad_gains,
        mom_in_new,
        mom_out_new,
        gain_m_new,
        gain_v_new,
        w_in_new,
        w_out_new,
        gains_new,
    )


def solution(mesh):
    rows = P(("nar", "wide"), None)
    wide = P("wide", None)
    return jax.shard_map(
        on_device,
        mesh=mesh,
        in_specs=(rows, rows, rows, wide, wide, P(), wide, wide, P(), P()),
        out_specs=(rows, rows, wide, wide, P(), wide, wide, P(), P(), wide, wide, P()),
        check_vma=False,
    )
```

```python
from functools import partial

import jax
import jax.numpy as jnp
from jax import lax
from jax.experimental import pallas as pl
from jax.experimental.pallas import tpu as pltpu
from jax.sharding import PartitionSpec as P

D = 768
HEADS = 12
HEAD = 64
LEN = 1024
STEP = 10
FIN = 5376
FOUT = 3840
QKV = 3 * D

f32 = jnp.float32
bf16 = jnp.bfloat16
ns_linear = 3.4445
ns_cubic = -4.775
ns_quintic = 2.0315
muon_beta = 0.5
muon_rate = 0.8
muon_decay = 0.1
adam_rate = 0.8
adam_first = 0.9
adam_second = 0.95
adam_eps = 1e-08
norm_eps = 1e-06
penalty = 16384.0
vmem_bytes = 60 * 1024 * 1024
tile_rows = 256
extra_rows = 32
pair = 2 * HEAD


def normalize(values):
    center = values - jnp.mean(values, axis=-1, keepdims=True)
    variance = jnp.mean(center * center, axis=-1, keepdims=True)
    inverse = lax.rsqrt(variance + norm_eps)
    return (center * inverse, inverse)


def norm_backward(grad_scaled, normed, inverse, axis=-1):
    mean_grad = jnp.mean(grad_scaled, axis=axis, keepdims=True)
    mean_cross = jnp.mean(grad_scaled * normed, axis=axis, keepdims=True)
    return inverse * (grad_scaled - mean_grad - normed * mean_cross)


def nn(a, b):
    return jnp.dot(a, b, preferred_element_type=f32)


def contract(a, b, dim_a, dim_b):
    return lax.dot_general(a, b, (((dim_a,), (dim_b,)), ((), ())), preferred_element_type=f32)


def normalize_columns(columns):
    center = columns - jnp.mean(columns, axis=0, keepdims=True)
    variance = jnp.mean(center * center, axis=0, keepdims=True)
    inverse = lax.rsqrt(variance + norm_eps)
    return (center * inverse, inverse)


core_spec = pl.BlockSpec(memory_space=pltpu.SMEM)


def halves(values, core_ref, keep_ref, send_ref):
    half = D // 2
    left, right = values[:, :half], values[:, half:]
    first = core_ref[0] == 0
    keep_ref[...] = jnp.where(first, left, right).reshape(keep_ref.shape)
    send_ref[...] = jnp.where(first, right, left).reshape(send_ref.shape)


def forward_kernel(
    x_ref, gy_ref, wq_ref, wk_ref, wv_ref, wa_ref, onek_ref, penq_ref, gq_ref, gk_ref, core_ref,
    joined_ref, do_ref, att_ref, terms_ref, exact_ref, sum_ref, keep_ref, send_ref, kaug, qaug_t, vaug_t,
):
    length = x_ref.shape[0]
    weights = jnp.concatenate([wq_ref[...], wk_ref[...], wv_ref[...]], axis=0)
    joined = contract(weights, x_ref[...], 1, 1).astype(bf16)
    for i in range(3):
        joined_ref[i] = joined[i * pair : (i + 1) * pair]
    do_ref[...] = contract(wa_ref[...], gy_ref[...], 1, 1).astype(bf16)
    parts = []
    for h in range(2):
        rows = slice(HEAD * h, HEAD * (h + 1))
        q_hat, _ = normalize_columns(joined_ref[0, rows, :].astype(f32))
        k_hat, _ = normalize_columns(joined_ref[1, rows, :].astype(f32))
        q_low = (q_hat * gq_ref[:, :1]).astype(bf16)
        k_low = (k_hat * gk_ref[:, :1]).astype(bf16)
        kaug[h, :, :HEAD] = k_low.T
        kaug[h, :, HEAD:] = onek_ref[...]
        qaug_t[h, :HEAD, :] = (q_low.astype(f32) * HEAD ** (-0.5)).astype(bf16)
        qaug_t[h, HEAD:, :] = penq_ref[...]
        vaug_t[h, :HEAD, :] = joined_ref[2, rows, :]
        vaug_t[h, HEAD:, :] = jnp.ones((16, length), bf16)
        terms_ref[h] = jnp.exp(nn(kaug[h], qaug_t[h])).astype(bf16)
        summed = nn(vaug_t[h], terms_ref[h])
        inverse_sum = 1.0 / summed[HEAD : HEAD + 1]
        sum_ref[0, h : h + 1, :] = inverse_sum
        attended = summed[:HEAD] * inverse_sum
        exact_ref[rows, :] = attended
        parts.append(attended)
    attended = jnp.concatenate(parts, 0).astype(bf16)
    halves(nn(attended, gy_ref[...]).astype(bf16), core_ref, keep_ref, send_ref)
    att_ref[...] = attended.T


def image_columns(ids):
    image = jnp.where(ids < 0, 4, ids)
    number = jnp.arange(16)
    onek = (image[:, None] == number[None, :]).astype(bf16)
    penq = jnp.where(image[None, :] == number[:, None], 0.0, -penalty).astype(bf16)
    return (onek, penq)


def attention_forward(x_low, grad_y, w_in_all, w_out_all, onek, penq, q_gain, k_gain, core):
    length = x_low.shape[0]
    pairs = D // pair

    def rows(part):
        return pl.BlockSpec((pair, D), lambda p: (part * pairs + p, 0))

    def whole(shape):
        return pl.BlockSpec(shape, lambda p: (0, 0))

    call = pl.pallas_call(
        forward_kernel,
        grid=(pairs,),
        in_specs=[
            whole((length, D)), whole((length, D)), rows(0), rows(1), rows(2), rows(0),
            whole((length, 16)), whole((16, length)), whole((HEAD, 128)), whole((HEAD, 128)), core_spec,
        ],
        out_specs=[
            pl.BlockSpec((3, pair, length), lambda p: (0, p, 0)),
            pl.BlockSpec((pair, length), lambda p: (p, 0)),
            pl.BlockSpec((length, pair), lambda p: (0, p)),
            pl.BlockSpec((2, length, length), lambda p: (p, 0, 0)),
            pl.BlockSpec((pair, length), lambda p: (p, 0)),
            pl.BlockSpec((1, 8, length), lambda p: (p, 0, 0)),
            *[pl.BlockSpec((pair, D // 2), lambda p: (p, 0))] * 2,
        ],
        out_shape=[
            jax.ShapeDtypeStruct((3, D, length), bf16),
            jax.ShapeDtypeStruct((D, length), bf16),
            jax.ShapeDtypeStruct((length, D), bf16),
            jax.ShapeDtypeStruct((HEADS, length, length), bf16),
            jax.ShapeDtypeStruct((D, length), f32),
            jax.ShapeDtypeStruct((pairs, 8, length), f32),
            *[jax.ShapeDtypeStruct((D, D // 2), bf16)] * 2,
        ],
        scratch_shapes=[
            pltpu.VMEM((2, length, HEAD + 16), bf16),
            pltpu.VMEM((2, HEAD + 16, length), bf16),
            pltpu.VMEM((2, HEAD + 16, length), bf16),
        ],
        compiler_params=pltpu.CompilerParams(vmem_limit_bytes=vmem_bytes),
        cost_estimate=pl.CostEstimate(
            flops=HEADS * 4 * length * length * 256,
            bytes_accessed=16 * length * D + 2 * HEADS * length * length,
            transcendentals=HEADS * length * length,
        ),
        name="attention_forward",
    )
    return call(
        x_low, grad_y, w_in_all, w_in_all, w_in_all, w_out_all, onek, penq,
        q_gain, k_gain, core,
    )


def backward_kernel(
    joined_ref, do_ref, terms_ref, exact_ref, sum_ref, gq_ref, gk_ref, x_ref, core_ref, *refs, folds,
):
    *refs, vaug, qlow_t, klow_t, doaug_t = refs
    if folds:
        *refs, folded_ref = refs
    *refs, grads_ref, keep_ref, send_ref, ggq_ref, ggk_ref = refs
    if folds:
        size = folded_ref.shape[0] // 2
        for i in range(2):
            near_ref, far_ref = refs[-4 + 2 * i], refs[-3 + 2 * i]
            folded_ref[i * size : (i + 1) * size, :] = added(near_ref[...], far_ref[...])
    length = x_ref.shape[0]
    step = pl.program_id(0)
    q_gain = gq_ref[:, :1]
    k_gain = gk_ref[:, :1]
    dq_parts, dk_parts, dv_parts = [], [], []
    q_gain_grad = jnp.zeros((HEAD, 1), f32)
    k_gain_grad = jnp.zeros((HEAD, 1), f32)
    kept = []
    for h in range(2):
        rows = slice(HEAD * h, HEAD * (h + 1))
        q_hat, q_inverse = normalize_columns(joined_ref[0, rows, :].astype(f32))
        k_hat, k_inverse = normalize_columns(joined_ref[1, rows, :].astype(f32))
        klow_t[h] = (k_hat * k_gain).astype(bf16)
        qlow_t[h] = (q_hat * q_gain).astype(bf16)
        vaug[h, :, :HEAD] = joined_ref[2, rows, :].T
        vaug[h, :, HEAD:] = jnp.ones((length, 16), bf16)
        inverse_sum = sum_ref[0, h : h + 1, :]
        do_head = do_ref[rows, :].astype(f32)
        inner = -jnp.sum(do_head * exact_ref[rows, :], axis=0, keepdims=True) * inverse_sum
        do_low = (do_head * inverse_sum).astype(bf16)
        inner_high = inner.astype(bf16).astype(f32)
        extra = lax.broadcasted_iota(jnp.int32, (16, length), 0)
        extra = jnp.where(extra == 0, inner_high, jnp.where(extra == 1, inner - inner_high, 0.0))
        doaug_t[h, :HEAD, :] = do_low
        doaug_t[h, HEAD:, :] = extra.astype(bf16)
        kept.append((q_hat, q_inverse, k_hat, k_inverse))
    sums = [[None] * 3 for _ in range(2)]
    for k in range(0, length, tile_rows):
        for h in range(2):
            span = slice(k, k + tile_rows)
            terms = terms_ref[h, span, :]
            dscores = (terms.astype(f32) * nn(vaug[h, span, :], doaug_t[h])).astype(bf16)
            dv = contract(doaug_t[h, :HEAD, :], terms, 1, 1)
            dk = contract(qlow_t[h], dscores, 1, 1)
            dq = nn(klow_t[h, :, span], dscores)
            sums[h][0] = dq if sums[h][0] is None else sums[h][0] + dq
            sums[h][1] = [dk] if sums[h][1] is None else sums[h][1] + [dk]
            sums[h][2] = [dv] if sums[h][2] is None else sums[h][2] + [dv]
    for h in range(2):
        q_hat, q_inverse, k_hat, k_inverse = kept[h]
        dquery = sums[h][0] * HEAD ** (-0.5)
        dkey = jnp.concatenate(sums[h][1], axis=1) * HEAD ** (-0.5)
        dvalue = jnp.concatenate(sums[h][2], axis=1)
        q_gain_grad += jnp.sum(dquery * q_hat, axis=1, keepdims=True)
        k_gain_grad += jnp.sum(dkey * k_hat, axis=1, keepdims=True)
        dq_parts.append(norm_backward(dquery * q_gain, q_hat, q_inverse, 0))
        dk_parts.append(norm_backward(dkey * k_gain, k_hat, k_inverse, 0))
        dv_parts.append(dvalue)
    grads = jnp.concatenate(dq_parts + dk_parts + dv_parts, 0).astype(bf16)
    halves(nn(grads, x_ref[...]).astype(bf16), core_ref, keep_ref, send_ref)
    grads_ref[0] = grads[:pair].T
    grads_ref[1] = grads[pair : 2 * pair].T
    grads_ref[2] = grads[2 * pair :].T

    @pl.when(step == 0)
    def _():
        ggq_ref[...] = jnp.zeros_like(ggq_ref)
        ggk_ref[...] = jnp.zeros_like(ggk_ref)

    ggq_ref[...] += jnp.broadcast_to(q_gain_grad, ggq_ref.shape)
    ggk_ref[...] += jnp.broadcast_to(k_gain_grad, ggk_ref.shape)


def attention_backward(
    joined, dattended, terms, exact, inverse_sum, q_gain, k_gain, x_low, core, first, count, room,
    place=0, into=(), fold=(), origin=0, size=0,
):
    length = x_low.shape[0]

    def whole(shape):
        return pl.BlockSpec(shape, lambda p: (0, 0))

    last = (fold[0].shape[0] - origin - size) // (FIN // 8) if fold else 0

    def segment(i):
        return pl.BlockSpec(
            (pl.Element(size), pl.Element(D // 2)),
            lambda p: (pl.multiple_of(origin + FIN // 8 * jnp.minimum(2 * p + i, last), 32), 0),
        )

    gain = jax.ShapeDtypeStruct((HEAD, 128), f32)
    call = pl.pallas_call(
        partial(backward_kernel, folds=bool(fold)),
        grid=(count,),
        in_specs=[
            pl.BlockSpec((3, pair, length), lambda p: (0, first + p, 0)),
            pl.BlockSpec((pair, length), lambda p: (first + p, 0)),
            pl.BlockSpec((2, length, length), lambda p: (first + p, 0, 0)),
            pl.BlockSpec((pair, length), lambda p: (first + p, 0)),
            pl.BlockSpec((1, 8, length), lambda p: (first + p, 0, 0)),
            whole((HEAD, 128)), whole((HEAD, 128)), whole((length, D)), core_spec,
            *[pl.BlockSpec(memory_space=pl.ANY)] * len(into),
            *[segment(i) for i in range(2) for _ in fold],
        ],
        out_specs=[pl.BlockSpec((3, length, pair), lambda p: (0, 0, p))]
        + [pl.BlockSpec((3, pair, D // 2), lambda p: (0, place + p, 0))] * 2
        + [whole((HEAD, 128))] * 2
        + [pl.BlockSpec((2 * size, D // 2), lambda p: (p, 0))] * bool(fold),
        out_shape=[jax.ShapeDtypeStruct((3, length, count * pair), bf16)]
        + [jax.ShapeDtypeStruct((3, room * pair, D // 2), bf16)] * 2 + [gain] * 2
        + [jax.ShapeDtypeStruct(((last + 1) * size, D // 2), bf16)] * bool(fold),
        input_output_aliases={9 + i: 1 + i for i in range(len(into))},
        scratch_shapes=[
            pltpu.VMEM((2, length, HEAD + 16), bf16),
            pltpu.VMEM((2, HEAD, length), bf16),
            pltpu.VMEM((2, HEAD, length), bf16),
            pltpu.VMEM((2, HEAD + 16, length), bf16),
        ],
        compiler_params=pltpu.CompilerParams(vmem_limit_bytes=vmem_bytes),
        cost_estimate=pl.CostEstimate(
            flops=2 * count * 8 * length * length * 256,
            bytes_accessed=24 * length * count * pair + 4 * count * length * length,
            transcendentals=0,
        ),
        name="attention_backward",
    )
    outs = call(joined, dattended, terms, exact, inverse_sum, q_gain, k_gain, x_low, core, *into, *fold, *fold)
    return outs


def gelu_pair(u):
    z = jnp.abs(u) * 0.7071067811865476
    t = 1.0 / (1.0 + 0.3275911 * z)
    e = jnp.exp(-z * z)
    poly = t * (0.127414796 + t * (-0.142248368 + t * (0.7107068705 + t * (-0.7265760135 + t * 0.5307027145))))
    half = poly * e
    phi = jnp.where(u >= 0, 1.0 - half, half)
    return (u * phi, phi + u * (0.3989422804014327 * e))


def mlp_kernel(
    x_ref, gy_ref, wu_ref, wd_ref, core_ref,
    res_ref, gn_ref, keep_up, send_up, keep_down, send_down, act_ref, dup_ref,
):
    @pl.when(pl.program_id(0) == 0)
    def _():
        res_ref[...] = jnp.zeros_like(res_ref)
        gn_ref[...] = jnp.zeros_like(gn_ref)

    for begin in range(0, wu_ref.shape[0], tile_rows):
        units = slice(begin, begin + tile_rows)
        upward = contract(x_ref[...], wu_ref[units], 1, 1).astype(bf16).astype(f32)
        grad_hidden = contract(gy_ref[...], wd_ref[units], 1, 1)
        active, slope = gelu_pair(upward)
        act_ref[:, units] = active.astype(bf16)
        dup_ref[:, units] = (grad_hidden * slope).astype(bf16)
    active, dupward = act_ref[...], dup_ref[...]
    res_ref[...] += nn(active, wd_ref[...])
    gn_ref[...] += nn(dupward, wu_ref[...])
    halves(contract(active, gy_ref[...], 0, 0).astype(bf16), core_ref, keep_down, send_down)
    halves(contract(dupward, x_ref[...], 0, 0).astype(bf16), core_ref, keep_up, send_up)


def mlp(x_low, grad_y, w_in_all, w_out_all, core):
    length = x_low.shape[0]
    hidden = w_in_all.shape[0] - QKV
    tile = D
    whole = pl.BlockSpec((length, D), lambda t: (0, 0))
    total = jax.ShapeDtypeStruct((length, D), f32)
    grad = jax.ShapeDtypeStruct((hidden, D // 2), bf16)
    call = pl.pallas_call(
        mlp_kernel,
        grid=(hidden // tile,),
        in_specs=[
            whole,
            whole,
            pl.BlockSpec((tile, D), lambda t: (t + QKV // tile, 0)),
            pl.BlockSpec((tile, D), lambda t: (t + D // tile, 0)),
            core_spec,
        ],
        out_specs=[whole, whole] + [pl.BlockSpec((tile, D // 2), lambda t: (t, 0))] * 4,
        out_shape=[total, total] + [grad] * 4,
        scratch_shapes=[pltpu.VMEM((length, tile), bf16)] * 2,
        compiler_params=pltpu.CompilerParams(vmem_limit_bytes=vmem_bytes),
        cost_estimate=pl.CostEstimate(
            flops=18 * length * D * hidden,
            bytes_accessed=12 * length * D + 8 * hidden * D,
            transcendentals=length * hidden,
        ),
        name="mlp",
    )
    return call(x_low, grad_y, w_in_all, w_out_all, core)


def input_kernel(*refs, calls):
    grads = refs[:calls]
    w_ref, normed_ref, tokens_ref, gy_ref, gain_ref, out_ref, ln_ref, total = refs[calls:]
    step = pl.program_id(0)

    @pl.when(step == 0)
    def _():
        total[...] = normed_ref[...]

    begin = 0
    sums = []
    for ref in grads:
        sums.append(nn(ref[0], w_ref[begin : begin + ref.shape[2], :]))
        begin += ref.shape[2]
    total[...] += sum(sums)

    @pl.when(step == pl.num_programs(0) - 1)
    def _():
        x_hat, x_inverse = normalize(tokens_ref[...].astype(f32))
        grad_normed = total[...]
        ln_ref[...] = jnp.sum(grad_normed * x_hat, axis=0, keepdims=True)
        back = norm_backward(grad_normed * gain_ref[...], x_hat, x_inverse)
        out_ref[...] = (gy_ref[...].astype(f32) + back).astype(bf16)


def input_gradient(grads, w_in_all, normed, tokens, grad_y, gain):
    length = tokens.shape[0]
    whole = pl.BlockSpec((length, D), lambda p: (0, 0))
    row = pl.BlockSpec((1, D), lambda p: (0, 0))
    call = pl.pallas_call(
        partial(input_kernel, calls=len(grads)),
        grid=(3,),
        in_specs=[pl.BlockSpec((1, length, grad.shape[2]), lambda p: (p, 0, 0)) for grad in grads]
        + [pl.BlockSpec((D, D), lambda p: (p, 0)), whole, whole, whole, row],
        out_specs=[whole, row],
        out_shape=[jax.ShapeDtypeStruct((length, D), bf16), jax.ShapeDtypeStruct((1, D), f32)],
        scratch_shapes=[pltpu.VMEM((length, D), f32)],
        compiler_params=pltpu.CompilerParams(vmem_limit_bytes=vmem_bytes),
        cost_estimate=pl.CostEstimate(
            flops=2 * length * D * QKV, bytes_accessed=20 * length * D, transcendentals=length
        ),
        name="input_gradient",
    )
    out, ln_grad = call(*grads, w_in_all, normed, tokens, grad_y, gain.reshape(1, D))
    return (out, ln_grad[0])


def split(values):
    high = values.astype(bf16)
    return (high, (values - high.astype(f32)).astype(bf16))


def newton_kernel(
    near_ref, other_ref, own_ref, far_ref, core_ref, o_ref, gh, gl, sh, sl, ph, pw, g32, x32
):
    count = D // tile_rows

    def span(i):
        return slice(i * tile_rows, (i + 1) * tile_rows)

    def store(high_ref, low_ref, i, j, value):
        high_ref[span(i), span(j)], low_ref[span(i), span(j)] = split(value)
        if i != j:
            high_ref[span(j), span(i)], low_ref[span(j), span(i)] = split(value.T)

    def symmetric(ah, al, bh, bl, post):
        for i in range(count):
            for j in range(i, count):
                rows, columns = span(i), span(j)
                post(
                    i,
                    j,
                    nn(ah[rows, :], bh[:, columns])
                    + (nn(ah[rows, :], bl[:, columns]) + nn(al[rows, :], bh[:, columns])),
                )

    def squared(ah, al, post):
        for i in range(count):
            for j in range(i, count):
                rows, columns = span(i), span(j)
                mixed = nn(ah[rows, :], al[:, columns])
                other = mixed if i == j else nn(ah[columns, :], al[:, rows])
                post(i, j, nn(ah[rows, :], ah[:, columns]) + (mixed + other.T))

    def sweep(last):
        def keep_factor(i, j, value):
            value = ns_cubic * g32[span(i), span(j)] + ns_quintic * value
            if i == j:
                shape = (tile_rows, tile_rows)
                diagonal = lax.broadcasted_iota(jnp.int32, shape, 0) == lax.broadcasted_iota(jnp.int32, shape, 1)
                value = value + jnp.where(diagonal, ns_linear, 0.0)
            store(ph, pw, i, j, value)

        def keep_gram(i, j, value):
            g32[span(i), span(j)] = value
            store(gh, gl, i, j, value)

        squared(gh, gl, keep_factor)
        xh, xl = split(x32[...])
        x32[...] = nn(xh, ph[...]) + (nn(xh, pw[...]) + nn(xl, ph[...]))
        if not last:
            symmetric(gh, gl, ph, pw, partial(store, sh, sl))
            symmetric(sh, sl, ph, pw, keep_gram)

    half = D // 2
    first_core = core_ref[0] == 0
    left = jnp.where(first_core, near_ref[...], other_ref[...])
    side = jnp.where(first_core, other_ref[:half], near_ref[:half])
    corner = left[:half]
    i = lax.broadcasted_iota(jnp.int32, (half, half), 0)
    j = lax.broadcasted_iota(jnp.int32, (half, half), 1)
    corner_t = corner.T
    first = jnp.where(i <= j, corner, corner_t)
    last = jnp.where(i > j, corner, jnp.where(i == j, left[half : half + 1], corner_t))
    trace = jnp.sum(jnp.where(i == j, first + last, 0.0), axis=0, keepdims=True)
    trace = jnp.sum(trace, axis=1, keepdims=True)
    inverse = 1.0 / (jnp.sqrt(trace) + 1e-07)
    square = inverse * inverse
    g32[:half, :half] = first * square
    g32[half:, half:] = last * square
    g32[:half, half:] = side * square
    g32[half:, :half] = side.T * square
    rows = own_ref.shape[0]
    x32[:rows] = own_ref[...] * inverse
    x32[rows:] = far_ref[...] * inverse
    gh[...], gl[...] = split(g32[...])

    @pl.loop(0, 4)
    def _(k):
        sweep(False)

    sweep(True)
    o_ref[...] = x32[...].astype(bf16)


def newton(folded, far_folded, own_rows, far_rows, core):
    rows = own_rows.shape[0] + far_rows.shape[0]
    whole = pl.BlockSpec(memory_space=pltpu.VMEM)
    call = pl.pallas_call(
        newton_kernel,
        in_specs=[whole] * 4 + [core_spec],
        out_specs=whole,
        out_shape=jax.ShapeDtypeStruct((rows, D), bf16),
        scratch_shapes=[pltpu.VMEM((D, D), bf16)] * 6 + [pltpu.VMEM((D, D), f32), pltpu.VMEM((rows, D), f32)],
        compiler_params=pltpu.CompilerParams(vmem_limit_bytes=vmem_bytes),
        cost_estimate=pl.CostEstimate(
            flops=30 * D * D * (2 * D + rows), bytes_accessed=4 * D * D + 6 * rows * D, transcendentals=0
        ),
        name="newton",
    )
    return call(folded, far_folded, own_rows, far_rows, core)


def update_kernel(in_ref, in_far_ref, out_ref, out_far_ref, wi_ref, wo_ref, place_ref, in_new, out_new, held, *, first):
    def new(weights, ortho, size):
        rate = muon_rate * (size / D) ** 0.5
        return weights.astype(f32) * (1 - muon_rate * muon_decay) - rate * ortho.astype(f32)

    first_core = place_ref[0] == 0
    for near_ref, far_ref, total in ((in_ref, in_far_ref, None), (out_ref, out_far_ref, out_new)):
        size = far_ref.shape[0] // 2
        all_near, all_far, weights = near_ref[...].astype(f32), far_ref[...].astype(f32), wo_ref[...].astype(f32)
        for chip in range(2):
            rows = slice(chip * size, (chip + 1) * size)
            near, far = all_near[rows], all_far[rows]
            begin = 2 * chip * size
            both = (jnp.where(first_core, near, far), jnp.where(first_core, far, near))
            for i in range(2):
                spot = slice(begin + i * size, begin + (i + 1) * size)
                if total is None:
                    held[spot] = both[i]
                else:
                    total[spot] = new(weights[spot], both[i], FOUT)
    rows = in_new.shape[0]
    if first == rows:
        in_new[...] = new(wi_ref[...], held[...], FIN)
        return
    start = pl.multiple_of(place_ref[1], 32)
    cut, rest = first // 2, (rows - first) // 2
    pieces = jnp.concatenate([held[cut : cut + rest], held[rows // 2 + cut :]], axis=0)
    in_new[: rows - first] = new(wi_ref[: rows - first], pieces, FIN)
    in_new[first:] = jnp.where(
        lax.broadcasted_iota(jnp.int32, (rows - first, 1), 0) < start, in_new[first:], new(wi_ref[first:], pieces, FIN)
    )
    spot = pl.ds(start, first)
    pieces = jnp.concatenate([held[:cut], held[rows // 2 : rows // 2 + cut]], axis=0)
    in_new[spot] = new(wi_ref[spot], pieces, FIN)


def update(ortho_in, far_in, ortho_out, far_out, w_in, w_out, place, first):
    whole = pl.BlockSpec(memory_space=pltpu.VMEM)
    call = pl.pallas_call(
        partial(update_kernel, first=first),
        in_specs=[whole] * 6 + [core_spec],
        out_specs=[whole] * 2,
        out_shape=[jax.ShapeDtypeStruct(w.shape, f32) for w in (w_in, w_out)],
        scratch_shapes=[pltpu.VMEM(w_in.shape, f32)],
        compiler_params=pltpu.CompilerParams(vmem_limit_bytes=vmem_bytes),
        cost_estimate=pl.CostEstimate(flops=4 * w_in.size, bytes_accessed=14 * w_in.size, transcendentals=0),
        name="update",
    )
    return call(ortho_in, far_in, ortho_out, far_out, w_in, w_out, place)


def gram_kernel(m_ref, extra_ref, core_ref, o_ref):
    half = D // 2
    left, right = slice(0, half), slice(half, D)

    def product(a, b):
        ah, al = split(m_ref[:, a])
        bh, bl = split(m_ref[:, b])
        return contract(ah, bh, 0, 0) + (contract(ah, bl, 0, 0) + contract(al, bh, 0, 0))

    o_ref[half:, :] = extra_ref[...]

    @pl.when(core_ref[0] == 0)
    def _():
        i = lax.broadcasted_iota(jnp.int32, (half, half), 0)
        j = lax.broadcasted_iota(jnp.int32, (half, half), 1)
        last = product(right, right)
        o_ref[:half, :] = jnp.where(i <= j, product(left, left), last)
        o_ref[half : half + 1, :] = jnp.sum(jnp.where(i == j, last, 0.0), axis=0, keepdims=True)

    @pl.when(core_ref[0] != 0)
    def _():
        o_ref[:half, :] = product(left, right)


def folded_gram(rows, extra, core):
    rows = jnp.pad(rows, ((0, -rows.shape[0] % 16), (0, 0)))
    whole = pl.BlockSpec(memory_space=pltpu.VMEM)
    call = pl.pallas_call(
        gram_kernel,
        in_specs=[whole, whole, core_spec],
        out_specs=whole,
        out_shape=jax.ShapeDtypeStruct((D // 2 + extra_rows, D // 2), f32),
        compiler_params=pltpu.CompilerParams(vmem_limit_bytes=vmem_bytes),
        cost_estimate=pl.CostEstimate(
            flops=4 * rows.shape[0] * D * D, bytes_accessed=8 * rows.shape[0] * D, transcendentals=0
        ),
        name="gram",
    )
    return call(rows, extra, core)


def bits(size):
    return [1 << b for b in range(size.bit_length() - 1)]


def take(values, index, axis):
    return lax.dynamic_index_in_dim(values, index, axis, keepdims=False)


def after(value, *others):
    return lax.optimization_barrier((value, *others))[0]


def exchange(values, axis, bit, fill=()):
    size = lax.axis_size(axis)
    return after(lax.ppermute(values, axis, [(i, i ^ bit) for i in range(size)]), *fill)


def sum_steps(values, halving, full):
    fill = yield values
    for axis, bit in halving:
        side = (lax.axis_index(axis) // bit) % 2
        pieces = values.reshape(2, values.shape[0] // 2, values.shape[1])
        values = take(pieces, side, 0) + exchange(take(pieces, 1 - side, 0), axis, bit, fill)
        fill = yield values
    for axis, bit in full:
        values = values + exchange(values, axis, bit, fill)
        fill = yield values


def halve(parts, axis, name, bit):
    side = (lax.axis_index(name) // bit) % 2
    sent = [take(part, 1 - side, axis) for part in parts]

    def receive(*fill):
        kept = jnp.concatenate([take(part, side, axis) for part in parts], axis=0)
        return (kept, exchange(jnp.concatenate(sent, axis=0), name, bit, fill))

    return sent, receive


def added(kept, other):
    return (kept.astype(f32) + other.astype(f32)).astype(bf16)


def scatter_one(*parts):
    wide = lax.axis_size("wide")
    columns = parts[0].shape[-1]
    rows = sum(part.size for part in parts) // (2 * wide * columns)
    cut = rows // 16 * 8
    parts = [part.reshape(-1, 2, 2, rows, columns) for part in parts]
    sent_a, receive_a = halve([part[:, :, :, :cut] for part in parts], 1, "wide", 1)
    sent_b, receive_b = halve([part[:, :, :, cut:] for part in parts], 2, "nar", 2)
    return sent_a + sent_b, lambda *fill: (added(*receive_a(*fill)), added(*receive_b(*fill)))


def split_kernel(*refs, pairs, rows):
    *parts, place_ref, sent_y, kept_y, sent_x, kept_x, held = refs
    begin = 0
    for paired in pairs:
        values = parts.pop(0)[...].astype(f32)
        if paired:
            values = values + parts.pop(0)[...].astype(f32)
        held[begin : begin + values.shape[0]] = values
        begin += values.shape[0]
    cut = kept_y.shape[2]
    for z in range(kept_y.shape[0]):
        for j in range(2):
            for near, out_y, out_x in ((True, kept_y, kept_x), (False, sent_y, sent_x)):
                y = place_ref[0] if near else 1 - place_ref[0]
                x = place_ref[1] if near else 1 - place_ref[1]
                first = pl.ds(pl.multiple_of(((2 * z + y) * 2 + j) * rows, 8), cut)
                out_y[z, j] = held[first].astype(bf16)
                second = pl.ds(pl.multiple_of(((2 * z + j) * 2 + x) * rows + cut, 8), rows - cut)
                out_x[z, j] = held[second].astype(bf16)


def split_one(rows, *parts):
    half = D // 2
    cut = rows // 16 * 8
    far = lax.axis_size("wide") // 2
    place = jnp.stack([lax.axis_index("wide") % 2, lax.axis_index("nar") // 2])
    terms = [term.reshape(-1, half) for part in parts for term in (part if isinstance(part, tuple) else (part,))]
    whole = pl.BlockSpec(memory_space=pltpu.VMEM)
    shapes = [(far, 2, cut, half)] * 2 + [(far, 2, rows - cut, half)] * 2
    call = pl.pallas_call(
        partial(split_kernel, pairs=[isinstance(part, tuple) for part in parts], rows=rows),
        in_specs=[whole] * len(terms) + [core_spec],
        out_specs=[whole] * 4,
        out_shape=[jax.ShapeDtypeStruct(shape, bf16) for shape in shapes],
        scratch_shapes=[pltpu.VMEM((4 * far * rows, half), f32)],
        compiler_params=pltpu.CompilerParams(vmem_limit_bytes=vmem_bytes),
        cost_estimate=pl.CostEstimate(
            flops=8 * far * rows * half, bytes_accessed=24 * far * rows * half, transcendentals=0
        ),
        name="split",
    )
    sent_y, kept_y, sent_x, kept_x = call(*terms, place)

    def arrive(*fill):
        return (exchange(sent_y, "wide", 1, fill), exchange(sent_x, "nar", 2, fill))

    return [sent_y, sent_x], arrive, lambda other_y, other_x: (added(kept_y, other_y), added(kept_x, other_x))


def scatter_two(held):
    sent_a, receive_a = halve(held[:1], 1, "nar", 2)
    sent_b, receive_b = halve(held[1:], 1, "wide", 1)

    def receive(*fill):
        kept, other = zip(receive_a(*fill), receive_b(*fill), strict=True)
        return added(jnp.concatenate(kept, axis=1), jnp.concatenate(other, axis=1))

    return sent_a + sent_b, receive


def scatter_rest(held):
    wide = lax.axis_size("wide")
    far = wide // 2
    place = lax.axis_index("wide") // 2
    sent = [take(held, place ^ shift, 0) for shift in range(1, far)]

    def receive(*fill):
        total = take(held, place, 0).astype(f32)
        for shift in reversed(range(1, far)):
            pairs = [(i, i ^ (2 * shift)) for i in range(wide)]
            total = total + after(lax.ppermute(sent[shift - 1], "wide", pairs), *fill).astype(f32)
        return total.astype(bf16)

    return sent, receive


def both_cores(values, *fill):
    other = exchange(values, "nar", 1, fill)
    return join(values, other, lax.axis_index("nar") % 2, 1).reshape(values.shape[0], D)


def ordered(values, other, side):
    return (jnp.where(side == 0, values, other), jnp.where(side == 0, other, values))


def join(values, other, side, axis):
    return jnp.stack(ordered(values, other, side), axis)


def gather(values):
    wide = lax.axis_size("wide")
    rows = values.shape[0]
    far = wide // 2
    place, side = lax.axis_index("wide") // 2, lax.axis_index("wide") % 2
    chip, core = lax.axis_index("nar") // 2, lax.axis_index("nar") % 2
    held = lax.dynamic_update_index_in_dim(jnp.zeros((far, rows, D), values.dtype), values, place, 0)
    for shift in range(1, far):
        pairs = [(i, i ^ (2 * shift)) for i in range(wide)]
        held = lax.dynamic_update_index_in_dim(held, lax.ppermute(values, "wide", pairs), place ^ shift, 0)
    cut = rows // 32 * 16
    first, second = held[:, :cut], held[:, cut:]
    first = join(first, exchange(first, "wide", 1), side, 1)
    second = join(second, exchange(second, "nar", 2), chip, 1)
    first = join(first, exchange(first, "nar", 2), chip, 2)
    second = join(second, exchange(second, "wide", 1), side, 1)
    held = jnp.concatenate([first, second], axis=3)
    return join(held, exchange(held, "nar", 1), core, 3).reshape(-1, D)


def on_device(tokens, cotangent, image_ids, w_in, w_out, gains, mom_in, mom_out, gain_m, gain_v):
    row_count = tokens.shape[0]
    rows_in = w_in.shape[0]
    rows_out = w_out.shape[0]
    nar_count = lax.axis_size("nar")
    wide_count = lax.axis_size("wide")
    nar_place = lax.axis_index("nar")
    share_in = rows_in // nar_count
    share_out = rows_out // nar_count
    everyone = ("wide", "nar")

    def share(rows, size):
        return lax.dynamic_slice_in_dim(rows, nar_place * size, size, 0)

    w_in_all = lax.all_gather(share(w_in, share_in), everyone, axis=0, tiled=True)
    w_out_all = gather(share(w_out, share_out))

    x_float = tokens.astype(f32)
    ln_gain = gains[:D]
    x_hat, x_inverse = normalize(x_float)
    x_low = (x_hat * ln_gain).astype(bf16)
    live = (image_ids.reshape(row_count) >= 0)[:, None]
    grad_y = jnp.where(live, cotangent, jnp.zeros_like(cotangent))

    core = (nar_place % 2).reshape(1)
    chip = nar_place // 2
    half = D // 2
    pairs = D // pair
    q_gain, k_gain = (
        jnp.broadcast_to(gain[:, None], (HEAD, 128)) for gain in (gains[D : D + HEAD], gains[D + HEAD :])
    )
    onek, penq = image_columns(image_ids.reshape(row_count))
    x_low = after(x_low, q_gain, k_gain, onek, penq)
    first = rows_in * 4 // 7
    second = rows_in - first
    parted = wide_count == 8 and first == half and rows_in == 672
    mlp_result, mlp_normed, keep_up, send_up, keep_down, send_down = mlp(x_low, grad_y, w_in_all, w_out_all, core)
    joined, dattended, attended, terms, exact, inverse_sum, keep_att, send_att = attention_forward(
        after(x_low, keep_down), grad_y, w_in_all, w_out_all, onek, penq, q_gain, k_gain, core
    )

    def backward(begin, count, earlier=(), **buffers):
        return attention_backward(
            joined, dattended, terms, exact, inverse_sum, q_gain, k_gain, after(x_low, *earlier), core, begin, count,
            **buffers,
        )

    def cores(keep, send, *fill):
        return added(keep, exchange(send, "nar", 1, fill)).reshape(-1, half)

    start = 96 * jnp.minimum(lax.axis_index("wide"), 3)
    row = lax.broadcasted_iota(jnp.int32, (rows_in, 1), 0)
    half_mom_out = lax.dynamic_slice_in_dim(mom_out, chip * (rows_out // 2), rows_out // 2, 0)
    wide_bits = bits(wide_count)
    halving = [("wide", wide_bits[0]), ("nar", 2)]
    full = [("wide", bit) for bit in wide_bits[1:]]

    def begin_out(part):
        zeros = jnp.zeros((extra_rows, half), f32)
        steps = sum_steps(folded_gram(muon_beta * half_mom_out + part.astype(f32), zeros, core), halving, full)
        return (steps, next(steps))

    if parted:
        def pair_of(keep, send, *fill):
            return (keep, exchange(send, "nar", 1, fill))

        down = pair_of(keep_down, send_down, keep_att)
        up = pair_of(keep_up, send_up, keep_att)
        sent, arrive, combine = split_one(rows_out // 2, pair_of(keep_att, send_att), down)
        dqkv_a, keep_a, send_a, q_grad_a, k_grad_a, up_a = backward(0, 3, sent, room=3, fold=up, size=first)
        sent, receive = scatter_two(combine(*arrive(keep_a)))
        dqkv_b, keep_b, send_b, q_grad_b, k_grad_b = backward(3, 1, [keep_a, *sent], room=3)
        sent_o, receive_o = scatter_rest(receive(dqkv_b))
        sent_a, arrive_a, combine_a = split_one(first // 2, pair_of(keep_a, send_a, dqkv_b), up_a)
        dqkv_c, keep_b, send_b, q_grad_c, k_grad_c, up_b = backward(
            4, 2, [*sent_a, *sent_o], room=3, place=1, into=(keep_b, send_b), fold=up, origin=first, size=second
        )
        part_out = receive_o(dqkv_c)
        sent_a, receive_a = scatter_two(combine_a(*arrive_a(dqkv_c)))
        sent_b, arrive_b, combine_b = split_one(second // 2, pair_of(keep_b, send_b, part_out, *sent_a), up_b)
        part_out = both_cores(part_out, *sent_b)
        steps_out, folded_out = begin_out(after(part_out, *sent_b))
        mom_in_late = after(mom_in, folded_out)
        held_b = combine_b(*arrive_b(folded_out))
        sent_b, receive_b = scatter_two(held_b)
        folded_out = steps_out.send(sent_b)
        held_a = receive_a(*sent_b)
        held_b = receive_b(held_a, folded_out)
        sent, receive = scatter_rest(jnp.concatenate([held_a, held_b], axis=1))
        grad_tokens, ln_grad = input_gradient(
            [dqkv_a, dqkv_b, dqkv_c], w_in_all, after(mlp_normed, *sent), tokens, grad_y, ln_gain
        )
        far_out = exchange(after(part_out, *sent), "nar", 2, (grad_tokens,))
        folded_out = steps_out.send((grad_tokens,))
        part_in = receive(grad_tokens, far_out, folded_out)
        steps_done = 2
        q_gain_grad = (q_grad_a + q_grad_b + after(q_grad_c, grad_tokens))[:, 0]
        k_gain_grad = (k_grad_a + k_grad_b + after(k_grad_c, grad_tokens))[:, 0]

        def halved(rows, chip):
            inside = lax.dynamic_slice_in_dim(rows, start, first, 0)
            others = jnp.where(row[:second] < start, rows[:second], rows[first:])
            return jnp.concatenate(
                [
                    lax.dynamic_slice_in_dim(inside, chip * (first // 2), first // 2, 0),
                    lax.dynamic_slice_in_dim(others, chip * (second // 2), second // 2, 0),
                ],
                axis=0,
            )

        def rejoined(near, far):
            cut = first // 2
            a, b = jnp.concatenate([near[:cut], far[:cut]], 0), jnp.concatenate([near[cut:], far[cut:]], 0)
            a = lax.dynamic_update_slice_in_dim(jnp.zeros((rows_in, D), a.dtype), a, start, 0)
            empty = jnp.zeros((first, D), b.dtype)
            below = jnp.concatenate([b, empty], axis=0)
            above = jnp.concatenate([empty, b], axis=0)
            inside = (row >= start) & (row < start + first)
            return jnp.where(inside, a, jnp.where(row < start, below, above))

    else:
        dqkv, keep_a, send_a, q_gain_grad, k_gain_grad = backward(0, pairs, room=pairs)
        q_gain_grad, k_gain_grad = q_gain_grad[:, 0], k_gain_grad[:, 0]
        grad_tokens, ln_grad = input_gradient([dqkv], w_in_all, mlp_normed, tokens, grad_y, ln_gain)

        def scattered(*parts):
            held = scatter_one(jnp.concatenate(parts, axis=0))[1]()
            return scatter_rest(scatter_two(held)[1]())[1]()

        part_out = both_cores(scattered(cores(keep_att, send_att), cores(keep_down, send_down)))
        steps_out, folded_out = begin_out(part_out)
        mom_in_late = mom_in
        steps_done = 0
        far_out = exchange(part_out, "nar", 2)
        part_in = scattered(cores(keep_a, send_a), cores(keep_up, send_up))

        def halved(rows, chip):
            return lax.dynamic_slice_in_dim(rows, chip * (rows_in // 2), rows_in // 2, 0)

        def rejoined(near, far):
            return jnp.concatenate([near, far], axis=0)

    part_in = both_cores(part_in)
    gain_terms = jnp.concatenate([ln_grad, q_gain_grad, k_gain_grad])
    count = gain_terms.shape[0]
    extra = jnp.pad(gain_terms, (half, (extra_rows - 1) * half - count)).reshape(extra_rows, half)
    momenta_in = muon_beta * halved(mom_in_late, chip) + part_in.astype(f32)
    steps_in = sum_steps(folded_gram(momenta_in, extra, core), halving, full)
    folded_in = next(steps_in)

    half_in, half_out = rows_in // 4, rows_out // 4

    def mine(rows, size):
        return lax.dynamic_slice_in_dim(rows, core[0] * size, size, 0)

    def fitted(rows):
        return jnp.pad(rows, ((0, half_in - half_out), (0, 0)))

    far_in = exchange(part_in, "nar", 2)
    own_rows = jnp.where(
        chip == 0,
        mine(momenta_in, half_in),
        fitted(mine(muon_beta * half_mom_out + part_out.astype(f32), half_out)),
    )
    far_mom = jnp.where(
        chip == 0,
        mine(halved(mom_in_late, 1 - chip), half_in),
        fitted(mine(lax.dynamic_slice_in_dim(mom_out, (1 - chip) * (rows_out // 2), rows_out // 2, 0), half_out)),
    )
    far_rows = jnp.where(chip == 0, mine(far_in, half_in), fitted(mine(far_out, half_out)))
    far_rows = muon_beta * far_mom + far_rows.astype(f32)
    steps = len(halving) + len(full)
    folded_out = steps_out.send((folded_in,))
    steps_done += 1
    for step in range(steps):
        fill = {0: (far_in, folded_out), len(halving) + 1: (own_rows, far_rows)}.get(step, ())
        folded_in = steps_in.send(fill)
        if steps_done < steps:
            folded_out = steps_out.send((folded_in,))
            steps_done += 1
    own, far = ordered(folded_in, folded_out, chip)
    folded = join(own, exchange(far, "nar", 2), chip, 0).reshape(-1, half)
    branch = mlp_result + nn(after(attended, folded), w_out_all[:D])
    result = (tokens.astype(f32) + branch).astype(bf16)
    side = lax.axis_index("wide") % 2
    folded = join(folded, exchange(folded, "wide", 1, (result,)), side, 0).reshape(-1, half)
    far_folded = exchange(folded, "nar", 1)
    ortho = newton(folded, far_folded, own_rows, far_rows, core)
    extra = folded[half : half + 8] + far_folded[half : half + 8]
    extra = ordered(extra, exchange(after(extra, ortho), "nar", 2), chip)[0].reshape(8 * half)
    grad_gains = extra[half : half + count]
    far_out, far_in = after(far_out, ortho), after(far_in, ortho)
    grad_w_out = join(part_out, far_out, chip, 0).reshape(rows_out, D).astype(f32)
    mom_out_new = muon_beta * mom_out + grad_w_out
    grad_w_in = after(rejoined(*ordered(part_in, far_in, chip))).astype(f32)
    mom_in_new = muon_beta * mom_in + grad_w_in

    other = exchange(ortho, "nar", 2, (mom_in_new, mom_out_new, grad_gains))
    ortho_in, ortho_out = ordered(ortho, other, chip)
    ortho_out = jnp.concatenate([ortho_out[half_in : half_in + half_out], ortho_out[:half_out]], axis=0)
    far_in, far_out = (exchange(rows, "nar", 1) for rows in (ortho_in, ortho_out))
    w_in_new, w_out_new = update(
        ortho_in, far_in, ortho_out, far_out, w_in, w_out, jnp.stack([core[0], start]), first if parted else rows_in
    )
    gain_m_new = adam_first * gain_m + (1 - adam_first) * grad_gains
    gain_v_new = adam_second * gain_v + (1 - adam_second) * grad_gains * grad_gains
    gains_new = gains - adam_rate * (gain_m_new / (1 - adam_first**STEP)) / (
        jnp.sqrt(gain_v_new / (1 - adam_second**STEP)) + adam_eps
    )
    return (
        result,
        grad_tokens,
        grad_w_in,
        grad_w_out,
        grad_gains,
        mom_in_new,
        mom_out_new,
        gain_m_new,
        gain_v_new,
        w_in_new,
        w_out_new,
        gains_new,
    )


def solution(mesh):
    rows = P(("nar", "wide"), None)
    wide = P("wide", None)
    return jax.shard_map(
        on_device,
        mesh=mesh,
        in_specs=(rows, rows, rows, wide, wide, P(), wide, wide, P(), P()),
        out_specs=(rows, rows, wide, wide, P(), wide, wide, P(), P(), wide, wide, P()),
        check_vma=False,
    )
```
